32 devices in a mesh: fsdp: 4 (over x, core), ctx: 8 (over z, y).
Axes of the slice: x: 2, y: 2, z: 4, core: 2. Of those that a mesh axis runs over, the one named last changes fastest.
Arguments:
- inputs: bfloat16 [4, 1024, 1600], P('fsdp', 'ctx'), may hold values from -6 to 6
- cotangent: bfloat16 [4, 1024, 1600], P('fsdp', 'ctx'), may hold values from -6 to 6
- slot_order: int32 [4, 16], P('fsdp'), may hold values from 0 to 15, each once within a row
- weights: bfloat16 [240000, 128], P(('fsdp', 'ctx')), may hold values from -0.61 to 0.61
- vectors: bfloat16 [12, 1600], P('fsdp', 'ctx'), may hold values from -1.2 to 1.4
- first_w: float32 [240000, 128], P(('fsdp', 'ctx')), may hold values from -25.728 to 25.728
- second_w: float32 [240000, 128], P(('fsdp', 'ctx')), may hold values from 0.025 to 5.912986
- first_vec: float32 [12, 1600], P('fsdp', 'ctx'), may hold values from -42.624 to 42.624
- second_vec: float32 [12, 1600], P('fsdp', 'ctx'), may hold values from 0.36864 to 16.42496
Outputs:
- outputs: bfloat16 [4, 1024, 1600], P('fsdp', 'ctx')
- input_grad: bfloat16 [4, 1024, 1600], P('fsdp', 'ctx')
- moment_w: float32 [240000, 128], P(('fsdp', 'ctx'))
- squares_w: float32 [240000, 128], P(('fsdp', 'ctx'))
- weight_w: float32 [240000, 128], P(('fsdp', 'ctx'))
- moment_vec: float32 [12, 1600], P('fsdp', 'ctx')
- squares_vec: float32 [12, 1600], P('fsdp', 'ctx')
- weight_vec: float32 [12, 1600], P('fsdp', 'ctx')
The draws below stay inside these ranges and needn't reach their ends.
Inputs may be any that keep to these rules, and one draw needn't show every extreme that they name: Each row is a permutation: slot j of a sequence (its rows j * 64 to j * 64 + 63) holds the positions slot_order[seq, j] * 64 onward.
All inputs are finite; a program needn't handle non-finite values.
Results may differ from the reference program's by a relative error of at most 0.025.
Values may be sent and summed in bfloat16 or wider, within the bound.
A program may use at most 512 MiB of HBM per device.

```python
import math
import jax
import jax.numpy as jnp
from jax import lax

D = 1600
HEADS = 25
HD = 64
FF = 6400
VECS = 12
STEP = 10
BLK = 64
NSEQ = 4
LEN = 1024
ALLTOK = 4096
PROWS = 240000
N_CTX = 8


def row_scales():
    return jnp.array([0.9, 0.9, 0.5, 0.5, 1.0, 0.6, 0.6, 1.0, 0.3, 0.3, 0.3, 0.3], jnp.float32)


def segment_scale(first_scale, second_scale, third_scale, fourth_scale):
    rows_index = lax.broadcasted_iota(jnp.int32, (PROWS, 128), 0)
    cols_index = lax.broadcasted_iota(jnp.int32, (PROWS, 128), 1)
    entry = rows_index * 128 + cols_index
    first_end = 3 * D * D
    second_end = 4 * D * D
    third_end = 4 * D * D + D * FF
    return jnp.where(entry < first_end, first_scale, jnp.where(entry < second_end, second_scale, jnp.where(entry < third_end, third_scale, fourth_scale))).astype(jnp.float32)


def draw_weights(key, part):
    key = jax.random.fold_in(key, 5)
    scale = segment_scale(D ** (-0.5), (D * 64 // LEN) ** (-0.5), D ** (-0.5), FF ** (-0.5))
    values = jax.random.truncated_normal(key, -6.0, 6.0, (PROWS, 128), jnp.float32)
    return (values * scale).astype(jnp.bfloat16)


def draw_first_w(key, part):
    key = jax.random.fold_in(key, 7)
    scale = segment_scale(0.055 * ALLTOK ** 0.5, 0.28 * NSEQ ** 0.5, 0.033 * ALLTOK ** 0.5, 0.067 * ALLTOK ** 0.5)
    values = jax.random.truncated_normal(key, -6.0, 6.0, (PROWS, 128), jnp.float32)
    return (values * scale).astype(jnp.float32)


def draw_second_w(key, part):
    key = jax.random.fold_in(key, 9)
    lowest = segment_scale(0.00025 * ALLTOK, 0.00625 * NSEQ, 9e-05 * ALLTOK, 0.00036 * ALLTOK)
    factor = jnp.exp(jax.random.uniform(key, (PROWS, 128), jnp.float32, 0.0, 1.3862944))
    return (lowest * factor).astype(jnp.float32)


def draw_vectors(key, part):
    key = jax.random.fold_in(key, 11)
    gain_key, bias_key = jax.random.split(key)
    gains = jax.random.uniform(gain_key, (VECS, D), jnp.float32, 0.6, 1.4)
    biases = 0.3 * jax.random.truncated_normal(bias_key, -4.0, 4.0, (VECS, D), jnp.float32)
    row_index = jnp.arange(VECS)[:, None]
    picked = jnp.where((row_index == 0) | (row_index == 5), gains, biases)
    return picked.astype(jnp.bfloat16)


def draw_first_vec(key, part):
    key = jax.random.fold_in(key, 23)
    scale = row_scales()[:, None] * 0.111 * ALLTOK ** 0.5
    values = jax.random.truncated_normal(key, -6.0, 6.0, (VECS, D), jnp.float32)
    return (values * scale).astype(jnp.float32)


def draw_second_vec(key, part):
    key = jax.random.fold_in(key, 37)
    factor = jnp.exp(jax.random.uniform(key, (VECS, D), jnp.float32, 0.0, 1.3862944))
    rows = row_scales()[:, None]
    return (factor * 0.001 * ALLTOK * rows * rows).astype(jnp.float32)


def levels(own_key, dims, cuts, smallest, largest):
    def one(dim, shards_of):
        steps = jax.random.uniform(jax.random.fold_in(jax.random.fold_in(own_key, 6), dim), (shards_of,), jnp.float32, smallest / len(cuts), largest / len(cuts))
        return jnp.repeat(jnp.exp(steps), dims[dim] // shards_of).reshape((-1,) + (1,) * (len(dims) - dim - 1))

    level = one(*cuts[0])
    for cut in cuts[1:]:
        level = level * one(*cut)
    return level


def gaussian(stream_key, extent, deviation, limit, cuts=(), kind=jnp.bfloat16):
    entries = jax.random.normal(stream_key, extent, jnp.float32) * deviation
    if len(cuts) > 0:
        entries = levels(stream_key, extent, cuts, -0.22, 0.18) * entries
    return jnp.clip(entries, min=-limit, max=limit).astype(kind)


def setup_inputs(seed: int = 0) -> dict:
    key_of = jax.random.split(jax.random.key(seed), 10)
    inputs = gaussian(key_of[0], (NSEQ, LEN, D), 1.0, 6.0, ((0, 4), (1, 8)))
    cotangent = gaussian(key_of[1], (NSEQ, LEN, D), 1.0, 6.0, ((0, 4), (1, 8)))
    slot_order = jax.vmap(lambda own: jax.random.permutation(own, 2 * N_CTX))(jax.random.split(key_of[2], NSEQ)).reshape((NSEQ, 2 * N_CTX)).astype(jnp.int32)
    weights = draw_weights(jax.random.fold_in(key_of[9], 71), 0)
    vectors = draw_vectors(jax.random.fold_in(key_of[9], 71), 0)
    first_w = draw_first_w(jax.random.fold_in(key_of[9], 71), 0)
    second_w = draw_second_w(jax.random.fold_in(key_of[9], 71), 0)
    first_vec = draw_first_vec(jax.random.fold_in(key_of[9], 71), 0)
    second_vec = draw_second_vec(jax.random.fold_in(key_of[9], 71), 0)
    return {"inputs": inputs, "cotangent": cotangent, "slot_order": slot_order, "weights": weights, "vectors": vectors, "first_w": first_w, "second_w": second_w, "first_vec": first_vec, "second_vec": second_vec}


highest = lax.Precision.HIGHEST
epsilon_norm = 1e-05
beta_first = 0.9
beta_second = 0.999
epsilon_adam = 1e-08
weight_decay = 0.1
rate_matrix = 0.1
rate_vector = 0.8

@jax.custom_vjp
def low(v):
    return lax.optimization_barrier(v.astype(jnp.bfloat16)).astype(jnp.float32)

@jax.custom_vjp
def low_back(v):
    return v

def low_keep(v):
    return (low(v), None)

def low_pass(kept, grad):
    return (grad,)

def back_keep(v):
    return (v, None)

def back_low(kept, grad):
    return (low(grad),)
low.defvjp(low_keep, low_pass)
low_back.defvjp(back_keep, back_low)

def unpack(flat):
    flat = flat.reshape(-1)
    first_end = 3 * D * D
    second_end = 4 * D * D
    third_end = 4 * D * D + D * FF
    return (flat[:first_end].reshape(D, 3 * D), flat[first_end:second_end].reshape(D, D), flat[second_end:third_end].reshape(D, FF), flat[third_end:].reshape(FF, D))

def normalize(value):
    center = value - lax.optimization_barrier(jnp.mean(value, -1, keepdims=True))
    spread = lax.optimization_barrier(jnp.mean(center * center, -1, keepdims=True))
    return center * lax.rsqrt(spread + epsilon_norm)

def attend(query, keys, values, query_pos, key_pos):
    scores = jnp.einsum('qhd,khd->hqk', query, keys, precision=highest) * 0.125
    scores = low_back(scores)
    allowed = key_pos[None, None, :] <= query_pos[None, :, None]
    scores = jnp.where(allowed, scores, -1e+30)
    peak = lax.optimization_barrier(jnp.max(scores, -1, keepdims=True))
    weights = jnp.exp(scores - peak)
    weights = weights / lax.optimization_barrier(jnp.sum(weights, -1, keepdims=True))
    weights = low(weights)
    return jnp.einsum('hqk,khd->qhd', weights, values, precision=highest)

def layer(tokens, w_qkv, w_out, w_fc, w_proj, vectors, positions):
    bias_fc = vectors[8:12].reshape(FF)
    h_first = low(normalize(tokens) * vectors[0] + vectors[1])
    zero_row = jnp.zeros((D,), jnp.float32)
    qkv = jnp.dot(h_first, w_qkv, precision=highest) + jnp.concatenate([vectors[2], zero_row, vectors[3]])
    qkv = low_back(low(qkv))
    query = qkv[:, :D].reshape(LEN, HEADS, HD)
    keys = qkv[:, D:2 * D].reshape(LEN, HEADS, HD)
    values = qkv[:, 2 * D:].reshape(LEN, HEADS, HD)
    span = math.gcd(512, LEN)
    blocks = LEN // span

    def one_block(item):
        return attend(item[0], keys, values, item[1], positions)
    mixed = lax.map(jax.checkpoint(one_block), (query.reshape(blocks, span, HEADS, HD), positions.reshape(blocks, span)))
    attn = low_back(low(mixed.reshape(LEN, D)))
    branch = low_back(jnp.dot(attn, w_out, precision=highest) + vectors[4])
    resid = tokens + branch
    h_second = low(normalize(resid) * vectors[5] + vectors[6])
    pre = low_back(jnp.dot(h_second, w_fc, precision=highest) + bias_fc)
    act = low(jax.nn.gelu(pre, approximate=True))
    return resid + jnp.dot(act, w_proj, precision=highest) + vectors[7]

def adamw(weight, grad, first, second, rate, decay):
    first = beta_first * first + (1.0 - beta_first) * grad
    second = beta_second * second + (1.0 - beta_second) * grad * grad
    first_hat = first / (1.0 - beta_first ** STEP)
    second_hat = second / (1.0 - beta_second ** STEP)
    weight = weight.astype(jnp.float32)
    updated = weight - rate * (first_hat / (jnp.sqrt(second_hat) + epsilon_adam) + decay * weight)
    return (first, second, updated)

def reference(inputs, cotangent, slot_order, weights, vectors, first_w, second_w, first_vec, second_vec):
    params = tuple(unpack(weights.astype(jnp.float32))) + (vectors.astype(jnp.float32),)
    place = jnp.arange(LEN, dtype=jnp.int32)

    def one_sequence(totals, item):
        tokens, back, order_row = item
        positions = (order_row[place // BLK] * BLK + place % BLK).astype(jnp.int32)

        def forward(x_in, p_qkv, p_out, p_fc, p_proj, p_vec):
            return layer(x_in, p_qkv, p_out, p_fc, p_proj, p_vec, positions)
        result, pull = jax.vjp(forward, tokens.astype(jnp.float32), *params)
        grads = pull(back.astype(jnp.float32))
        totals = tuple((total + grad for total, grad in zip(totals, grads[1:])))
        return (totals, (result.astype(jnp.bfloat16), grads[0].astype(jnp.bfloat16)))
    zeros = tuple((jnp.zeros_like(param) for param in params))
    totals, (outputs, input_grad) = lax.scan(one_sequence, zeros, (inputs, cotangent, slot_order))
    grad_flat = jnp.concatenate([totals[0].reshape(-1), totals[1].reshape(-1), totals[2].reshape(-1), totals[3].reshape(-1)]).reshape(PROWS, 128)
    new_w = adamw(weights, grad_flat, first_w, second_w, rate_matrix, weight_decay)
    new_vec = adamw(vectors, totals[4], first_vec, second_vec, rate_vector, 0.0)
    return (outputs, input_grad, new_w[0], new_w[1], new_w[2], new_vec[0], new_vec[1], new_vec[2])
```

```python
import jax
import jax.numpy as jnp
from jax import lax
from jax.experimental import pallas as pl
from jax.experimental.pallas import tpu as pltpu
from jax.sharding import PartitionSpec as P

HEADS = 25
HD = 64
FF = 6400
STEP = 10


epsilon_norm = 1e-05
beta_first = 0.9
beta_second = 0.999
epsilon_adam = 1e-08
weight_decay = 0.1
rate_matrix = 0.1
rate_vector = 0.8


def shifted(value, axis, steps):
    count = lax.axis_size(axis)
    pairs = [(source, (source + steps) % count) for source in range(count)]
    return lax.ppermute(value, axis, pairs)


def layer_norm(value, gain, shift):
    center = value - jnp.mean(value, -1, keepdims=True)
    spread = jnp.mean(center * center, -1, keepdims=True)
    return center * lax.rsqrt(spread + epsilon_norm) * gain + shift


def gelu_tanh(value):
    return jax.nn.gelu(value, approximate=True)


def key_positions(slot_order, first_slot, slots, block):
    groups = lax.dynamic_slice_in_dim(slot_order, first_slot, slots, 1)
    offsets = jnp.arange(block, dtype=jnp.int32)
    return (groups[:, :, None] * block + offsets).reshape(slot_order.shape[0], slots * block)


def unpack_flat(flat, width, hidden):
    flat = flat.reshape(-1)
    first_end = 3 * width * width
    second_end = 4 * width * width
    third_end = 4 * width * width + width * hidden
    return (
        flat[:first_end].reshape(width, 3 * width),
        flat[first_end:second_end].reshape(width, width),
        flat[second_end:third_end].reshape(width, hidden),
        flat[third_end:].reshape(hidden, width),
    )


def gather_params(weights, vectors):
    local = weights.reshape(1, weights.shape[0], weights.shape[1])
    part = (
        lax.all_gather(local, "fsdp", axis=0, tiled=True),
        lax.all_gather(vectors, "fsdp", axis=0, tiled=True),
    )
    return (
        lax.all_gather(part[0], "ctx", axis=1, tiled=True),
        lax.all_gather(part[1], "ctx", axis=1, tiled=True),
    )


def reduce_grads(grad_flat, grad_vec):
    part = (
        lax.psum_scatter(
            grad_flat.astype(jnp.bfloat16), "fsdp", scatter_dimension=0, tiled=True
        ).astype(jnp.float32),
        lax.psum_scatter(
            grad_vec.astype(jnp.bfloat16), "fsdp", scatter_dimension=0, tiled=True
        ).astype(jnp.float32),
    )
    return (
        lax.psum_scatter(
            part[0].astype(jnp.bfloat16), "ctx", scatter_dimension=1, tiled=True
        ).astype(jnp.float32),
        lax.psum_scatter(
            part[1].astype(jnp.bfloat16), "ctx", scatter_dimension=1, tiled=True
        ).astype(jnp.float32),
    )


def pass_grads(grad_pairs):
    return shifted(grad_pairs.astype(jnp.bfloat16), "ctx", 1).astype(grad_pairs.dtype)


def adamw(weight, grad, first, second, rate, decay):
    first = beta_first * first + (1.0 - beta_first) * grad
    second = beta_second * second + (1.0 - beta_second) * grad * grad
    first_hat = first / (1.0 - beta_first**STEP)
    second_hat = second / (1.0 - beta_second**STEP)
    weight = weight.astype(jnp.float32)
    updated = weight - rate * (first_hat / (jnp.sqrt(second_hat) + epsilon_adam) + decay * weight)
    return (first, second, updated)


def per_device_ring(
    inputs, cotangent, slot_order, weights, vectors, first_w, second_w, first_vec, second_vec
):
    seqs, rows, width = inputs.shape
    tokens = seqs * rows
    block = rows // 2
    cycle = lax.axis_size("ctx")
    shards = lax.axis_size("fsdp")
    me = lax.axis_index("ctx")
    full_flat, full_vec = gather_params(weights, vectors)
    full_qkv, full_out, full_fc, full_proj = unpack_flat(full_flat, width, FF)
    vec = full_vec.astype(jnp.float32)
    bias_fc = vec[8:].reshape(-1)
    x_in = inputs.reshape(tokens, width).astype(jnp.float32)
    h_first, pull_first = jax.vjp(layer_norm, x_in, vec[0], vec[1])
    h_first_b = h_first.astype(jnp.bfloat16)
    zero_row = jnp.zeros((width,), jnp.float32)
    qkv = jnp.dot(h_first_b, full_qkv, preferred_element_type=jnp.float32)
    qkv_b = (qkv + jnp.concatenate([vec[2], zero_row, vec[3]])).astype(jnp.bfloat16)
    query_heads = qkv_b[:, :width].reshape(seqs, rows, HEADS, HD)
    key_value = qkv_b[:, width:].reshape(seqs, rows, 2, width)
    query_pos = key_positions(slot_order, 2 * me, 2, block)

    def online(state, item):
        top, total, accum = state
        keys_i, values_i, pos_i = item
        scores = (
            jnp.einsum("sqhd,skhd->shqk", query_heads, keys_i, preferred_element_type=jnp.float32)
            * 0.125
        )
        allowed = pos_i[:, None, None, :] <= query_pos[:, None, :, None]
        scores = jnp.where(allowed, scores, -1e30)
        peak = jnp.maximum(top, jnp.max(scores, -1))
        weights_p = jnp.where(allowed, jnp.exp(scores - peak[..., None]), 0.0)
        factor = jnp.exp(top - peak)
        total = total * factor + jnp.sum(weights_p, -1)
        mixed = jnp.einsum(
            "shqk,skhd->sqhd",
            weights_p.astype(jnp.bfloat16),
            values_i,
            preferred_element_type=jnp.float32,
        )
        accum = accum * jnp.transpose(factor, (0, 2, 1))[..., None] + mixed
        return ((peak, total, accum), None)

    start_state = (
        jnp.full((seqs, HEADS, rows), -1e30, jnp.float32),
        jnp.zeros((seqs, HEADS, rows), jnp.float32),
        jnp.zeros((seqs, rows, HEADS, HD), jnp.float32),
    )
    state = start_state
    piece = lax.all_gather(key_value, "ctx", axis=1, tiled=True)
    count = piece.shape[1]
    turns = count // rows
    pos_all = key_positions(slot_order, jnp.int32(0) // block, count // block, block)
    stack = piece.reshape(seqs, turns, rows, 2, HEADS, HD).transpose(1, 0, 2, 3, 4, 5)
    pos_stack = pos_all.reshape(seqs, turns, rows).transpose(1, 0, 2)
    state, _ = lax.scan(online, state, (stack[:, :, :, 0], stack[:, :, :, 1], pos_stack))
    top, total, accum = state
    attn = accum / jnp.transpose(total, (0, 2, 1))[..., None]
    logsum = top + jnp.log(total)
    attn_b = attn.reshape(tokens, width).astype(jnp.bfloat16)
    resid = x_in + jnp.dot(attn_b, full_out, preferred_element_type=jnp.float32) + vec[4]
    h_second, pull_second = jax.vjp(layer_norm, resid, vec[5], vec[6])
    h_second_b = h_second.astype(jnp.bfloat16)
    pre = jnp.dot(h_second_b, full_fc, preferred_element_type=jnp.float32) + bias_fc
    act, pull_gelu = jax.vjp(gelu_tanh, pre)
    act_b = act.astype(jnp.bfloat16)
    result = resid + jnp.dot(act_b, full_proj, preferred_element_type=jnp.float32) + vec[7]
    outputs = result.astype(jnp.bfloat16).reshape(seqs, rows, width)
    back_b = cotangent.reshape(tokens, width)
    back = back_b.astype(jnp.float32)
    grad_proj = jnp.einsum("tf,td->fd", act_b, back_b, preferred_element_type=jnp.float32)
    grad_bp = jnp.sum(back, 0)
    dact = jnp.einsum("td,fd->tf", back_b, full_proj, preferred_element_type=jnp.float32)
    dpre_b = pull_gelu(dact)[0].astype(jnp.bfloat16)
    grad_fc = jnp.einsum("td,tf->df", h_second_b, dpre_b, preferred_element_type=jnp.float32)
    grad_bf = jnp.sum(dpre_b, 0, dtype=jnp.float32)
    dh_second = jnp.einsum("tf,df->td", dpre_b, full_fc, preferred_element_type=jnp.float32)
    dres_ln, grad_g2, grad_b2 = pull_second(dh_second)
    dresid = back + dres_ln
    dbranch_b = dresid.astype(jnp.bfloat16)
    grad_bo = jnp.sum(dbranch_b, 0, dtype=jnp.float32)
    grad_out = jnp.einsum("td,te->de", attn_b, dbranch_b, preferred_element_type=jnp.float32)
    dattn_b = jnp.einsum(
        "te,de->td", dbranch_b, full_out, preferred_element_type=jnp.float32
    ).astype(jnp.bfloat16)
    grad_heads = dattn_b.reshape(seqs, rows, HEADS, HD)
    delta = jnp.transpose(jnp.sum(grad_heads.astype(jnp.float32) * attn, -1), (0, 2, 1))

    def contribute(pair, source):
        pos_k = key_positions(slot_order, 2 * source, 2, block)
        key_h = pair[:, :, 0].reshape(seqs, rows, HEADS, HD)
        value_h = pair[:, :, 1].reshape(seqs, rows, HEADS, HD)
        scores = (
            jnp.einsum("sqhd,skhd->shqk", query_heads, key_h, preferred_element_type=jnp.float32)
            * 0.125
        )
        allowed = pos_k[:, None, None, :] <= query_pos[:, None, :, None]
        probs = jnp.where(allowed, jnp.exp(scores - logsum[..., None]), 0.0)
        dvalue = jnp.einsum(
            "shqk,sqhd->skhd",
            probs.astype(jnp.bfloat16),
            grad_heads,
            preferred_element_type=jnp.float32,
        )
        dprobs = jnp.einsum(
            "sqhd,skhd->shqk", grad_heads, value_h, preferred_element_type=jnp.float32
        )
        dscores = (probs * (dprobs - delta[..., None])).astype(jnp.bfloat16)
        dquery = (
            jnp.einsum("shqk,skhd->sqhd", dscores, key_h, preferred_element_type=jnp.float32)
            * 0.125
        )
        dkey = (
            jnp.einsum("shqk,sqhd->skhd", dscores, query_heads, preferred_element_type=jnp.float32)
            * 0.125
        )
        return (dquery, jnp.stack((dkey, dvalue), 2))

    dq_own, dkv_own = contribute(key_value, me)

    def turn(step, state):
        pair, dkv_acc, dq_acc = state
        pair = shifted(pair, "ctx", 1)
        dkv_acc = pass_grads(dkv_acc)
        source = (me - step) % cycle
        dq_part, dkv_part = contribute(pair, source)
        return (pair, dkv_acc + dkv_part, dq_acc + dq_part)

    final = lax.fori_loop(1, cycle, turn, (key_value, dkv_own, dq_own))
    dkv = pass_grads(final[1])
    dqkv_b = jnp.concatenate(
        [final[2].reshape(tokens, width), dkv.reshape(tokens, 2 * width)], 1
    ).astype(jnp.bfloat16)
    grad_qkv = jnp.einsum("td,te->de", h_first_b, dqkv_b, preferred_element_type=jnp.float32)
    bias_sums = jnp.sum(dqkv_b, 0, dtype=jnp.float32)
    dh_first = jnp.einsum("te,de->td", dqkv_b, full_qkv, preferred_element_type=jnp.float32)
    dx_ln, grad_g1, grad_b1 = pull_first(dh_first)
    input_grad = (dresid + dx_ln).astype(jnp.bfloat16).reshape(seqs, rows, width)
    grad_vec = jnp.concatenate(
        [
            jnp.stack(
                [
                    grad_g1,
                    grad_b1,
                    bias_sums[:width],
                    bias_sums[2 * width :],
                    grad_bo,
                    grad_g2,
                    grad_b2,
                    grad_bp,
                ]
            ),
            grad_bf.reshape(-1, width),
        ],
        0,
    )
    grad_flat = jnp.concatenate(
        [grad_qkv.reshape(-1), grad_out.reshape(-1), grad_fc.reshape(-1), grad_proj.reshape(-1)]
    ).reshape(shards, -1, 128)
    owned_flat, owned_vec = reduce_grads(grad_flat, grad_vec)
    owned_flat = owned_flat.reshape(weights.shape[0], 128)
    new_w = adamw(weights, owned_flat, first_w, second_w, rate_matrix, weight_decay)
    new_vec = adamw(vectors, owned_vec, first_vec, second_vec, rate_vector, 0.0)
    return (outputs, input_grad, new_w[0], new_w[1], new_w[2], new_vec[0], new_vec[1], new_vec[2])


MEMBERS = 8
GROUPS = 4
DEVICES = MEMBERS * GROUPS
MESH = pl.DeviceIdType.MESH
SLOTS = 4
VMEM_BYTES = 60 * 1024 * 1024
OUT_FIRST = 24
FC_FIRST = 32
PROJ_FIRST = 64


def head_start(member):
    return HEADS * member // MEMBERS


class Place:
    def __init__(self):
        self.fsdp, self.ctx = lax.axis_index("fsdp"), lax.axis_index("ctx")
        self.x, self.core = self.fsdp // 2, self.fsdp % 2
        self.far, self.near, self.y = self.ctx // 4, self.ctx // 2 % 2, self.ctx % 2
        self.me = self.member()
        self.group = 2 * self.y + self.far
        self.linear = self.fsdp * MEMBERS + self.ctx

    def member(self, x=None, near=None, core=None):
        x = self.x if x is None else x
        near = self.near if near is None else near
        core = self.core if core is None else core
        return 4 * core + 2 * near + x

    def target(self, x=None, core=None, far=None, near=None, y=None):
        x = self.x if x is None else x
        near = self.near if near is None else near
        core = self.core if core is None else core
        far = self.far if far is None else far
        y = self.y if y is None else y
        return (2 * x + core, 4 * far + 2 * near + y)

    def is_me(self, target):
        return jnp.logical_and(target[0] == self.fsdp, target[1] == self.ctx)


def greet_all(place):
    barrier = pltpu.get_barrier_semaphore()

    def one(step, carry):
        other = (place.linear + step) % DEVICES
        pl.semaphore_signal(
            barrier, inc=1, device_id=(other // MEMBERS, other % MEMBERS), device_id_type=MESH
        )
        return carry

    lax.fori_loop(1, DEVICES, one, 0)
    pl.semaphore_wait(barrier, DEVICES - 1)


def greet(targets):
    barrier = pltpu.get_barrier_semaphore()
    for target in targets:
        pl.semaphore_signal(barrier, inc=1, device_id=target, device_id_type=MESH)
    pl.semaphore_wait(barrier, len(targets))


def remote(source, landing, sems, index, target):
    return pltpu.make_async_remote_copy(
        src_ref=source,
        dst_ref=landing,
        send_sem=sems.at[0, index],
        recv_sem=sems.at[1, index],
        device_id=target,
        device_id_type=MESH,
    )


def arrived(landing, sem):
    pltpu.make_async_copy(landing, landing, sem).wait()


class Move:
    def __init__(self, place, source, landing, send_sem, recv_sem, target, valid=None):
        here = place.is_me(target)
        away = jnp.logical_not(here)
        if valid is not None:
            here, away = jnp.logical_and(here, valid), jnp.logical_and(away, valid)
        self.away = away
        self.copy = pltpu.make_async_remote_copy(
            src_ref=source,
            dst_ref=landing,
            send_sem=send_sem,
            recv_sem=recv_sem,
            device_id=target,
            device_id_type=MESH,
        )

        @pl.when(here)
        def _():
            pltpu.make_async_copy(source, landing, recv_sem).start()

        @pl.when(away)
        def _():
            self.copy.start()

    def sent(self):
        @pl.when(self.away)
        def _():
            self.copy.wait_send()


class Gather:
    def __init__(self, place, out, sems):
        p = place
        step, turn = 1 - p.core, p.core
        x1, near1 = p.x + step * (1 - 2 * p.x), p.near + turn * (1 - 2 * p.near)
        x2, near2 = p.x + turn * (1 - 2 * p.x), p.near + step * (1 - 2 * p.near)
        self.out, self.sems, self.me = out, sems, p.me
        self.first = p.target(x=x1, near=near1)
        self.second = p.target(x=x2, near=near2)
        self.other = p.target(core=1 - p.core)
        self.of_first = p.member(x=x1, near=near1)
        self.of_second = p.member(x=x2, near=near2)
        self.of_both = p.member(x=1 - p.x, near=1 - p.near)
        self.copies = {}

    def _go(self, name, index, block, target):
        item = remote(self.out.at[block], self.out.at[block], self.sems, index, target)
        item.start()
        self.copies[name] = item

    def begin(self):
        self._go("a", 0, self.me, self.first)
        self._go("b", 1, self.me, self.second)
        self._go("c", 2, self.me, self.other)

    def second_hop(self):
        self.copies["a"].wait_recv()
        self._go("d", 3, self.of_first, self.second)
        self._go("e", 4, self.of_first, self.other)

    def third_hop(self):
        self.copies["b"].wait_recv()
        self._go("f", 5, self.of_second, self.other)

    def last_hop(self):
        self.copies["d"].wait_recv()
        self._go("g", 6, self.of_both, self.other)

    def finish(self):
        for name in "cefg":
            self.copies[name].wait_recv()
        for item in self.copies.values():
            item.wait_send()


class Spread:
    def __init__(self, place, at, sems, first):
        p = place
        self.at, self.sems, self.first = at, sems, first
        self.mine, self.theirs = at(p.far, p.y), at(1 - p.far, p.y)
        self.to_far, self.to_y = p.target(far=1 - p.far), p.target(y=1 - p.y)

    def begin(self):
        self.a = remote(self.mine, self.mine, self.sems, self.first, self.to_far)
        self.b = remote(self.mine, self.mine, self.sems, self.first + 1, self.to_y)
        self.a.start()
        self.b.start()

    def middle(self):
        self.a.wait_recv()
        self.c = remote(self.theirs, self.theirs, self.sems, self.first + 2, self.to_y)
        self.c.start()

    def finish(self):
        self.b.wait_recv()
        self.c.wait_recv()
        for item in (self.a, self.b, self.c):
            item.wait_send()


def shard_of(third):
    shard = third // 3
    return (shard // MEMBERS, shard % MEMBERS), third % 3


def intake_kernel(
    x_in, back_in, order_in, vec_in, qkv_in, fc_in, rows_in,
    x_all, back_all, order, vec_all, qkv, fc, proj, out,
    move_sem, qkv_sem, fc_send, fc_recv, rows_sem, x_sem, back_sem, out_sem, spread_sem, tree_sem,
):
    p = Place()
    greet_all(p)
    home = p.target(
        x=p.ctx % 2, near=p.ctx // 2 % 2, core=p.ctx // 4, y=p.fsdp // 2, far=p.fsdp % 2
    )
    home_member = p.ctx
    x_move = Move(
        p, x_in, x_all.at[home_member], move_sem.at[0, 0], move_sem.at[1, 0], home
    )
    order_move = Move(p, order_in, order, move_sem.at[0, 1], move_sem.at[1, 1], home)
    owner = p.fsdp == 0
    qkv_moves = []
    for member in (1, 0, 3, 2, 5, 4, 7, 6):
        target = p.target(x=member % 2, near=member // 2 % 2, core=member // 4)
        qkv_moves.append(
            Move(
                p, qkv_in.at[member], qkv.at[p.far, p.near, p.y],
                qkv_sem.at[0, member], qkv_sem.at[1, p.near], target, owner,
            )
        )
    def vec_copy(step):
        other = (p.linear + step) % DEVICES
        return pltpu.make_async_remote_copy(
            src_ref=vec_in,
            dst_ref=vec_all.at[p.linear],
            send_sem=move_sem.at[0, 2],
            recv_sem=move_sem.at[1, 2],
            device_id=(other // MEMBERS, other % MEMBERS),
            device_id_type=MESH,
        )

    def vec_send(step, carry):
        vec_copy(step).start()
        return carry

    lax.fori_loop(1, DEVICES, vec_send, 0)
    pltpu.make_async_copy(vec_in, vec_all.at[p.linear], move_sem.at[1, 2]).start()

    arrived(x_all.at[p.me], move_sem.at[1, 0])
    gather_x = Gather(p, x_all, x_sem)
    gather_x.begin()
    back_move = Move(
        p, back_in, back_all.at[home_member], move_sem.at[0, 3], move_sem.at[1, 3], home
    )
    spreads = []
    for near in range(2):
        spreads.append(
            Spread(p, lambda far, y, near=near: qkv.at[far, near, y], spread_sem, 3 * near)
        )
    for near in range(2):
        arrived(qkv.at[p.far, near, p.y], qkv_sem.at[1, near])
        spreads[near].begin()
    gather_x.second_hop()
    gather_x.third_hop()
    fc_moves, rows_moves = [], []
    for part in range(3):
        third = 3 * p.linear + part
        unit = third - FC_FIRST
        valid = jnp.logical_and(unit >= 0, third < PROJ_FIRST)
        unit = jnp.where(valid, unit, 0)
        ctx, slot = unit // 4, unit % 4
        far, near, y = ctx // 4, ctx // 2 % 2, ctx % 2
        for member in (1, 0, 3, 2, 5, 4, 7, 6):
            target = p.target(
                x=member % 2, near=member // 2 % 2, core=member // 4, far=far, y=y
            )
            fc_moves.append(
                Move(
                    p, fc_in.at[part, member], fc.at[far, near, y, slot],
                    fc_send.at[part, member], fc_recv.at[4 * near + slot], target, valid,
                )
            )
    for part in range(3):
        third = 3 * p.linear + part
        valid = third >= PROJ_FIRST
        unit = jnp.where(valid, third - PROJ_FIRST, 0)
        member, group = unit // 4, unit % 4
        target = p.target(
            x=member % 2, near=member // 2 % 2, core=member // 4, y=group // 2, far=group % 2
        )
        rows_moves.append(
            Move(
                p, rows_in.at[part], proj.at[group // 2, group % 2],
                rows_sem.at[0, part], rows_sem.at[1, 0], target, valid,
            )
        )
        valid = jnp.logical_and(third >= OUT_FIRST, third < FC_FIRST)
        member = jnp.where(valid, third - OUT_FIRST, 0)
        group = member % 4
        target = p.target(
            x=member % 2, near=member // 2 % 2, core=member // 4, y=group // 2, far=group % 2
        )
        rows_moves.append(
            Move(
                p, rows_in.at[part], out.at[member],
                rows_sem.at[0, part], rows_sem.at[1, 1], target, valid,
            )
        )
    gather_x.last_hop()
    for near in range(2):
        spreads[near].middle()
    arrived(back_all.at[p.me], move_sem.at[1, 3])
    gather_back = Gather(p, back_all, back_sem)
    gather_back.begin()
    for near in range(2):
        for slot in range(4):
            arrived(fc.at[p.far, near, p.y, slot], fc_recv.at[4 * near + slot])
        item = Spread(p, lambda far, y, near=near: fc.at[far, near, y], spread_sem, 6 + 3 * near)
        item.begin()
        spreads.append(item)
    root_y, root_far = p.me % 4 // 2, p.me % 2
    same_y, same_far = p.y == root_y, p.far == root_far
    mine = out.at[p.me]
    to_far, to_y = p.target(far=1 - p.far), p.target(y=1 - p.y)
    root = jnp.logical_and(same_y, same_far)
    beside = jnp.logical_and(same_y, jnp.logical_not(same_far))
    opposite = jnp.logical_not(same_y)
    over_far = remote(mine, mine, tree_sem, 0, to_far)
    over_y = remote(mine, mine, tree_sem, 1, to_y)

    @pl.when(root)
    def _():
        arrived(mine, rows_sem.at[1, 1])
        over_far.start()
        over_y.start()

    arrived(proj.at[p.y, p.far], rows_sem.at[1, 0])
    item = Spread(p, lambda far, y: proj.at[y, far], spread_sem, 12)
    item.begin()
    spreads.append(item)
    gather_back.second_hop()
    gather_back.third_hop()
    gather_back.last_hop()
    for item in spreads[2:4]:
        item.middle()

    @pl.when(beside)
    def _():
        over_far.wait_recv()
        over_y.start()

    @pl.when(opposite)
    def _():
        over_y.wait_recv()

    gather_out = Gather(p, out, out_sem)
    gather_out.begin()
    spreads[4].middle()
    gather_out.second_hop()
    gather_out.third_hop()
    gather_out.last_hop()
    for item in (gather_x, gather_back, gather_out):
        item.finish()
    for item in spreads:
        item.finish()

    @pl.when(root)
    def _():
        over_far.wait_send()

    @pl.when(same_y)
    def _():
        over_y.wait_send()

    for item in [x_move, order_move, back_move] + qkv_moves + fc_moves + rows_moves:
        item.sent()
    arrived(order, move_sem.at[1, 1])
    arrived(vec_all, move_sem.at[1, 2])
    sent = vec_all.at[pl.ds(1, DEVICES - 1)]
    arrived(sent, move_sem.at[0, 2])


def intake(x, back, order, vectors, qkv_pieces, fc_pieces, row_blocks):
    rows, width = x.shape
    low = jnp.bfloat16
    _, four, wide = qkv_pieces.shape
    _, _, unit, hidden = fc_pieces.shape
    any_space = pl.BlockSpec(memory_space=pl.ANY)

    def like(*shape, kind=low):
        return jax.ShapeDtypeStruct(shape, kind)

    return pl.pallas_call(
        intake_kernel,
        out_shape=[
            like(MEMBERS, rows, width),
            like(MEMBERS, rows, width),
            like(*order.shape, kind=order.dtype),
            like(DEVICES, *vectors.shape),
            like(2, 2, 2, four, wide),
            like(2, 2, 2, 4, unit, hidden),
            like(2, 2, four, width),
            like(MEMBERS, four, width),
        ],
        in_specs=[any_space] * 7,
        out_specs=[any_space] * 8,
        scratch_shapes=[
            pltpu.SemaphoreType.DMA((2, 4)),
            pltpu.SemaphoreType.DMA((2, 8)),
            pltpu.SemaphoreType.DMA((3, 8)),
            pltpu.SemaphoreType.DMA((8,)),
            pltpu.SemaphoreType.DMA((2, 3)),
            pltpu.SemaphoreType.DMA((2, 7)),
            pltpu.SemaphoreType.DMA((2, 7)),
            pltpu.SemaphoreType.DMA((2, 7)),
            pltpu.SemaphoreType.DMA((2, 15)),
            pltpu.SemaphoreType.DMA((2, 2)),
        ],
        compiler_params=pltpu.CompilerParams(collective_id=1, has_side_effects=True),
        name="intake",
    )(x, back, order, vectors, qkv_pieces, fc_pieces, row_blocks)


def gather_kernel(own, out, local_sem, sems):
    p = Place()
    item = Gather(p, out, sems)
    greet((item.first, item.second, item.other))
    for name, index, target in (("a", 0, item.first), ("b", 1, item.second), ("c", 2, item.other)):
        copy = remote(own, out.at[p.me], sems, index, target)
        copy.start()
        item.copies[name] = copy
    local = pltpu.make_async_copy(own, out.at[p.me], local_sem)
    local.start()
    item.second_hop()
    item.third_hop()
    item.last_hop()
    item.finish()
    local.wait()


def group_gather(value, ident):
    any_space = pl.BlockSpec(memory_space=pl.ANY)
    return pl.pallas_call(
        gather_kernel,
        out_shape=jax.ShapeDtypeStruct((MEMBERS,) + value.shape, value.dtype),
        in_specs=[any_space],
        out_specs=any_space,
        scratch_shapes=[pltpu.SemaphoreType.DMA, pltpu.SemaphoreType.DMA((2, 7))],
        compiler_params=pltpu.CompilerParams(collective_id=ident, has_side_effects=True),
        name="group_gather",
    )(value)


def scatter_kernel(part, out, from_core, sums, two, got, last, done, sems):
    p = Place()
    route = Gather(p, None, None)
    greet((route.first, route.second, route.other))
    copies = []
    for j in (3, 2, 1, 0):
        item = remote(part.at[4 * (1 - p.core) + j], from_core.at[j], sems, j, route.other)
        item.start()
        copies.append(item)
    mine = 4 * p.core
    here, there = p.me - mine, route.of_first - mine
    beyond, across = route.of_second - mine, route.of_both - mine
    for item in copies:
        item.wait_recv()

    def summed(block):
        return part[mine + block].astype(jnp.float32) + from_core[block].astype(jnp.float32)

    two[0] = summed(across).astype(jnp.bfloat16)
    send_across = remote(two.at[0], got.at[0], sems, 4, route.second)
    send_across.start()
    two[1] = summed(beyond).astype(jnp.bfloat16)
    send_beyond = remote(two.at[1], got.at[1], sems, 5, route.second)
    send_beyond.start()
    sums[...] = summed(there)
    send_across.wait_recv()
    last[...] = (sums[...] + got[0].astype(jnp.float32)).astype(jnp.bfloat16)
    send_last = remote(last, done, sems, 6, route.first)
    send_last.start()
    sums[...] = summed(here)
    send_beyond.wait_recv()
    sums[...] += got[1].astype(jnp.float32)
    send_last.wait_recv()
    out[...] = sums[...] + done[...].astype(jnp.float32)
    for item in copies + [send_across, send_beyond, send_last]:
        item.wait_send()


def group_scatter(value, ident):
    rows, width = value.shape
    rows = rows // MEMBERS
    low = jnp.bfloat16
    vmem = pl.BlockSpec(memory_space=pltpu.VMEM)
    return pl.pallas_call(
        scatter_kernel,
        out_shape=jax.ShapeDtypeStruct((rows, width), jnp.float32),
        in_specs=[vmem],
        out_specs=vmem,
        scratch_shapes=[
            pltpu.VMEM((4, rows, width), low),
            pltpu.VMEM((rows, width), jnp.float32),
            pltpu.VMEM((2, rows, width), low),
            pltpu.VMEM((2, rows, width), low),
            pltpu.VMEM((rows, width), low),
            pltpu.VMEM((rows, width), low),
            pltpu.SemaphoreType.DMA((2, 7)),
        ],
        compiler_params=pltpu.CompilerParams(
            collective_id=ident, has_side_effects=True, vmem_limit_bytes=VMEM_BYTES
        ),
        name="group_scatter",
    )(value.reshape(MEMBERS, rows, width))


def wide(value):
    return value.astype(jnp.float32)


def low(value):
    return value.astype(jnp.bfloat16)


class Fold:
    def __init__(self, place, at, landing, leaving, last, sems, first):
        p = place
        self.p, self.at, self.landing, self.leaving, self.last = p, at, landing, leaving, last
        self.to_far, self.to_y = p.target(far=1 - p.far), p.target(y=1 - p.y)
        self.sems, self.first = sems, first

    def begin(self):
        p = self.p
        other = 1 - p.far
        self.a = remote(
            self.at(other, 1 - p.y), self.landing(other), self.sems, self.first, self.to_y
        )
        self.b = remote(
            self.at(p.far, 1 - p.y), self.landing(p.far), self.sems, self.first + 1, self.to_y
        )
        self.a.start()
        self.b.start()

    def middle(self):
        p = self.p
        other = 1 - p.far
        self.a.wait_recv()
        self.leaving[...] = low(wide(self.at(other, p.y)[...]) + wide(self.landing(other)[...]))
        self.c = remote(self.leaving, self.last, self.sems, self.first + 2, self.to_far)
        self.c.start()

    def end(self):
        p = self.p
        self.b.wait_recv()
        partial = wide(self.at(p.far, p.y)[...]) + wide(self.landing(p.far)[...])
        self.c.wait_recv()
        return low(partial + wide(self.last[...]))

    def sent(self):
        for item in (self.a, self.b, self.c):
            item.wait_send()


def yield_kernel(
    qkv, fc, proj, out, vec,
    qkv_back, fc_back, rows_back, vec_back,
    qkv_y, fc_y, proj_y, out_y, qkv_go, fc_go, proj_go, out_go,
    qkv_far, fc_far, proj_far, out_far, qkv_sum, fc_sum, proj_sum, out_sum, vec_got,
    fold_sem, tree_sem, vec_sem, qkv_send, qkv_recv, fc_send, fc_recv, rows_send, rows_recv,
):
    p = Place()
    unit = fc_back.shape[2]
    greet_all(p)
    folds = [
        Fold(
            p, lambda far, y: proj.at[y, far], lambda far: proj_y.at[far],
            proj_go, proj_far, fold_sem, 0,
        )
    ]
    for near in range(2):
        folds.append(
            Fold(
                p, lambda far, y, near=near: fc.at[far, near, y],
                lambda far, near=near: fc_y.at[far, near],
                fc_go.at[near], fc_far.at[near], fold_sem, 3 + 3 * near,
            )
        )
    for near in range(2):
        folds.append(
            Fold(
                p, lambda far, y, near=near: qkv.at[far, near, y],
                lambda far, near=near: qkv_y.at[far, near],
                qkv_go.at[near], qkv_far.at[near], fold_sem, 9 + 3 * near,
            )
        )
    for item in folds:
        item.begin()
    root_y, root_far = p.me % 4 // 2, p.me % 2
    same_y, same_far = p.y == root_y, p.far == root_far
    root = jnp.logical_and(same_y, same_far)
    beside = jnp.logical_and(same_y, jnp.logical_not(same_far))
    over_y = remote(out, out_y, tree_sem, 0, p.target(y=1 - p.y))
    over_far = remote(out_go, out_far, tree_sem, 1, p.target(far=1 - p.far))

    @pl.when(jnp.logical_not(same_y))
    def _():
        over_y.start()

    def vec_copy(step):
        other = (p.linear + step) % DEVICES
        return pltpu.make_async_remote_copy(
            src_ref=vec.at[other],
            dst_ref=vec_got.at[p.linear],
            send_sem=vec_sem.at[0],
            recv_sem=vec_sem.at[1],
            device_id=(other // MEMBERS, other % MEMBERS),
            device_id_type=MESH,
        )

    def vec_send(step, carry):
        vec_copy(step).start()
        return carry

    lax.fori_loop(1, DEVICES, vec_send, 0)
    pltpu.make_async_copy(vec.at[p.linear], vec_got.at[p.linear], vec_sem.at[1]).start()
    for item in folds:
        item.middle()

    @pl.when(same_y)
    def _():
        over_y.wait_recv()

    @pl.when(beside)
    def _():
        out_go[...] = low(wide(out[...]) + wide(out_y[...]))
        over_far.start()

    moves = []
    proj_sum[...] = folds[0].end()
    target, part = shard_of(PROJ_FIRST + 4 * p.me + p.group)
    moves.append(
        Move(p, proj_sum, rows_back.at[part], rows_send.at[0], rows_recv.at[part], target)
    )
    for near in range(2):
        block = folds[1 + near].end()
        for slot in range(4):
            fc_sum[near, slot] = block[slot * unit : (slot + 1) * unit]
            third = FC_FIRST + 4 * (4 * p.far + 2 * near + p.y) + slot
            target, part = shard_of(third)
            moves.append(
                Move(
                    p, fc_sum.at[near, slot], fc_back.at[part, p.me],
                    fc_send.at[near, slot], fc_recv.at[part, p.me], target,
                )
            )

    @pl.when(root)
    def _():
        over_far.wait_recv()
        out_sum[...] = low(wide(out[...]) + wide(out_y[...]) + wide(out_far[...]))

    target, part = shard_of(OUT_FIRST + p.me)
    moves.append(
        Move(p, out_sum, rows_back.at[part], rows_send.at[1], rows_recv.at[part], target, root)
    )
    for near in range(2):
        qkv_sum[near] = folds[3 + near].end()
        target = (0 * p.fsdp, 4 * p.far + 2 * near + p.y)
        moves.append(
            Move(
                p, qkv_sum.at[near], qkv_back.at[p.me], qkv_send.at[near], qkv_recv.at[p.me],
                target,
            )
        )
    @pl.when(p.fsdp == 0)
    def _():
        for member in range(MEMBERS):
            arrived(qkv_back.at[member], qkv_recv.at[member])

    for part in range(3):
        third = 3 * p.linear + part
        is_fc = jnp.logical_and(third >= FC_FIRST, third < PROJ_FIRST)
        is_rows = jnp.logical_and(third >= OUT_FIRST, jnp.logical_not(is_fc))

        @pl.when(is_fc)
        def _(part=part):
            for member in range(MEMBERS):
                arrived(fc_back.at[part, member], fc_recv.at[part, member])

        @pl.when(is_rows)
        def _(part=part):
            arrived(rows_back.at[part], rows_recv.at[part])

    arrived(vec_got, vec_sem.at[1])
    vec_back[...] = jnp.sum(vec_got[...], 0)
    arrived(vec_got.at[pl.ds(1, DEVICES - 1)], vec_sem.at[0])
    for item in folds:
        item.sent()

    @pl.when(jnp.logical_not(same_y))
    def _():
        over_y.wait_send()

    @pl.when(beside)
    def _():
        over_far.wait_send()

    for item in moves:
        item.sent()


def yield_grads(qkv, fc, proj, out, vec):
    kind = jnp.bfloat16
    four, wide_qkv = qkv.shape[-2:]
    hidden = fc.shape[-1]
    width = proj.shape[-1]
    unit = four // 4
    any_space = pl.BlockSpec(memory_space=pl.ANY)
    vmem = pl.BlockSpec(memory_space=pltpu.VMEM)

    def buffer(*shape, dtype=kind):
        return pltpu.VMEM(shape, dtype)

    dma = pltpu.SemaphoreType.DMA
    return pl.pallas_call(
        yield_kernel,
        out_shape=[
            jax.ShapeDtypeStruct((MEMBERS, four, wide_qkv), kind),
            jax.ShapeDtypeStruct((3, MEMBERS, unit, hidden), kind),
            jax.ShapeDtypeStruct((3, four, width), kind),
            jax.ShapeDtypeStruct(vec.shape[1:], vec.dtype),
        ],
        in_specs=[vmem] * 5,
        out_specs=[any_space, any_space, any_space, vmem],
        scratch_shapes=[
            buffer(2, 2, four, wide_qkv),
            buffer(2, 2, four, hidden),
            buffer(2, four, width),
            buffer(four, width),
            buffer(2, four, wide_qkv),
            buffer(2, four, hidden),
            buffer(four, width),
            buffer(four, width),
            buffer(2, four, wide_qkv),
            buffer(2, four, hidden),
            buffer(four, width),
            buffer(four, width),
            buffer(2, four, wide_qkv),
            buffer(2, 4, unit, hidden),
            buffer(four, width),
            buffer(four, width),
            buffer(*vec.shape, dtype=vec.dtype),
            dma((2, 15)),
            dma((2, 2)),
            dma((2,)),
            dma((2,)),
            dma((8,)),
            dma((2, 4)),
            dma((3, 8)),
            dma((2,)),
            dma((3,)),
        ],
        compiler_params=pltpu.CompilerParams(
            collective_id=2, has_side_effects=True, vmem_limit_bytes=VMEM_BYTES
        ),
        name="yield_grads",
    )(qkv, fc, proj, out, vec)


def lane_of(shape):
    return lax.broadcasted_iota(jnp.int32, shape, 1) // HD


def dot_nt(a, b):
    return lax.dot_general(a, b, (((1,), (1,)), ((), ())), preferred_element_type=jnp.float32)


def dot_tn(a, b):
    return lax.dot_general(a, b, (((0,), (0,)), ((), ())), preferred_element_type=jnp.float32)


def probabilities(query, keys, row_pos, col_pos):
    scores = dot_nt(query, keys) * 0.125
    scores = jnp.where(col_pos <= row_pos, scores, -1e30)
    weights = jnp.exp(scores - jnp.max(scores, -1, keepdims=True))
    return weights / jnp.sum(weights, -1, keepdims=True)


def attend_kernel(query, keys, values, row_pos, col_pos, out):
    lanes = lane_of(query.shape)
    result = jnp.zeros(query.shape, jnp.float32)
    for head in range(2):
        mine = lanes == head
        own = jnp.where(mine, query[...], jnp.zeros_like(query))
        probs = probabilities(own, keys[...], row_pos[...], col_pos[...])
        mixed = jnp.dot(
            probs.astype(jnp.bfloat16), values[...], preferred_element_type=jnp.float32
        )
        result = jnp.where(mine, mixed, result)
    out[...] = result.astype(jnp.bfloat16)


def attend_back_kernel(
    query, keys, values, grad, row_pos, col_pos, dquery, dkeys, dvalues, key_sum, value_sum
):
    step = pl.program_id(1)

    @pl.when(step == 0)
    def _():
        key_sum[...] = jnp.zeros_like(key_sum)
        value_sum[...] = jnp.zeros_like(value_sum)

    lanes = lane_of(query.shape)
    result = jnp.zeros(query.shape, jnp.float32)
    add_keys = add_values = 0.0
    for head in range(2):
        mine = lanes == head
        own = jnp.where(mine, query[...], jnp.zeros_like(query))
        own_grad = jnp.where(mine, grad[...], jnp.zeros_like(grad))
        probs = probabilities(own, keys[...], row_pos[...], col_pos[...])
        dprobs = dot_nt(own_grad, values[...])
        delta = jnp.sum(probs * dprobs, -1, keepdims=True)
        dscores = (probs * (dprobs - delta)).astype(jnp.bfloat16)
        mixed = jnp.dot(dscores, keys[...], preferred_element_type=jnp.float32)
        result = jnp.where(mine, mixed, result)
        add_keys = add_keys + dot_tn(dscores, own)
        add_values = add_values + dot_tn(probs.astype(jnp.bfloat16), own_grad)
    dquery[...] = (result * 0.125).astype(jnp.bfloat16)
    key_sum[...] += add_keys
    value_sum[...] += add_values

    @pl.when(step == pl.num_programs(1) - 1)
    def _():
        dkeys[...] = (key_sum[...] * 0.125).astype(jnp.bfloat16)
        dvalues[...] = value_sum[...].astype(jnp.bfloat16)


def attend(qkv, row_pos, col_pos, span):
    length = qkv.shape[0]
    wide = 2 * HD
    return pl.pallas_call(
        attend_kernel,
        grid=(SLOTS // 2, length // span),
        in_specs=[
            pl.BlockSpec((span, wide), lambda h, i: (i, h)),
            pl.BlockSpec((length, wide), lambda h, i: (0, SLOTS // 2 + h)),
            pl.BlockSpec((length, wide), lambda h, i: (0, SLOTS + h)),
            pl.BlockSpec((span, 1), lambda h, i: (i, 0)),
            pl.BlockSpec((1, length), lambda h, i: (0, 0)),
        ],
        out_specs=pl.BlockSpec((span, wide), lambda h, i: (i, h)),
        out_shape=jax.ShapeDtypeStruct((length, SLOTS * HD), jnp.bfloat16),
        compiler_params=pltpu.CompilerParams(vmem_limit_bytes=VMEM_BYTES),
        name="attend",
    )(qkv, qkv, qkv, row_pos, col_pos)


def attend_back(qkv, grad, row_pos, col_pos, span):
    length = qkv.shape[0]
    wide = 2 * HD
    whole = jax.ShapeDtypeStruct((length, SLOTS * HD), jnp.bfloat16)
    return pl.pallas_call(
        attend_back_kernel,
        grid=(SLOTS // 2, length // span),
        in_specs=[
            pl.BlockSpec((span, wide), lambda h, i: (i, h)),
            pl.BlockSpec((length, wide), lambda h, i: (0, SLOTS // 2 + h)),
            pl.BlockSpec((length, wide), lambda h, i: (0, SLOTS + h)),
            pl.BlockSpec((span, wide), lambda h, i: (i, h)),
            pl.BlockSpec((span, 1), lambda h, i: (i, 0)),
            pl.BlockSpec((1, length), lambda h, i: (0, 0)),
        ],
        out_specs=[
            pl.BlockSpec((span, wide), lambda h, i: (i, h)),
            pl.BlockSpec((length, wide), lambda h, i: (0, h)),
            pl.BlockSpec((length, wide), lambda h, i: (0, h)),
        ],
        out_shape=[whole, whole, whole],
        scratch_shapes=[
            pltpu.VMEM((length, wide), jnp.float32),
            pltpu.VMEM((length, wide), jnp.float32),
        ],
        compiler_params=pltpu.CompilerParams(vmem_limit_bytes=VMEM_BYTES),
        name="attend_back",
    )(qkv, qkv, qkv, grad, row_pos, col_pos)


def head_columns(rows, width):
    pieces = []
    for member in range(MEMBERS):
        first = head_start(member) * HD
        pieces.append(
            jnp.concatenate(
                [
                    rows[:, part * width + first : part * width + first + SLOTS * HD]
                    for part in range(3)
                ],
                1,
            )
        )
    return jnp.stack(pieces)


def own_heads(member):
    return (head_start(member + 1) - head_start(member)) * HD


def all_heads(pieces):
    return jnp.concatenate([pieces[m][:, : own_heads(m)] for m in range(MEMBERS)], 1)


def to_group(value):
    pairs = []
    for f in range(GROUPS):
        for c in range(MEMBERS):
            core, near, x = c // 4, c // 2 % 2, c % 2
            y, far = f // 2, f % 2
            pairs.append((f * MEMBERS + c, (2 * x + core) * MEMBERS + 4 * far + 2 * near + y))
    return lax.ppermute(value, ("fsdp", "ctx"), pairs)


def per_device_groups(
    inputs, cotangent, slot_order, weights, vectors, first_w, second_w, first_vec, second_vec
):
    seqs, rows, width = inputs.shape
    kind, high = jnp.bfloat16, jnp.float32
    fsdp, ctx = lax.axis_index("fsdp"), lax.axis_index("ctx")
    member = 4 * (fsdp % 2) + 2 * (ctx // 2 % 2) + fsdp // 2
    length = rows * MEMBERS
    hidden = FF // MEMBERS
    local = weights.shape[0]
    third = local // 3
    unit = width // DEVICES
    four = 4 * unit
    per_part = SLOTS * HD

    qkv_pieces = head_columns(weights.reshape(four, 3 * width), width)
    fc_pieces = weights.reshape(3, unit, MEMBERS, hidden).transpose(0, 2, 1, 3)
    row_blocks = weights.reshape(3, four, width)
    order = jnp.pad(slot_order, ((0, 7), (0, 128 - slot_order.shape[1])))
    vec_rows, vec_cols = vectors.shape
    padded = jnp.pad(vectors, ((0, 16 - vec_rows), (0, -vec_cols % 128)))
    x_all, back_all, order, full_vec, own_qkv, own_fc, own_proj, full_out = intake(
        inputs.reshape(rows, width), cotangent.reshape(rows, width), order, padded,
        qkv_pieces, fc_pieces, row_blocks,
    )
    x_all, back_all = x_all.reshape(length, width), back_all.reshape(length, width)
    own_qkv = own_qkv.reshape(width, 3 * per_part)
    own_fc = own_fc.reshape(width, hidden)
    own_proj = own_proj.reshape(hidden, width)
    full_out = full_out.reshape(width, width)
    order = order[0, : slot_order.shape[1]]
    block = length // order.shape[0]
    pos = (order[:, None] * block + jnp.arange(block, dtype=jnp.int32)).reshape(-1)
    row_pos, col_pos = pos[:, None], pos[None, :]
    full_vec = full_vec[:, :vec_rows, :vec_cols].reshape(GROUPS, MEMBERS, vec_rows, vec_cols)
    vec = full_vec.transpose(0, 2, 1, 3).reshape(-1, width).astype(high)
    head_at = HEADS * member // MEMBERS * HD
    bias_q = lax.dynamic_slice(vec[2], (head_at,), (per_part,))
    bias_v = lax.dynamic_slice(vec[3], (head_at,), (per_part,))
    bias_qkv = jnp.concatenate([bias_q, jnp.zeros_like(bias_q), bias_v])
    bias_fc = lax.dynamic_slice(vec[8:].reshape(-1), (member * hidden,), (hidden,))

    mine = member * rows
    h_first = layer_norm(x_all.astype(high), vec[0], vec[1]).astype(kind)
    qkv = jnp.dot(h_first, own_qkv, preferred_element_type=high) + bias_qkv
    qkv = qkv.astype(kind)
    span = min(length, 256)
    attn = attend(qkv, row_pos, col_pos, span)
    attn_all = all_heads(group_gather(attn, 3))
    resid = x_all.astype(high) + jnp.dot(attn_all, full_out, preferred_element_type=high) + vec[4]
    h_second = layer_norm(resid, vec[5], vec[6]).astype(kind)
    pre = jnp.dot(h_second, own_fc, preferred_element_type=high) + bias_fc
    act, pull_gelu = jax.vjp(gelu_tanh, pre)
    act = act.astype(kind)
    made = group_scatter(jnp.dot(act, own_proj, preferred_element_type=high).astype(kind), 4)
    resid_own = lax.dynamic_slice_in_dim(resid, mine, rows, 0)
    outputs = (resid_own + made + vec[7]).astype(kind)

    back_own = lax.dynamic_slice_in_dim(back_all, mine, rows, 0).astype(high)
    grad_proj = jnp.einsum("tf,td->fd", act, back_all, preferred_element_type=high).astype(kind)
    grad_bp = jnp.sum(back_own, 0)
    dact = jnp.einsum("td,fd->tf", back_all, own_proj, preferred_element_type=high)
    dpre = pull_gelu(dact)[0].astype(kind)
    grad_fc = jnp.einsum("td,tf->df", h_second, dpre, preferred_element_type=high).astype(kind)
    grad_bf = jnp.sum(dpre, 0, dtype=high)
    dh_second = group_scatter(
        jnp.einsum("tf,df->td", dpre, own_fc, preferred_element_type=high).astype(kind), 4
    )
    _, pull_second = jax.vjp(layer_norm, resid_own, vec[5], vec[6])
    dres_ln, grad_g2, grad_b2 = pull_second(dh_second)
    dresid = back_own + dres_ln
    dbranch = dresid.astype(kind)
    grad_bo = jnp.sum(dbranch, 0, dtype=high)
    dbranch_all = group_gather(dbranch, 5).reshape(length, width)
    out_heads = lax.dynamic_slice_in_dim(full_out, head_at, per_part, 0)
    dattn = jnp.einsum("te,de->td", dbranch_all, out_heads, preferred_element_type=high)
    dattn = dattn.astype(kind)
    attn_cols = lax.dynamic_slice_in_dim(attn_all, member * four, four, 1)
    grad_out = jnp.einsum("td,te->de", attn_cols, dbranch_all, preferred_element_type=high)
    dqkv = jnp.concatenate(attend_back(qkv, dattn, row_pos, col_pos, span), 1)
    lane = jnp.arange(per_part)
    keep = lane < jnp.where(member == MEMBERS - 1, per_part, (SLOTS - 1) * HD)
    dqkv = jnp.where(jnp.tile(keep, 3), dqkv, jnp.zeros_like(dqkv))
    grad_qkv = jnp.einsum("td,te->de", h_first, dqkv, preferred_element_type=high).astype(kind)
    bias_sums = jnp.sum(dqkv, 0, dtype=high)
    dh_first = group_scatter(
        jnp.einsum("te,de->td", dqkv, own_qkv, preferred_element_type=high).astype(kind), 4
    )
    x_own = lax.dynamic_slice_in_dim(x_all, mine, rows, 0).astype(high)
    _, pull_first = jax.vjp(layer_norm, x_own, vec[0], vec[1])
    dx_ln, grad_g1, grad_b1 = pull_first(dh_first)
    input_grad = (dresid + dx_ln).astype(kind)
    results = to_group(jnp.concatenate([outputs, input_grad], 1))
    outputs = results[:, :width].reshape(seqs, rows, width)
    input_grad = results[:, width:].reshape(seqs, rows, width)

    zero_row = jnp.zeros((width,), high)
    row_q = lax.dynamic_update_slice(zero_row, bias_sums[:per_part], (head_at,))
    row_v = lax.dynamic_update_slice(zero_row, bias_sums[2 * per_part :], (head_at,))
    row_f = lax.dynamic_update_slice(jnp.zeros((FF,), high), grad_bf, (member * hidden,))
    grad_vec = jnp.concatenate(
        [
            jnp.stack([grad_g1, grad_b1, row_q, row_v, grad_bo, grad_g2, grad_b2, grad_bp]),
            row_f.reshape(-1, width),
        ],
        0,
    )
    grad_vec = grad_vec.reshape(GROUPS, vec_rows, MEMBERS, vec_cols).transpose(0, 2, 1, 3)
    grad_vec = grad_vec.reshape(DEVICES, vec_rows, vec_cols)
    grad_vec = jnp.pad(grad_vec, ((0, 0), (0, 8 - vec_rows), (0, -vec_cols % 128)))
    qkv_back, fc_back, rows_back, vec_back = yield_grads(
        grad_qkv.reshape(2, 2, 2, four, 3 * per_part),
        grad_fc.reshape(2, 2, 2, four, hidden),
        grad_proj.reshape(2, 2, four, width),
        grad_out.astype(kind),
        grad_vec,
    )
    qkv_flat = jnp.concatenate(
        [all_heads(qkv_back[:, :, p * per_part : (p + 1) * per_part]) for p in range(3)], 1
    ).reshape(local, 128)
    fc_flat = fc_back.transpose(0, 2, 1, 3).reshape(3, third, 128)
    rows_flat = rows_back.reshape(3, third, 128)
    thirds = 3 * (fsdp * MEMBERS + ctx) + jnp.arange(3)
    is_fc = jnp.logical_and(thirds >= FC_FIRST, thirds < PROJ_FIRST)
    others = jnp.where(is_fc[:, None, None], fc_flat, rows_flat).reshape(local, 128)
    owned = jnp.where(fsdp == 0, qkv_flat, others).astype(high)
    new_w = adamw(weights, owned, first_w, second_w, rate_matrix, weight_decay)
    owned_vec = vec_back[:vec_rows, :vec_cols]
    new_vec = adamw(vectors, owned_vec, first_vec, second_vec, rate_vector, 0.0)
    return (outputs, input_grad, new_w[0], new_w[1], new_w[2], new_vec[0], new_vec[1], new_vec[2])


def solution(mesh):
    in_specs = (
        P("fsdp", "ctx", None),
        P("fsdp", "ctx", None),
        P("fsdp", None),
        P(("fsdp", "ctx"), None),
        P("fsdp", "ctx"),
        P(("fsdp", "ctx"), None),
        P(("fsdp", "ctx"), None),
        P("fsdp", "ctx"),
        P("fsdp", "ctx"),
    )
    out_specs = (
        P("fsdp", "ctx", None),
        P("fsdp", "ctx", None),
        P(("fsdp", "ctx"), None),
        P(("fsdp", "ctx"), None),
        P(("fsdp", "ctx"), None),
        P("fsdp", "ctx"),
        P("fsdp", "ctx"),
        P("fsdp", "ctx"),
    )
    per_device = per_device_groups if mesh.shape["ctx"] == MEMBERS else per_device_ring
    return jax.shard_map(
        per_device, mesh=mesh, in_specs=in_specs, out_specs=out_specs, check_vma=False
    )
```

```python
import jax
import jax.numpy as jnp
from jax import lax
from jax.experimental import pallas as pl
from jax.experimental.pallas import tpu as pltpu
from jax.sharding import PartitionSpec as P

HEADS = 25
HD = 64
FF = 6400
STEP = 10


epsilon_norm = 1e-05
beta_first = 0.9
beta_second = 0.999
epsilon_adam = 1e-08
weight_decay = 0.1
rate_matrix = 0.1
rate_vector = 0.8


def shifted(value, axis, steps):
    count = lax.axis_size(axis)
    pairs = [(source, (source + steps) % count) for source in range(count)]
    return lax.ppermute(value, axis, pairs)


def layer_norm(value, gain, shift):
    center = value - jnp.mean(value, -1, keepdims=True)
    spread = jnp.mean(center * center, -1, keepdims=True)
    return center * lax.rsqrt(spread + epsilon_norm) * gain + shift


def gelu_tanh(value):
    return jax.nn.gelu(value, approximate=True)


def key_positions(slot_order, first_slot, slots, block):
    groups = lax.dynamic_slice_in_dim(slot_order, first_slot, slots, 1)
    offsets = jnp.arange(block, dtype=jnp.int32)
    return (groups[:, :, None] * block + offsets).reshape(slot_order.shape[0], slots * block)


def unpack_flat(flat, width, hidden):
    flat = flat.reshape(-1)
    first_end = 3 * width * width
    second_end = 4 * width * width
    third_end = 4 * width * width + width * hidden
    return (
        flat[:first_end].reshape(width, 3 * width),
        flat[first_end:second_end].reshape(width, width),
        flat[second_end:third_end].reshape(width, hidden),
        flat[third_end:].reshape(hidden, width),
    )


def gather_params(weights, vectors):
    local = weights.reshape(1, weights.shape[0], weights.shape[1])
    part = (
        lax.all_gather(local, "fsdp", axis=0, tiled=True),
        lax.all_gather(vectors, "fsdp", axis=0, tiled=True),
    )
    return (
        lax.all_gather(part[0], "ctx", axis=1, tiled=True),
        lax.all_gather(part[1], "ctx", axis=1, tiled=True),
    )


def reduce_grads(grad_flat, grad_vec):
    part = (
        lax.psum_scatter(
            grad_flat.astype(jnp.bfloat16), "fsdp", scatter_dimension=0, tiled=True
        ).astype(jnp.float32),
        lax.psum_scatter(
            grad_vec.astype(jnp.bfloat16), "fsdp", scatter_dimension=0, tiled=True
        ).astype(jnp.float32),
    )
    return (
        lax.psum_scatter(
            part[0].astype(jnp.bfloat16), "ctx", scatter_dimension=1, tiled=True
        ).astype(jnp.float32),
        lax.psum_scatter(
            part[1].astype(jnp.bfloat16), "ctx", scatter_dimension=1, tiled=True
        ).astype(jnp.float32),
    )


def pass_grads(grad_pairs):
    return shifted(grad_pairs.astype(jnp.bfloat16), "ctx", 1).astype(grad_pairs.dtype)


def adamw(weight, grad, first, second, rate, decay):
    first = beta_first * first + (1.0 - beta_first) * grad
    second = beta_second * second + (1.0 - beta_second) * grad * grad
    first_hat = first / (1.0 - beta_first**STEP)
    second_hat = second / (1.0 - beta_second**STEP)
    weight = weight.astype(jnp.float32)
    updated = weight - rate * (first_hat / (jnp.sqrt(second_hat) + epsilon_adam) + decay * weight)
    return (first, second, updated)


def per_device_ring(
    inputs, cotangent, slot_order, weights, vectors, first_w, second_w, first_vec, second_vec
):
    seqs, rows, width = inputs.shape
    tokens = seqs * rows
    block = rows // 2
    cycle = lax.axis_size("ctx")
    shards = lax.axis_size("fsdp")
    me = lax.axis_index("ctx")
    full_flat, full_vec = gather_params(weights, vectors)
    full_qkv, full_out, full_fc, full_proj = unpack_flat(full_flat, width, FF)
    vec = full_vec.astype(jnp.float32)
    bias_fc = vec[8:].reshape(-1)
    x_in = inputs.reshape(tokens, width).astype(jnp.float32)
    h_first, pull_first = jax.vjp(layer_norm, x_in, vec[0], vec[1])
    h_first_b = h_first.astype(jnp.bfloat16)
    zero_row = jnp.zeros((width,), jnp.float32)
    qkv = jnp.dot(h_first_b, full_qkv, preferred_element_type=jnp.float32)
    qkv_b = (qkv + jnp.concatenate([vec[2], zero_row, vec[3]])).astype(jnp.bfloat16)
    query_heads = qkv_b[:, :width].reshape(seqs, rows, HEADS, HD)
    key_value = qkv_b[:, width:].reshape(seqs, rows, 2, width)
    query_pos = key_positions(slot_order, 2 * me, 2, block)

    def online(state, item):
        top, total, accum = state
        keys_i, values_i, pos_i = item
        scores = (
            jnp.einsum("sqhd,skhd->shqk", query_heads, keys_i, preferred_element_type=jnp.float32)
            * 0.125
        )
        allowed = pos_i[:, None, None, :] <= query_pos[:, None, :, None]
        scores = jnp.where(allowed, scores, -1e30)
        peak = jnp.maximum(top, jnp.max(scores, -1))
        weights_p = jnp.where(allowed, jnp.exp(scores - peak[..., None]), 0.0)
        factor = jnp.exp(top - peak)
        total = total * factor + jnp.sum(weights_p, -1)
        mixed = jnp.einsum(
            "shqk,skhd->sqhd",
            weights_p.astype(jnp.bfloat16),
            values_i,
            preferred_element_type=jnp.float32,
        )
        accum = accum * jnp.transpose(factor, (0, 2, 1))[..., None] + mixed
        return ((peak, total, accum), None)

    start_state = (
        jnp.full((seqs, HEADS, rows), -1e30, jnp.float32),
        jnp.zeros((seqs, HEADS, rows), jnp.float32),
        jnp.zeros((seqs, rows, HEADS, HD), jnp.float32),
    )
    state = start_state
    piece = lax.all_gather(key_value, "ctx", axis=1, tiled=True)
    count = piece.shape[1]
    turns = count // rows
    pos_all = key_positions(slot_order, jnp.int32(0) // block, count // block, block)
    stack = piece.reshape(seqs, turns, rows, 2, HEADS, HD).transpose(1, 0, 2, 3, 4, 5)
    pos_stack = pos_all.reshape(seqs, turns, rows).transpose(1, 0, 2)
    state, _ = lax.scan(online, state, (stack[:, :, :, 0], stack[:, :, :, 1], pos_stack))
    top, total, accum = state
    attn = accum / jnp.transpose(total, (0, 2, 1))[..., None]
    logsum = top + jnp.log(total)
    attn_b = attn.reshape(tokens, width).astype(jnp.bfloat16)
    resid = x_in + jnp.dot(attn_b, full_out, preferred_element_type=jnp.float32) + vec[4]
    h_second, pull_second = jax.vjp(layer_norm, resid, vec[5], vec[6])
    h_second_b = h_second.astype(jnp.bfloat16)
    pre = jnp.dot(h_second_b, full_fc, preferred_element_type=jnp.float32) + bias_fc
    act, pull_gelu = jax.vjp(gelu_tanh, pre)
    act_b = act.astype(jnp.bfloat16)
    result = resid + jnp.dot(act_b, full_proj, preferred_element_type=jnp.float32) + vec[7]
    outputs = result.astype(jnp.bfloat16).reshape(seqs, rows, width)
    back_b = cotangent.reshape(tokens, width)
    back = back_b.astype(jnp.float32)
    grad_proj = jnp.einsum("tf,td->fd", act_b, back_b, preferred_element_type=jnp.float32)
    grad_bp = jnp.sum(back, 0)
    dact = jnp.einsum("td,fd->tf", back_b, full_proj, preferred_element_type=jnp.float32)
    dpre_b = pull_gelu(dact)[0].astype(jnp.bfloat16)
    grad_fc = jnp.einsum("td,tf->df", h_second_b, dpre_b, preferred_element_type=jnp.float32)
    grad_bf = jnp.sum(dpre_b, 0, dtype=jnp.float32)
    dh_second = jnp.einsum("tf,df->td", dpre_b, full_fc, preferred_element_type=jnp.float32)
    dres_ln, grad_g2, grad_b2 = pull_second(dh_second)
    dresid = back + dres_ln
    dbranch_b = dresid.astype(jnp.bfloat16)
    grad_bo = jnp.sum(dbranch_b, 0, dtype=jnp.float32)
    grad_out = jnp.einsum("td,te->de", attn_b, dbranch_b, preferred_element_type=jnp.float32)
    dattn_b = jnp.einsum(
        "te,de->td", dbranch_b, full_out, preferred_element_type=jnp.float32
    ).astype(jnp.bfloat16)
    grad_heads = dattn_b.reshape(seqs, rows, HEADS, HD)
    delta = jnp.transpose(jnp.sum(grad_heads.astype(jnp.float32) * attn, -1), (0, 2, 1))

    def contribute(pair, source):
        pos_k = key_positions(slot_order, 2 * source, 2, block)
        key_h = pair[:, :, 0].reshape(seqs, rows, HEADS, HD)
        value_h = pair[:, :, 1].reshape(seqs, rows, HEADS, HD)
        scores = (
            jnp.einsum("sqhd,skhd->shqk", query_heads, key_h, preferred_element_type=jnp.float32)
            * 0.125
        )
        allowed = pos_k[:, None, None, :] <= query_pos[:, None, :, None]
        probs = jnp.where(allowed, jnp.exp(scores - logsum[..., None]), 0.0)
        dvalue = jnp.einsum(
            "shqk,sqhd->skhd",
            probs.astype(jnp.bfloat16),
            grad_heads,
            preferred_element_type=jnp.float32,
        )
        dprobs = jnp.einsum(
            "sqhd,skhd->shqk", grad_heads, value_h, preferred_element_type=jnp.float32
        )
        dscores = (probs * (dprobs - delta[..., None])).astype(jnp.bfloat16)
        dquery = (
            jnp.einsum("shqk,skhd->sqhd", dscores, key_h, preferred_element_type=jnp.float32)
            * 0.125
        )
        dkey = (
            jnp.einsum("shqk,sqhd->skhd", dscores, query_heads, preferred_element_type=jnp.float32)
            * 0.125
        )
        return (dquery, jnp.stack((dkey, dvalue), 2))

    dq_own, dkv_own = contribute(key_value, me)

    def turn(step, state):
        pair, dkv_acc, dq_acc = state
        pair = shifted(pair, "ctx", 1)
        dkv_acc = pass_grads(dkv_acc)
        source = (me - step) % cycle
        dq_part, dkv_part = contribute(pair, source)
        return (pair, dkv_acc + dkv_part, dq_acc + dq_part)

    final = lax.fori_loop(1, cycle, turn, (key_value, dkv_own, dq_own))
    dkv = pass_grads(final[1])
    dqkv_b = jnp.concatenate(
        [final[2].reshape(tokens, width), dkv.reshape(tokens, 2 * width)], 1
    ).astype(jnp.bfloat16)
    grad_qkv = jnp.einsum("td,te->de", h_first_b, dqkv_b, preferred_element_type=jnp.float32)
    bias_sums = jnp.sum(dqkv_b, 0, dtype=jnp.float32)
    dh_first = jnp.einsum("te,de->td", dqkv_b, full_qkv, preferred_element_type=jnp.float32)
    dx_ln, grad_g1, grad_b1 = pull_first(dh_first)
    input_grad = (dresid + dx_ln).astype(jnp.bfloat16).reshape(seqs, rows, width)
    grad_vec = jnp.concatenate(
        [
            jnp.stack(
                [
                    grad_g1,
                    grad_b1,
                    bias_sums[:width],
                    bias_sums[2 * width :],
                    grad_bo,
                    grad_g2,
                    grad_b2,
                    grad_bp,
                ]
            ),
            grad_bf.reshape(-1, width),
        ],
        0,
    )
    grad_flat = jnp.concatenate(
        [grad_qkv.reshape(-1), grad_out.reshape(-1), grad_fc.reshape(-1), grad_proj.reshape(-1)]
    ).reshape(shards, -1, 128)
    owned_flat, owned_vec = reduce_grads(grad_flat, grad_vec)
    owned_flat = owned_flat.reshape(weights.shape[0], 128)
    new_w = adamw(weights, owned_flat, first_w, second_w, rate_matrix, weight_decay)
    new_vec = adamw(vectors, owned_vec, first_vec, second_vec, rate_vector, 0.0)
    return (outputs, input_grad, new_w[0], new_w[1], new_w[2], new_vec[0], new_vec[1], new_vec[2])


MEMBERS = 8
GROUPS = 4
DEVICES = MEMBERS * GROUPS
MESH = pl.DeviceIdType.MESH
BLOCK = 64
SLOTS = 4
VMEM_BYTES = 60 * 1024 * 1024
OUT_FIRST = 24
FC_FIRST = 32
PROJ_FIRST = 64


def head_start(member):
    return HEADS * member // MEMBERS


class Place:
    def __init__(self):
        self.fsdp, self.ctx = lax.axis_index("fsdp"), lax.axis_index("ctx")
        self.x, self.core = self.fsdp // 2, self.fsdp % 2
        self.far, self.near, self.y = self.ctx // 4, self.ctx // 2 % 2, self.ctx % 2
        self.me = self.member()
        self.group = 2 * self.y + self.far
        self.linear = self.fsdp * MEMBERS + self.ctx

    def member(self, x=None, near=None, core=None):
        x = self.x if x is None else x
        near = self.near if near is None else near
        core = self.core if core is None else core
        return 4 * core + 2 * near + x

    def target(self, x=None, core=None, far=None, near=None, y=None):
        x = self.x if x is None else x
        near = self.near if near is None else near
        core = self.core if core is None else core
        far = self.far if far is None else far
        y = self.y if y is None else y
        return (2 * x + core, 4 * far + 2 * near + y)

    def is_me(self, target):
        return jnp.logical_and(target[0] == self.fsdp, target[1] == self.ctx)


def greet_all(place):
    barrier = pltpu.get_barrier_semaphore()

    def one(step, carry):
        other = (place.linear + step) % DEVICES
        pl.semaphore_signal(
            barrier, inc=1, device_id=(other // MEMBERS, other % MEMBERS), device_id_type=MESH
        )
        return carry

    lax.fori_loop(1, DEVICES, one, 0)
    pl.semaphore_wait(barrier, DEVICES - 1)


def greet(targets):
    barrier = pltpu.get_barrier_semaphore()
    for target in targets:
        pl.semaphore_signal(barrier, inc=1, device_id=target, device_id_type=MESH)
    pl.semaphore_wait(barrier, len(targets))


def remote(source, landing, sems, index, target):
    return pltpu.make_async_remote_copy(
        src_ref=source,
        dst_ref=landing,
        send_sem=sems.at[0, index],
        recv_sem=sems.at[1, index],
        device_id=target,
        device_id_type=MESH,
    )


def arrived(landing, sem):
    pltpu.make_async_copy(landing, landing, sem).wait()


class Move:
    def __init__(self, place, source, landing, send_sem, recv_sem, target, valid=None):
        here = place.is_me(target)
        away = jnp.logical_not(here)
        if valid is not None:
            here, away = jnp.logical_and(here, valid), jnp.logical_and(away, valid)
        self.away = away
        self.copy = pltpu.make_async_remote_copy(
            src_ref=source,
            dst_ref=landing,
            send_sem=send_sem,
            recv_sem=recv_sem,
            device_id=target,
            device_id_type=MESH,
        )

        @pl.when(here)
        def _():
            pltpu.make_async_copy(source, landing, recv_sem).start()

        @pl.when(away)
        def _():
            self.copy.start()

    def sent(self):
        @pl.when(self.away)
        def _():
            self.copy.wait_send()


class Gather:
    def __init__(self, place, out, sems):
        p = place
        step, turn = 1 - p.core, p.core
        x1, near1 = p.x + step * (1 - 2 * p.x), p.near + turn * (1 - 2 * p.near)
        x2, near2 = p.x + turn * (1 - 2 * p.x), p.near + step * (1 - 2 * p.near)
        self.out, self.sems, self.me = out, sems, p.me
        self.first = p.target(x=x1, near=near1)
        self.second = p.target(x=x2, near=near2)
        self.other = p.target(core=1 - p.core)
        self.of_first = p.member(x=x1, near=near1)
        self.of_second = p.member(x=x2, near=near2)
        self.of_both = p.member(x=1 - p.x, near=1 - p.near)
        self.copies = {}

    def _go(self, name, index, block, target):
        item = remote(self.out.at[block], self.out.at[block], self.sems, index, target)
        item.start()
        self.copies[name] = item

    def begin(self):
        self._go("a", 0, self.me, self.first)
        self._go("b", 1, self.me, self.second)
        self._go("c", 2, self.me, self.other)

    def second_hop(self):
        self.copies["a"].wait_recv()
        self._go("d", 3, self.of_first, self.second)
        self._go("e", 4, self.of_first, self.other)

    def third_hop(self):
        self.copies["b"].wait_recv()
        self._go("f", 5, self.of_second, self.other)

    def last_hop(self):
        self.copies["d"].wait_recv()
        self._go("g", 6, self.of_both, self.other)

    def finish(self):
        for name in "cefg":
            self.copies[name].wait_recv()
        for item in self.copies.values():
            item.wait_send()


class Spread:
    def __init__(self, place, at, sems, first):
        p = place
        self.at, self.sems, self.first = at, sems, first
        self.mine, self.theirs = at(p.far, p.y), at(1 - p.far, p.y)
        self.to_far, self.to_y = p.target(far=1 - p.far), p.target(y=1 - p.y)

    def begin(self):
        self.a = remote(self.mine, self.mine, self.sems, self.first, self.to_far)
        self.b = remote(self.mine, self.mine, self.sems, self.first + 1, self.to_y)
        self.a.start()
        self.b.start()

    def middle(self):
        self.a.wait_recv()
        self.c = remote(self.theirs, self.theirs, self.sems, self.first + 2, self.to_y)
        self.c.start()

    def finish(self):
        self.b.wait_recv()
        self.c.wait_recv()
        for item in (self.a, self.b, self.c):
            item.wait_send()


def shard_of(third):
    shard = third // 3
    return (shard // MEMBERS, shard % MEMBERS), third % 3


def lookup(table, index):
    result = 0
    for place, entry in enumerate(table):
        if entry:
            result = result + jnp.where(index == place, entry, 0)
    return result


FC_OF_GROUP = (
    (0, 1, 16, 17, 18, 22, 23, 24),
    (2, 3, 19, 20, 21, 25, 26, 27),
    (4, 5, 6, 10, 11, 12, 28, 29),
    (7, 8, 9, 13, 14, 15, 30, 31),
)
FC_SLOT = [0] * 32
FC_Y = [0] * 32
for _group, _units in enumerate(FC_OF_GROUP):
    for _slot, _unit in enumerate(_units):
        FC_SLOT[_unit] = _slot
        FC_Y[_unit] = _group % 2


def fc_unit(far, y, slot):
    return lookup([units[slot] for units in FC_OF_GROUP], 2 * far + y)


def fc_home(place, unit):
    return lookup(FC_SLOT, unit), lookup(FC_Y, unit)


def out_root(member):
    return jnp.where(member // 3 == 1, 1, 0)


def half_tile(flat, first, count, stride, half):
    at = half // 2
    tile = flat[pl.ds(first + at, count, stride=stride), :]
    if half % 2 == 0:
        return tile
    after = flat[pl.ds(first + at + 1, count, stride=stride), :]
    lane = lax.broadcasted_iota(jnp.int32, tile.shape, 1)
    return pltpu.roll(jnp.where(lane < HD, after, tile), HD, 1)


def lay_qkv(flat, rows, pieces, member):
    count = rows.shape[1] // 2
    halves = 3 * HEADS
    for part in range(3):
        for odd in range(2):
            for tile in range(SLOTS // 2):
                half = halves * odd + HEADS * part + head_start(member) + 2 * tile
                rows[SLOTS // 2 * part + tile, pl.ds(odd, count, stride=2), :] = half_tile(
                    flat, 0, count, halves, half
                )
    for tile in range(3 * SLOTS // 2):
        pieces[member, :, 128 * tile : 128 * tile + 128] = rows[tile].astype(jnp.bfloat16)


def lay_fc(flat, first, pieces, part):
    count, hidden = pieces.shape[-2:]
    stride = FF // 128
    for member in range(MEMBERS):
        start, shift = divmod(member * hidden, 128)
        for tile in range(-(-hidden // 128)):
            value = flat[pl.ds(first + start + tile, count, stride=stride), :]
            size = min(128, hidden - 128 * tile)
            if shift:
                if shift + size > 128:
                    after = flat[pl.ds(first + start + tile + 1, count, stride=stride), :]
                    lane = lax.broadcasted_iota(jnp.int32, value.shape, 1)
                    value = jnp.where(lane < shift, after, value)
                value = pltpu.roll(value, 128 - shift, 1)
            pieces[part, member, :, 128 * tile : 128 * tile + size] = value[:, :size].astype(
                jnp.bfloat16
            )


def lay_rows(flat, first, rows, blocks, part):
    count = rows.shape[1] // 2
    width = blocks.shape[-1]
    halves = width // HD
    for odd in range(2):
        for tile in range(-(-width // 128)):
            half = halves * odd + 2 * tile
            size = min(128, width - 128 * tile)
            if size == 128 or half % 2 == 0:
                value = half_tile(flat, first, count, halves, half)
            else:
                value = pltpu.roll(
                    flat[pl.ds(first + half // 2, count, stride=halves), :], HD, 1
                )
            rows[tile, pl.ds(odd, count, stride=2), :] = value
    for tile in range(-(-width // 128)):
        size = min(128, width - 128 * tile)
        blocks[part, :, 128 * tile : 128 * tile + size] = rows[tile, :, :size].astype(
            jnp.bfloat16
        )


def norm_rows(value, gain, shift):
    center = value - jnp.mean(value, -1, keepdims=True)
    spread = jnp.mean(center * center, -1, keepdims=True)
    return center * lax.rsqrt(spread + epsilon_norm) * gain + shift


def member_lanes(row, member, count):
    result = jnp.zeros((row.shape[0], count), row.dtype)
    for other in range(MEMBERS):
        first = head_start(other) * HD
        result = result + jnp.where(member == other, row[:, first : first + count], 0.0)
    return result


def attend_block(query, keys, values, row_pos, col_pos):
    lanes = lane_of(query.shape)
    result = jnp.zeros(query.shape, jnp.float32)
    for head in range(2):
        mine = lanes == head
        own = jnp.where(mine, query, jnp.zeros_like(query))
        probs = probabilities(own, keys, row_pos, col_pos)
        mixed = jnp.dot(probs.astype(jnp.bfloat16), values, preferred_element_type=jnp.float32)
        result = jnp.where(mine, mixed, result)
    return result.astype(jnp.bfloat16)


def forward_kernel(
    x_in, back_in, order_in, vec_in, weights,
    x_all, back_all, vecs, row_pos, col_pos, w_qkv, h_first, qkv, attn_all, fc, proj, out,
    flat, rows, qkv_pieces, fc_pieces, blocks, order, vec_all, qkv_land, attn,
    fc_part, proj_part, out_part,
    move_sem, qkv_sem, fc_send, fc_recv, rows_sem, x_sem, back_sem, spread_sem,
    own_sem, fc_sem, proj_sem, tree_sem, out_sem, attn_sem,
):
    p = Place()
    third_rows = weights.shape[0] // 3
    count, width = x_in.shape
    length = MEMBERS * count
    pairs = SLOTS // 2
    barrier = pltpu.get_barrier_semaphore()

    def signal(step, carry):
        other = (p.linear + step) % DEVICES
        pl.semaphore_signal(
            barrier, inc=1, device_id=(other // MEMBERS, other % MEMBERS), device_id_type=MESH
        )
        return carry

    lax.fori_loop(1, DEVICES, signal, 0)
    flat[...] = weights[...].astype(jnp.float32)
    pl.semaphore_wait(barrier, DEVICES - 1)
    home = p.target(
        x=p.ctx % 2, near=p.ctx // 2 % 2, core=p.ctx // 4, y=p.fsdp // 2, far=p.fsdp % 2
    )
    x_move = Move(p, x_in, x_all.at[p.ctx], move_sem.at[0, 0], move_sem.at[1, 0], home)
    order_move = Move(p, order_in, order, move_sem.at[0, 1], move_sem.at[1, 1], home)
    owner = p.fsdp == 0
    qkv_moves = []
    for member in (7, 6, 3, 2, 5, 4, 1, 0):

        @pl.when(owner)
        def _(member=member):
            lay_qkv(flat, rows, qkv_pieces, member)

        target = p.target(x=member % 2, near=member // 2 % 2, core=member // 4)
        qkv_moves.append(
            Move(
                p, qkv_pieces.at[member], qkv_land.at[p.far, p.near, p.y],
                qkv_sem.at[0, member], qkv_sem.at[1, p.near], target, owner,
            )
        )

    def vec_send(step, carry):
        other = (p.linear + step) % DEVICES
        pltpu.make_async_remote_copy(
            src_ref=vec_in,
            dst_ref=vec_all.at[p.linear],
            send_sem=move_sem.at[0, 2],
            recv_sem=move_sem.at[1, 2],
            device_id=(other // MEMBERS, other % MEMBERS),
            device_id_type=MESH,
        ).start()
        return carry

    lax.fori_loop(1, DEVICES, vec_send, 0)
    pltpu.make_async_copy(vec_in, vec_all.at[p.linear], move_sem.at[1, 2]).start()
    for part in range(3):
        third = 3 * p.linear + part
        is_fc = jnp.logical_and(third >= FC_FIRST, third < PROJ_FIRST)
        is_rows = jnp.logical_and(third >= OUT_FIRST, jnp.logical_not(is_fc))

        @pl.when(is_fc)
        def _(part=part):
            lay_fc(flat, part * third_rows, fc_pieces, part)

        @pl.when(is_rows)
        def _(part=part):
            lay_rows(flat, part * third_rows, rows, blocks, part)

    arrived(x_all.at[p.me], move_sem.at[1, 0])
    gather_x = Gather(p, x_all, x_sem)
    gather_x.begin()
    spreads = []
    for near in range(2):
        arrived(qkv_land.at[p.far, near, p.y], qkv_sem.at[1, near])
        item = Spread(p, lambda far, y, near=near: qkv_land.at[far, near, y], spread_sem, 3 * near)
        item.begin()
        spreads.append(item)
    gather_x.second_hop()
    gather_x.third_hop()
    fc_moves, rows_moves = [], []
    for part in range(3):
        third = 3 * p.linear + part
        valid = jnp.logical_and(third >= FC_FIRST, third < PROJ_FIRST)
        slot, y = fc_home(p, jnp.where(valid, third - FC_FIRST, 0))
        for member in (7, 6, 3, 2, 5, 4, 1, 0):
            target = p.target(x=member % 2, near=member // 2 % 2, core=member // 4, y=y)
            fc_moves.append(
                Move(
                    p, fc_pieces.at[part, member], fc_part.at[slot],
                    fc_send.at[part, member], fc_recv.at[slot], target, valid,
                )
            )
    for part in range(3):
        third = 3 * p.linear + part
        valid = third >= PROJ_FIRST
        unit = jnp.where(valid, third - PROJ_FIRST, 0)
        member, group = unit // 4, unit % 4
        target = p.target(
            x=member % 2, near=member // 2 % 2, core=member // 4, y=group // 2, far=group % 2
        )
        rows_moves.append(
            Move(
                p, blocks.at[part], proj_part,
                rows_sem.at[0, part], rows_sem.at[1, 0], target, valid,
            )
        )
        valid = jnp.logical_and(third >= OUT_FIRST, third < FC_FIRST)
        member = jnp.where(valid, third - OUT_FIRST, 0)
        target = p.target(
            x=member % 2, near=member // 2 % 2, core=member // 4, y=out_root(member), far=0
        )
        rows_moves.append(
            Move(
                p, blocks.at[part], out_part,
                rows_sem.at[0, part], rows_sem.at[1, 1], target, valid,
            )
        )
    gather_x.last_hop()
    back_move = Move(p, back_in, back_all.at[p.ctx], move_sem.at[0, 3], move_sem.at[1, 3], home)
    arrived(vec_all, move_sem.at[1, 2])
    cols = vec_in.shape[-1]
    used = width // MEMBERS
    total = jnp.zeros(vecs.shape, jnp.float32)
    for ctx in range(MEMBERS):
        block = jnp.concatenate([vec_all[MEMBERS * f + ctx] for f in range(GROUPS)], 0)
        lane = lax.broadcasted_iota(jnp.int32, (cols, width), 0)
        at = lax.broadcasted_iota(jnp.int32, (cols, width), 1) - used * ctx
        spot = jnp.where(jnp.logical_and(lane == at, lane < used), 1.0, 0.0)
        total = total + jnp.dot(
            block, spot.astype(jnp.bfloat16), preferred_element_type=jnp.float32
        )
    vecs[...] = total
    arrived(order, move_sem.at[1, 1])
    slots = order[0:1, :].astype(jnp.float32)
    lane = lax.broadcasted_iota(jnp.int32, (length, 128), 1)
    row = lax.broadcasted_iota(jnp.int32, (length, 128), 0)
    spot = jnp.where(lane == row // BLOCK, slots, 0.0)
    inner = lax.broadcasted_iota(jnp.int32, (length, 1), 0) % BLOCK
    row_pos[...] = jnp.sum(spot, 1, keepdims=True) * BLOCK + inner.astype(jnp.float32)
    lane = lax.broadcasted_iota(jnp.int32, (128, length), 1)
    row = lax.broadcasted_iota(jnp.int32, (128, length), 0)
    spot = jnp.where(row == lane // BLOCK, 1.0, 0.0)
    inner = lax.broadcasted_iota(jnp.int32, (1, length), 1) % BLOCK
    found = jnp.dot(
        order[...].astype(jnp.bfloat16), spot.astype(jnp.bfloat16),
        preferred_element_type=jnp.float32,
    )
    col_pos[...] = found[0:1, :] * BLOCK + inner.astype(jnp.float32)
    for item in spreads:
        item.middle()
    arrived(back_all.at[p.me], move_sem.at[1, 3])
    gather_back = Gather(p, back_all, back_sem)
    gather_back.begin()
    gather_x.finish()

    def norm_block(step, carry):
        value = norm_rows(x_all[step].astype(jnp.float32), vecs[0:1, :], vecs[1:2, :])
        h_first[pl.ds(pl.multiple_of(step * count, count), count), :] = value.astype(jnp.bfloat16)
        return carry

    lax.fori_loop(0, MEMBERS, norm_block, 0)
    to_far, to_y = p.target(far=1 - p.far), p.target(y=1 - p.y)
    fc_far, fc_y, fc_later, own_copies = [], [], [], []
    for slot in range(8):
        arrived(fc_part.at[slot], fc_recv.at[slot])
        landing = fc.at[fc_unit(p.far, p.y, slot)]
        fc_far.append(remote(fc_part.at[slot], landing, fc_sem, slot, to_far))
        fc_far[slot].start()
        fc_y.append(remote(fc_part.at[slot], landing, fc_sem, 8 + slot, to_y))
        fc_y[slot].start()
        own_copies.append(pltpu.make_async_copy(fc_part.at[slot], landing, own_sem.at[slot]))
        own_copies[slot].start()
    gather_back.second_hop()
    gather_back.third_hop()
    root_y = out_root(p.me)
    same_y = p.y == root_y
    root = jnp.logical_and(same_y, p.far == 0)
    beside = jnp.logical_and(same_y, p.far == 1)
    mine = out.at[p.me]
    out_far = remote(out_part, mine, tree_sem, 0, to_far)
    out_y = remote(out_part, mine, tree_sem, 1, to_y)
    out_later = remote(mine, mine, tree_sem, 2, to_y)
    out_own = pltpu.make_async_copy(out_part, mine, own_sem.at[8])

    @pl.when(root)
    def _():
        arrived(out_part, rows_sem.at[1, 1])
        out_far.start()
        out_y.start()
        out_own.start()

    arrived(proj_part, rows_sem.at[1, 0])
    my_proj, far_proj = proj.at[p.y, p.far], proj.at[p.y, 1 - p.far]
    proj_far = remote(proj_part, my_proj, proj_sem, 0, to_far)
    proj_y = remote(proj_part, my_proj, proj_sem, 1, to_y)
    proj_far.start()
    proj_y.start()
    proj_own = pltpu.make_async_copy(proj_part, my_proj, own_sem.at[9])
    proj_own.start()
    for item in spreads:
        item.finish()
    four = qkv_land.shape[3]
    for far in range(2):
        for near in range(2):
            for y in range(2):
                first = four * (4 * far + 2 * near + y)
                w_qkv[first : first + four, :] = qkv_land[far, near, y]
    per_part = SLOTS * HD
    bias = jnp.concatenate(
        [
            member_lanes(vecs[2:3, :], p.me, per_part),
            jnp.zeros((1, per_part), jnp.float32),
            member_lanes(vecs[16:17, :], p.me, per_part),
        ],
        1,
    )

    def qkv_block(step, carry):
        at = pl.ds(pl.multiple_of(step * 2 * count, 2 * count), 2 * count)
        value = jnp.dot(h_first[at, :], w_qkv[...], preferred_element_type=jnp.float32)
        qkv[at, :] = (value + bias).astype(jnp.bfloat16)
        return carry

    lax.fori_loop(0, MEMBERS // 2, qkv_block, 0)
    gather_back.last_hop()
    span = 2 * count

    def one_pair(pair):
        def one_block(step, carry):
            at = pl.ds(pl.multiple_of(step * span, span), span)
            attn[pair, at, :] = attend_block(
                qkv[at, 128 * pair : 128 * pair + 128],
                qkv[:, 128 * (pairs + pair) : 128 * (pairs + pair) + 128],
                qkv[:, 128 * (2 * pairs + pair) : 128 * (2 * pairs + pair) + 128],
                row_pos[at, :],
                col_pos[...],
            )
            return carry

        lax.fori_loop(0, length // span, one_block, 0)

    def share(pair):
        item = Gather(p, attn_all.at[pair], attn_sem.at[pair])
        for name, index, target in (
            ("a", 0, item.first), ("b", 1, item.second), ("c", 2, item.other),
        ):
            copy = remote(attn.at[pair], attn_all.at[pair, p.me], attn_sem.at[pair], index, target)
            copy.start()
            item.copies[name] = copy
        copy = pltpu.make_async_copy(
            attn.at[pair], attn_all.at[pair, p.me], own_sem.at[10 + pair]
        )
        copy.start()
        own_copies.append(copy)
        return item

    one_pair(0)
    gathers = [share(0)]
    for slot in range(8):
        fc_far[slot].wait_recv()
        landing = fc.at[fc_unit(1 - p.far, p.y, slot)]
        copy = remote(landing, landing, fc_sem, 16 + slot, to_y)
        copy.start()
        fc_later.append(copy)

    @pl.when(beside)
    def _():
        out_far.wait_recv()
        out_later.start()

    gathers[0].second_hop()
    gathers[0].third_hop()
    gathers[0].last_hop()
    one_pair(1)
    gathers.append(share(1))
    proj_far.wait_recv()
    proj_later = remote(far_proj, far_proj, proj_sem, 2, to_y)
    proj_later.start()
    gathers[1].second_hop()
    gathers[1].third_hop()
    gathers[1].last_hop()

    @pl.when(root)
    def _():
        out_own.wait()

    @pl.when(jnp.logical_and(jnp.logical_not(same_y), p.far == 0))
    def _():
        out_y.wait_recv()

    @pl.when(jnp.logical_and(jnp.logical_not(same_y), p.far == 1))
    def _():
        out_later.wait_recv()

    gather_out = Gather(p, out, out_sem)
    gather_out.begin()
    gather_out.second_hop()
    gather_out.third_hop()
    gather_out.last_hop()
    for item in gathers + [gather_out, gather_back]:
        item.finish()
    for item in fc_y + fc_later + [proj_y, proj_later]:
        item.wait_recv()
    for item in fc_far + fc_y + fc_later + [proj_far, proj_y, proj_later]:
        item.wait_send()

    @pl.when(root)
    def _():
        out_far.wait_send()
        out_y.wait_send()

    @pl.when(beside)
    def _():
        out_later.wait_send()

    for item in own_copies + [proj_own]:
        item.wait()
    for item in [x_move, order_move, back_move] + qkv_moves + fc_moves + rows_moves:
        item.sent()
    arrived(vec_all.at[pl.ds(1, DEVICES - 1)], move_sem.at[0, 2])


def forward(x, back, order, vectors, weights):
    rows, width = x.shape
    kind, high = jnp.bfloat16, jnp.float32
    unit, hidden = width // DEVICES, FF // MEMBERS
    four, cols = 4 * unit, 3 * SLOTS * HD
    length, pairs = MEMBERS * rows, SLOTS // 2
    any_space = pl.BlockSpec(memory_space=pl.ANY)
    vmem = pl.BlockSpec(memory_space=pltpu.VMEM)
    dma = pltpu.SemaphoreType.DMA

    def like(*shape, dtype=kind):
        return jax.ShapeDtypeStruct(shape, dtype)

    return pl.pallas_call(
        forward_kernel,
        out_shape=[
            like(MEMBERS, rows, width),
            like(MEMBERS, rows, width),
            like(GROUPS * vectors.shape[0], width, dtype=high),
            like(length, 1, dtype=high),
            like(1, length, dtype=high),
            like(width, cols),
            like(length, width),
            like(length, cols),
            like(pairs, MEMBERS, length, 2 * HD),
            like(DEVICES, unit, hidden),
            like(2, 2, four, width),
            like(MEMBERS, four, width),
        ],
        in_specs=[any_space] * 4 + [vmem],
        out_specs=[vmem, any_space] + [vmem] * 6 + [any_space] * 4,
        scratch_shapes=[
            pltpu.VMEM(weights.shape, high),
            pltpu.VMEM((-(-width // 128), four, 128), high),
            pltpu.VMEM((MEMBERS, four, cols), kind),
            pltpu.VMEM((3, MEMBERS, unit, hidden), kind),
            pltpu.VMEM((3, four, width), kind),
            pltpu.VMEM(order.shape, order.dtype),
            pltpu.VMEM((DEVICES,) + vectors.shape, kind),
            pltpu.VMEM((2, 2, 2, four, cols), kind),
            pltpu.VMEM((pairs, length, 2 * HD), kind),
            pltpu.VMEM((8, unit, hidden), kind),
            pltpu.VMEM((four, width), kind),
            pltpu.VMEM((four, width), kind),
            dma((2, 4)),
            dma((2, 8)),
            dma((3, 8)),
            dma((8,)),
            dma((2, 3)),
            dma((2, 7)),
            dma((2, 7)),
            dma((2, 6)),
            dma((12,)),
            dma((2, 24)),
            dma((2, 3)),
            dma((2, 3)),
            dma((2, 7)),
            dma((pairs, 2, 7)),
        ],
        compiler_params=pltpu.CompilerParams(
            collective_id=1, has_side_effects=True, vmem_limit_bytes=VMEM_BYTES
        ),
        name="forward",
    )(x, back, order, vectors, weights)


def gather_kernel(own, out, local_sem, sems):
    p = Place()
    item = Gather(p, out, sems)
    greet((item.first, item.second, item.other))
    for name, index, target in (("a", 0, item.first), ("b", 1, item.second), ("c", 2, item.other)):
        copy = remote(own, out.at[p.me], sems, index, target)
        copy.start()
        item.copies[name] = copy
    local = pltpu.make_async_copy(own, out.at[p.me], local_sem)
    local.start()
    item.second_hop()
    item.third_hop()
    item.last_hop()
    item.finish()
    local.wait()


def group_gather(value, ident):
    any_space = pl.BlockSpec(memory_space=pl.ANY)
    return pl.pallas_call(
        gather_kernel,
        out_shape=jax.ShapeDtypeStruct((MEMBERS,) + value.shape, value.dtype),
        in_specs=[any_space],
        out_specs=any_space,
        scratch_shapes=[pltpu.SemaphoreType.DMA, pltpu.SemaphoreType.DMA((2, 7))],
        compiler_params=pltpu.CompilerParams(collective_id=ident, has_side_effects=True),
        name="group_gather",
    )(value)


def scatter_kernel(part, out, from_core, sums, two, got, last, done, sems):
    p = Place()
    route = Gather(p, None, None)
    greet((route.first, route.second, route.other))
    copies = []
    for j in (3, 2, 1, 0):
        item = remote(part.at[4 * (1 - p.core) + j], from_core.at[j], sems, j, route.other)
        item.start()
        copies.append(item)
    mine = 4 * p.core
    here, there = p.me - mine, route.of_first - mine
    beyond, across = route.of_second - mine, route.of_both - mine
    for item in copies:
        item.wait_recv()

    def summed(block):
        return part[mine + block].astype(jnp.float32) + from_core[block].astype(jnp.float32)

    two[0] = summed(across).astype(jnp.bfloat16)
    send_across = remote(two.at[0], got.at[0], sems, 4, route.second)
    send_across.start()
    two[1] = summed(beyond).astype(jnp.bfloat16)
    send_beyond = remote(two.at[1], got.at[1], sems, 5, route.second)
    send_beyond.start()
    sums[...] = summed(there)
    send_across.wait_recv()
    last[...] = (sums[...] + got[0].astype(jnp.float32)).astype(jnp.bfloat16)
    send_last = remote(last, done, sems, 6, route.first)
    send_last.start()
    sums[...] = summed(here)
    send_beyond.wait_recv()
    sums[...] += got[1].astype(jnp.float32)
    send_last.wait_recv()
    out[...] = sums[...] + done[...].astype(jnp.float32)
    for item in copies + [send_across, send_beyond, send_last]:
        item.wait_send()


def group_scatter(value, ident):
    rows, width = value.shape
    rows = rows // MEMBERS
    low = jnp.bfloat16
    vmem = pl.BlockSpec(memory_space=pltpu.VMEM)
    return pl.pallas_call(
        scatter_kernel,
        out_shape=jax.ShapeDtypeStruct((rows, width), jnp.float32),
        in_specs=[vmem],
        out_specs=vmem,
        scratch_shapes=[
            pltpu.VMEM((4, rows, width), low),
            pltpu.VMEM((rows, width), jnp.float32),
            pltpu.VMEM((2, rows, width), low),
            pltpu.VMEM((2, rows, width), low),
            pltpu.VMEM((rows, width), low),
            pltpu.VMEM((rows, width), low),
            pltpu.SemaphoreType.DMA((2, 7)),
        ],
        compiler_params=pltpu.CompilerParams(
            collective_id=ident, has_side_effects=True, vmem_limit_bytes=VMEM_BYTES
        ),
        name="group_scatter",
    )(value.reshape(MEMBERS, rows, width))


def wide(value):
    return value.astype(jnp.float32)


def low(value):
    return value.astype(jnp.bfloat16)


class Fold:
    def __init__(self, place, at, landing, leaving, last, sems, first):
        p = place
        self.p, self.at, self.landing, self.leaving, self.last = p, at, landing, leaving, last
        self.to_far, self.to_y = p.target(far=1 - p.far), p.target(y=1 - p.y)
        self.sems, self.first = sems, first

    def begin(self):
        p = self.p
        other = 1 - p.far
        self.a = remote(
            self.at(other, 1 - p.y), self.landing(other), self.sems, self.first, self.to_y
        )
        self.b = remote(
            self.at(p.far, 1 - p.y), self.landing(p.far), self.sems, self.first + 1, self.to_y
        )
        self.a.start()
        self.b.start()

    def middle(self):
        p = self.p
        other = 1 - p.far
        self.a.wait_recv()
        self.leaving[...] = low(wide(self.at(other, p.y)[...]) + wide(self.landing(other)[...]))
        self.c = remote(self.leaving, self.last, self.sems, self.first + 2, self.to_far)
        self.c.start()

    def end(self):
        p = self.p
        self.b.wait_recv()
        partial = wide(self.at(p.far, p.y)[...]) + wide(self.landing(p.far)[...])
        self.c.wait_recv()
        return low(partial + wide(self.last[...]))

    def sent(self):
        for item in (self.a, self.b, self.c):
            item.wait_send()


def yield_kernel(
    qkv, fc, proj, out, vec,
    qkv_back, fc_back, rows_back, vec_back,
    qkv_y, fc_y, proj_y, out_y, qkv_go, fc_go, proj_go, out_go,
    qkv_far, fc_far, proj_far, out_far, qkv_sum, fc_sum, proj_sum, out_sum, vec_got,
    fold_sem, tree_sem, vec_sem, qkv_send, qkv_recv, fc_send, fc_recv, rows_send, rows_recv,
):
    p = Place()
    unit = fc_back.shape[2]
    greet_all(p)
    folds = [
        Fold(
            p, lambda far, y: proj.at[y, far], lambda far: proj_y.at[far],
            proj_go, proj_far, fold_sem, 0,
        )
    ]
    for near in range(2):
        folds.append(
            Fold(
                p, lambda far, y, near=near: fc.at[far, near, y],
                lambda far, near=near: fc_y.at[far, near],
                fc_go.at[near], fc_far.at[near], fold_sem, 3 + 3 * near,
            )
        )
    for near in range(2):
        folds.append(
            Fold(
                p, lambda far, y, near=near: qkv.at[far, near, y],
                lambda far, near=near: qkv_y.at[far, near],
                qkv_go.at[near], qkv_far.at[near], fold_sem, 9 + 3 * near,
            )
        )
    for item in folds:
        item.begin()
    root_y, root_far = p.me % 4 // 2, p.me % 2
    same_y, same_far = p.y == root_y, p.far == root_far
    root = jnp.logical_and(same_y, same_far)
    beside = jnp.logical_and(same_y, jnp.logical_not(same_far))
    over_y = remote(out, out_y, tree_sem, 0, p.target(y=1 - p.y))
    over_far = remote(out_go, out_far, tree_sem, 1, p.target(far=1 - p.far))

    @pl.when(jnp.logical_not(same_y))
    def _():
        over_y.start()

    def vec_copy(step):
        other = (p.linear + step) % DEVICES
        return pltpu.make_async_remote_copy(
            src_ref=vec.at[other],
            dst_ref=vec_got.at[p.linear],
            send_sem=vec_sem.at[0],
            recv_sem=vec_sem.at[1],
            device_id=(other // MEMBERS, other % MEMBERS),
            device_id_type=MESH,
        )

    def vec_send(step, carry):
        vec_copy(step).start()
        return carry

    lax.fori_loop(1, DEVICES, vec_send, 0)
    pltpu.make_async_copy(vec.at[p.linear], vec_got.at[p.linear], vec_sem.at[1]).start()
    for item in folds:
        item.middle()

    @pl.when(same_y)
    def _():
        over_y.wait_recv()

    @pl.when(beside)
    def _():
        out_go[...] = low(wide(out[...]) + wide(out_y[...]))
        over_far.start()

    moves = []
    proj_sum[...] = folds[0].end()
    target, part = shard_of(PROJ_FIRST + 4 * p.me + p.group)
    moves.append(
        Move(p, proj_sum, rows_back.at[part], rows_send.at[0], rows_recv.at[part], target)
    )
    for near in range(2):
        block = folds[1 + near].end()
        for slot in range(4):
            fc_sum[near, slot] = block[slot * unit : (slot + 1) * unit]
            third = FC_FIRST + 4 * (4 * p.far + 2 * near + p.y) + slot
            target, part = shard_of(third)
            moves.append(
                Move(
                    p, fc_sum.at[near, slot], fc_back.at[part, p.me],
                    fc_send.at[near, slot], fc_recv.at[part, p.me], target,
                )
            )

    @pl.when(root)
    def _():
        over_far.wait_recv()
        out_sum[...] = low(wide(out[...]) + wide(out_y[...]) + wide(out_far[...]))

    target, part = shard_of(OUT_FIRST + p.me)
    moves.append(
        Move(p, out_sum, rows_back.at[part], rows_send.at[1], rows_recv.at[part], target, root)
    )
    for near in range(2):
        qkv_sum[near] = folds[3 + near].end()
        target = (0 * p.fsdp, 4 * p.far + 2 * near + p.y)
        moves.append(
            Move(
                p, qkv_sum.at[near], qkv_back.at[p.me], qkv_send.at[near], qkv_recv.at[p.me],
                target,
            )
        )
    @pl.when(p.fsdp == 0)
    def _():
        for member in range(MEMBERS):
            arrived(qkv_back.at[member], qkv_recv.at[member])

    for part in range(3):
        third = 3 * p.linear + part
        is_fc = jnp.logical_and(third >= FC_FIRST, third < PROJ_FIRST)
        is_rows = jnp.logical_and(third >= OUT_FIRST, jnp.logical_not(is_fc))

        @pl.when(is_fc)
        def _(part=part):
            for member in range(MEMBERS):
                arrived(fc_back.at[part, member], fc_recv.at[part, member])

        @pl.when(is_rows)
        def _(part=part):
            arrived(rows_back.at[part], rows_recv.at[part])

    arrived(vec_got, vec_sem.at[1])
    vec_back[...] = jnp.sum(vec_got[...], 0)
    arrived(vec_got.at[pl.ds(1, DEVICES - 1)], vec_sem.at[0])
    for item in folds:
        item.sent()

    @pl.when(jnp.logical_not(same_y))
    def _():
        over_y.wait_send()

    @pl.when(beside)
    def _():
        over_far.wait_send()

    for item in moves:
        item.sent()


def yield_grads(qkv, fc, proj, out, vec):
    kind = jnp.bfloat16
    four, wide_qkv = qkv.shape[-2:]
    hidden = fc.shape[-1]
    width = proj.shape[-1]
    unit = four // 4
    any_space = pl.BlockSpec(memory_space=pl.ANY)
    vmem = pl.BlockSpec(memory_space=pltpu.VMEM)

    def buffer(*shape, dtype=kind):
        return pltpu.VMEM(shape, dtype)

    dma = pltpu.SemaphoreType.DMA
    return pl.pallas_call(
        yield_kernel,
        out_shape=[
            jax.ShapeDtypeStruct((MEMBERS, four, wide_qkv), kind),
            jax.ShapeDtypeStruct((3, MEMBERS, unit, hidden), kind),
            jax.ShapeDtypeStruct((3, four, width), kind),
            jax.ShapeDtypeStruct(vec.shape[1:], vec.dtype),
        ],
        in_specs=[vmem] * 5,
        out_specs=[any_space, any_space, any_space, vmem],
        scratch_shapes=[
            buffer(2, 2, four, wide_qkv),
            buffer(2, 2, four, hidden),
            buffer(2, four, width),
            buffer(four, width),
            buffer(2, four, wide_qkv),
            buffer(2, four, hidden),
            buffer(four, width),
            buffer(four, width),
            buffer(2, four, wide_qkv),
            buffer(2, four, hidden),
            buffer(four, width),
            buffer(four, width),
            buffer(2, four, wide_qkv),
            buffer(2, 4, unit, hidden),
            buffer(four, width),
            buffer(four, width),
            buffer(*vec.shape, dtype=vec.dtype),
            dma((2, 15)),
            dma((2, 2)),
            dma((2,)),
            dma((2,)),
            dma((8,)),
            dma((2, 4)),
            dma((3, 8)),
            dma((2,)),
            dma((3,)),
        ],
        compiler_params=pltpu.CompilerParams(
            collective_id=2, has_side_effects=True, vmem_limit_bytes=VMEM_BYTES
        ),
        name="yield_grads",
    )(qkv, fc, proj, out, vec)


def lane_of(shape):
    return lax.broadcasted_iota(jnp.int32, shape, 1) // HD


def dot_nt(a, b):
    return lax.dot_general(a, b, (((1,), (1,)), ((), ())), preferred_element_type=jnp.float32)


def dot_tn(a, b):
    return lax.dot_general(a, b, (((0,), (0,)), ((), ())), preferred_element_type=jnp.float32)


def probabilities(query, keys, row_pos, col_pos):
    scores = dot_nt(query, keys) * 0.125
    scores = jnp.where(col_pos <= row_pos, scores, -1e30)
    weights = jnp.exp(scores - jnp.max(scores, -1, keepdims=True))
    return weights / jnp.sum(weights, -1, keepdims=True)


def attend_back_kernel(
    query, keys, values, grad, row_pos, col_pos, dquery, dkeys, dvalues, key_sum, value_sum
):
    step = pl.program_id(1)

    @pl.when(step == 0)
    def _():
        key_sum[...] = jnp.zeros_like(key_sum)
        value_sum[...] = jnp.zeros_like(value_sum)

    lanes = lane_of(query.shape)
    result = jnp.zeros(query.shape, jnp.float32)
    add_keys = add_values = 0.0
    for head in range(2):
        mine = lanes == head
        own = jnp.where(mine, query[...], jnp.zeros_like(query))
        own_grad = jnp.where(mine, grad[...], jnp.zeros_like(grad))
        probs = probabilities(own, keys[...], row_pos[...], col_pos[...])
        dprobs = dot_nt(own_grad, values[...])
        delta = jnp.sum(probs * dprobs, -1, keepdims=True)
        dscores = (probs * (dprobs - delta)).astype(jnp.bfloat16)
        mixed = jnp.dot(dscores, keys[...], preferred_element_type=jnp.float32)
        result = jnp.where(mine, mixed, result)
        add_keys = add_keys + dot_tn(dscores, own)
        add_values = add_values + dot_tn(probs.astype(jnp.bfloat16), own_grad)
    dquery[...] = (result * 0.125).astype(jnp.bfloat16)
    key_sum[...] += add_keys
    value_sum[...] += add_values

    @pl.when(step == pl.num_programs(1) - 1)
    def _():
        dkeys[...] = (key_sum[...] * 0.125).astype(jnp.bfloat16)
        dvalues[...] = value_sum[...].astype(jnp.bfloat16)


def attend_back(qkv, grad, row_pos, col_pos, span):
    length = qkv.shape[0]
    wide = 2 * HD
    whole = jax.ShapeDtypeStruct((length, SLOTS * HD), jnp.bfloat16)
    return pl.pallas_call(
        attend_back_kernel,
        grid=(SLOTS // 2, length // span),
        in_specs=[
            pl.BlockSpec((span, wide), lambda h, i: (i, h)),
            pl.BlockSpec((length, wide), lambda h, i: (0, SLOTS // 2 + h)),
            pl.BlockSpec((length, wide), lambda h, i: (0, SLOTS + h)),
            pl.BlockSpec((span, wide), lambda h, i: (i, h)),
            pl.BlockSpec((span, 1), lambda h, i: (i, 0)),
            pl.BlockSpec((1, length), lambda h, i: (0, 0)),
        ],
        out_specs=[
            pl.BlockSpec((span, wide), lambda h, i: (i, h)),
            pl.BlockSpec((length, wide), lambda h, i: (0, h)),
            pl.BlockSpec((length, wide), lambda h, i: (0, h)),
        ],
        out_shape=[whole, whole, whole],
        scratch_shapes=[
            pltpu.VMEM((length, wide), jnp.float32),
            pltpu.VMEM((length, wide), jnp.float32),
        ],
        compiler_params=pltpu.CompilerParams(vmem_limit_bytes=VMEM_BYTES),
        name="attend_back",
    )(qkv, qkv, qkv, grad, row_pos, col_pos)


def own_heads(member):
    return (head_start(member + 1) - head_start(member)) * HD


def all_heads(pieces):
    return jnp.concatenate([pieces[m][:, : own_heads(m)] for m in range(MEMBERS)], 1)


def to_group(value):
    pairs = []
    for f in range(GROUPS):
        for c in range(MEMBERS):
            core, near, x = c // 4, c // 2 % 2, c % 2
            y, far = f // 2, f % 2
            pairs.append((f * MEMBERS + c, (2 * x + core) * MEMBERS + 4 * far + 2 * near + y))
    return lax.ppermute(value, ("fsdp", "ctx"), pairs)


def per_device_groups(
    inputs, cotangent, slot_order, weights, vectors, first_w, second_w, first_vec, second_vec
):
    seqs, rows, width = inputs.shape
    kind, high = jnp.bfloat16, jnp.float32
    fsdp, ctx = lax.axis_index("fsdp"), lax.axis_index("ctx")
    member = 4 * (fsdp % 2) + 2 * (ctx // 2 % 2) + fsdp // 2
    length = rows * MEMBERS
    hidden = FF // MEMBERS
    local = weights.shape[0]
    third = local // 3
    unit = width // DEVICES
    four = 4 * unit
    per_part = SLOTS * HD

    order = jnp.pad(slot_order, ((0, 127), (0, 128 - slot_order.shape[1])))
    vec_rows, vec_cols = vectors.shape
    padded = jnp.pad(vectors, ((0, 16 - vec_rows), (0, -vec_cols % 128)))
    (
        x_all, back_all, vec, row_pos, col_pos, own_qkv, h_first, qkv, attn_all,
        own_fc, own_proj, full_out,
    ) = forward(
        inputs.reshape(rows, width), cotangent.reshape(rows, width), order, padded, weights
    )
    x_all, back_all = x_all.reshape(length, width), back_all.reshape(length, width)
    own_fc = own_fc.reshape(width, hidden)
    own_proj = own_proj.reshape(hidden, width)
    full_out = full_out.reshape(width, width)
    attn_all = all_heads(jnp.concatenate([attn_all[0], attn_all[1]], 2))
    vec = vec.reshape(GROUPS, -1, width)[:, :vec_rows].reshape(-1, width)
    head_at = HEADS * member // MEMBERS * HD
    bias_fc = lax.dynamic_slice(vec[8:].reshape(-1), (member * hidden,), (hidden,))
    mine = member * rows
    span = min(length, 256)
    resid = x_all.astype(high) + jnp.dot(attn_all, full_out, preferred_element_type=high) + vec[4]
    h_second = layer_norm(resid, vec[5], vec[6]).astype(kind)
    pre = jnp.dot(h_second, own_fc, preferred_element_type=high) + bias_fc
    act, pull_gelu = jax.vjp(gelu_tanh, pre)
    act = act.astype(kind)
    made = group_scatter(jnp.dot(act, own_proj, preferred_element_type=high).astype(kind), 4)
    resid_own = lax.dynamic_slice_in_dim(resid, mine, rows, 0)
    outputs = (resid_own + made + vec[7]).astype(kind)

    back_own = lax.dynamic_slice_in_dim(back_all, mine, rows, 0).astype(high)
    grad_proj = jnp.einsum("tf,td->fd", act, back_all, preferred_element_type=high).astype(kind)
    grad_bp = jnp.sum(back_own, 0)
    dact = jnp.einsum("td,fd->tf", back_all, own_proj, preferred_element_type=high)
    dpre = pull_gelu(dact)[0].astype(kind)
    grad_fc = jnp.einsum("td,tf->df", h_second, dpre, preferred_element_type=high).astype(kind)
    grad_bf = jnp.sum(dpre, 0, dtype=high)
    dh_second = group_scatter(
        jnp.einsum("tf,df->td", dpre, own_fc, preferred_element_type=high).astype(kind), 4
    )
    _, pull_second = jax.vjp(layer_norm, resid_own, vec[5], vec[6])
    dres_ln, grad_g2, grad_b2 = pull_second(dh_second)
    dresid = back_own + dres_ln
    dbranch = dresid.astype(kind)
    grad_bo = jnp.sum(dbranch, 0, dtype=high)
    dbranch_all = group_gather(dbranch, 5).reshape(length, width)
    out_heads = lax.dynamic_slice_in_dim(full_out, head_at, per_part, 0)
    dattn = jnp.einsum("te,de->td", dbranch_all, out_heads, preferred_element_type=high)
    dattn = dattn.astype(kind)
    attn_cols = lax.dynamic_slice_in_dim(attn_all, member * four, four, 1)
    grad_out = jnp.einsum("td,te->de", attn_cols, dbranch_all, preferred_element_type=high)
    dqkv = jnp.concatenate(attend_back(qkv, dattn, row_pos, col_pos, span), 1)
    lane = jnp.arange(per_part)
    keep = lane < jnp.where(member == MEMBERS - 1, per_part, (SLOTS - 1) * HD)
    dqkv = jnp.where(jnp.tile(keep, 3), dqkv, jnp.zeros_like(dqkv))
    grad_qkv = jnp.einsum("td,te->de", h_first, dqkv, preferred_element_type=high).astype(kind)
    bias_sums = jnp.sum(dqkv, 0, dtype=high)
    dh_first = group_scatter(
        jnp.einsum("te,de->td", dqkv, own_qkv, preferred_element_type=high).astype(kind), 4
    )
    x_own = lax.dynamic_slice_in_dim(x_all, mine, rows, 0).astype(high)
    _, pull_first = jax.vjp(layer_norm, x_own, vec[0], vec[1])
    dx_ln, grad_g1, grad_b1 = pull_first(dh_first)
    input_grad = (dresid + dx_ln).astype(kind)
    results = to_group(jnp.concatenate([outputs, input_grad], 1))
    outputs = results[:, :width].reshape(seqs, rows, width)
    input_grad = results[:, width:].reshape(seqs, rows, width)

    zero_row = jnp.zeros((width,), high)
    row_q = lax.dynamic_update_slice(zero_row, bias_sums[:per_part], (head_at,))
    row_v = lax.dynamic_update_slice(zero_row, bias_sums[2 * per_part :], (head_at,))
    row_f = lax.dynamic_update_slice(jnp.zeros((FF,), high), grad_bf, (member * hidden,))
    grad_vec = jnp.concatenate(
        [
            jnp.stack([grad_g1, grad_b1, row_q, row_v, grad_bo, grad_g2, grad_b2, grad_bp]),
            row_f.reshape(-1, width),
        ],
        0,
    )
    grad_vec = grad_vec.reshape(GROUPS, vec_rows, MEMBERS, vec_cols).transpose(0, 2, 1, 3)
    grad_vec = grad_vec.reshape(DEVICES, vec_rows, vec_cols)
    grad_vec = jnp.pad(grad_vec, ((0, 0), (0, 8 - vec_rows), (0, -vec_cols % 128)))
    qkv_back, fc_back, rows_back, vec_back = yield_grads(
        grad_qkv.reshape(2, 2, 2, four, 3 * per_part),
        grad_fc.reshape(2, 2, 2, four, hidden),
        grad_proj.reshape(2, 2, four, width),
        grad_out.astype(kind),
        grad_vec,
    )
    qkv_flat = jnp.concatenate(
        [all_heads(qkv_back[:, :, p * per_part : (p + 1) * per_part]) for p in range(3)], 1
    ).reshape(local, 128)
    fc_flat = fc_back.transpose(0, 2, 1, 3).reshape(3, third, 128)
    rows_flat = rows_back.reshape(3, third, 128)
    thirds = 3 * (fsdp * MEMBERS + ctx) + jnp.arange(3)
    is_fc = jnp.logical_and(thirds >= FC_FIRST, thirds < PROJ_FIRST)
    others = jnp.where(is_fc[:, None, None], fc_flat, rows_flat).reshape(local, 128)
    owned = jnp.where(fsdp == 0, qkv_flat, others).astype(high)
    new_w = adamw(weights, owned, first_w, second_w, rate_matrix, weight_decay)
    owned_vec = vec_back[:vec_rows, :vec_cols]
    new_vec = adamw(vectors, owned_vec, first_vec, second_vec, rate_vector, 0.0)
    return (outputs, input_grad, new_w[0], new_w[1], new_w[2], new_vec[0], new_vec[1], new_vec[2])


def solution(mesh):
    in_specs = (
        P("fsdp", "ctx", None),
        P("fsdp", "ctx", None),
        P("fsdp", None),
        P(("fsdp", "ctx"), None),
        P("fsdp", "ctx"),
        P(("fsdp", "ctx"), None),
        P(("fsdp", "ctx"), None),
        P("fsdp", "ctx"),
        P("fsdp", "ctx"),
    )
    out_specs = (
        P("fsdp", "ctx", None),
        P("fsdp", "ctx", None),
        P(("fsdp", "ctx"), None),
        P(("fsdp", "ctx"), None),
        P(("fsdp", "ctx"), None),
        P("fsdp", "ctx"),
        P("fsdp", "ctx"),
        P("fsdp", "ctx"),
    )
    per_device = per_device_groups if mesh.shape["ctx"] == MEMBERS else per_device_ring
    return jax.shard_map(
        per_device, mesh=mesh, in_specs=in_specs, out_specs=out_specs, check_vma=False
    )
```

```python
import jax
import jax.numpy as jnp
from jax import lax
from jax.experimental import pallas as pl
from jax.experimental.pallas import tpu as pltpu
from jax.sharding import PartitionSpec as P

HEADS = 25
HD = 64
FF = 6400
STEP = 10


epsilon_norm = 1e-05
beta_first = 0.9
beta_second = 0.999
epsilon_adam = 1e-08
weight_decay = 0.1
rate_matrix = 0.1
rate_vector = 0.8


def shifted(value, axis, steps):
    count = lax.axis_size(axis)
    pairs = [(source, (source + steps) % count) for source in range(count)]
    return lax.ppermute(value, axis, pairs)


def layer_norm(value, gain, shift):
    center = value - jnp.mean(value, -1, keepdims=True)
    spread = jnp.mean(center * center, -1, keepdims=True)
    return center * lax.rsqrt(spread + epsilon_norm) * gain + shift


def gelu_tanh(value):
    return jax.nn.gelu(value, approximate=True)


def key_positions(slot_order, first_slot, slots, block):
    groups = lax.dynamic_slice_in_dim(slot_order, first_slot, slots, 1)
    offsets = jnp.arange(block, dtype=jnp.int32)
    return (groups[:, :, None] * block + offsets).reshape(slot_order.shape[0], slots * block)


def unpack_flat(flat, width, hidden):
    flat = flat.reshape(-1)
    first_end = 3 * width * width
    second_end = 4 * width * width
    third_end = 4 * width * width + width * hidden
    return (
        flat[:first_end].reshape(width, 3 * width),
        flat[first_end:second_end].reshape(width, width),
        flat[second_end:third_end].reshape(width, hidden),
        flat[third_end:].reshape(hidden, width),
    )


def gather_params(weights, vectors):
    local = weights.reshape(1, weights.shape[0], weights.shape[1])
    part = (
        lax.all_gather(local, "fsdp", axis=0, tiled=True),
        lax.all_gather(vectors, "fsdp", axis=0, tiled=True),
    )
    return (
        lax.all_gather(part[0], "ctx", axis=1, tiled=True),
        lax.all_gather(part[1], "ctx", axis=1, tiled=True),
    )


def reduce_grads(grad_flat, grad_vec):
    part = (
        lax.psum_scatter(
            grad_flat.astype(jnp.bfloat16), "fsdp", scatter_dimension=0, tiled=True
        ).astype(jnp.float32),
        lax.psum_scatter(
            grad_vec.astype(jnp.bfloat16), "fsdp", scatter_dimension=0, tiled=True
        ).astype(jnp.float32),
    )
    return (
        lax.psum_scatter(
            part[0].astype(jnp.bfloat16), "ctx", scatter_dimension=1, tiled=True
        ).astype(jnp.float32),
        lax.psum_scatter(
            part[1].astype(jnp.bfloat16), "ctx", scatter_dimension=1, tiled=True
        ).astype(jnp.float32),
    )


def pass_grads(grad_pairs):
    return shifted(grad_pairs.astype(jnp.bfloat16), "ctx", 1).astype(grad_pairs.dtype)


def adamw(weight, grad, first, second, rate, decay):
    first = beta_first * first + (1.0 - beta_first) * grad
    second = beta_second * second + (1.0 - beta_second) * grad * grad
    first_hat = first / (1.0 - beta_first**STEP)
    second_hat = second / (1.0 - beta_second**STEP)
    weight = weight.astype(jnp.float32)
    updated = weight - rate * (first_hat / (jnp.sqrt(second_hat) + epsilon_adam) + decay * weight)
    return (first, second, updated)


def per_device_ring(
    inputs, cotangent, slot_order, weights, vectors, first_w, second_w, first_vec, second_vec
):
    seqs, rows, width = inputs.shape
    tokens = seqs * rows
    block = rows // 2
    cycle = lax.axis_size("ctx")
    shards = lax.axis_size("fsdp")
    me = lax.axis_index("ctx")
    full_flat, full_vec = gather_params(weights, vectors)
    full_qkv, full_out, full_fc, full_proj = unpack_flat(full_flat, width, FF)
    vec = full_vec.astype(jnp.float32)
    bias_fc = vec[8:].reshape(-1)
    x_in = inputs.reshape(tokens, width).astype(jnp.float32)
    h_first, pull_first = jax.vjp(layer_norm, x_in, vec[0], vec[1])
    h_first_b = h_first.astype(jnp.bfloat16)
    zero_row = jnp.zeros((width,), jnp.float32)
    qkv = jnp.dot(h_first_b, full_qkv, preferred_element_type=jnp.float32)
    qkv_b = (qkv + jnp.concatenate([vec[2], zero_row, vec[3]])).astype(jnp.bfloat16)
    query_heads = qkv_b[:, :width].reshape(seqs, rows, HEADS, HD)
    key_value = qkv_b[:, width:].reshape(seqs, rows, 2, width)
    query_pos = key_positions(slot_order, 2 * me, 2, block)

    def online(state, item):
        top, total, accum = state
        keys_i, values_i, pos_i = item
        scores = (
            jnp.einsum("sqhd,skhd->shqk", query_heads, keys_i, preferred_element_type=jnp.float32)
            * 0.125
        )
        allowed = pos_i[:, None, None, :] <= query_pos[:, None, :, None]
        scores = jnp.where(allowed, scores, -1e30)
        peak = jnp.maximum(top, jnp.max(scores, -1))
        weights_p = jnp.where(allowed, jnp.exp(scores - peak[..., None]), 0.0)
        factor = jnp.exp(top - peak)
        total = total * factor + jnp.sum(weights_p, -1)
        mixed = jnp.einsum(
            "shqk,skhd->sqhd",
            weights_p.astype(jnp.bfloat16),
            values_i,
            preferred_element_type=jnp.float32,
        )
        accum = accum * jnp.transpose(factor, (0, 2, 1))[..., None] + mixed
        return ((peak, total, accum), None)

    start_state = (
        jnp.full((seqs, HEADS, rows), -1e30, jnp.float32),
        jnp.zeros((seqs, HEADS, rows), jnp.float32),
        jnp.zeros((seqs, rows, HEADS, HD), jnp.float32),
    )
    state = start_state
    piece = lax.all_gather(key_value, "ctx", axis=1, tiled=True)
    count = piece.shape[1]
    turns = count // rows
    pos_all = key_positions(slot_order, jnp.int32(0) // block, count // block, block)
    stack = piece.reshape(seqs, turns, rows, 2, HEADS, HD).transpose(1, 0, 2, 3, 4, 5)
    pos_stack = pos_all.reshape(seqs, turns, rows).transpose(1, 0, 2)
    state, _ = lax.scan(online, state, (stack[:, :, :, 0], stack[:, :, :, 1], pos_stack))
    top, total, accum = state
    attn = accum / jnp.transpose(total, (0, 2, 1))[..., None]
    logsum = top + jnp.log(total)
    attn_b = attn.reshape(tokens, width).astype(jnp.bfloat16)
    resid = x_in + jnp.dot(attn_b, full_out, preferred_element_type=jnp.float32) + vec[4]
    h_second, pull_second = jax.vjp(layer_norm, resid, vec[5], vec[6])
    h_second_b = h_second.astype(jnp.bfloat16)
    pre = jnp.dot(h_second_b, full_fc, preferred_element_type=jnp.float32) + bias_fc
    act, pull_gelu = jax.vjp(gelu_tanh, pre)
    act_b = act.astype(jnp.bfloat16)
    result = resid + jnp.dot(act_b, full_proj, preferred_element_type=jnp.float32) + vec[7]
    outputs = result.astype(jnp.bfloat16).reshape(seqs, rows, width)
    back_b = cotangent.reshape(tokens, width)
    back = back_b.astype(jnp.float32)
    grad_proj = jnp.einsum("tf,td->fd", act_b, back_b, preferred_element_type=jnp.float32)
    grad_bp = jnp.sum(back, 0)
    dact = jnp.einsum("td,fd->tf", back_b, full_proj, preferred_element_type=jnp.float32)
    dpre_b = pull_gelu(dact)[0].astype(jnp.bfloat16)
    grad_fc = jnp.einsum("td,tf->df", h_second_b, dpre_b, preferred_element_type=jnp.float32)
    grad_bf = jnp.sum(dpre_b, 0, dtype=jnp.float32)
    dh_second = jnp.einsum("tf,df->td", dpre_b, full_fc, preferred_element_type=jnp.float32)
    dres_ln, grad_g2, grad_b2 = pull_second(dh_second)
    dresid = back + dres_ln
    dbranch_b = dresid.astype(jnp.bfloat16)
    grad_bo = jnp.sum(dbranch_b, 0, dtype=jnp.float32)
    grad_out = jnp.einsum("td,te->de", attn_b, dbranch_b, preferred_element_type=jnp.float32)
    dattn_b = jnp.einsum(
        "te,de->td", dbranch_b, full_out, preferred_element_type=jnp.float32
    ).astype(jnp.bfloat16)
    grad_heads = dattn_b.reshape(seqs, rows, HEADS, HD)
    delta = jnp.transpose(jnp.sum(grad_heads.astype(jnp.float32) * attn, -1), (0, 2, 1))

    def contribute(pair, source):
        pos_k = key_positions(slot_order, 2 * source, 2, block)
        key_h = pair[:, :, 0].reshape(seqs, rows, HEADS, HD)
        value_h = pair[:, :, 1].reshape(seqs, rows, HEADS, HD)
        scores = (
            jnp.einsum("sqhd,skhd->shqk", query_heads, key_h, preferred_element_type=jnp.float32)
            * 0.125
        )
        allowed = pos_k[:, None, None, :] <= query_pos[:, None, :, None]
        probs = jnp.where(allowed, jnp.exp(scores - logsum[..., None]), 0.0)
        dvalue = jnp.einsum(
            "shqk,sqhd->skhd",
            probs.astype(jnp.bfloat16),
            grad_heads,
            preferred_element_type=jnp.float32,
        )
        dprobs = jnp.einsum(
            "sqhd,skhd->shqk", grad_heads, value_h, preferred_element_type=jnp.float32
        )
        dscores = (probs * (dprobs - delta[..., None])).astype(jnp.bfloat16)
        dquery = (
            jnp.einsum("shqk,skhd->sqhd", dscores, key_h, preferred_element_type=jnp.float32)
            * 0.125
        )
        dkey = (
            jnp.einsum("shqk,sqhd->skhd", dscores, query_heads, preferred_element_type=jnp.float32)
            * 0.125
        )
        return (dquery, jnp.stack((dkey, dvalue), 2))

    dq_own, dkv_own = contribute(key_value, me)

    def turn(step, state):
        pair, dkv_acc, dq_acc = state
        pair = shifted(pair, "ctx", 1)
        dkv_acc = pass_grads(dkv_acc)
        source = (me - step) % cycle
        dq_part, dkv_part = contribute(pair, source)
        return (pair, dkv_acc + dkv_part, dq_acc + dq_part)

    final = lax.fori_loop(1, cycle, turn, (key_value, dkv_own, dq_own))
    dkv = pass_grads(final[1])
    dqkv_b = jnp.concatenate(
        [final[2].reshape(tokens, width), dkv.reshape(tokens, 2 * width)], 1
    ).astype(jnp.bfloat16)
    grad_qkv = jnp.einsum("td,te->de", h_first_b, dqkv_b, preferred_element_type=jnp.float32)
    bias_sums = jnp.sum(dqkv_b, 0, dtype=jnp.float32)
    dh_first = jnp.einsum("te,de->td", dqkv_b, full_qkv, preferred_element_type=jnp.float32)
    dx_ln, grad_g1, grad_b1 = pull_first(dh_first)
    input_grad = (dresid + dx_ln).astype(jnp.bfloat16).reshape(seqs, rows, width)
    grad_vec = jnp.concatenate(
        [
            jnp.stack(
                [
                    grad_g1,
                    grad_b1,
                    bias_sums[:width],
                    bias_sums[2 * width :],
                    grad_bo,
                    grad_g2,
                    grad_b2,
                    grad_bp,
                ]
            ),
            grad_bf.reshape(-1, width),
        ],
        0,
    )
    grad_flat = jnp.concatenate(
        [grad_qkv.reshape(-1), grad_out.reshape(-1), grad_fc.reshape(-1), grad_proj.reshape(-1)]
    ).reshape(shards, -1, 128)
    owned_flat, owned_vec = reduce_grads(grad_flat, grad_vec)
    owned_flat = owned_flat.reshape(weights.shape[0], 128)
    new_w = adamw(weights, owned_flat, first_w, second_w, rate_matrix, weight_decay)
    new_vec = adamw(vectors, owned_vec, first_vec, second_vec, rate_vector, 0.0)
    return (outputs, input_grad, new_w[0], new_w[1], new_w[2], new_vec[0], new_vec[1], new_vec[2])


MEMBERS = 8
GROUPS = 4
DEVICES = MEMBERS * GROUPS
MESH = pl.DeviceIdType.MESH
BLOCK = 64
SLOTS = 4
VMEM_BYTES = 60 * 1024 * 1024
OUT_FIRST = 24
FC_FIRST = 32
PROJ_FIRST = 64


def head_start(member):
    return HEADS * member // MEMBERS


class Place:
    def __init__(self):
        self.fsdp, self.ctx = lax.axis_index("fsdp"), lax.axis_index("ctx")
        self.x, self.core = self.fsdp // 2, self.fsdp % 2
        self.far, self.near, self.y = self.ctx // 4, self.ctx // 2 % 2, self.ctx % 2
        self.me = self.member()
        self.group = 2 * self.y + self.far
        self.linear = self.fsdp * MEMBERS + self.ctx

    def member(self, x=None, near=None, core=None):
        x = self.x if x is None else x
        near = self.near if near is None else near
        core = self.core if core is None else core
        return 4 * core + 2 * near + x

    def target(self, x=None, core=None, far=None, near=None, y=None):
        x = self.x if x is None else x
        near = self.near if near is None else near
        core = self.core if core is None else core
        far = self.far if far is None else far
        y = self.y if y is None else y
        return (2 * x + core, 4 * far + 2 * near + y)

    def is_me(self, target):
        return jnp.logical_and(target[0] == self.fsdp, target[1] == self.ctx)


def greet_all(place):
    barrier = pltpu.get_barrier_semaphore()

    def one(step, carry):
        other = (place.linear + step) % DEVICES
        pl.semaphore_signal(
            barrier, inc=1, device_id=(other // MEMBERS, other % MEMBERS), device_id_type=MESH
        )
        return carry

    lax.fori_loop(1, DEVICES, one, 0)
    pl.semaphore_wait(barrier, DEVICES - 1)


def greet(targets):
    barrier = pltpu.get_barrier_semaphore()
    for target in targets:
        pl.semaphore_signal(barrier, inc=1, device_id=target, device_id_type=MESH)
    pl.semaphore_wait(barrier, len(targets))


def remote(source, landing, sems, index, target):
    return pltpu.make_async_remote_copy(
        src_ref=source,
        dst_ref=landing,
        send_sem=sems.at[0, index],
        recv_sem=sems.at[1, index],
        device_id=target,
        device_id_type=MESH,
    )


def arrived(landing, sem):
    pltpu.make_async_copy(landing, landing, sem).wait()


class Move:
    def __init__(self, place, source, landing, send_sem, recv_sem, target, valid=None):
        here = place.is_me(target)
        away = jnp.logical_not(here)
        if valid is not None:
            here, away = jnp.logical_and(here, valid), jnp.logical_and(away, valid)
        self.away = away
        self.copy = pltpu.make_async_remote_copy(
            src_ref=source,
            dst_ref=landing,
            send_sem=send_sem,
            recv_sem=recv_sem,
            device_id=target,
            device_id_type=MESH,
        )

        @pl.when(here)
        def _():
            pltpu.make_async_copy(source, landing, recv_sem).start()

        @pl.when(away)
        def _():
            self.copy.start()

    def sent(self):
        @pl.when(self.away)
        def _():
            self.copy.wait_send()


class Gather:
    def __init__(self, place, out, sems):
        p = place
        step, turn = 1 - p.core, p.core
        x1, near1 = p.x + step * (1 - 2 * p.x), p.near + turn * (1 - 2 * p.near)
        x2, near2 = p.x + turn * (1 - 2 * p.x), p.near + step * (1 - 2 * p.near)
        self.out, self.sems, self.me = out, sems, p.me
        self.first = p.target(x=x1, near=near1)
        self.second = p.target(x=x2, near=near2)
        self.other = p.target(core=1 - p.core)
        self.of_first = p.member(x=x1, near=near1)
        self.of_second = p.member(x=x2, near=near2)
        self.of_both = p.member(x=1 - p.x, near=1 - p.near)
        self.copies = {}

    def _go(self, name, index, block, target):
        item = remote(self.out.at[block], self.out.at[block], self.sems, index, target)
        item.start()
        self.copies[name] = item

    def begin(self):
        self._go("a", 0, self.me, self.first)
        self._go("b", 1, self.me, self.second)
        self._go("c", 2, self.me, self.other)

    def second_hop(self):
        self.copies["a"].wait_recv()
        self._go("d", 3, self.of_first, self.second)
        self._go("e", 4, self.of_first, self.other)

    def third_hop(self):
        self.copies["b"].wait_recv()
        self._go("f", 5, self.of_second, self.other)

    def last_hop(self):
        self.copies["d"].wait_recv()
        self._go("g", 6, self.of_both, self.other)

    def finish(self):
        for name in "cefg":
            self.copies[name].wait_recv()
        for item in self.copies.values():
            item.wait_send()


class Spread:
    def __init__(self, place, at, sems, first):
        p = place
        self.at, self.sems, self.first = at, sems, first
        self.mine, self.theirs = at(p.far, p.y), at(1 - p.far, p.y)
        self.to_far, self.to_y = p.target(far=1 - p.far), p.target(y=1 - p.y)

    def begin(self):
        self.a = remote(self.mine, self.mine, self.sems, self.first, self.to_far)
        self.b = remote(self.mine, self.mine, self.sems, self.first + 1, self.to_y)
        self.a.start()
        self.b.start()

    def middle(self):
        self.a.wait_recv()
        self.c = remote(self.theirs, self.theirs, self.sems, self.first + 2, self.to_y)
        self.c.start()

    def finish(self):
        self.b.wait_recv()
        self.c.wait_recv()
        for item in (self.a, self.b, self.c):
            item.wait_send()


def shard_of(third):
    shard = third // 3
    return (shard // MEMBERS, shard % MEMBERS), third % 3


def lookup(table, index):
    result = 0
    for place, entry in enumerate(table):
        if entry:
            result = result + jnp.where(index == place, entry, 0)
    return result


FC_OF_GROUP = (
    (0, 1, 16, 17, 18, 22, 23, 24),
    (2, 3, 19, 20, 21, 25, 26, 27),
    (4, 5, 6, 10, 11, 12, 28, 29),
    (7, 8, 9, 13, 14, 15, 30, 31),
)
FC_SLOT = [0] * 32
FC_Y = [0] * 32
for _group, _units in enumerate(FC_OF_GROUP):
    for _slot, _unit in enumerate(_units):
        FC_SLOT[_unit] = _slot
        FC_Y[_unit] = _group % 2


def fc_unit(far, y, slot):
    return lookup([units[slot] for units in FC_OF_GROUP], 2 * far + y)


def fc_home(place, unit):
    return lookup(FC_SLOT, unit), lookup(FC_Y, unit)


def out_root(member):
    return jnp.where(member // 3 == 1, 1, 0)


def half_tile(flat, first, count, stride, half):
    at = half // 2
    tile = flat[pl.ds(first + at, count, stride=stride), :]
    if half % 2 == 0:
        return tile
    after = flat[pl.ds(first + at + 1, count, stride=stride), :]
    lane = lax.broadcasted_iota(jnp.int32, tile.shape, 1)
    return pltpu.roll(jnp.where(lane < HD, after, tile), HD, 1)


def lay_qkv(flat, rows, pieces, member):
    count = rows.shape[1] // 2
    halves = 3 * HEADS
    for part in range(3):
        for odd in range(2):
            for tile in range(SLOTS // 2):
                half = halves * odd + HEADS * part + head_start(member) + 2 * tile
                rows[SLOTS // 2 * part + tile, pl.ds(odd, count, stride=2), :] = half_tile(
                    flat, 0, count, halves, half
                )
    for tile in range(3 * SLOTS // 2):
        pieces[member, :, 128 * tile : 128 * tile + 128] = rows[tile].astype(jnp.bfloat16)


def lay_fc(flat, first, pieces, part):
    count, hidden = pieces.shape[-2:]
    stride = FF // 128
    for member in range(MEMBERS):
        start, shift = divmod(member * hidden, 128)
        for tile in range(-(-hidden // 128)):
            value = flat[pl.ds(first + start + tile, count, stride=stride), :]
            size = min(128, hidden - 128 * tile)
            if shift:
                if shift + size > 128:
                    after = flat[pl.ds(first + start + tile + 1, count, stride=stride), :]
                    lane = lax.broadcasted_iota(jnp.int32, value.shape, 1)
                    value = jnp.where(lane < shift, after, value)
                value = pltpu.roll(value, 128 - shift, 1)
            pieces[part, member, :, 128 * tile : 128 * tile + size] = value[:, :size].astype(
                jnp.bfloat16
            )


def lay_rows(flat, first, rows, blocks, part):
    count = rows.shape[1] // 2
    width = blocks.shape[-1]
    halves = width // HD
    for odd in range(2):
        for tile in range(-(-width // 128)):
            half = halves * odd + 2 * tile
            size = min(128, width - 128 * tile)
            if size == 128 or half % 2 == 0:
                value = half_tile(flat, first, count, halves, half)
            else:
                value = pltpu.roll(
                    flat[pl.ds(first + half // 2, count, stride=halves), :], HD, 1
                )
            rows[tile, pl.ds(odd, count, stride=2), :] = value
    for tile in range(-(-width // 128)):
        size = min(128, width - 128 * tile)
        blocks[part, :, 128 * tile : 128 * tile + size] = rows[tile, :, :size].astype(
            jnp.bfloat16
        )


def norm_rows(value, gain, shift):
    center = value - jnp.mean(value, -1, keepdims=True)
    spread = jnp.mean(center * center, -1, keepdims=True)
    return center * lax.rsqrt(spread + epsilon_norm) * gain + shift


def member_lanes(row, member, count):
    result = jnp.zeros((row.shape[0], count), row.dtype)
    for other in range(MEMBERS):
        first = head_start(other) * HD
        result = result + jnp.where(member == other, row[:, first : first + count], 0.0)
    return result


def attend_block(query, keys, values, row_pos, col_pos):
    lanes = lane_of(query.shape)
    result = jnp.zeros(query.shape, jnp.float32)
    for head in range(2):
        mine = lanes == head
        own = jnp.where(mine, query, jnp.zeros_like(query))
        probs = probabilities(own, keys, row_pos, col_pos)
        mixed = jnp.dot(probs.astype(jnp.bfloat16), values, preferred_element_type=jnp.float32)
        result = jnp.where(mine, mixed, result)
    return result.astype(jnp.bfloat16)


def forward_kernel(
    x_in, back_in, order_in, vec_in, weights,
    x_all, back_all, vecs, row_pos, col_pos, w_qkv, h_first, qkv, attn_all, attn,
    w_fc, w_proj, w_out,
    flat, rows, qkv_pieces, fc_pieces, blocks, order, vec_all, qkv_land,
    fc, proj, out, fc_part, proj_part, out_part,
    move_sem, qkv_sem, fc_send, fc_recv, rows_sem, x_sem, back_sem, spread_sem,
    own_sem, fc_sem, proj_sem, tree_sem, out_sem, attn_sem,
):
    p = Place()
    third_rows = weights.shape[0] // 3
    count, width = x_in.shape
    length = MEMBERS * count
    pairs = SLOTS // 2
    barrier = pltpu.get_barrier_semaphore()

    def signal(step, carry):
        other = (p.linear + step) % DEVICES
        pl.semaphore_signal(
            barrier, inc=1, device_id=(other // MEMBERS, other % MEMBERS), device_id_type=MESH
        )
        return carry

    lax.fori_loop(1, DEVICES, signal, 0)
    flat[...] = weights[...].astype(jnp.float32)
    pl.semaphore_wait(barrier, DEVICES - 1)
    home = p.target(
        x=p.ctx % 2, near=p.ctx // 2 % 2, core=p.ctx // 4, y=p.fsdp // 2, far=p.fsdp % 2
    )
    x_move = Move(p, x_in, x_all.at[p.ctx], move_sem.at[0, 0], move_sem.at[1, 0], home)
    order_move = Move(p, order_in, order, move_sem.at[0, 1], move_sem.at[1, 1], home)
    owner = p.fsdp == 0
    qkv_moves = []
    for member in (7, 6, 3, 2, 5, 4, 1, 0):

        @pl.when(owner)
        def _(member=member):
            lay_qkv(flat, rows, qkv_pieces, member)

        target = p.target(x=member % 2, near=member // 2 % 2, core=member // 4)
        qkv_moves.append(
            Move(
                p, qkv_pieces.at[member], qkv_land.at[p.far, p.near, p.y],
                qkv_sem.at[0, member], qkv_sem.at[1, p.near], target, owner,
            )
        )

    def vec_send(step, carry):
        other = (p.linear + step) % DEVICES
        pltpu.make_async_remote_copy(
            src_ref=vec_in,
            dst_ref=vec_all.at[p.linear],
            send_sem=move_sem.at[0, 2],
            recv_sem=move_sem.at[1, 2],
            device_id=(other // MEMBERS, other % MEMBERS),
            device_id_type=MESH,
        ).start()
        return carry

    lax.fori_loop(1, DEVICES, vec_send, 0)
    pltpu.make_async_copy(vec_in, vec_all.at[p.linear], move_sem.at[1, 2]).start()
    for part in range(3):
        third = 3 * p.linear + part
        is_fc = jnp.logical_and(third >= FC_FIRST, third < PROJ_FIRST)
        is_rows = jnp.logical_and(third >= OUT_FIRST, jnp.logical_not(is_fc))

        @pl.when(is_fc)
        def _(part=part):
            lay_fc(flat, part * third_rows, fc_pieces, part)

        @pl.when(is_rows)
        def _(part=part):
            lay_rows(flat, part * third_rows, rows, blocks, part)

    arrived(x_all.at[p.me], move_sem.at[1, 0])
    gather_x = Gather(p, x_all, x_sem)
    gather_x.begin()
    spreads = []
    for near in range(2):
        arrived(qkv_land.at[p.far, near, p.y], qkv_sem.at[1, near])
        item = Spread(p, lambda far, y, near=near: qkv_land.at[far, near, y], spread_sem, 3 * near)
        item.begin()
        spreads.append(item)
    gather_x.second_hop()
    gather_x.third_hop()
    fc_moves, rows_moves = [], []
    for part in range(3):
        third = 3 * p.linear + part
        valid = jnp.logical_and(third >= FC_FIRST, third < PROJ_FIRST)
        slot, y = fc_home(p, jnp.where(valid, third - FC_FIRST, 0))
        for member in (7, 6, 3, 2, 5, 4, 1, 0):
            target = p.target(x=member % 2, near=member // 2 % 2, core=member // 4, y=y)
            fc_moves.append(
                Move(
                    p, fc_pieces.at[part, member], fc_part.at[slot],
                    fc_send.at[part, member], fc_recv.at[slot], target, valid,
                )
            )
    for part in range(3):
        third = 3 * p.linear + part
        valid = third >= PROJ_FIRST
        unit = jnp.where(valid, third - PROJ_FIRST, 0)
        member, group = unit // 4, unit % 4
        target = p.target(
            x=member % 2, near=member // 2 % 2, core=member // 4, y=group // 2, far=group % 2
        )
        rows_moves.append(
            Move(
                p, blocks.at[part], proj_part,
                rows_sem.at[0, part], rows_sem.at[1, 0], target, valid,
            )
        )
        valid = jnp.logical_and(third >= OUT_FIRST, third < FC_FIRST)
        member = jnp.where(valid, third - OUT_FIRST, 0)
        target = p.target(
            x=member % 2, near=member // 2 % 2, core=member // 4, y=out_root(member), far=0
        )
        rows_moves.append(
            Move(
                p, blocks.at[part], out_part,
                rows_sem.at[0, part], rows_sem.at[1, 1], target, valid,
            )
        )
    gather_x.last_hop()
    back_move = Move(p, back_in, back_all.at[p.ctx], move_sem.at[0, 3], move_sem.at[1, 3], home)
    arrived(vec_all, move_sem.at[1, 2])
    cols = vec_in.shape[-1]
    used = width // MEMBERS
    total = jnp.zeros(vecs.shape, jnp.float32)
    for ctx in range(MEMBERS):
        block = jnp.concatenate([vec_all[MEMBERS * f + ctx] for f in range(GROUPS)], 0)
        lane = lax.broadcasted_iota(jnp.int32, (cols, width), 0)
        at = lax.broadcasted_iota(jnp.int32, (cols, width), 1) - used * ctx
        spot = jnp.where(jnp.logical_and(lane == at, lane < used), 1.0, 0.0)
        total = total + jnp.dot(
            block, spot.astype(jnp.bfloat16), preferred_element_type=jnp.float32
        )
    vecs[...] = total
    arrived(order, move_sem.at[1, 1])
    slots = order[0:1, :].astype(jnp.float32)
    lane = lax.broadcasted_iota(jnp.int32, (length, 128), 1)
    row = lax.broadcasted_iota(jnp.int32, (length, 128), 0)
    spot = jnp.where(lane == row // BLOCK, slots, 0.0)
    inner = lax.broadcasted_iota(jnp.int32, (length, 1), 0) % BLOCK
    row_pos[...] = jnp.sum(spot, 1, keepdims=True) * BLOCK + inner.astype(jnp.float32)
    lane = lax.broadcasted_iota(jnp.int32, (128, length), 1)
    row = lax.broadcasted_iota(jnp.int32, (128, length), 0)
    spot = jnp.where(row == lane // BLOCK, 1.0, 0.0)
    inner = lax.broadcasted_iota(jnp.int32, (1, length), 1) % BLOCK
    found = jnp.dot(
        order[...].astype(jnp.bfloat16), spot.astype(jnp.bfloat16),
        preferred_element_type=jnp.float32,
    )
    col_pos[...] = found[0:1, :] * BLOCK + inner.astype(jnp.float32)
    for item in spreads:
        item.middle()
    arrived(back_all.at[p.me], move_sem.at[1, 3])
    gather_back = Gather(p, back_all, back_sem)
    gather_back.begin()
    gather_x.finish()

    def norm_block(step, carry):
        value = norm_rows(x_all[step].astype(jnp.float32), vecs[0:1, :], vecs[1:2, :])
        h_first[pl.ds(pl.multiple_of(step * count, count), count), :] = value.astype(jnp.bfloat16)
        return carry

    lax.fori_loop(0, MEMBERS, norm_block, 0)
    to_far, to_y = p.target(far=1 - p.far), p.target(y=1 - p.y)
    fc_far, fc_y, fc_later, own_copies = [], [], [], []
    for slot in range(8):
        arrived(fc_part.at[slot], fc_recv.at[slot])
        landing = fc.at[fc_unit(p.far, p.y, slot)]
        fc_far.append(remote(fc_part.at[slot], landing, fc_sem, slot, to_far))
        fc_far[slot].start()
        fc_y.append(remote(fc_part.at[slot], landing, fc_sem, 8 + slot, to_y))
        fc_y[slot].start()
        own_copies.append(pltpu.make_async_copy(fc_part.at[slot], landing, own_sem.at[slot]))
        own_copies[slot].start()
    gather_back.second_hop()
    gather_back.third_hop()
    root_y = out_root(p.me)
    same_y = p.y == root_y
    root = jnp.logical_and(same_y, p.far == 0)
    beside = jnp.logical_and(same_y, p.far == 1)
    mine = out.at[p.me]
    out_far = remote(out_part, mine, tree_sem, 0, to_far)
    out_y = remote(out_part, mine, tree_sem, 1, to_y)
    out_later = remote(mine, mine, tree_sem, 2, to_y)
    out_own = pltpu.make_async_copy(out_part, mine, own_sem.at[8])

    @pl.when(root)
    def _():
        arrived(out_part, rows_sem.at[1, 1])
        out_far.start()
        out_y.start()
        out_own.start()

    arrived(proj_part, rows_sem.at[1, 0])
    my_proj, far_proj = proj.at[p.y, p.far], proj.at[p.y, 1 - p.far]
    proj_far = remote(proj_part, my_proj, proj_sem, 0, to_far)
    proj_y = remote(proj_part, my_proj, proj_sem, 1, to_y)
    proj_far.start()
    proj_y.start()
    proj_own = pltpu.make_async_copy(proj_part, my_proj, own_sem.at[9])
    proj_own.start()
    for item in spreads:
        item.finish()
    four = qkv_land.shape[3]
    for far in range(2):
        for near in range(2):
            for y in range(2):
                first = four * (4 * far + 2 * near + y)
                w_qkv[first : first + four, :] = qkv_land[far, near, y]
    per_part = SLOTS * HD
    bias = jnp.concatenate(
        [
            member_lanes(vecs[2:3, :], p.me, per_part),
            jnp.zeros((1, per_part), jnp.float32),
            member_lanes(vecs[16:17, :], p.me, per_part),
        ],
        1,
    )

    def qkv_block(step, carry):
        at = pl.ds(pl.multiple_of(step * 2 * count, 2 * count), 2 * count)
        value = jnp.dot(h_first[at, :], w_qkv[...], preferred_element_type=jnp.float32)
        qkv[at, :] = (value + bias).astype(jnp.bfloat16)
        return carry

    lax.fori_loop(0, MEMBERS // 2, qkv_block, 0)
    gather_back.last_hop()
    span = 2 * count

    def one_pair(pair):
        def one_block(step, carry):
            at = pl.ds(pl.multiple_of(step * span, span), span)
            attn[pair, at, :] = attend_block(
                qkv[at, 128 * pair : 128 * pair + 128],
                qkv[:, 128 * (pairs + pair) : 128 * (pairs + pair) + 128],
                qkv[:, 128 * (2 * pairs + pair) : 128 * (2 * pairs + pair) + 128],
                row_pos[at, :],
                col_pos[...],
            )
            return carry

        lax.fori_loop(0, length // span, one_block, 0)

    def share(pair):
        item = Gather(p, attn_all.at[pair], attn_sem.at[pair])
        for name, index, target in (
            ("a", 0, item.first), ("b", 1, item.second), ("c", 2, item.other),
        ):
            copy = remote(attn.at[pair], attn_all.at[pair, p.me], attn_sem.at[pair], index, target)
            copy.start()
            item.copies[name] = copy
        copy = pltpu.make_async_copy(
            attn.at[pair], attn_all.at[pair, p.me], own_sem.at[10 + pair]
        )
        copy.start()
        own_copies.append(copy)
        return item

    one_pair(0)
    gathers = [share(0)]
    for slot in range(8):
        fc_far[slot].wait_recv()
        landing = fc.at[fc_unit(1 - p.far, p.y, slot)]
        copy = remote(landing, landing, fc_sem, 16 + slot, to_y)
        copy.start()
        fc_later.append(copy)

    @pl.when(beside)
    def _():
        out_far.wait_recv()
        out_later.start()

    gathers[0].second_hop()
    gathers[0].third_hop()
    gathers[0].last_hop()
    one_pair(1)
    gathers.append(share(1))
    proj_far.wait_recv()
    proj_later = remote(far_proj, far_proj, proj_sem, 2, to_y)
    proj_later.start()
    gathers[1].second_hop()
    gathers[1].third_hop()
    gathers[1].last_hop()

    @pl.when(root)
    def _():
        out_own.wait()

    @pl.when(jnp.logical_and(jnp.logical_not(same_y), p.far == 0))
    def _():
        out_y.wait_recv()

    @pl.when(jnp.logical_and(jnp.logical_not(same_y), p.far == 1))
    def _():
        out_later.wait_recv()

    gather_out = Gather(p, out, out_sem)
    gather_out.begin()
    gather_out.second_hop()
    for item in fc_y + fc_later:
        item.wait_recv()
    for item in own_copies[:8]:
        item.wait()
    gather_out.third_hop()
    unit = fc.shape[1]
    for block in range(DEVICES):
        w_fc[unit * block : unit * block + unit, :] = fc[block]
    gather_out.last_hop()
    proj_y.wait_recv()
    proj_later.wait_recv()
    proj_own.wait()
    for group in range(GROUPS):
        w_proj[four * group : four * group + four, :] = proj[group // 2, group % 2]
    for item in gathers + [gather_out, gather_back]:
        item.finish()
    for block in range(MEMBERS):
        w_out[four * block : four * block + four, :] = out[block]
    for item in fc_far + fc_y + fc_later + [proj_far, proj_y, proj_later]:
        item.wait_send()

    @pl.when(root)
    def _():
        out_far.wait_send()
        out_y.wait_send()

    @pl.when(beside)
    def _():
        out_later.wait_send()

    for item in own_copies[8:]:
        item.wait()
    for item in [x_move, order_move, back_move] + qkv_moves + fc_moves + rows_moves:
        item.sent()
    arrived(vec_all.at[pl.ds(1, DEVICES - 1)], move_sem.at[0, 2])


def forward(x, back, order, vectors, weights):
    rows, width = x.shape
    kind, high = jnp.bfloat16, jnp.float32
    unit, hidden = width // DEVICES, FF // MEMBERS
    four, cols = 4 * unit, 3 * SLOTS * HD
    length, pairs = MEMBERS * rows, SLOTS // 2
    any_space = pl.BlockSpec(memory_space=pl.ANY)
    vmem = pl.BlockSpec(memory_space=pltpu.VMEM)
    dma = pltpu.SemaphoreType.DMA

    def like(*shape, dtype=kind):
        return jax.ShapeDtypeStruct(shape, dtype)

    return pl.pallas_call(
        forward_kernel,
        out_shape=[
            like(MEMBERS, rows, width),
            like(MEMBERS, rows, width),
            like(GROUPS * vectors.shape[0], width, dtype=high),
            like(length, 1, dtype=high),
            like(1, length, dtype=high),
            like(width, cols),
            like(length, width),
            like(length, cols),
            like(pairs, MEMBERS, length, 2 * HD),
            like(pairs, length, 2 * HD),
            like(width, hidden),
            like(hidden, width),
            like(width, width),
        ],
        in_specs=[any_space] * 4 + [vmem],
        out_specs=[vmem, any_space] + [vmem] * 6 + [any_space] + [vmem] * 4,
        scratch_shapes=[
            pltpu.VMEM(weights.shape, high),
            pltpu.VMEM((-(-width // 128), four, 128), high),
            pltpu.VMEM((MEMBERS, four, cols), kind),
            pltpu.VMEM((3, MEMBERS, unit, hidden), kind),
            pltpu.VMEM((3, four, width), kind),
            pltpu.VMEM(order.shape, order.dtype),
            pltpu.VMEM((DEVICES,) + vectors.shape, kind),
            pltpu.VMEM((2, 2, 2, four, cols), kind),
            pltpu.VMEM((DEVICES, unit, hidden), kind),
            pltpu.VMEM((2, 2, four, width), kind),
            pltpu.VMEM((MEMBERS, four, width), kind),
            pltpu.VMEM((8, unit, hidden), kind),
            pltpu.VMEM((four, width), kind),
            pltpu.VMEM((four, width), kind),
            dma((2, 4)),
            dma((2, 8)),
            dma((3, 8)),
            dma((8,)),
            dma((2, 3)),
            dma((2, 7)),
            dma((2, 7)),
            dma((2, 6)),
            dma((12,)),
            dma((2, 24)),
            dma((2, 3)),
            dma((2, 3)),
            dma((2, 7)),
            dma((pairs, 2, 7)),
        ],
        compiler_params=pltpu.CompilerParams(
            collective_id=1, has_side_effects=True, vmem_limit_bytes=VMEM_BYTES
        ),
        name="forward",
    )(x, back, order, vectors, weights)


def wide(value):
    return value.astype(jnp.float32)


def low(value):
    return value.astype(jnp.bfloat16)


GELU_SCALE = 0.7978845608028654
GELU_CUBE = 0.044715


class Reduce:
    def __init__(self, place, part, from_core, two, got, last, done, sems):
        self.p, self.part, self.from_core = place, part, from_core
        self.two, self.got, self.last, self.done, self.sems = two, got, last, done, sems
        self.route = Gather(place, None, None)
        self.copies = []

    def _go(self, source, landing, index, target):
        item = remote(source, landing, self.sems, index, target)
        item.start()
        self.copies.append(item)
        return item

    def begin(self):
        p = self.p
        for j in (3, 2, 1, 0):
            self._go(
                self.part.at[4 * (1 - p.core) + j], self.from_core.at[j], j, self.route.other
            )

    def _summed(self, member):
        block = member - 4 * self.p.core
        return wide(self.part[member]) + wide(self.from_core[block])

    def second(self):
        for item in self.copies[:4]:
            item.wait_recv()
        self.two[0] = low(self._summed(self.route.of_both))
        self.across = self._go(self.two.at[0], self.got.at[0], 4, self.route.second)
        self.two[1] = low(self._summed(self.route.of_second))
        self.beyond = self._go(self.two.at[1], self.got.at[1], 5, self.route.second)

    def third(self):
        self.across.wait_recv()
        self.last[...] = low(self._summed(self.route.of_first) + wide(self.got[0]))
        self.final = self._go(self.last, self.done, 6, self.route.first)

    def result(self):
        self.beyond.wait_recv()
        value = self._summed(self.p.me) + wide(self.got[1])
        self.final.wait_recv()
        return value + wide(self.done[...])

    def sent(self):
        for item in self.copies:
            item.wait_send()


def reduce_buffers(rows, width):
    kind = jnp.bfloat16
    return [
        pltpu.VMEM((4, rows, width), kind),
        pltpu.VMEM((2, rows, width), kind),
        pltpu.VMEM((2, rows, width), kind),
        pltpu.VMEM((rows, width), kind),
        pltpu.VMEM((rows, width), kind),
        pltpu.SemaphoreType.DMA((2, 7)),
    ]


def store_rows(target, first, value, lanes=slice(None)):
    size = target.shape[1]
    row = 0
    while row < value.shape[0]:
        block, at = divmod(first + row, size)
        count = min(size - at, value.shape[0] - row)
        target[block, at : at + count, lanes] = low(value[row : row + count])
        row += count


def middle_kernel(
    x_all, attn_all, back_all, vecs, w_out_in, w_fc_in, w_proj_in,
    grad_fc, grad_proj, made, resid_own, dresid, dbranch, sums, fc_sums,
    h_second, attn, back, w_out, w_fc, w_proj, act, dpre, dh_part, made_part, g_fc, g_proj,
    resid, from_core, two, got, last, done, reduce_sem, load_sem, store_sem,
):
    p = Place()
    length, width = h_second.shape
    count = length // MEMBERS
    hidden = act.shape[1]
    pairs = attn.shape[0]
    loads = []
    for index, (source, target) in enumerate(
        (
            (attn_all, attn), (w_out_in, w_out), (x_all, h_second),
            (w_fc_in, w_fc), (back_all, back), (w_proj_in, w_proj),
        )
    ):
        copy = pltpu.make_async_copy(source, target, load_sem.at[index])
        copy.start()
        loads.append(copy)
    reduce = Reduce(p, dh_part, from_core, two, got, last, done, reduce_sem)
    route = reduce.route
    greet((route.first, route.second, route.other))
    bias_fc = jnp.zeros((1, hidden), jnp.float32)
    for member in range(MEMBERS):
        row = (34, 48, 49, 50)[member // 2]
        first = hidden * (member % 2)
        bias_fc = bias_fc + jnp.where(
            p.me == member, vecs[row : row + 1, first : first + hidden], 0.0
        )
    fc_sums[...] = jnp.zeros_like(fc_sums)
    for copy in loads:
        copy.wait()
    span = 2 * count

    def one_block(step, carry):
        at = pl.ds(pl.multiple_of(step * span, span), span)
        total = wide(h_second[at, :]) + vecs[17:18, :]
        for member in range(MEMBERS):
            first = head_start(member) * HD
            used = (head_start(member + 1) - head_start(member)) * HD
            heads = jnp.concatenate([attn[pair, member, at, :] for pair in range(pairs)], 1)
            if used < SLOTS * HD:
                lane = lax.broadcasted_iota(jnp.int32, heads.shape, 1)
                heads = jnp.where(lane < used, heads, jnp.zeros_like(heads))
            total = total + jnp.dot(
                heads, w_out[first : first + SLOTS * HD, :], preferred_element_type=jnp.float32
            )
        resid[...] = total

        @pl.when(step == p.me // 2)
        def _():
            resid_own[...] = resid[pl.ds(pl.multiple_of(p.me % 2 * count, count), count), :]

        normed = low(norm_rows(total, vecs[18:19, :], vecs[32:33, :]))
        h_second[at, :] = normed
        pre = jnp.dot(normed, w_fc[...], preferred_element_type=jnp.float32) + bias_fc
        square = pre * pre
        slope = jnp.tanh(GELU_SCALE * (pre + GELU_CUBE * pre * square))
        act[at, :] = low(0.5 * pre * (1.0 + slope))
        tilt = 0.5 * (1.0 + slope) + 0.5 * pre * (1.0 - slope * slope) * GELU_SCALE * (
            1.0 + 3.0 * GELU_CUBE * square
        )
        dpre_block = low(dot_nt(back[at, :], w_proj[...]) * tilt)
        dpre[at, :] = dpre_block
        fc_sums[...] += jnp.sum(wide(dpre_block), 0, keepdims=True)
        value = low(dot_nt(dpre_block, w_fc[...]))
        dh_part[2 * step] = value[:count]
        dh_part[2 * step + 1] = value[count:]
        return carry

    lax.fori_loop(0, MEMBERS // 2, one_block, 0)
    reduce.begin()
    chunk = 256

    def one_proj(step, carry):
        lanes = pl.ds(pl.multiple_of(step * chunk, chunk), chunk)
        store_rows(g_proj, 0, dot_tn(act[...], back[:, lanes]), lanes)
        return carry

    lax.fori_loop(0, 3, one_proj, 0)
    reduce.second()
    lax.fori_loop(3, width // chunk, one_proj, 0)
    tail = slice(width // chunk * chunk, width)
    if width % chunk:
        store_rows(g_proj, 0, dot_tn(act[...], back[:, tail]), tail)
    stores = [pltpu.make_async_copy(g_proj, grad_proj, store_sem.at[0])]
    stores[0].start()
    for first in range(0, width, chunk):
        size = min(chunk, width - first)
        store_rows(g_fc, first, dot_tn(h_second[:, first : first + size], dpre[...]))
        if first + size == 4 * chunk:
            reduce.third()
    stores.append(pltpu.make_async_copy(g_fc, grad_fc, store_sem.at[1]))
    stores[1].start()

    def one_made(step, carry):
        at = pl.ds(pl.multiple_of(step * span, span), span)
        value = low(jnp.dot(act[at, :], w_proj[...], preferred_element_type=jnp.float32))
        made_part[2 * step] = value[:count]
        made_part[2 * step + 1] = value[count:]
        return carry

    lax.fori_loop(0, MEMBERS // 2, one_made, 0)
    stores.append(pltpu.make_async_copy(made_part, made, store_sem.at[2]))
    stores[2].start()
    dh = reduce.result()
    center = resid_own[...] - jnp.mean(resid_own[...], -1, keepdims=True)
    scale = lax.rsqrt(jnp.mean(center * center, -1, keepdims=True) + epsilon_norm)
    hat = center * scale
    back_own = wide(back[pl.ds(pl.multiple_of(p.me * count, count), count), :])
    scaled = dh * vecs[18:19, :]
    inner = jnp.mean(scaled * hat, -1, keepdims=True)
    value = back_own + (scaled - jnp.mean(scaled, -1, keepdims=True) - hat * inner) * scale
    dresid[...] = value
    branch = low(value)
    dbranch[...] = branch
    sums[0:1, :] = jnp.sum(dh * hat, 0, keepdims=True)
    sums[1:2, :] = jnp.sum(dh, 0, keepdims=True)
    sums[2:3, :] = jnp.sum(wide(branch), 0, keepdims=True)
    sums[3:4, :] = jnp.sum(back_own, 0, keepdims=True)
    sums[4:8, :] = jnp.zeros((4, width), jnp.float32)
    reduce.sent()
    for copy in stores:
        copy.wait()


def middle(x_all, attn_all, back_all, vecs, w_out, w_fc, w_proj):
    kind, high = jnp.bfloat16, jnp.float32
    length, width = x_all.shape
    rows = length // MEMBERS
    hidden = w_proj.shape[0]
    four = width // MEMBERS
    any_space = pl.BlockSpec(memory_space=pl.ANY)
    vmem = pl.BlockSpec(memory_space=pltpu.VMEM)
    dma = pltpu.SemaphoreType.DMA

    def like(*shape, dtype=kind):
        return jax.ShapeDtypeStruct(shape, dtype)

    def buffer(*shape, dtype=kind):
        return pltpu.VMEM(shape, dtype)

    return pl.pallas_call(
        middle_kernel,
        out_shape=[
            like(MEMBERS, four, hidden),
            like(GROUPS, four, width),
            like(MEMBERS, rows, width),
            like(rows, width, dtype=high),
            like(rows, width, dtype=high),
            like(rows, width),
            like(8, width, dtype=high),
            like(1, hidden, dtype=high),
        ],
        in_specs=[any_space] * 3 + [vmem] + [any_space] * 3,
        out_specs=[any_space] * 3 + [vmem] * 5,
        scratch_shapes=[
            buffer(*x_all.shape),
            buffer(*attn_all.shape),
            buffer(*back_all.shape),
            buffer(*w_out.shape),
            buffer(*w_fc.shape),
            buffer(*w_proj.shape),
            buffer(length, hidden),
            buffer(length, hidden),
            buffer(MEMBERS, rows, width),
            buffer(MEMBERS, rows, width),
            buffer(MEMBERS, four, hidden),
            buffer(GROUPS, four, width),
            buffer(2 * rows, width, dtype=high),
        ]
        + reduce_buffers(rows, width)
        + [dma((6,)), dma((3,))],
        compiler_params=pltpu.CompilerParams(
            collective_id=3, has_side_effects=True, vmem_limit_bytes=VMEM_BYTES
        ),
        name="middle",
    )(x_all, attn_all, back_all, vecs, w_out, w_fc, w_proj)


class Fold:
    def __init__(self, place, away, kept, landing, leaving, last, sems, first):
        p = place
        self.p, self.away, self.kept, self.landing = p, away, kept, landing
        self.leaving, self.last = leaving, last
        self.to_far, self.to_y = p.target(far=1 - p.far), p.target(y=1 - p.y)
        self.sems, self.first = sems, first

    def begin(self):
        other = 1 - self.p.far
        self.a = remote(
            self.away(other), self.landing(other), self.sems, self.first, self.to_y
        )
        self.a.start()

    def rest(self):
        far = self.p.far
        self.b = remote(
            self.away(far), self.landing(far), self.sems, self.first + 1, self.to_y
        )
        self.b.start()

    def middle(self):
        other = 1 - self.p.far
        self.a.wait_recv()
        self.leaving[...] = low(wide(self.kept(other)[...]) + wide(self.landing(other)[...]))
        self.c = remote(self.leaving, self.last, self.sems, self.first + 2, self.to_far)
        self.c.start()

    def end(self):
        far = self.p.far
        self.b.wait_recv()
        partial = wide(self.kept(far)[...]) + wide(self.landing(far)[...])
        self.c.wait_recv()
        return low(partial + wide(self.last[...]))

    def sent(self):
        for item in (self.a, self.b, self.c):
            item.wait_send()


def backward_kernel(
    dbranch, made_in, grad_fc, grad_proj, attn, qkv, row_pos, col_pos, w_out, w_qkv_in,
    h_in, x_all, resid_own, dresid, vecs, sums, fc_sums,
    out_home, grad_home, qkv_back, fc_back, rows_back, vec_back,
    branch_all, dattn, dqkv, key_sum, value_sum, w_heads, w_qkv, h_first, x_own, made, dh_part,
    fc_own, proj_own, g_qkv, g_heads, g_out, result, input_grad, vec_rows, vec_go, vec_got,
    fc_y, proj_y, qkv_y, out_y, fc_go, proj_go, qkv_go, out_go,
    fc_far, proj_far, qkv_far, out_far, fc_sum, proj_sum, qkv_sum, out_sum,
    core_a, two_a, got_a, last_a, done_a, sem_a, core_b, two_b, got_b, last_b, done_b, sem_b,
    load_sem, branch_sem, fold_sem, tree_sem, vec_sem, home_sem,
    qkv_send, qkv_recv, fc_send, fc_recv, rows_send, rows_recv,
):
    p = Place()
    count, width = dbranch.shape
    length = MEMBERS * count
    four, unit = grad_proj.shape[1], fc_back.shape[2]
    pairs = SLOTS // 2
    per_part = SLOTS * HD
    first_head = HEADS * p.me // MEMBERS * HD
    loads = []

    def load(source, target):
        copy = pltpu.make_async_copy(source, target, load_sem.at[len(loads)])
        copy.start()
        loads.append(copy)

    load(w_out.at[pl.ds(pl.multiple_of(first_head, HD), per_part)], w_heads)
    load(x_all.at[p.me], x_own)
    for far in range(2):
        load(grad_proj.at[2 * p.y + far], proj_own.at[far])
        for near in range(2):
            load(grad_fc.at[4 * far + 2 * near + p.y], fc_own.at[far, near])
    load(made_in, made)
    load(w_qkv_in, w_qkv)
    load(h_in, h_first)
    greet_all(p)
    gather = Gather(p, branch_all, branch_sem)
    for name, index, target in (
        ("a", 0, gather.first), ("b", 1, gather.second), ("c", 2, gather.other),
    ):
        copy = remote(dbranch, branch_all.at[p.me], branch_sem, index, target)
        copy.start()
        gather.copies[name] = copy
    load(dbranch, branch_all.at[p.me])
    proj_fold = Fold(
        p, lambda far: grad_proj.at[2 * (1 - p.y) + far], lambda far: proj_own.at[far],
        lambda far: proj_y.at[far], proj_go, proj_far, fold_sem, 0,
    )
    fc_folds = [
        Fold(
            p, lambda far, near=near: grad_fc.at[4 * far + 2 * near + 1 - p.y],
            lambda far, near=near: fc_own.at[far, near],
            lambda far, near=near: fc_y.at[far, near],
            fc_go.at[near], fc_far.at[near], fold_sem, 3 + 3 * near,
        )
        for near in range(2)
    ]
    qkv_folds = [
        Fold(
            p, lambda far, near=near: g_qkv.at[4 * far + 2 * near + 1 - p.y],
            lambda far, near=near: g_qkv.at[4 * far + 2 * near + p.y],
            lambda far, near=near: qkv_y.at[far, near],
            qkv_go.at[near], qkv_far.at[near], fold_sem, 9 + 3 * near,
        )
        for near in range(2)
    ]
    proj_fold.begin()
    for item in fc_folds:
        item.begin()
    gather.second_hop()
    gather.third_hop()
    gather.last_hop()
    for copy in loads:
        copy.wait()
    proj_fold.middle()
    gather.finish()
    span = 2 * count

    def one_dattn(step, carry):
        at = pl.ds(pl.multiple_of(step * span, span), span)
        grad = jnp.concatenate([branch_all[2 * step], branch_all[2 * step + 1]], 0)
        value = low(dot_nt(grad, w_heads[...]))
        for pair in range(pairs):
            dattn[pair, at, :] = value[:, 128 * pair : 128 * pair + 128]
        return carry

    lax.fori_loop(0, length // span, one_dattn, 0)
    reduce_made = Reduce(p, made, core_a, two_a, got_a, last_a, done_a, sem_a)
    reduce_made.begin()
    proj_fold.rest()

    def one_pair(pair):
        key_sum[...] = jnp.zeros_like(key_sum)
        value_sum[...] = jnp.zeros_like(value_sum)

        def columns(part):
            return slice(128 * (pairs * part + pair), 128 * (pairs * part + pair) + 128)

        def one_block(step, carry):
            at = pl.ds(pl.multiple_of(step * span, span), span)
            query, grad = qkv[at, columns(0)], dattn[pair, at, :]
            keys, values = qkv[:, columns(1)], qkv[:, columns(2)]
            lanes = lane_of(query.shape)
            total = jnp.zeros(query.shape, jnp.float32)
            add_keys = add_values = 0.0
            for head in range(2):
                mine = lanes == head
                own = jnp.where(mine, query, jnp.zeros_like(query))
                own_grad = jnp.where(mine, grad, jnp.zeros_like(grad))
                probs = probabilities(own, keys, row_pos[at, :], col_pos[...])
                dprobs = dot_nt(own_grad, values)
                delta = jnp.sum(probs * dprobs, -1, keepdims=True)
                dscores = low(probs * (dprobs - delta))
                mixed = jnp.dot(dscores, keys, preferred_element_type=jnp.float32)
                total = jnp.where(mine, mixed, total)
                add_keys = add_keys + dot_tn(dscores, own)
                add_values = add_values + dot_tn(low(probs), own_grad)
            dqkv[at, columns(0)] = low(total * 0.125)
            key_sum[...] += add_keys
            value_sum[...] += add_values
            return carry

        lax.fori_loop(0, length // span, one_block, 0)
        dqkv[:, columns(1)] = low(key_sum[...] * 0.125)
        dqkv[:, columns(2)] = low(value_sum[...])

    one_pair(0)
    for item in fc_folds:
        item.middle()
    for item in fc_folds:
        item.rest()
    reduce_made.second()
    one_pair(1)
    reduce_made.third()
    for part in range(3):
        last = 128 * (pairs * part + pairs - 1)
        value = dqkv[:, last : last + 128]
        keep = jnp.logical_or(lane_of(value.shape) == 0, p.me == MEMBERS - 1)
        dqkv[:, last : last + 128] = jnp.where(keep, value, jnp.zeros_like(value))

    def one_part(step, carry):
        at = pl.ds(pl.multiple_of(step * span, span), span)
        value = low(dot_nt(dqkv[at, :], w_qkv[...]))
        dh_part[2 * step] = value[:count]
        dh_part[2 * step + 1] = value[count:]
        return carry

    lax.fori_loop(0, length // span, one_part, 0)
    reduce_dh = Reduce(p, dh_part, core_b, two_b, got_b, last_b, done_b, sem_b)
    reduce_dh.begin()
    chunk = 256
    for first in range(0, width, chunk):
        size = min(chunk, width - first)
        store_rows(g_qkv, first, dot_tn(h_first[:, first : first + size], dqkv[...]))
    for item in qkv_folds:
        item.begin()
    for item in qkv_folds:
        item.rest()
    reduce_dh.second()
    for pair in range(pairs):
        total = 0.0
        for block in range(MEMBERS):
            at = slice(block * count, block * count + count)
            total = total + dot_tn(attn[pair, at, :], branch_all[block])
        g_heads[128 * pair : 128 * pair + 128, :] = total
    g_out[...] = low(g_heads[pl.ds(pl.multiple_of(four * p.me - first_head, 8), four), :])
    root_y = out_root(p.me)
    same_y = p.y == root_y
    root = jnp.logical_and(same_y, p.far == 0)
    beside = jnp.logical_and(same_y, p.far == 1)
    over_y = remote(g_out, out_y, tree_sem, 0, p.target(y=1 - p.y))
    over_far = remote(out_go, out_far, tree_sem, 1, p.target(far=1 - p.far))

    @pl.when(jnp.logical_not(same_y))
    def _():
        over_y.start()

    reduce_dh.third()
    result[...] = low(resid_own[...] + reduce_made.result() + vecs[33:34, :])
    home = p.target(
        x=p.ctx % 2, near=p.ctx // 2 % 2, core=p.ctx // 4, y=p.fsdp // 2, far=p.fsdp % 2
    )
    moves = [Move(p, result, out_home, home_sem.at[0, 0], home_sem.at[1, 0], home)]

    @pl.when(same_y)
    def _():
        over_y.wait_recv()

    @pl.when(beside)
    def _():
        out_go[...] = low(wide(g_out[...]) + wide(out_y[...]))
        over_far.start()

    dh = reduce_dh.result()
    x = wide(x_own[...])
    center = x - jnp.mean(x, -1, keepdims=True)
    scale = lax.rsqrt(jnp.mean(center * center, -1, keepdims=True) + epsilon_norm)
    hat = center * scale
    scaled = dh * vecs[0:1, :]
    inner = jnp.mean(scaled * hat, -1, keepdims=True)
    value = (scaled - jnp.mean(scaled, -1, keepdims=True) - hat * inner) * scale
    input_grad[...] = low(dresid[...] + value)
    moves.append(Move(p, input_grad, grad_home, home_sem.at[0, 1], home_sem.at[1, 1], home))
    bias_sums = jnp.sum(wide(dqkv[...]), 0, keepdims=True)

    def placed(value, starts, me):
        total = jnp.zeros((1, width), jnp.float32)
        for index, start in enumerate(starts):
            parts = [value]
            if start:
                parts.insert(0, jnp.zeros((1, start), jnp.float32))
            after = width - start - value.shape[1]
            if after:
                parts.append(jnp.zeros((1, after), jnp.float32))
            row = jnp.concatenate(parts, 1) if len(parts) > 1 else value
            total = total + jnp.where(me == index, row, 0.0)
        return total

    heads = [head_start(member) * HD for member in range(MEMBERS)]
    vec_rows[0:1, :] = jnp.sum(dh * hat, 0, keepdims=True)
    vec_rows[1:2, :] = jnp.sum(dh, 0, keepdims=True)
    vec_rows[2:3, :] = placed(bias_sums[:, :per_part], heads, p.me)
    vec_rows[3:4, :] = placed(bias_sums[:, 2 * per_part :], heads, p.me)
    vec_rows[4:5, :] = sums[2:3, :]
    vec_rows[5:7, :] = sums[0:2, :]
    vec_rows[7:8, :] = sums[3:4, :]
    hidden = fc_sums.shape[1]
    fc_row = placed(fc_sums[...], (0, hidden), p.me % 2)
    for row in range(GROUPS):
        vec_rows[8 + row : 9 + row, :] = jnp.where(p.me // 2 == row, fc_row, 0.0)
    used = width // MEMBERS
    vec_go[...] = jnp.zeros_like(vec_go)
    for f in range(GROUPS):
        for c in range(MEMBERS):
            vec_go[MEMBERS * f + c, 0:3, 0:used] = vec_rows[
                3 * f : 3 * f + 3, used * c : used * c + used
            ]

    def vec_send(step, carry):
        other = (p.linear + step) % DEVICES
        pltpu.make_async_remote_copy(
            src_ref=vec_go.at[other],
            dst_ref=vec_got.at[p.linear],
            send_sem=vec_sem.at[0],
            recv_sem=vec_sem.at[1],
            device_id=(other // MEMBERS, other % MEMBERS),
            device_id_type=MESH,
        ).start()
        return carry

    lax.fori_loop(1, DEVICES, vec_send, 0)
    pltpu.make_async_copy(vec_go.at[p.linear], vec_got.at[p.linear], vec_sem.at[1]).start()
    for item in qkv_folds:
        item.middle()
    proj_sum[...] = proj_fold.end()
    target, part = shard_of(PROJ_FIRST + 4 * p.me + p.group)
    moves.append(
        Move(p, proj_sum, rows_back.at[part], rows_send.at[0], rows_recv.at[part], target)
    )
    for near in range(2):
        block = fc_folds[near].end()
        for slot in range(4):
            fc_sum[near, slot] = block[slot * unit : (slot + 1) * unit]
            third = FC_FIRST + 4 * (4 * p.far + 2 * near + p.y) + slot
            target, part = shard_of(third)
            moves.append(
                Move(
                    p, fc_sum.at[near, slot], fc_back.at[part, p.me],
                    fc_send.at[near, slot], fc_recv.at[part, p.me], target,
                )
            )

    @pl.when(root)
    def _():
        over_far.wait_recv()
        out_sum[...] = low(wide(g_out[...]) + wide(out_y[...]) + wide(out_far[...]))

    target, part = shard_of(OUT_FIRST + p.me)
    moves.append(
        Move(p, out_sum, rows_back.at[part], rows_send.at[1], rows_recv.at[part], target, root)
    )
    for near in range(2):
        qkv_sum[near] = qkv_folds[near].end()
        target = (0 * p.fsdp, 4 * p.far + 2 * near + p.y)
        moves.append(
            Move(
                p, qkv_sum.at[near], qkv_back.at[p.me], qkv_send.at[near], qkv_recv.at[p.me],
                target,
            )
        )
    arrived(vec_got, vec_sem.at[1])
    vec_back[...] = jnp.sum(vec_got[...], 0)

    @pl.when(p.fsdp == 0)
    def _():
        for member in range(MEMBERS):
            arrived(qkv_back.at[member], qkv_recv.at[member])

    for part in range(3):
        third = 3 * p.linear + part
        is_fc = jnp.logical_and(third >= FC_FIRST, third < PROJ_FIRST)
        is_rows = jnp.logical_and(third >= OUT_FIRST, jnp.logical_not(is_fc))

        @pl.when(is_fc)
        def _(part=part):
            for member in range(MEMBERS):
                arrived(fc_back.at[part, member], fc_recv.at[part, member])

        @pl.when(is_rows)
        def _(part=part):
            arrived(rows_back.at[part], rows_recv.at[part])

    arrived(out_home, home_sem.at[1, 0])
    arrived(grad_home, home_sem.at[1, 1])
    arrived(vec_got.at[pl.ds(1, DEVICES - 1)], vec_sem.at[0])
    for item in [proj_fold, reduce_made, reduce_dh] + fc_folds + qkv_folds + moves:
        item.sent()

    @pl.when(jnp.logical_not(same_y))
    def _():
        over_y.wait_send()

    @pl.when(beside)
    def _():
        over_far.wait_send()


def backward(
    dbranch, made, grad_fc, grad_proj, attn, qkv, row_pos, col_pos, w_out, w_qkv,
    h_first, x_all, resid_own, dresid, vecs, sums, fc_sums,
):
    kind, high = jnp.bfloat16, jnp.float32
    rows, width = dbranch.shape
    length = MEMBERS * rows
    four, cols = width // MEMBERS, qkv.shape[1]
    unit, hidden = four // 4, fc_sums.shape[1]
    per_part = SLOTS * HD
    any_space = pl.BlockSpec(memory_space=pl.ANY)
    vmem = pl.BlockSpec(memory_space=pltpu.VMEM)
    dma = pltpu.SemaphoreType.DMA

    def like(*shape, dtype=kind):
        return jax.ShapeDtypeStruct(shape, dtype)

    def buffer(*shape, dtype=kind):
        return pltpu.VMEM(shape, dtype)

    used = -(-width // MEMBERS // 128) * 128
    return pl.pallas_call(
        backward_kernel,
        out_shape=[
            like(rows, width),
            like(rows, width),
            like(MEMBERS, four, cols),
            like(3, MEMBERS, unit, hidden),
            like(3, four, width),
            like(8, used, dtype=high),
        ],
        in_specs=[vmem] + [any_space] * 3 + [vmem] * 4 + [any_space] * 4 + [vmem] * 5,
        out_specs=[any_space] * 5 + [vmem],
        scratch_shapes=[
            buffer(MEMBERS, rows, width),
            buffer(SLOTS // 2, length, 2 * HD),
            buffer(length, cols),
            buffer(length, 2 * HD, dtype=high),
            buffer(length, 2 * HD, dtype=high),
            buffer(per_part, width),
            buffer(*w_qkv.shape),
            buffer(*h_first.shape),
            buffer(rows, width),
            buffer(MEMBERS, rows, width),
            buffer(MEMBERS, rows, width),
            buffer(2, 2, four, hidden),
            buffer(2, four, width),
            buffer(MEMBERS, four, cols),
            buffer(per_part, width, dtype=high),
            buffer(four, width),
            buffer(rows, width),
            buffer(rows, width),
            buffer(16, width, dtype=high),
            buffer(DEVICES, 8, used, dtype=high),
            buffer(DEVICES, 8, used, dtype=high),
        ]
        + [
            buffer(2, 2, four, hidden), buffer(2, four, width), buffer(2, 2, four, cols),
            buffer(four, width),
        ]
        + [
            buffer(2, four, hidden), buffer(four, width), buffer(2, four, cols),
            buffer(four, width),
        ]
        * 2
        + [
            buffer(2, 4, unit, hidden), buffer(four, width), buffer(2, four, cols),
            buffer(four, width),
        ]
        + reduce_buffers(rows, width)
        + reduce_buffers(rows, width)
        + [
            dma((12,)),
            dma((2, 7)),
            dma((2, 15)),
            dma((2, 2)),
            dma((2,)),
            dma((2, 2)),
            dma((2,)),
            dma((8,)),
            dma((2, 4)),
            dma((3, 8)),
            dma((2,)),
            dma((3,)),
        ],
        compiler_params=pltpu.CompilerParams(
            collective_id=2, has_side_effects=True, vmem_limit_bytes=VMEM_BYTES
        ),
        name="backward",
    )(
        dbranch, made, grad_fc, grad_proj, attn, qkv, row_pos, col_pos, w_out, w_qkv,
        h_first, x_all, resid_own, dresid, vecs, sums, fc_sums,
    )


def lane_of(shape):
    return lax.broadcasted_iota(jnp.int32, shape, 1) // HD


def dot_nt(a, b):
    return lax.dot_general(a, b, (((1,), (1,)), ((), ())), preferred_element_type=jnp.float32)


def dot_tn(a, b):
    return lax.dot_general(a, b, (((0,), (0,)), ((), ())), preferred_element_type=jnp.float32)


def probabilities(query, keys, row_pos, col_pos):
    scores = dot_nt(query, keys) * 0.125
    scores = jnp.where(col_pos <= row_pos, scores, -1e30)
    weights = jnp.exp(scores - jnp.max(scores, -1, keepdims=True))
    return weights / jnp.sum(weights, -1, keepdims=True)


def own_heads(member):
    return (head_start(member + 1) - head_start(member)) * HD


def all_heads(pieces):
    return jnp.concatenate([pieces[m][:, : own_heads(m)] for m in range(MEMBERS)], 1)


def per_device_groups(
    inputs, cotangent, slot_order, weights, vectors, first_w, second_w, first_vec, second_vec
):
    seqs, rows, width = inputs.shape
    kind, high = jnp.bfloat16, jnp.float32
    fsdp, ctx = lax.axis_index("fsdp"), lax.axis_index("ctx")
    member = 4 * (fsdp % 2) + 2 * (ctx // 2 % 2) + fsdp // 2
    length = rows * MEMBERS
    hidden = FF // MEMBERS
    local = weights.shape[0]
    third = local // 3
    unit = width // DEVICES
    four = 4 * unit
    per_part = SLOTS * HD

    order = jnp.pad(slot_order, ((0, 127), (0, 128 - slot_order.shape[1])))
    vec_rows, vec_cols = vectors.shape
    padded = jnp.pad(vectors, ((0, 16 - vec_rows), (0, -vec_cols % 128)))
    (
        x_all, back_all, vecs, row_pos, col_pos, own_qkv, h_first, qkv, attn_all, attn,
        own_fc, own_proj, full_out,
    ) = forward(
        inputs.reshape(rows, width), cotangent.reshape(rows, width), order, padded, weights
    )
    grad_fc, grad_proj, made, resid_own, dresid, dbranch, sums, grad_bf = middle(
        x_all.reshape(length, width), attn_all, back_all.reshape(length, width), vecs,
        full_out, own_fc, own_proj,
    )
    outputs, input_grad, qkv_back, fc_back, rows_back, vec_back = backward(
        dbranch, made, grad_fc, grad_proj, attn, qkv, row_pos, col_pos, full_out, own_qkv,
        h_first, x_all, resid_own, dresid, vecs, sums, grad_bf,
    )
    outputs = outputs.reshape(seqs, rows, width)
    input_grad = input_grad.reshape(seqs, rows, width)
    qkv_flat = jnp.concatenate(
        [all_heads(qkv_back[:, :, p * per_part : (p + 1) * per_part]) for p in range(3)], 1
    ).reshape(local, 128)
    fc_flat = fc_back.transpose(0, 2, 1, 3).reshape(3, third, 128)
    rows_flat = rows_back.reshape(3, third, 128)
    thirds = 3 * (fsdp * MEMBERS + ctx) + jnp.arange(3)
    is_fc = jnp.logical_and(thirds >= FC_FIRST, thirds < PROJ_FIRST)
    others = jnp.where(is_fc[:, None, None], fc_flat, rows_flat).reshape(local, 128)
    owned = jnp.where(fsdp == 0, qkv_flat, others).astype(high)
    new_w = adamw(weights, owned, first_w, second_w, rate_matrix, weight_decay)
    owned_vec = vec_back[:vec_rows, :vec_cols]
    new_vec = adamw(vectors, owned_vec, first_vec, second_vec, rate_vector, 0.0)
    return (outputs, input_grad, new_w[0], new_w[1], new_w[2], new_vec[0], new_vec[1], new_vec[2])


def solution(mesh):
    in_specs = (
        P("fsdp", "ctx", None),
        P("fsdp", "ctx", None),
        P("fsdp", None),
        P(("fsdp", "ctx"), None),
        P("fsdp", "ctx"),
        P(("fsdp", "ctx"), None),
        P(("fsdp", "ctx"), None),
        P("fsdp", "ctx"),
        P("fsdp", "ctx"),
    )
    out_specs = (
        P("fsdp", "ctx", None),
        P("fsdp", "ctx", None),
        P(("fsdp", "ctx"), None),
        P(("fsdp", "ctx"), None),
        P(("fsdp", "ctx"), None),
        P("fsdp", "ctx"),
        P("fsdp", "ctx"),
        P("fsdp", "ctx"),
    )
    per_device = per_device_groups if mesh.shape["ctx"] == MEMBERS else per_device_ring
    return jax.shard_map(
        per_device, mesh=mesh, in_specs=in_specs, out_specs=out_specs, check_vma=False
    )
```

```python
import jax
import jax.numpy as jnp
from jax import lax
from jax.experimental import pallas as pl
from jax.experimental.pallas import tpu as pltpu
from jax.sharding import PartitionSpec as P

HEADS = 25
HD = 64
FF = 6400
STEP = 10


epsilon_norm = 1e-05
beta_first = 0.9
beta_second = 0.999
epsilon_adam = 1e-08
weight_decay = 0.1
rate_matrix = 0.1
rate_vector = 0.8


def shifted(value, axis, steps):
    count = lax.axis_size(axis)
    pairs = [(source, (source + steps) % count) for source in range(count)]
    return lax.ppermute(value, axis, pairs)


def layer_norm(value, gain, shift):
    center = value - jnp.mean(value, -1, keepdims=True)
    spread = jnp.mean(center * center, -1, keepdims=True)
    return center * lax.rsqrt(spread + epsilon_norm) * gain + shift


def gelu_tanh(value):
    return jax.nn.gelu(value, approximate=True)


def key_positions(slot_order, first_slot, slots, block):
    groups = lax.dynamic_slice_in_dim(slot_order, first_slot, slots, 1)
    offsets = jnp.arange(block, dtype=jnp.int32)
    return (groups[:, :, None] * block + offsets).reshape(slot_order.shape[0], slots * block)


def unpack_flat(flat, width, hidden):
    flat = flat.reshape(-1)
    first_end = 3 * width * width
    second_end = 4 * width * width
    third_end = 4 * width * width + width * hidden
    return (
        flat[:first_end].reshape(width, 3 * width),
        flat[first_end:second_end].reshape(width, width),
        flat[second_end:third_end].reshape(width, hidden),
        flat[third_end:].reshape(hidden, width),
    )


def gather_params(weights, vectors):
    local = weights.reshape(1, weights.shape[0], weights.shape[1])
    part = (
        lax.all_gather(local, "fsdp", axis=0, tiled=True),
        lax.all_gather(vectors, "fsdp", axis=0, tiled=True),
    )
    return (
        lax.all_gather(part[0], "ctx", axis=1, tiled=True),
        lax.all_gather(part[1], "ctx", axis=1, tiled=True),
    )


def reduce_grads(grad_flat, grad_vec):
    part = (
        lax.psum_scatter(
            grad_flat.astype(jnp.bfloat16), "fsdp", scatter_dimension=0, tiled=True
        ).astype(jnp.float32),
        lax.psum_scatter(
            grad_vec.astype(jnp.bfloat16), "fsdp", scatter_dimension=0, tiled=True
        ).astype(jnp.float32),
    )
    return (
        lax.psum_scatter(
            part[0].astype(jnp.bfloat16), "ctx", scatter_dimension=1, tiled=True
        ).astype(jnp.float32),
        lax.psum_scatter(
            part[1].astype(jnp.bfloat16), "ctx", scatter_dimension=1, tiled=True
        ).astype(jnp.float32),
    )


def pass_grads(grad_pairs):
    return shifted(grad_pairs.astype(jnp.bfloat16), "ctx", 1).astype(grad_pairs.dtype)


def adamw(weight, grad, first, second, rate, decay):
    first = beta_first * first + (1.0 - beta_first) * grad
    second = beta_second * second + (1.0 - beta_second) * grad * grad
    first_hat = first / (1.0 - beta_first**STEP)
    second_hat = second / (1.0 - beta_second**STEP)
    weight = weight.astype(jnp.float32)
    updated = weight - rate * (first_hat / (jnp.sqrt(second_hat) + epsilon_adam) + decay * weight)
    return (first, second, updated)


def per_device_ring(
    inputs, cotangent, slot_order, weights, vectors, first_w, second_w, first_vec, second_vec
):
    seqs, rows, width = inputs.shape
    tokens = seqs * rows
    block = rows // 2
    cycle = lax.axis_size("ctx")
    shards = lax.axis_size("fsdp")
    me = lax.axis_index("ctx")
    full_flat, full_vec = gather_params(weights, vectors)
    full_qkv, full_out, full_fc, full_proj = unpack_flat(full_flat, width, FF)
    vec = full_vec.astype(jnp.float32)
    bias_fc = vec[8:].reshape(-1)
    x_in = inputs.reshape(tokens, width).astype(jnp.float32)
    h_first, pull_first = jax.vjp(layer_norm, x_in, vec[0], vec[1])
    h_first_b = h_first.astype(jnp.bfloat16)
    zero_row = jnp.zeros((width,), jnp.float32)
    qkv = jnp.dot(h_first_b, full_qkv, preferred_element_type=jnp.float32)
    qkv_b = (qkv + jnp.concatenate([vec[2], zero_row, vec[3]])).astype(jnp.bfloat16)
    query_heads = qkv_b[:, :width].reshape(seqs, rows, HEADS, HD)
    key_value = qkv_b[:, width:].reshape(seqs, rows, 2, width)
    query_pos = key_positions(slot_order, 2 * me, 2, block)

    def online(state, item):
        top, total, accum = state
        keys_i, values_i, pos_i = item
        scores = (
            jnp.einsum("sqhd,skhd->shqk", query_heads, keys_i, preferred_element_type=jnp.float32)
            * 0.125
        )
        allowed = pos_i[:, None, None, :] <= query_pos[:, None, :, None]
        scores = jnp.where(allowed, scores, -1e30)
        peak = jnp.maximum(top, jnp.max(scores, -1))
        weights_p = jnp.where(allowed, jnp.exp(scores - peak[..., None]), 0.0)
        factor = jnp.exp(top - peak)
        total = total * factor + jnp.sum(weights_p, -1)
        mixed = jnp.einsum(
            "shqk,skhd->sqhd",
            weights_p.astype(jnp.bfloat16),
            values_i,
            preferred_element_type=jnp.float32,
        )
        accum = accum * jnp.transpose(factor, (0, 2, 1))[..., None] + mixed
        return ((peak, total, accum), None)

    start_state = (
        jnp.full((seqs, HEADS, rows), -1e30, jnp.float32),
        jnp.zeros((seqs, HEADS, rows), jnp.float32),
        jnp.zeros((seqs, rows, HEADS, HD), jnp.float32),
    )
    state = start_state
    piece = lax.all_gather(key_value, "ctx", axis=1, tiled=True)
    count = piece.shape[1]
    turns = count // rows
    pos_all = key_positions(slot_order, jnp.int32(0) // block, count // block, block)
    stack = piece.reshape(seqs, turns, rows, 2, HEADS, HD).transpose(1, 0, 2, 3, 4, 5)
    pos_stack = pos_all.reshape(seqs, turns, rows).transpose(1, 0, 2)
    state, _ = lax.scan(online, state, (stack[:, :, :, 0], stack[:, :, :, 1], pos_stack))
    top, total, accum = state
    attn = accum / jnp.transpose(total, (0, 2, 1))[..., None]
    logsum = top + jnp.log(total)
    attn_b = attn.reshape(tokens, width).astype(jnp.bfloat16)
    resid = x_in + jnp.dot(attn_b, full_out, preferred_element_type=jnp.float32) + vec[4]
    h_second, pull_second = jax.vjp(layer_norm, resid, vec[5], vec[6])
    h_second_b = h_second.astype(jnp.bfloat16)
    pre = jnp.dot(h_second_b, full_fc, preferred_element_type=jnp.float32) + bias_fc
    act, pull_gelu = jax.vjp(gelu_tanh, pre)
    act_b = act.astype(jnp.bfloat16)
    result = resid + jnp.dot(act_b, full_proj, preferred_element_type=jnp.float32) + vec[7]
    outputs = result.astype(jnp.bfloat16).reshape(seqs, rows, width)
    back_b = cotangent.reshape(tokens, width)
    back = back_b.astype(jnp.float32)
    grad_proj = jnp.einsum("tf,td->fd", act_b, back_b, preferred_element_type=jnp.float32)
    grad_bp = jnp.sum(back, 0)
    dact = jnp.einsum("td,fd->tf", back_b, full_proj, preferred_element_type=jnp.float32)
    dpre_b = pull_gelu(dact)[0].astype(jnp.bfloat16)
    grad_fc = jnp.einsum("td,tf->df", h_second_b, dpre_b, preferred_element_type=jnp.float32)
    grad_bf = jnp.sum(dpre_b, 0, dtype=jnp.float32)
    dh_second = jnp.einsum("tf,df->td", dpre_b, full_fc, preferred_element_type=jnp.float32)
    dres_ln, grad_g2, grad_b2 = pull_second(dh_second)
    dresid = back + dres_ln
    dbranch_b = dresid.astype(jnp.bfloat16)
    grad_bo = jnp.sum(dbranch_b, 0, dtype=jnp.float32)
    grad_out = jnp.einsum("td,te->de", attn_b, dbranch_b, preferred_element_type=jnp.float32)
    dattn_b = jnp.einsum(
        "te,de->td", dbranch_b, full_out, preferred_element_type=jnp.float32
    ).astype(jnp.bfloat16)
    grad_heads = dattn_b.reshape(seqs, rows, HEADS, HD)
    delta = jnp.transpose(jnp.sum(grad_heads.astype(jnp.float32) * attn, -1), (0, 2, 1))

    def contribute(pair, source):
        pos_k = key_positions(slot_order, 2 * source, 2, block)
        key_h = pair[:, :, 0].reshape(seqs, rows, HEADS, HD)
        value_h = pair[:, :, 1].reshape(seqs, rows, HEADS, HD)
        scores = (
            jnp.einsum("sqhd,skhd->shqk", query_heads, key_h, preferred_element_type=jnp.float32)
            * 0.125
        )
        allowed = pos_k[:, None, None, :] <= query_pos[:, None, :, None]
        probs = jnp.where(allowed, jnp.exp(scores - logsum[..., None]), 0.0)
        dvalue = jnp.einsum(
            "shqk,sqhd->skhd",
            probs.astype(jnp.bfloat16),
            grad_heads,
            preferred_element_type=jnp.float32,
        )
        dprobs = jnp.einsum(
            "sqhd,skhd->shqk", grad_heads, value_h, preferred_element_type=jnp.float32
        )
        dscores = (probs * (dprobs - delta[..., None])).astype(jnp.bfloat16)
        dquery = (
            jnp.einsum("shqk,skhd->sqhd", dscores, key_h, preferred_element_type=jnp.float32)
            * 0.125
        )
        dkey = (
            jnp.einsum("shqk,sqhd->skhd", dscores, query_heads, preferred_element_type=jnp.float32)
            * 0.125
        )
        return (dquery, jnp.stack((dkey, dvalue), 2))

    dq_own, dkv_own = contribute(key_value, me)

    def turn(step, state):
        pair, dkv_acc, dq_acc = state
        pair = shifted(pair, "ctx", 1)
        dkv_acc = pass_grads(dkv_acc)
        source = (me - step) % cycle
        dq_part, dkv_part = contribute(pair, source)
        return (pair, dkv_acc + dkv_part, dq_acc + dq_part)

    final = lax.fori_loop(1, cycle, turn, (key_value, dkv_own, dq_own))
    dkv = pass_grads(final[1])
    dqkv_b = jnp.concatenate(
        [final[2].reshape(tokens, width), dkv.reshape(tokens, 2 * width)], 1
    ).astype(jnp.bfloat16)
    grad_qkv = jnp.einsum("td,te->de", h_first_b, dqkv_b, preferred_element_type=jnp.float32)
    bias_sums = jnp.sum(dqkv_b, 0, dtype=jnp.float32)
    dh_first = jnp.einsum("te,de->td", dqkv_b, full_qkv, preferred_element_type=jnp.float32)
    dx_ln, grad_g1, grad_b1 = pull_first(dh_first)
    input_grad = (dresid + dx_ln).astype(jnp.bfloat16).reshape(seqs, rows, width)
    grad_vec = jnp.concatenate(
        [
            jnp.stack(
                [
                    grad_g1,
                    grad_b1,
                    bias_sums[:width],
                    bias_sums[2 * width :],
                    grad_bo,
                    grad_g2,
                    grad_b2,
                    grad_bp,
                ]
            ),
            grad_bf.reshape(-1, width),
        ],
        0,
    )
    grad_flat = jnp.concatenate(
        [grad_qkv.reshape(-1), grad_out.reshape(-1), grad_fc.reshape(-1), grad_proj.reshape(-1)]
    ).reshape(shards, -1, 128)
    owned_flat, owned_vec = reduce_grads(grad_flat, grad_vec)
    owned_flat = owned_flat.reshape(weights.shape[0], 128)
    new_w = adamw(weights, owned_flat, first_w, second_w, rate_matrix, weight_decay)
    new_vec = adamw(vectors, owned_vec, first_vec, second_vec, rate_vector, 0.0)
    return (outputs, input_grad, new_w[0], new_w[1], new_w[2], new_vec[0], new_vec[1], new_vec[2])


MEMBERS = 8
GROUPS = 4
DEVICES = MEMBERS * GROUPS
MESH = pl.DeviceIdType.MESH
BLOCK = 64
SLOTS = 4
VMEM_BYTES = 60 * 1024 * 1024
OUT_FIRST = 24
FC_FIRST = 32
PROJ_FIRST = 64


def head_start(member):
    return HEADS * member // MEMBERS


class Place:
    def __init__(self):
        self.fsdp, self.ctx = lax.axis_index("fsdp"), lax.axis_index("ctx")
        self.x, self.core = self.fsdp // 2, self.fsdp % 2
        self.far, self.near, self.y = self.ctx // 4, self.ctx // 2 % 2, self.ctx % 2
        self.me = self.member()
        self.group = 2 * self.y + self.far
        self.linear = self.fsdp * MEMBERS + self.ctx

    def member(self, x=None, near=None, core=None):
        x = self.x if x is None else x
        near = self.near if near is None else near
        core = self.core if core is None else core
        return 4 * core + 2 * near + x

    def target(self, x=None, core=None, far=None, near=None, y=None):
        x = self.x if x is None else x
        near = self.near if near is None else near
        core = self.core if core is None else core
        far = self.far if far is None else far
        y = self.y if y is None else y
        return (2 * x + core, 4 * far + 2 * near + y)

    def is_me(self, target):
        return jnp.logical_and(target[0] == self.fsdp, target[1] == self.ctx)


def greet_all(place):
    barrier = pltpu.get_barrier_semaphore()

    def one(step, carry):
        other = (place.linear + step) % DEVICES
        pl.semaphore_signal(
            barrier, inc=1, device_id=(other // MEMBERS, other % MEMBERS), device_id_type=MESH
        )
        return carry

    lax.fori_loop(1, DEVICES, one, 0)
    pl.semaphore_wait(barrier, DEVICES - 1)


def greet(targets):
    barrier = pltpu.get_barrier_semaphore()
    for target in targets:
        pl.semaphore_signal(barrier, inc=1, device_id=target, device_id_type=MESH)
    pl.semaphore_wait(barrier, len(targets))


def remote(source, landing, sems, index, target):
    return pltpu.make_async_remote_copy(
        src_ref=source,
        dst_ref=landing,
        send_sem=sems.at[0, index],
        recv_sem=sems.at[1, index],
        device_id=target,
        device_id_type=MESH,
    )


def arrived(landing, sem):
    pltpu.make_async_copy(landing, landing, sem).wait()


class Move:
    def __init__(self, place, source, landing, send_sem, recv_sem, target, valid=None):
        here = place.is_me(target)
        away = jnp.logical_not(here)
        if valid is not None:
            here, away = jnp.logical_and(here, valid), jnp.logical_and(away, valid)
        self.away = away
        self.copy = pltpu.make_async_remote_copy(
            src_ref=source,
            dst_ref=landing,
            send_sem=send_sem,
            recv_sem=recv_sem,
            device_id=target,
            device_id_type=MESH,
        )

        @pl.when(here)
        def _():
            pltpu.make_async_copy(source, landing, recv_sem).start()

        @pl.when(away)
        def _():
            self.copy.start()

    def sent(self):
        @pl.when(self.away)
        def _():
            self.copy.wait_send()


class Gather:
    def __init__(self, place, out, sems):
        p = place
        step, turn = 1 - p.core, p.core
        x1, near1 = p.x + step * (1 - 2 * p.x), p.near + turn * (1 - 2 * p.near)
        x2, near2 = p.x + turn * (1 - 2 * p.x), p.near + step * (1 - 2 * p.near)
        self.out, self.sems, self.me = out, sems, p.me
        self.first = p.target(x=x1, near=near1)
        self.second = p.target(x=x2, near=near2)
        self.other = p.target(core=1 - p.core)
        self.of_first = p.member(x=x1, near=near1)
        self.of_second = p.member(x=x2, near=near2)
        self.of_both = p.member(x=1 - p.x, near=1 - p.near)
        self.copies = {}

    def _go(self, name, index, block, target):
        item = remote(self.out.at[block], self.out.at[block], self.sems, index, target)
        item.start()
        self.copies[name] = item

    def begin(self):
        self._go("a", 0, self.me, self.first)
        self._go("b", 1, self.me, self.second)
        self._go("c", 2, self.me, self.other)

    def second_hop(self):
        self.copies["a"].wait_recv()
        self._go("d", 3, self.of_first, self.second)
        self._go("e", 4, self.of_first, self.other)

    def third_hop(self):
        self.copies["b"].wait_recv()
        self._go("f", 5, self.of_second, self.other)

    def last_hop(self):
        self.copies["d"].wait_recv()
        self._go("g", 6, self.of_both, self.other)

    def finish(self):
        for name in "cefg":
            self.copies[name].wait_recv()
        for item in self.copies.values():
            item.wait_send()


class Spread:
    def __init__(self, place, at, sems, first):
        p = place
        self.at, self.sems, self.first = at, sems, first
        self.mine, self.theirs = at(p.far, p.y), at(1 - p.far, p.y)
        self.to_far, self.to_y = p.target(far=1 - p.far), p.target(y=1 - p.y)

    def begin(self):
        self.a = remote(self.mine, self.mine, self.sems, self.first, self.to_far)
        self.b = remote(self.mine, self.mine, self.sems, self.first + 1, self.to_y)
        self.a.start()
        self.b.start()

    def middle(self):
        self.a.wait_recv()
        self.c = remote(self.theirs, self.theirs, self.sems, self.first + 2, self.to_y)
        self.c.start()

    def finish(self):
        self.b.wait_recv()
        self.c.wait_recv()
        for item in (self.a, self.b, self.c):
            item.wait_send()


def shard_of(third):
    shard = third // 3
    return (shard // MEMBERS, shard % MEMBERS), third % 3


def lookup(table, index):
    result = 0
    for place, entry in enumerate(table):
        if entry:
            result = result + jnp.where(index == place, entry, 0)
    return result


FC_OF_GROUP = (
    (0, 1, 16, 17, 18, 22, 23, 24),
    (2, 3, 19, 20, 21, 25, 26, 27),
    (4, 5, 6, 10, 11, 12, 28, 29),
    (7, 8, 9, 13, 14, 15, 30, 31),
)
FC_SLOT = [0] * 32
FC_Y = [0] * 32
for _group, _units in enumerate(FC_OF_GROUP):
    for _slot, _unit in enumerate(_units):
        FC_SLOT[_unit] = _slot
        FC_Y[_unit] = _group % 2


def fc_unit(far, y, slot):
    return lookup([units[slot] for units in FC_OF_GROUP], 2 * far + y)


def fc_home(place, unit):
    return lookup(FC_SLOT, unit), lookup(FC_Y, unit)


PROJ_OF_CTX = (
    (8, 9, 10, 20),
    (11, 12, 13, 0),
    (14, 15, 16, 2),
    (17, 18, 19, 5),
    (21, 22, 3, 4),
    (1, 23, 24, 25),
    (26, 27, 28, 6),
    (7, 29, 30, 31),
)


def hidden_of(member):
    core, near, x = member // 4, member // 2 % 2, member % 2
    return [
        PROJ_OF_CTX[4 * far + 2 * near + y][2 * core + x] for y in range(2) for far in range(2)
    ]


HIDDEN = [hidden_of(_member) for _member in range(8)]
HOLDER = {unit: (m, i) for m, units in enumerate(HIDDEN) for i, unit in enumerate(units)}
PROJ_FSDP, PROJ_CTX = [0] * 32, [0] * 32
PROJ_UNIT = [0] * 32
for _ctx, _units in enumerate(PROJ_OF_CTX):
    for _place, _unit in enumerate(_units):
        _fsdp = 2 * (_place % 2) + _place // 2
        PROJ_FSDP[_unit], PROJ_CTX[_unit] = _fsdp, _ctx
        PROJ_UNIT[8 * _fsdp + _ctx] = _unit
FC_POSITION = [0] * 32
for _group, _units in enumerate(FC_OF_GROUP):
    for _slot, _unit in enumerate(_units):
        FC_POSITION[_unit] = 8 * _group + _slot


def piece(tile_of, col, lane, size):
    start = col % 128
    value = tile_of(col // 128)
    if start + size > 128:
        lanes = lax.broadcasted_iota(jnp.int32, value.shape, 1)
        value = jnp.where(lanes < start, tile_of(col // 128 + 1), value)
    shift = (lane - start) % 128
    return pltpu.roll(value, shift, 1) if shift else value


def join(parts):
    result = parts[0][1]
    for lane, value in parts[1:]:
        lanes = lax.broadcasted_iota(jnp.int32, value.shape, 1)
        result = jnp.where(lanes < lane, result, value)
    return result


def out_root(member):
    return jnp.where(member // 3 == 1, 1, 0)


def half_tile(flat, first, count, stride, half):
    at = half // 2
    tile = flat[pl.ds(first + at, count, stride=stride), :]
    if half % 2 == 0:
        return tile
    after = flat[pl.ds(first + at + 1, count, stride=stride), :]
    lane = lax.broadcasted_iota(jnp.int32, tile.shape, 1)
    return pltpu.roll(jnp.where(lane < HD, after, tile), HD, 1)


def lay_qkv(flat, rows, pieces, member):
    count = rows.shape[1] // 2
    halves = 3 * HEADS
    for part in range(3):
        for odd in range(2):
            for tile in range(SLOTS // 2):
                half = halves * odd + HEADS * part + head_start(member) + 2 * tile
                rows[SLOTS // 2 * part + tile, pl.ds(odd, count, stride=2), :] = half_tile(
                    flat, 0, count, halves, half
                )
    for tile in range(3 * SLOTS // 2):
        pieces[member, :, 128 * tile : 128 * tile + 128] = rows[tile].astype(jnp.bfloat16)


def lay_fc(flat, first, pieces, part):
    count, hidden = pieces.shape[-2:]
    stride = FF // 128
    block = hidden // GROUPS

    def tile_of(tile):
        return flat[pl.ds(first + tile, count, stride=stride), :]

    for member in range(MEMBERS):
        for tile in range(-(-hidden // 128)):
            size = min(128, hidden - 128 * tile)
            parts, at = [], 128 * tile
            while at < 128 * tile + size:
                which, inside = divmod(at, block)
                length = min(block - inside, 128 * tile + size - at)
                col = block * HIDDEN[member][which] + inside
                parts.append((at - 128 * tile, piece(tile_of, col, at - 128 * tile, length)))
                at += length
            pieces[part, member, :, 128 * tile : 128 * tile + size] = join(parts)[
                :, :size
            ].astype(jnp.bfloat16)


def lay_rows(flat, first, rows, blocks, part):
    count = rows.shape[1] // 2
    width = blocks.shape[-1]
    halves = width // HD
    for odd in range(2):
        for tile in range(-(-width // 128)):
            half = halves * odd + 2 * tile
            size = min(128, width - 128 * tile)
            if size == 128 or half % 2 == 0:
                value = half_tile(flat, first, count, halves, half)
            else:
                value = pltpu.roll(
                    flat[pl.ds(first + half // 2, count, stride=halves), :], HD, 1
                )
            rows[tile, pl.ds(odd, count, stride=2), :] = value
    for tile in range(-(-width // 128)):
        size = min(128, width - 128 * tile)
        blocks[part, :, 128 * tile : 128 * tile + size] = rows[tile, :, :size].astype(
            jnp.bfloat16
        )


def wide(value):
    return value.astype(jnp.float32)


def low(value):
    return value.astype(jnp.bfloat16)


def half_of(blocks, core):
    return blocks.at[pl.ds(4 * core, 4)]


class Reduce:
    def __init__(self, place, away, kept, from_core, two, got, last, done, sems):
        self.p, self.away, self.kept, self.from_core = place, away, kept, from_core
        self.two, self.got, self.last, self.done, self.sems = two, got, last, done, sems
        self.route = Gather(place, None, None)
        self.copies = []

    def _go(self, source, landing, index, target):
        item = remote(source, landing, self.sems, index, target)
        item.start()
        self.copies.append(item)
        return item

    def begin(self):
        for j in (3, 2, 1, 0):
            self._go(self.away.at[j], self.from_core.at[j], j, self.route.other)

    def _summed(self, member):
        block = member - 4 * self.p.core
        return wide(self.kept[block]) + wide(self.from_core[block])

    def second(self):
        for item in self.copies[:4]:
            item.wait_recv()
        self.two[0] = low(self._summed(self.route.of_both))
        self.across = self._go(self.two.at[0], self.got.at[0], 4, self.route.second)
        self.two[1] = low(self._summed(self.route.of_second))
        self.beyond = self._go(self.two.at[1], self.got.at[1], 5, self.route.second)

    def third(self):
        self.across.wait_recv()
        self.last[...] = low(self._summed(self.route.of_first) + wide(self.got[0]))
        self.final = self._go(self.last, self.done, 6, self.route.first)

    def result(self):
        self.beyond.wait_recv()
        value = self._summed(self.p.me) + wide(self.got[1])
        self.final.wait_recv()
        return value + wide(self.done[...])

    def sent(self):
        for item in self.copies:
            item.wait_send()


def reduce_buffers(rows, width):
    kind = jnp.bfloat16
    return [
        pltpu.VMEM((4, rows, width), kind),
        pltpu.VMEM((2, rows, width), kind),
        pltpu.VMEM((2, rows, width), kind),
        pltpu.VMEM((rows, width), kind),
        pltpu.VMEM((rows, width), kind),
        pltpu.SemaphoreType.DMA((2, 7)),
    ]


def norm_rows(value, gain, shift):
    center = value - jnp.mean(value, -1, keepdims=True)
    spread = jnp.mean(center * center, -1, keepdims=True)
    return center * lax.rsqrt(spread + epsilon_norm) * gain + shift


def head_rows(member):
    return 8 * member


def member_lanes(row, member, count):
    result = jnp.zeros((row.shape[0], count), row.dtype)
    for other in range(MEMBERS):
        first = head_start(other) * HD
        result = result + jnp.where(member == other, row[:, first : first + count], 0.0)
    return result


def attend_block(query, keys, values, row_pos, col_pos):
    lanes = lane_of(query.shape)
    result = jnp.zeros(query.shape, jnp.float32)
    for head in range(2):
        mine = lanes == head
        own = jnp.where(mine, query, jnp.zeros_like(query))
        probs = probabilities(own, keys, row_pos, col_pos)
        mixed = jnp.dot(probs.astype(jnp.bfloat16), values, preferred_element_type=jnp.float32)
        result = jnp.where(mine, mixed, result)
    return result.astype(jnp.bfloat16)


def forward_kernel(
    x_in, back_in, order_in, vec_in, weights,
    back_all, vecs, row_pos, col_pos, w_qkv_out, h_first_out, qkv_out, attn, w_fc_out, w_proj_out,
    w_heads, x_own, resid_own, h_second,
    x_all, w_qkv, h_first, qkv, w_fc, w_proj,
    flat, rows, qkv_pieces, fc_pieces, blocks, order, vec_all, qkv_land,
    fc, proj, out, fc_part, proj_part, out_part, tail, next_tail, window, unit_rows, h_own,
    branch, from_core, two, got, last, done, reduce_sem,
    move_sem, qkv_sem, fc_send, fc_recv, rows_sem, x_sem, back_sem, spread_sem,
    own_sem, fc_sem, proj_sem, tree_sem, h_sem, store_sem,
):
    p = Place()
    third_rows = weights.shape[0] // 3
    count, width = x_in.shape
    length = MEMBERS * count
    pairs = SLOTS // 2
    barrier = pltpu.get_barrier_semaphore()

    def signal(step, carry):
        other = (p.linear + step) % DEVICES
        pl.semaphore_signal(
            barrier, inc=1, device_id=(other // MEMBERS, other % MEMBERS), device_id_type=MESH
        )
        return carry

    lax.fori_loop(1, DEVICES, signal, 0)
    flat[...] = weights[...].astype(jnp.float32)
    pl.semaphore_wait(barrier, DEVICES - 1)
    home = p.target(
        x=p.ctx % 2, near=p.ctx // 2 % 2, core=p.ctx // 4, y=p.fsdp // 2, far=p.fsdp % 2
    )
    x_move = Move(p, x_in, x_all.at[p.ctx], move_sem.at[0, 0], move_sem.at[1, 0], home)
    order_move = Move(p, order_in, order, move_sem.at[0, 1], move_sem.at[1, 1], home)
    owner = p.fsdp == 0
    qkv_moves = []
    for member in (7, 6, 3, 2, 5, 4, 1, 0):

        @pl.when(owner)
        def _(member=member):
            lay_qkv(flat, rows, qkv_pieces, member)

        target = p.target(x=member % 2, near=member // 2 % 2, core=member // 4)
        qkv_moves.append(
            Move(
                p, qkv_pieces.at[member], qkv_land.at[p.far, p.near, p.y],
                qkv_sem.at[0, member], qkv_sem.at[1, p.near], target, owner,
            )
        )

    def vec_send(step, carry):
        other = (p.linear + step) % DEVICES
        pltpu.make_async_remote_copy(
            src_ref=vec_in,
            dst_ref=vec_all.at[p.linear],
            send_sem=move_sem.at[0, 2],
            recv_sem=move_sem.at[1, 2],
            device_id=(other // MEMBERS, other % MEMBERS),
            device_id_type=MESH,
        ).start()
        return carry

    lax.fori_loop(1, DEVICES, vec_send, 0)
    pltpu.make_async_copy(vec_in, vec_all.at[p.linear], move_sem.at[1, 2]).start()
    for part in range(3):
        third = 3 * p.linear + part
        is_fc = jnp.logical_and(third >= FC_FIRST, third < PROJ_FIRST)
        is_rows = jnp.logical_and(third >= OUT_FIRST, jnp.logical_not(is_fc))

        @pl.when(is_fc)
        def _(part=part):
            lay_fc(flat, part * third_rows, fc_pieces, part)

        @pl.when(is_rows)
        def _(part=part):
            lay_rows(flat, part * third_rows, rows, blocks, part)

    arrived(x_all.at[p.me], move_sem.at[1, 0])
    gather_x = Gather(p, x_all, x_sem)
    gather_x.begin()
    spreads = []
    for near in range(2):
        arrived(qkv_land.at[p.far, near, p.y], qkv_sem.at[1, near])
        item = Spread(p, lambda far, y, near=near: qkv_land.at[far, near, y], spread_sem, 3 * near)
        item.begin()
        spreads.append(item)
    gather_x.second_hop()
    gather_x.third_hop()
    fc_moves, rows_moves = [], []
    for part in range(3):
        third = 3 * p.linear + part
        valid = jnp.logical_and(third >= OUT_FIRST, third < FC_FIRST)
        member = jnp.where(valid, third - OUT_FIRST, 0)
        target = p.target(
            x=member % 2, near=member // 2 % 2, core=member // 4, y=out_root(member), far=0
        )
        rows_moves.append(
            Move(
                p, blocks.at[part], out_part,
                rows_sem.at[0, part], rows_sem.at[1, 1], target, valid,
            )
        )
    for part in range(3):
        third = 3 * p.linear + part
        valid = jnp.logical_and(third >= FC_FIRST, third < PROJ_FIRST)
        slot, y = fc_home(p, jnp.where(valid, third - FC_FIRST, 0))
        for member in (7, 6, 3, 2, 5, 4, 1, 0):
            target = p.target(x=member % 2, near=member // 2 % 2, core=member // 4, y=y)
            fc_moves.append(
                Move(
                    p, fc_pieces.at[part, member], fc_part.at[slot],
                    fc_send.at[part, member], fc_recv.at[slot], target, valid,
                )
            )
    for part in range(3):
        third = 3 * p.linear + part
        valid = third >= PROJ_FIRST
        unit = jnp.where(valid, third - PROJ_FIRST, 0)
        target = (lookup(PROJ_FSDP, unit), lookup(PROJ_CTX, unit))
        rows_moves.append(
            Move(
                p, blocks.at[part], proj_part,
                rows_sem.at[0, part], rows_sem.at[1, 0], target, valid,
            )
        )
    gather_x.last_hop()
    back_move = Move(p, back_in, back_all.at[p.ctx], move_sem.at[0, 3], move_sem.at[1, 3], home)
    arrived(vec_all, move_sem.at[1, 2])
    cols = vec_in.shape[-1]
    used = width // MEMBERS
    total = jnp.zeros(vecs.shape, jnp.float32)
    for ctx in range(MEMBERS):
        block = jnp.concatenate([vec_all[MEMBERS * f + ctx] for f in range(GROUPS)], 0)
        lane = lax.broadcasted_iota(jnp.int32, (cols, width), 0)
        at = lax.broadcasted_iota(jnp.int32, (cols, width), 1) - used * ctx
        spot = jnp.where(jnp.logical_and(lane == at, lane < used), 1.0, 0.0)
        total = total + jnp.dot(
            block, spot.astype(jnp.bfloat16), preferred_element_type=jnp.float32
        )
    vecs[...] = total
    arrived(order, move_sem.at[1, 1])
    slots = order[0:1, :].astype(jnp.float32)
    lane = lax.broadcasted_iota(jnp.int32, (length, 128), 1)
    row = lax.broadcasted_iota(jnp.int32, (length, 128), 0)
    spot = jnp.where(lane == row // BLOCK, slots, 0.0)
    inner = lax.broadcasted_iota(jnp.int32, (length, 1), 0) % BLOCK
    row_pos[...] = jnp.sum(spot, 1, keepdims=True) * BLOCK + inner.astype(jnp.float32)
    lane = lax.broadcasted_iota(jnp.int32, (128, length), 1)
    row = lax.broadcasted_iota(jnp.int32, (128, length), 0)
    spot = jnp.where(row == lane // BLOCK, 1.0, 0.0)
    inner = lax.broadcasted_iota(jnp.int32, (1, length), 1) % BLOCK
    found = jnp.dot(
        order[...].astype(jnp.bfloat16), spot.astype(jnp.bfloat16),
        preferred_element_type=jnp.float32,
    )
    col_pos[...] = found[0:1, :] * BLOCK + inner.astype(jnp.float32)
    for item in spreads:
        item.middle()
    arrived(back_all.at[p.me], move_sem.at[1, 3])
    gather_back = Gather(p, back_all, back_sem)
    gather_back.begin()
    gather_x.finish()

    def norm_block(step, carry):
        value = norm_rows(x_all[step].astype(jnp.float32), vecs[0:1, :], vecs[1:2, :])
        h_first[pl.ds(pl.multiple_of(step * count, count), count), :] = value.astype(jnp.bfloat16)
        return carry

    lax.fori_loop(0, MEMBERS, norm_block, 0)
    x_own[...] = x_all[p.me]
    stores = []

    def store(source, target):
        copy = pltpu.make_async_copy(source, target, store_sem.at[len(stores)])
        copy.start()
        stores.append(copy)

    store(h_first, h_first_out)
    to_far, to_y = p.target(far=1 - p.far), p.target(y=1 - p.y)
    same_y = p.y == out_root(p.me)
    root = jnp.logical_and(same_y, p.far == 0)
    beside = jnp.logical_and(same_y, p.far == 1)
    out_far = remote(out_part, out, tree_sem, 0, to_far)
    out_y = remote(out_part, out, tree_sem, 1, to_y)
    out_later = remote(out, out, tree_sem, 2, to_y)
    out_own = pltpu.make_async_copy(out_part, out, own_sem.at[8])

    @pl.when(root)
    def _():
        arrived(out_part, rows_sem.at[1, 1])
        out_far.start()
        out_y.start()
        out_own.start()

    fc_far, fc_y, fc_later, own_copies = [], [], [], []
    for slot in range(8):
        arrived(fc_part.at[slot], fc_recv.at[slot])
        landing = fc.at[fc_unit(p.far, p.y, slot)]
        fc_far.append(remote(fc_part.at[slot], landing, fc_sem, slot, to_far))
        fc_far[slot].start()
        fc_y.append(remote(fc_part.at[slot], landing, fc_sem, 8 + slot, to_y))
        fc_y[slot].start()
        own_copies.append(pltpu.make_async_copy(fc_part.at[slot], landing, own_sem.at[slot]))
        own_copies[slot].start()
    gather_back.second_hop()
    gather_back.third_hop()
    arrived(proj_part, rows_sem.at[1, 0])
    my_proj, far_proj = proj.at[p.y, p.far], proj.at[p.y, 1 - p.far]
    proj_far = remote(proj_part, my_proj, proj_sem, 0, to_far)
    proj_y = remote(proj_part, my_proj, proj_sem, 1, to_y)
    proj_far.start()
    proj_y.start()
    proj_own = pltpu.make_async_copy(proj_part, my_proj, own_sem.at[9])
    proj_own.start()
    for item in spreads:
        item.finish()
    four = qkv_land.shape[3]
    for far in range(2):
        for near in range(2):
            for y in range(2):
                first = four * (4 * far + 2 * near + y)
                w_qkv[first : first + four, :] = qkv_land[far, near, y]
    store(w_qkv, w_qkv_out)
    per_part = SLOTS * HD
    bias = jnp.concatenate(
        [
            member_lanes(vecs[2:3, :], p.me, per_part),
            jnp.zeros((1, per_part), jnp.float32),
            member_lanes(vecs[16:17, :], p.me, per_part),
        ],
        1,
    )

    def qkv_block(step, carry):
        at = pl.ds(pl.multiple_of(step * 2 * count, 2 * count), 2 * count)
        value = jnp.dot(h_first[at, :], w_qkv[...], preferred_element_type=jnp.float32)
        qkv[at, :] = (value + bias).astype(jnp.bfloat16)
        return carry

    lax.fori_loop(0, MEMBERS // 2, qkv_block, 0)
    store(qkv, qkv_out)
    gather_back.last_hop()
    span = 2 * count

    def one_pair(pair):
        def one_block(step, carry):
            at = pl.ds(pl.multiple_of(step * span, span), span)
            attn[pair, at, :] = attend_block(
                qkv[at, 128 * pair : 128 * pair + 128],
                qkv[:, 128 * (pairs + pair) : 128 * (pairs + pair) + 128],
                qkv[:, 128 * (2 * pairs + pair) : 128 * (2 * pairs + pair) + 128],
                row_pos[at, :],
                col_pos[...],
            )
            return carry

        lax.fori_loop(0, length // span, one_block, 0)

    one_pair(0)

    @pl.when(beside)
    def _():
        out_far.wait_recv()
        out_later.start()

    for slot in range(8):
        fc_far[slot].wait_recv()
        landing = fc.at[fc_unit(1 - p.far, p.y, slot)]
        copy = remote(landing, landing, fc_sem, 16 + slot, to_y)
        copy.start()
        fc_later.append(copy)
    one_pair(1)

    @pl.when(root)
    def _():
        out_own.wait()

    @pl.when(jnp.logical_and(jnp.logical_not(same_y), p.far == 0))
    def _():
        out_y.wait_recv()

    @pl.when(jnp.logical_and(jnp.logical_not(same_y), p.far == 1))
    def _():
        out_later.wait_recv()

    reach = tail.shape[0]
    tail[...] = out[four - reach :, :]
    following, before = (p.me + 1) % MEMBERS, (p.me + MEMBERS - 1) % MEMBERS
    to_next = p.target(
        x=following % 2, near=following // 2 % 2, core=following // 4
    )
    send_tail = remote(tail, next_tail, tree_sem, 3, to_next)
    send_tail.start()
    begin = head_rows(p.me)
    window[...] = jnp.zeros_like(window)
    window[reach : reach + four, :] = wide(out[...])
    span_rows = SLOTS * HD
    unit_rows[...] = low(window[pl.ds(pl.multiple_of(reach - begin, 8), span_rows), :])

    def one_branch(step, carry):
        at = pl.ds(pl.multiple_of(step * span, span), span)
        heads = jnp.concatenate([attn[pair, at, :] for pair in range(pairs)], 1)
        value = low(jnp.dot(heads, unit_rows[...], preferred_element_type=jnp.float32))
        branch[2 * step] = value[:count]
        branch[2 * step + 1] = value[count:]
        return carry

    lax.fori_loop(0, length // span, one_branch, 0)
    reduce = Reduce(
        p, half_of(branch, 1 - p.core), half_of(branch, p.core), from_core, two, got, last, done,
        reduce_sem,
    )
    reduce.begin()
    proj_far.wait_recv()
    proj_later = remote(far_proj, far_proj, proj_sem, 2, to_y)
    proj_later.start()
    reduce.second()
    reduce.third()
    for item in fc_y + fc_later:
        item.wait_recv()
    for item in own_copies:
        item.wait()
    value = wide(x_own[...]) + reduce.result() + vecs[17:18, :]
    resid_own[...] = value
    h_own[...] = low(norm_rows(value, vecs[18:19, :], vecs[32:33, :]))
    gather_h = Gather(p, h_second, h_sem)
    for name, index, target in (
        ("a", 0, gather_h.first), ("b", 1, gather_h.second), ("c", 2, gather_h.other),
    ):
        copy = remote(h_own, h_second.at[p.me], h_sem, index, target)
        copy.start()
        gather_h.copies[name] = copy
    store(h_own, h_second.at[p.me])
    unit = fc.shape[1]
    for block in range(DEVICES):
        w_fc[unit * block : unit * block + unit, :] = fc[block]
    store(w_fc, w_fc_out)
    gather_h.second_hop()
    gather_h.third_hop()
    proj_y.wait_recv()
    proj_later.wait_recv()
    proj_own.wait()
    for group in range(GROUPS):
        w_proj[four * group : four * group + four, :] = proj[group // 2, group % 2]
    store(w_proj, w_proj_out)
    gather_h.last_hop()
    send_tail.wait_recv()
    window[:reach, :] = wide(next_tail[...])
    w_heads[...] = low(window[pl.ds(pl.multiple_of(reach - begin, 8), span_rows), :])
    for item in (gather_h, gather_back):
        item.finish()
    for item in fc_far + fc_y + fc_later + [proj_far, proj_y, proj_later, send_tail]:
        item.wait_send()
    reduce.sent()

    @pl.when(root)
    def _():
        out_far.wait_send()
        out_y.wait_send()

    @pl.when(beside)
    def _():
        out_later.wait_send()

    for copy in stores:
        copy.wait()
    for item in [x_move, order_move, back_move] + qkv_moves + fc_moves + rows_moves:
        item.sent()
    arrived(vec_all.at[pl.ds(1, DEVICES - 1)], move_sem.at[0, 2])


def forward(x, back, order, vectors, weights):
    rows, width = x.shape
    kind, high = jnp.bfloat16, jnp.float32
    unit, hidden = width // DEVICES, FF // MEMBERS
    four, cols = 4 * unit, 3 * SLOTS * HD
    length, pairs = MEMBERS * rows, SLOTS // 2
    any_space = pl.BlockSpec(memory_space=pl.ANY)
    vmem = pl.BlockSpec(memory_space=pltpu.VMEM)
    dma = pltpu.SemaphoreType.DMA

    def like(*shape, dtype=kind):
        return jax.ShapeDtypeStruct(shape, dtype)

    return pl.pallas_call(
        forward_kernel,
        out_shape=[
            like(MEMBERS, rows, width),
            like(GROUPS * vectors.shape[0], width, dtype=high),
            like(length, 1, dtype=high),
            like(1, length, dtype=high),
            like(width, cols),
            like(length, width),
            like(length, cols),
            like(pairs, length, 2 * HD),
            like(width, hidden),
            like(hidden, width),
            like(SLOTS * HD, width),
            like(rows, width),
            like(rows, width, dtype=high),
            like(MEMBERS, rows, width),
        ],
        in_specs=[any_space] * 4 + [vmem],
        out_specs=[any_space] + [vmem] * 3 + [any_space] * 3 + [vmem] + [any_space] * 2
        + [vmem] * 3 + [any_space],
        scratch_shapes=[
            pltpu.VMEM((MEMBERS, rows, width), kind),
            pltpu.VMEM((width, cols), kind),
            pltpu.VMEM((length, width), kind),
            pltpu.VMEM((length, cols), kind),
            pltpu.VMEM((width, hidden), kind),
            pltpu.VMEM((hidden, width), kind),
            pltpu.VMEM(weights.shape, high),
            pltpu.VMEM((-(-width // 128), four, 128), high),
            pltpu.VMEM((MEMBERS, four, cols), kind),
            pltpu.VMEM((3, MEMBERS, unit, hidden), kind),
            pltpu.VMEM((3, four, width), kind),
            pltpu.VMEM(order.shape, order.dtype),
            pltpu.VMEM((DEVICES,) + vectors.shape, kind),
            pltpu.VMEM((2, 2, 2, four, cols), kind),
            pltpu.VMEM((DEVICES, unit, hidden), kind),
            pltpu.VMEM((2, 2, four, width), kind),
            pltpu.VMEM((four, width), kind),
            pltpu.VMEM((8, unit, hidden), kind),
            pltpu.VMEM((four, width), kind),
            pltpu.VMEM((four, width), kind),
            pltpu.VMEM((64, width), kind),
            pltpu.VMEM((64, width), kind),
            pltpu.VMEM((64 + SLOTS * HD, width), high),
            pltpu.VMEM((SLOTS * HD, width), kind),
            pltpu.VMEM((rows, width), kind),
            pltpu.VMEM((MEMBERS, rows, width), kind),
        ]
        + reduce_buffers(rows, width)
        + [
            dma((2, 4)),
            dma((2, 8)),
            dma((3, 8)),
            dma((8,)),
            dma((2, 3)),
            dma((2, 7)),
            dma((2, 7)),
            dma((2, 6)),
            dma((9 + 1,)),
            dma((2, 24)),
            dma((2, 3)),
            dma((2, 4)),
            dma((2, 7)),
            dma((6,)),
        ],
        compiler_params=pltpu.CompilerParams(
            collective_id=1, has_side_effects=True, vmem_limit_bytes=VMEM_BYTES
        ),
        name="forward",
    )(x, back, order, vectors, weights)


GELU_SCALE = 0.7978845608028654
GELU_CUBE = 0.044715


def store_rows(target, first, value, lanes=slice(None), at=None):
    places = at
    size = target.shape[1]
    row = 0
    while row < value.shape[0]:
        block, at = divmod(first + row, size)
        count = min(size - at, value.shape[0] - row)
        block = block if places is None else places[block]
        target[block, at : at + count, lanes] = low(value[row : row + count])
        row += count


def middle_kernel(
    h_in, back_all, vecs, resid_own, w_fc_in, w_proj_in,
    grad_fc, grad_proj, made, dresid, dbranch, sums, fc_sums,
    h_second, back, w_fc, w_proj, act, dpre, dh_part, made_part, g_fc, g_proj,
    from_core, two, got, last, done, reduce_sem, load_sem, store_sem,
):
    p = Place()
    length, width = h_second.shape
    count = length // MEMBERS
    hidden = act.shape[1]
    loads = []
    for index, (source, target) in enumerate(
        (
            (h_in, h_second), (w_fc_in, w_fc), (back_all, back), (w_proj_in, w_proj),
        )
    ):
        copy = pltpu.make_async_copy(source, target, load_sem.at[index])
        copy.start()
        loads.append(copy)
    reduce = Reduce(p, half_of(dh_part, 1 - p.core), half_of(dh_part, p.core), from_core, two, got, last, done, reduce_sem)
    route = reduce.route
    greet((route.first, route.second, route.other))
    bias_fc = jnp.zeros((1, hidden), jnp.float32)
    block = hidden // GROUPS
    for member in range(MEMBERS):
        parts = []
        for unit in HIDDEN[member]:
            row, first = divmod(block * unit, width)
            row = (34, 48, 49, 50)[row]
            parts.append(vecs[row : row + 1, first : first + block])
        bias_fc = bias_fc + jnp.where(p.me == member, jnp.concatenate(parts, 1), 0.0)
    fc_sums[...] = jnp.zeros_like(fc_sums)
    for copy in loads:
        copy.wait()
    span = 2 * count

    def one_block(step, carry):
        at = pl.ds(pl.multiple_of(step * span, span), span)
        normed = h_second[at, :]
        pre = jnp.dot(normed, w_fc[...], preferred_element_type=jnp.float32) + bias_fc
        square = pre * pre
        slope = jnp.tanh(GELU_SCALE * (pre + GELU_CUBE * pre * square))
        act[at, :] = low(0.5 * pre * (1.0 + slope))
        tilt = 0.5 * (1.0 + slope) + 0.5 * pre * (1.0 - slope * slope) * GELU_SCALE * (
            1.0 + 3.0 * GELU_CUBE * square
        )
        dpre_block = low(dot_nt(back[at, :], w_proj[...]) * tilt)
        dpre[at, :] = dpre_block
        fc_sums[...] += jnp.sum(wide(dpre_block), 0, keepdims=True)
        value = low(dot_nt(dpre_block, w_fc[...]))
        dh_part[2 * step] = value[:count]
        dh_part[2 * step + 1] = value[count:]
        return carry

    lax.fori_loop(0, MEMBERS // 2, one_block, 0)
    reduce.begin()
    chunk = 256

    def one_proj(step, carry):
        lanes = pl.ds(pl.multiple_of(step * chunk, chunk), chunk)
        store_rows(g_proj, 0, dot_tn(act[...], back[:, lanes]), lanes)
        return carry

    lax.fori_loop(0, 3, one_proj, 0)
    reduce.second()
    lax.fori_loop(3, width // chunk, one_proj, 0)
    tail = slice(width // chunk * chunk, width)
    if width % chunk:
        store_rows(g_proj, 0, dot_tn(act[...], back[:, tail]), tail)
    stores = [pltpu.make_async_copy(g_proj, grad_proj, store_sem.at[0])]
    stores[0].start()
    for first in range(0, width, chunk):
        size = min(chunk, width - first)
        store_rows(
            g_fc, first, dot_tn(h_second[:, first : first + size], dpre[...]), at=FC_POSITION
        )
        if first + size == 4 * chunk:
            reduce.third()
    stores.append(pltpu.make_async_copy(g_fc, grad_fc, store_sem.at[1]))
    stores[1].start()

    def one_made(step, carry):
        at = pl.ds(pl.multiple_of(step * span, span), span)
        value = low(jnp.dot(act[at, :], w_proj[...], preferred_element_type=jnp.float32))
        made_part[2 * step] = value[:count]
        made_part[2 * step + 1] = value[count:]
        return carry

    lax.fori_loop(0, MEMBERS // 2, one_made, 0)
    stores.append(pltpu.make_async_copy(made_part, made, store_sem.at[2]))
    stores[2].start()
    dh = reduce.result()
    center = resid_own[...] - jnp.mean(resid_own[...], -1, keepdims=True)
    scale = lax.rsqrt(jnp.mean(center * center, -1, keepdims=True) + epsilon_norm)
    hat = center * scale
    back_own = wide(back[pl.ds(pl.multiple_of(p.me * count, count), count), :])
    scaled = dh * vecs[18:19, :]
    inner = jnp.mean(scaled * hat, -1, keepdims=True)
    value = back_own + (scaled - jnp.mean(scaled, -1, keepdims=True) - hat * inner) * scale
    dresid[...] = value
    branch = low(value)
    dbranch[...] = branch
    sums[0:1, :] = jnp.sum(dh * hat, 0, keepdims=True)
    sums[1:2, :] = jnp.sum(dh, 0, keepdims=True)
    sums[2:3, :] = jnp.sum(wide(branch), 0, keepdims=True)
    sums[3:4, :] = jnp.sum(back_own, 0, keepdims=True)
    sums[4:8, :] = jnp.zeros((4, width), jnp.float32)
    reduce.sent()
    for copy in stores:
        copy.wait()


def middle(h_second, back_all, vecs, resid_own, w_fc, w_proj):
    kind, high = jnp.bfloat16, jnp.float32
    length, width = h_second.shape
    rows = length // MEMBERS
    hidden = w_proj.shape[0]
    four = width // MEMBERS
    any_space = pl.BlockSpec(memory_space=pl.ANY)
    vmem = pl.BlockSpec(memory_space=pltpu.VMEM)
    dma = pltpu.SemaphoreType.DMA

    def like(*shape, dtype=kind):
        return jax.ShapeDtypeStruct(shape, dtype)

    def buffer(*shape, dtype=kind):
        return pltpu.VMEM(shape, dtype)

    return pl.pallas_call(
        middle_kernel,
        out_shape=[
            like(DEVICES, four // 4, hidden),
            like(GROUPS, four, width),
            like(MEMBERS, rows, width),
            like(rows, width, dtype=high),
            like(rows, width),
            like(8, width, dtype=high),
            like(1, hidden, dtype=high),
        ],
        in_specs=[any_space] * 2 + [vmem] * 2 + [any_space] * 2,
        out_specs=[any_space] * 3 + [vmem] * 4,
        scratch_shapes=[
            buffer(*h_second.shape),
            buffer(*back_all.shape),
            buffer(*w_fc.shape),
            buffer(*w_proj.shape),
            buffer(length, hidden),
            buffer(length, hidden),
            buffer(MEMBERS, rows, width),
            buffer(MEMBERS, rows, width),
            buffer(DEVICES, four // 4, hidden),
            buffer(GROUPS, four, width),
        ]
        + reduce_buffers(rows, width)
        + [dma((4,)), dma((3,))],
        compiler_params=pltpu.CompilerParams(
            collective_id=3, has_side_effects=True, vmem_limit_bytes=VMEM_BYTES
        ),
        name="middle",
    )(h_second, back_all, vecs, resid_own, w_fc, w_proj)


class Fold:
    def __init__(self, place, away, kept, landing, leaving, last, sems, first):
        p = place
        self.p, self.away, self.kept, self.landing = p, away, kept, landing
        self.leaving, self.last = leaving, last
        self.to_far, self.to_y = p.target(far=1 - p.far), p.target(y=1 - p.y)
        self.sems, self.first = sems, first

    def begin(self):
        other = 1 - self.p.far
        self.a = remote(
            self.away(other), self.landing(other), self.sems, self.first, self.to_y
        )
        self.a.start()

    def rest(self):
        far = self.p.far
        self.b = remote(
            self.away(far), self.landing(far), self.sems, self.first + 1, self.to_y
        )
        self.b.start()

    def middle(self):
        other = 1 - self.p.far
        self.a.wait_recv()
        self.leaving[...] = low(wide(self.kept(other)[...]) + wide(self.landing(other)[...]))
        self.c = remote(self.leaving, self.last, self.sems, self.first + 2, self.to_far)
        self.c.start()

    def end(self):
        far = self.p.far
        self.b.wait_recv()
        partial = wide(self.kept(far)[...]) + wide(self.landing(far)[...])
        self.c.wait_recv()
        return low(partial + wide(self.last[...]))

    def sent(self):
        for item in (self.a, self.b, self.c):
            item.wait_send()


def backward_kernel(
    dbranch, made_in, grad_fc, grad_proj, attn, qkv, row_pos, col_pos, w_heads, w_qkv_in,
    h_in, x_own, resid_own, dresid, vecs, sums, fc_sums,
    out_home, grad_home, qkv_back, fc_back, rows_back, vec_back,
    branch_all, dattn, dqkv, key_sum, value_sum, w_qkv, h_first, made, dh_part,
    fc_own, proj_own, g_qkv, g_heads, g_out, result, input_grad, vec_rows, vec_go, vec_got,
    fc_y, proj_y, qkv_y, out_y, fc_go, proj_go, qkv_go, out_go,
    fc_far, proj_far, qkv_far, out_far, fc_sum, proj_sum, qkv_sum, out_sum,
    core_a, two_a, got_a, last_a, done_a, sem_a, core_b, two_b, got_b, last_b, done_b, sem_b,
    load_sem, branch_sem, fold_sem, tree_sem, vec_sem, home_sem,
    qkv_send, qkv_recv, fc_send, fc_recv, rows_send, rows_recv,
):
    p = Place()
    count, width = dbranch.shape
    length = MEMBERS * count
    four = grad_proj.shape[1]
    pairs = SLOTS // 2
    per_part = SLOTS * HD
    loads = []

    def load(source, target):
        copy = pltpu.make_async_copy(source, target, load_sem.at[len(loads)])
        copy.start()
        loads.append(copy)

    for far in range(2):
        load(grad_proj.at[2 * p.y + far], proj_own.at[far])
        for near in range(2):
            load(grad_fc.at[far, p.y, near], fc_own.at[far, near])
    load(half_of(made_in, p.core), made)
    load(w_qkv_in, w_qkv)
    load(h_in, h_first)
    greet_all(p)
    gather = Gather(p, branch_all, branch_sem)
    for name, index, target in (
        ("a", 0, gather.first), ("b", 1, gather.second), ("c", 2, gather.other),
    ):
        copy = remote(dbranch, branch_all.at[p.me], branch_sem, index, target)
        copy.start()
        gather.copies[name] = copy
    load(dbranch, branch_all.at[p.me])
    proj_fold = Fold(
        p, lambda far: grad_proj.at[2 * (1 - p.y) + far], lambda far: proj_own.at[far],
        lambda far: proj_y.at[far], proj_go, proj_far, fold_sem, 0,
    )
    fc_folds = [
        Fold(
            p, lambda far, near=near: grad_fc.at[far, 1 - p.y, near],
            lambda far, near=near: fc_own.at[far, near],
            lambda far, near=near: fc_y.at[far, near],
            fc_go.at[near], fc_far.at[near], fold_sem, 3 + 3 * near,
        )
        for near in range(2)
    ]
    qkv_folds = [
        Fold(
            p, lambda far, near=near: g_qkv.at[4 * far + 2 * near + 1 - p.y],
            lambda far, near=near: g_qkv.at[4 * far + 2 * near + p.y],
            lambda far, near=near: qkv_y.at[far, near],
            qkv_go.at[near], qkv_far.at[near], fold_sem, 9 + 3 * near,
        )
        for near in range(2)
    ]
    proj_fold.begin()
    for item in fc_folds:
        item.begin()
    gather.second_hop()
    gather.third_hop()
    gather.last_hop()
    for copy in loads:
        copy.wait()
    proj_fold.middle()
    gather.finish()
    span = 2 * count

    def one_dattn(step, carry):
        at = pl.ds(pl.multiple_of(step * span, span), span)
        grad = jnp.concatenate([branch_all[2 * step], branch_all[2 * step + 1]], 0)
        value = low(dot_nt(grad, w_heads[...]))
        for pair in range(pairs):
            dattn[pair, at, :] = value[:, 128 * pair : 128 * pair + 128]
        return carry

    lax.fori_loop(0, length // span, one_dattn, 0)
    reduce_made = Reduce(
        p, half_of(made_in, 1 - p.core), made, core_a, two_a, got_a, last_a, done_a, sem_a
    )
    reduce_made.begin()
    proj_fold.rest()

    def one_pair(pair):
        key_sum[...] = jnp.zeros_like(key_sum)
        value_sum[...] = jnp.zeros_like(value_sum)

        def columns(part):
            return slice(128 * (pairs * part + pair), 128 * (pairs * part + pair) + 128)

        def one_block(step, carry):
            at = pl.ds(pl.multiple_of(step * span, span), span)
            query, grad = qkv[at, columns(0)], dattn[pair, at, :]
            keys, values = qkv[:, columns(1)], qkv[:, columns(2)]
            lanes = lane_of(query.shape)
            total = jnp.zeros(query.shape, jnp.float32)
            add_keys = add_values = 0.0
            for head in range(2):
                mine = lanes == head
                own = jnp.where(mine, query, jnp.zeros_like(query))
                own_grad = jnp.where(mine, grad, jnp.zeros_like(grad))
                probs = probabilities(own, keys, row_pos[at, :], col_pos[...])
                dprobs = dot_nt(own_grad, values)
                delta = jnp.sum(probs * dprobs, -1, keepdims=True)
                dscores = low(probs * (dprobs - delta))
                mixed = jnp.dot(dscores, keys, preferred_element_type=jnp.float32)
                total = jnp.where(mine, mixed, total)
                add_keys = add_keys + dot_tn(dscores, own)
                add_values = add_values + dot_tn(low(probs), own_grad)
            dqkv[at, columns(0)] = low(total * 0.125)
            key_sum[...] += add_keys
            value_sum[...] += add_values
            return carry

        lax.fori_loop(0, length // span, one_block, 0)
        dqkv[:, columns(1)] = low(key_sum[...] * 0.125)
        dqkv[:, columns(2)] = low(value_sum[...])

    one_pair(0)
    for item in fc_folds:
        item.middle()
    for item in fc_folds:
        item.rest()
    reduce_made.second()
    one_pair(1)
    reduce_made.third()
    for part in range(3):
        last = 128 * (pairs * part + pairs - 1)
        value = dqkv[:, last : last + 128]
        keep = jnp.logical_or(lane_of(value.shape) == 0, p.me == MEMBERS - 1)
        dqkv[:, last : last + 128] = jnp.where(keep, value, jnp.zeros_like(value))

    def one_part(step, carry):
        at = pl.ds(pl.multiple_of(step * span, span), span)
        value = low(dot_nt(dqkv[at, :], w_qkv[...]))
        dh_part[2 * step] = value[:count]
        dh_part[2 * step + 1] = value[count:]
        return carry

    lax.fori_loop(0, length // span, one_part, 0)
    reduce_dh = Reduce(
        p, half_of(dh_part, 1 - p.core), half_of(dh_part, p.core), core_b, two_b, got_b, last_b,
        done_b, sem_b,
    )
    reduce_dh.begin()
    chunk = 256
    for first in range(0, width, chunk):
        size = min(chunk, width - first)
        store_rows(g_qkv, first, dot_tn(h_first[:, first : first + size], dqkv[...]))
    for item in qkv_folds:
        item.begin()
    for item in qkv_folds:
        item.rest()
    reduce_dh.second()
    proj_sum[...] = proj_fold.end()
    target, part = shard_of(PROJ_FIRST + lookup(PROJ_UNIT, p.linear))
    moves = [
        Move(p, proj_sum, rows_back.at[part], rows_send.at[0], rows_recv.at[part], target)
    ]
    for pair in range(pairs):
        total = 0.0
        for block in range(MEMBERS):
            at = slice(block * count, block * count + count)
            total = total + dot_tn(attn[pair, at, :], branch_all[block])
        g_heads[128 * pair : 128 * pair + 128, :] = total
    g_out[...] = low(g_heads[pl.ds(pl.multiple_of(head_rows(p.me), 8), four), :])
    root_y = out_root(p.me)
    same_y = p.y == root_y
    root = jnp.logical_and(same_y, p.far == 0)
    beside = jnp.logical_and(same_y, p.far == 1)
    over_y = remote(g_out, out_y, tree_sem, 0, p.target(y=1 - p.y))
    over_far = remote(out_go, out_far, tree_sem, 1, p.target(far=1 - p.far))

    @pl.when(jnp.logical_not(same_y))
    def _():
        over_y.start()

    reduce_dh.third()
    result[...] = low(resid_own[...] + reduce_made.result() + vecs[33:34, :])
    home = p.target(
        x=p.ctx % 2, near=p.ctx // 2 % 2, core=p.ctx // 4, y=p.fsdp // 2, far=p.fsdp % 2
    )
    moves.append(Move(p, result, out_home, home_sem.at[0, 0], home_sem.at[1, 0], home))

    for near in range(2):
        fc_sum[near] = fc_folds[near].end()
        for slot in range(4):
            target, part = shard_of(FC_FIRST + fc_unit(p.far, p.y, 4 * near + slot))
            moves.append(
                Move(
                    p, fc_sum.at[near, slot], fc_back.at[part, p.me],
                    fc_send.at[near, slot], fc_recv.at[part, p.me], target,
                )
            )

    @pl.when(same_y)
    def _():
        over_y.wait_recv()

    @pl.when(beside)
    def _():
        out_go[...] = low(wide(g_out[...]) + wide(out_y[...]))
        over_far.start()

    dh = reduce_dh.result()
    x = wide(x_own[...])
    center = x - jnp.mean(x, -1, keepdims=True)
    scale = lax.rsqrt(jnp.mean(center * center, -1, keepdims=True) + epsilon_norm)
    hat = center * scale
    scaled = dh * vecs[0:1, :]
    inner = jnp.mean(scaled * hat, -1, keepdims=True)
    value = (scaled - jnp.mean(scaled, -1, keepdims=True) - hat * inner) * scale
    input_grad[...] = low(dresid[...] + value)
    moves.append(Move(p, input_grad, grad_home, home_sem.at[0, 1], home_sem.at[1, 1], home))
    bias_sums = jnp.sum(wide(dqkv[...]), 0, keepdims=True)

    def placed(value, starts, me):
        total = jnp.zeros((1, width), jnp.float32)
        for index, start in enumerate(starts):
            parts = [value]
            if start:
                parts.insert(0, jnp.zeros((1, start), jnp.float32))
            after = width - start - value.shape[1]
            if after:
                parts.append(jnp.zeros((1, after), jnp.float32))
            row = jnp.concatenate(parts, 1) if len(parts) > 1 else value
            total = total + jnp.where(me == index, row, 0.0)
        return total

    heads = [head_start(member) * HD for member in range(MEMBERS)]
    vec_rows[0:1, :] = jnp.sum(dh * hat, 0, keepdims=True)
    vec_rows[1:2, :] = jnp.sum(dh, 0, keepdims=True)
    vec_rows[2:3, :] = placed(bias_sums[:, :per_part], heads, p.me)
    vec_rows[3:4, :] = placed(bias_sums[:, 2 * per_part :], heads, p.me)
    vec_rows[4:5, :] = sums[2:3, :]
    vec_rows[5:7, :] = sums[0:2, :]
    vec_rows[7:8, :] = sums[3:4, :]
    used = width // MEMBERS
    vec_go[...] = jnp.zeros_like(vec_go)
    for f in range(GROUPS):
        for c in range(MEMBERS):
            vec_go[MEMBERS * f + c, 0:3, 0:used] = vec_rows[
                3 * f : 3 * f + 3, used * c : used * c + used
            ]
    for unit, (holder, which) in HOLDER.items():
        f, row = divmod(8 + unit // MEMBERS, 3)
        value = fc_sums[:, used * which : used * which + used]
        vec_go[MEMBERS * f + unit % MEMBERS, row : row + 1, 0:used] = jnp.where(
            p.me == holder, value, 0.0
        )

    def vec_send(step, carry):
        other = (p.linear + step) % DEVICES
        pltpu.make_async_remote_copy(
            src_ref=vec_go.at[other],
            dst_ref=vec_got.at[p.linear],
            send_sem=vec_sem.at[0],
            recv_sem=vec_sem.at[1],
            device_id=(other // MEMBERS, other % MEMBERS),
            device_id_type=MESH,
        ).start()
        return carry

    lax.fori_loop(1, DEVICES, vec_send, 0)
    pltpu.make_async_copy(vec_go.at[p.linear], vec_got.at[p.linear], vec_sem.at[1]).start()
    for item in qkv_folds:
        item.middle()
    @pl.when(root)
    def _():
        over_far.wait_recv()
        out_sum[...] = low(wide(g_out[...]) + wide(out_y[...]) + wide(out_far[...]))

    target, part = shard_of(OUT_FIRST + p.me)
    moves.append(
        Move(p, out_sum, rows_back.at[part], rows_send.at[1], rows_recv.at[part], target, root)
    )
    for near in range(2):
        qkv_sum[near] = qkv_folds[near].end()
        target = (0 * p.fsdp, 4 * p.far + 2 * near + p.y)
        moves.append(
            Move(
                p, qkv_sum.at[near], qkv_back.at[p.me], qkv_send.at[near], qkv_recv.at[p.me],
                target,
            )
        )
    arrived(vec_got, vec_sem.at[1])
    vec_back[...] = jnp.sum(vec_got[...], 0)

    @pl.when(p.fsdp == 0)
    def _():
        for member in range(MEMBERS):
            arrived(qkv_back.at[member], qkv_recv.at[member])

    for part in range(3):
        third = 3 * p.linear + part
        is_fc = jnp.logical_and(third >= FC_FIRST, third < PROJ_FIRST)
        is_rows = jnp.logical_and(third >= OUT_FIRST, jnp.logical_not(is_fc))

        @pl.when(is_fc)
        def _(part=part):
            for member in range(MEMBERS):
                arrived(fc_back.at[part, member], fc_recv.at[part, member])

        @pl.when(is_rows)
        def _(part=part):
            arrived(rows_back.at[part], rows_recv.at[part])

    arrived(out_home, home_sem.at[1, 0])
    arrived(grad_home, home_sem.at[1, 1])
    arrived(vec_got.at[pl.ds(1, DEVICES - 1)], vec_sem.at[0])
    for item in [proj_fold, reduce_made, reduce_dh] + fc_folds + qkv_folds + moves:
        item.sent()

    @pl.when(jnp.logical_not(same_y))
    def _():
        over_y.wait_send()

    @pl.when(beside)
    def _():
        over_far.wait_send()


def backward(
    dbranch, made, grad_fc, grad_proj, attn, qkv, row_pos, col_pos, w_heads, w_qkv,
    h_first, x_own, resid_own, dresid, vecs, sums, fc_sums,
):
    kind, high = jnp.bfloat16, jnp.float32
    rows, width = dbranch.shape
    length = MEMBERS * rows
    four, cols = width // MEMBERS, qkv.shape[1]
    unit, hidden = four // 4, fc_sums.shape[1]
    per_part = SLOTS * HD
    any_space = pl.BlockSpec(memory_space=pl.ANY)
    vmem = pl.BlockSpec(memory_space=pltpu.VMEM)
    dma = pltpu.SemaphoreType.DMA

    def like(*shape, dtype=kind):
        return jax.ShapeDtypeStruct(shape, dtype)

    def buffer(*shape, dtype=kind):
        return pltpu.VMEM(shape, dtype)

    used = -(-width // MEMBERS // 128) * 128
    return pl.pallas_call(
        backward_kernel,
        out_shape=[
            like(rows, width),
            like(rows, width),
            like(MEMBERS, four, cols),
            like(3, MEMBERS, unit, hidden),
            like(3, four, width),
            like(8, used, dtype=high),
        ],
        in_specs=[vmem] + [any_space] * 3 + [vmem] * 5 + [any_space] * 2 + [vmem] * 6,
        out_specs=[any_space] * 5 + [vmem],
        scratch_shapes=[
            buffer(MEMBERS, rows, width),
            buffer(SLOTS // 2, length, 2 * HD),
            buffer(length, cols),
            buffer(length, 2 * HD, dtype=high),
            buffer(length, 2 * HD, dtype=high),
            buffer(*w_qkv.shape),
            buffer(*h_first.shape),
            buffer(MEMBERS // 2, rows, width),
            buffer(MEMBERS, rows, width),
            buffer(2, 2, 4, unit, hidden),
            buffer(2, four, width),
            buffer(MEMBERS, four, cols),
            buffer(per_part, width, dtype=high),
            buffer(four, width),
            buffer(rows, width),
            buffer(rows, width),
            buffer(16, width, dtype=high),
            buffer(DEVICES, 8, used, dtype=high),
            buffer(DEVICES, 8, used, dtype=high),
        ]
        + [
            buffer(2, 2, 4, unit, hidden), buffer(2, four, width), buffer(2, 2, four, cols),
            buffer(four, width),
        ]
        + [
            buffer(2, 4, unit, hidden), buffer(four, width), buffer(2, four, cols),
            buffer(four, width),
        ]
        * 2
        + [
            buffer(2, 4, unit, hidden), buffer(four, width), buffer(2, four, cols),
            buffer(four, width),
        ]
        + reduce_buffers(rows, width)
        + reduce_buffers(rows, width)
        + [
            dma((12,)),
            dma((2, 7)),
            dma((2, 15)),
            dma((2, 2)),
            dma((2,)),
            dma((2, 2)),
            dma((2,)),
            dma((8,)),
            dma((2, 4)),
            dma((3, 8)),
            dma((2,)),
            dma((3,)),
        ],
        compiler_params=pltpu.CompilerParams(
            collective_id=2, has_side_effects=True, vmem_limit_bytes=VMEM_BYTES
        ),
        name="backward",
    )(
        dbranch, made, grad_fc, grad_proj, attn, qkv, row_pos, col_pos, w_heads, w_qkv,
        h_first, x_own, resid_own, dresid, vecs, sums, fc_sums,
    )


def lane_of(shape):
    return lax.broadcasted_iota(jnp.int32, shape, 1) // HD


def dot_nt(a, b):
    return lax.dot_general(a, b, (((1,), (1,)), ((), ())), preferred_element_type=jnp.float32)


def dot_tn(a, b):
    return lax.dot_general(a, b, (((0,), (0,)), ((), ())), preferred_element_type=jnp.float32)


def probabilities(query, keys, row_pos, col_pos):
    scores = dot_nt(query, keys) * 0.125
    scores = jnp.where(col_pos <= row_pos, scores, -1e30)
    weights = jnp.exp(scores - jnp.max(scores, -1, keepdims=True))
    return weights / jnp.sum(weights, -1, keepdims=True)


def head_place(head):
    member = max(m for m in range(MEMBERS) if head_start(m) <= head)
    return member, head - head_start(member)


def unlay_qkv(flat, tiles, back):
    count = back.shape[1] // 2
    for member in range(MEMBERS):
        for tile in range(back.shape[2] // 128):
            tiles[member * (back.shape[2] // 128) + tile] = wide(
                back[member, :, 128 * tile : 128 * tile + 128]
            )
    halves = 3 * HEADS

    def half(index, lane):
        odd, at = divmod(index, halves)
        part, head = divmod(at, HEADS)
        member, slot = head_place(head)
        col = 64 * (SLOTS * part + slot)
        tile = member * (back.shape[2] // 128) + col // 128
        return piece(
            lambda _: tiles[tile, pl.ds(odd, count, stride=2), :], col % 128, lane, HD
        )

    for row in range(halves):
        flat[pl.ds(row, count, stride=halves), :] = join(
            [(0, half(2 * row, 0)), (HD, half(2 * row + 1, HD))]
        )


def unlay_fc(flat, first, tiles, back, part):
    count, hidden = back.shape[-2:]
    each = -(-hidden // 128)
    for member in range(MEMBERS):
        for tile in range(each):
            size = min(128, hidden - 128 * tile)
            tiles[member * each + tile, :count, :size] = wide(
                back[part, member, :, 128 * tile : 128 * tile + size]
            )
    stride, block = FF // 128, hidden // GROUPS
    for row in range(stride):
        parts, col = [], 128 * row
        while col < 128 * row + 128:
            unit, inside = divmod(col, block)
            size = min(block - inside, 128 * row + 128 - col)
            member, which = HOLDER[unit]
            lane = col - 128 * row
            value = piece(
                lambda t, m=member: tiles[m * each + t, :count, :],
                block * which + inside, lane, size,
            )
            parts.append((lane, value))
            col += size
        flat[pl.ds(first + row, count, stride=stride), :] = join(parts)


def unlay_rows(flat, first, tiles, back, part):
    count, width = back.shape[1] // 2, back.shape[2]
    for tile in range(-(-width // 128)):
        size = min(128, width - 128 * tile)
        tiles[tile, :, :size] = wide(back[part, :, 128 * tile : 128 * tile + size])
    halves = width // HD

    def half(index, lane):
        odd, at = divmod(index, halves)
        return piece(
            lambda t: tiles[t, pl.ds(odd, count, stride=2), :], HD * at, lane, HD
        )

    for row in range(halves):
        flat[pl.ds(first + row, count, stride=halves), :] = join(
            [(0, half(2 * row, 0)), (HD, half(2 * row + 1, HD))]
        )


def update_kernel(
    qkv_in, fc_in, rows_in, weights, first, second, moment, squares, new,
    flat, tiles, qkv_back, fc_back, rows_back, sem,
):
    step = pl.program_id(0)
    linear = lax.axis_index("fsdp") * MEMBERS + lax.axis_index("ctx")

    @pl.when(step == 0)
    def _():
        @pl.when(linear < MEMBERS)
        def _():
            copy = pltpu.make_async_copy(qkv_in, qkv_back, sem.at[0])
            copy.start()
            copy.wait()
            unlay_qkv(flat, tiles, qkv_back)

        @pl.when(linear >= MEMBERS)
        def _():
            copies = [
                pltpu.make_async_copy(fc_in, fc_back, sem.at[0]),
                pltpu.make_async_copy(rows_in, rows_back, sem.at[1]),
            ]
            for copy in copies:
                copy.start()
            for copy in copies:
                copy.wait()
            third_rows = fc_back.shape[2] * FF // 128
            for part in range(3):
                third = 3 * linear + part
                is_fc = jnp.logical_and(third >= FC_FIRST, third < PROJ_FIRST)

                @pl.when(is_fc)
                def _(part=part):
                    unlay_fc(flat, part * third_rows, tiles, fc_back, part)

                @pl.when(jnp.logical_not(is_fc))
                def _(part=part):
                    unlay_rows(flat, part * third_rows, tiles, rows_back, part)

    size = weights.shape[0]
    grad = flat[pl.ds(pl.multiple_of(step * size, 8), size), :]
    result = adamw(weights[...], grad, first[...], second[...], rate_matrix, weight_decay)
    moment[...], squares[...], new[...] = result


def update(qkv_back, fc_back, rows_back, weights, first, second):
    high = jnp.float32
    local = weights.shape[0]
    steps = 10
    size = -(-local // (16 * steps)) * 16
    block = pl.BlockSpec((size, 128), lambda i: (i, 0))
    any_space = pl.BlockSpec(memory_space=pl.ANY)
    kind = jax.ShapeDtypeStruct((local, 128), high)
    tile_count = max(qkv_back.shape[0] * qkv_back.shape[2] // 128, MEMBERS * 7)
    return pl.pallas_call(
        update_kernel,
        grid=(steps,),
        in_specs=[any_space] * 3 + [block] * 3,
        out_specs=[block] * 3,
        out_shape=[kind] * 3,
        scratch_shapes=[
            pltpu.VMEM((size * steps, 128), high),
            pltpu.VMEM((tile_count, qkv_back.shape[1], 128), high),
            pltpu.VMEM(qkv_back.shape, qkv_back.dtype),
            pltpu.VMEM(fc_back.shape, fc_back.dtype),
            pltpu.VMEM(rows_back.shape, rows_back.dtype),
            pltpu.SemaphoreType.DMA((2,)),
        ],
        compiler_params=pltpu.CompilerParams(vmem_limit_bytes=VMEM_BYTES),
        name="update",
    )(qkv_back, fc_back, rows_back, weights, first, second)


def per_device_groups(
    inputs, cotangent, slot_order, weights, vectors, first_w, second_w, first_vec, second_vec
):
    seqs, rows, width = inputs.shape
    length = rows * MEMBERS
    order = jnp.pad(slot_order, ((0, 127), (0, 128 - slot_order.shape[1])))
    vec_rows, vec_cols = vectors.shape
    padded = jnp.pad(vectors, ((0, 16 - vec_rows), (0, -vec_cols % 128)))
    (
        back_all, vecs, row_pos, col_pos, own_qkv, h_first, qkv, attn, own_fc, own_proj, w_heads,
        x_own, resid_own, h_second,
    ) = forward(
        inputs.reshape(rows, width), cotangent.reshape(rows, width), order, padded, weights
    )
    grad_fc, grad_proj, made, dresid, dbranch, sums, fc_sums = middle(
        h_second.reshape(length, width), back_all.reshape(length, width), vecs, resid_own,
        own_fc, own_proj,
    )
    outputs, input_grad, qkv_back, fc_back, rows_back, vec_back = backward(
        dbranch, made, grad_fc.reshape((2, 2, 2, 4) + grad_fc.shape[1:]), grad_proj, attn, qkv,
        row_pos, col_pos, w_heads, own_qkv, h_first, x_own, resid_own, dresid, vecs, sums,
        fc_sums,
    )
    outputs = outputs.reshape(seqs, rows, width)
    input_grad = input_grad.reshape(seqs, rows, width)
    new_w = update(qkv_back, fc_back, rows_back, weights, first_w, second_w)
    owned_vec = vec_back[:vec_rows, :vec_cols]
    new_vec = adamw(vectors, owned_vec, first_vec, second_vec, rate_vector, 0.0)
    return (outputs, input_grad, new_w[0], new_w[1], new_w[2], new_vec[0], new_vec[1], new_vec[2])


def solution(mesh):
    in_specs = (
        P("fsdp", "ctx", None),
        P("fsdp", "ctx", None),
        P("fsdp", None),
        P(("fsdp", "ctx"), None),
        P("fsdp", "ctx"),
        P(("fsdp", "ctx"), None),
        P(("fsdp", "ctx"), None),
        P("fsdp", "ctx"),
        P("fsdp", "ctx"),
    )
    out_specs = (
        P("fsdp", "ctx", None),
        P("fsdp", "ctx", None),
        P(("fsdp", "ctx"), None),
        P(("fsdp", "ctx"), None),
        P(("fsdp", "ctx"), None),
        P("fsdp", "ctx"),
        P("fsdp", "ctx"),
        P("fsdp", "ctx"),
    )
    per_device = per_device_groups if mesh.shape["ctx"] == MEMBERS else per_device_ring
    return jax.shard_map(
        per_device, mesh=mesh, in_specs=in_specs, out_specs=out_specs, check_vma=False
    )
```

```python
import jax
import jax.numpy as jnp
from jax import lax
from jax.experimental import pallas as pl
from jax.experimental.pallas import tpu as pltpu
from jax.sharding import PartitionSpec as P

HEADS = 25
HD = 64
FF = 6400
STEP = 10


epsilon_norm = 1e-05
beta_first = 0.9
beta_second = 0.999
epsilon_adam = 1e-08
weight_decay = 0.1
rate_matrix = 0.1
rate_vector = 0.8


def shifted(value, axis, steps):
    count = lax.axis_size(axis)
    pairs = [(source, (source + steps) % count) for source in range(count)]
    return lax.ppermute(value, axis, pairs)


def layer_norm(value, gain, shift):
    center = value - jnp.mean(value, -1, keepdims=True)
    spread = jnp.mean(center * center, -1, keepdims=True)
    return center * lax.rsqrt(spread + epsilon_norm) * gain + shift


def gelu_tanh(value):
    return jax.nn.gelu(value, approximate=True)


def key_positions(slot_order, first_slot, slots, block):
    groups = lax.dynamic_slice_in_dim(slot_order, first_slot, slots, 1)
    offsets = jnp.arange(block, dtype=jnp.int32)
    return (groups[:, :, None] * block + offsets).reshape(slot_order.shape[0], slots * block)


def unpack_flat(flat, width, hidden):
    flat = flat.reshape(-1)
    first_end = 3 * width * width
    second_end = 4 * width * width
    third_end = 4 * width * width + width * hidden
    return (
        flat[:first_end].reshape(width, 3 * width),
        flat[first_end:second_end].reshape(width, width),
        flat[second_end:third_end].reshape(width, hidden),
        flat[third_end:].reshape(hidden, width),
    )


def gather_params(weights, vectors):
    local = weights.reshape(1, weights.shape[0], weights.shape[1])
    part = (
        lax.all_gather(local, "fsdp", axis=0, tiled=True),
        lax.all_gather(vectors, "fsdp", axis=0, tiled=True),
    )
    return (
        lax.all_gather(part[0], "ctx", axis=1, tiled=True),
        lax.all_gather(part[1], "ctx", axis=1, tiled=True),
    )


def reduce_grads(grad_flat, grad_vec):
    part = (
        lax.psum_scatter(
            grad_flat.astype(jnp.bfloat16), "fsdp", scatter_dimension=0, tiled=True
        ).astype(jnp.float32),
        lax.psum_scatter(
            grad_vec.astype(jnp.bfloat16), "fsdp", scatter_dimension=0, tiled=True
        ).astype(jnp.float32),
    )
    return (
        lax.psum_scatter(
            part[0].astype(jnp.bfloat16), "ctx", scatter_dimension=1, tiled=True
        ).astype(jnp.float32),
        lax.psum_scatter(
            part[1].astype(jnp.bfloat16), "ctx", scatter_dimension=1, tiled=True
        ).astype(jnp.float32),
    )


def pass_grads(grad_pairs):
    return shifted(grad_pairs.astype(jnp.bfloat16), "ctx", 1).astype(grad_pairs.dtype)


def adamw(weight, grad, first, second, rate, decay):
    first = beta_first * first + (1.0 - beta_first) * grad
    second = beta_second * second + (1.0 - beta_second) * grad * grad
    first_hat = first / (1.0 - beta_first**STEP)
    second_hat = second / (1.0 - beta_second**STEP)
    weight = weight.astype(jnp.float32)
    updated = weight - rate * (first_hat / (jnp.sqrt(second_hat) + epsilon_adam) + decay * weight)
    return (first, second, updated)


def per_device_ring(
    inputs, cotangent, slot_order, weights, vectors, first_w, second_w, first_vec, second_vec
):
    seqs, rows, width = inputs.shape
    tokens = seqs * rows
    block = rows // 2
    cycle = lax.axis_size("ctx")
    shards = lax.axis_size("fsdp")
    me = lax.axis_index("ctx")
    full_flat, full_vec = gather_params(weights, vectors)
    full_qkv, full_out, full_fc, full_proj = unpack_flat(full_flat, width, FF)
    vec = full_vec.astype(jnp.float32)
    bias_fc = vec[8:].reshape(-1)
    x_in = inputs.reshape(tokens, width).astype(jnp.float32)
    h_first, pull_first = jax.vjp(layer_norm, x_in, vec[0], vec[1])
    h_first_b = h_first.astype(jnp.bfloat16)
    zero_row = jnp.zeros((width,), jnp.float32)
    qkv = jnp.dot(h_first_b, full_qkv, preferred_element_type=jnp.float32)
    qkv_b = (qkv + jnp.concatenate([vec[2], zero_row, vec[3]])).astype(jnp.bfloat16)
    query_heads = qkv_b[:, :width].reshape(seqs, rows, HEADS, HD)
    key_value = qkv_b[:, width:].reshape(seqs, rows, 2, width)
    query_pos = key_positions(slot_order, 2 * me, 2, block)

    def online(state, item):
        top, total, accum = state
        keys_i, values_i, pos_i = item
        scores = (
            jnp.einsum("sqhd,skhd->shqk", query_heads, keys_i, preferred_element_type=jnp.float32)
            * 0.125
        )
        allowed = pos_i[:, None, None, :] <= query_pos[:, None, :, None]
        scores = jnp.where(allowed, scores, -1e30)
        peak = jnp.maximum(top, jnp.max(scores, -1))
        weights_p = jnp.where(allowed, jnp.exp(scores - peak[..., None]), 0.0)
        factor = jnp.exp(top - peak)
        total = total * factor + jnp.sum(weights_p, -1)
        mixed = jnp.einsum(
            "shqk,skhd->sqhd",
            weights_p.astype(jnp.bfloat16),
            values_i,
            preferred_element_type=jnp.float32,
        )
        accum = accum * jnp.transpose(factor, (0, 2, 1))[..., None] + mixed
        return ((peak, total, accum), None)

    start_state = (
        jnp.full((seqs, HEADS, rows), -1e30, jnp.float32),
        jnp.zeros((seqs, HEADS, rows), jnp.float32),
        jnp.zeros((seqs, rows, HEADS, HD), jnp.float32),
    )
    state = start_state
    piece = lax.all_gather(key_value, "ctx", axis=1, tiled=True)
    count = piece.shape[1]
    turns = count // rows
    pos_all = key_positions(slot_order, jnp.int32(0) // block, count // block, block)
    stack = piece.reshape(seqs, turns, rows, 2, HEADS, HD).transpose(1, 0, 2, 3, 4, 5)
    pos_stack = pos_all.reshape(seqs, turns, rows).transpose(1, 0, 2)
    state, _ = lax.scan(online, state, (stack[:, :, :, 0], stack[:, :, :, 1], pos_stack))
    top, total, accum = state
    attn = accum / jnp.transpose(total, (0, 2, 1))[..., None]
    logsum = top + jnp.log(total)
    attn_b = attn.reshape(tokens, width).astype(jnp.bfloat16)
    resid = x_in + jnp.dot(attn_b, full_out, preferred_element_type=jnp.float32) + vec[4]
    h_second, pull_second = jax.vjp(layer_norm, resid, vec[5], vec[6])
    h_second_b = h_second.astype(jnp.bfloat16)
    pre = jnp.dot(h_second_b, full_fc, preferred_element_type=jnp.float32) + bias_fc
    act, pull_gelu = jax.vjp(gelu_tanh, pre)
    act_b = act.astype(jnp.bfloat16)
    result = resid + jnp.dot(act_b, full_proj, preferred_element_type=jnp.float32) + vec[7]
    outputs = result.astype(jnp.bfloat16).reshape(seqs, rows, width)
    back_b = cotangent.reshape(tokens, width)
    back = back_b.astype(jnp.float32)
    grad_proj = jnp.einsum("tf,td->fd", act_b, back_b, preferred_element_type=jnp.float32)
    grad_bp = jnp.sum(back, 0)
    dact = jnp.einsum("td,fd->tf", back_b, full_proj, preferred_element_type=jnp.float32)
    dpre_b = pull_gelu(dact)[0].astype(jnp.bfloat16)
    grad_fc = jnp.einsum("td,tf->df", h_second_b, dpre_b, preferred_element_type=jnp.float32)
    grad_bf = jnp.sum(dpre_b, 0, dtype=jnp.float32)
    dh_second = jnp.einsum("tf,df->td", dpre_b, full_fc, preferred_element_type=jnp.float32)
    dres_ln, grad_g2, grad_b2 = pull_second(dh_second)
    dresid = back + dres_ln
    dbranch_b = dresid.astype(jnp.bfloat16)
    grad_bo = jnp.sum(dbranch_b, 0, dtype=jnp.float32)
    grad_out = jnp.einsum("td,te->de", attn_b, dbranch_b, preferred_element_type=jnp.float32)
    dattn_b = jnp.einsum(
        "te,de->td", dbranch_b, full_out, preferred_element_type=jnp.float32
    ).astype(jnp.bfloat16)
    grad_heads = dattn_b.reshape(seqs, rows, HEADS, HD)
    delta = jnp.transpose(jnp.sum(grad_heads.astype(jnp.float32) * attn, -1), (0, 2, 1))

    def contribute(pair, source):
        pos_k = key_positions(slot_order, 2 * source, 2, block)
        key_h = pair[:, :, 0].reshape(seqs, rows, HEADS, HD)
        value_h = pair[:, :, 1].reshape(seqs, rows, HEADS, HD)
        scores = (
            jnp.einsum("sqhd,skhd->shqk", query_heads, key_h, preferred_element_type=jnp.float32)
            * 0.125
        )
        allowed = pos_k[:, None, None, :] <= query_pos[:, None, :, None]
        probs = jnp.where(allowed, jnp.exp(scores - logsum[..., None]), 0.0)
        dvalue = jnp.einsum(
            "shqk,sqhd->skhd",
            probs.astype(jnp.bfloat16),
            grad_heads,
            preferred_element_type=jnp.float32,
        )
        dprobs = jnp.einsum(
            "sqhd,skhd->shqk", grad_heads, value_h, preferred_element_type=jnp.float32
        )
        dscores = (probs * (dprobs - delta[..., None])).astype(jnp.bfloat16)
        dquery = (
            jnp.einsum("shqk,skhd->sqhd", dscores, key_h, preferred_element_type=jnp.float32)
            * 0.125
        )
        dkey = (
            jnp.einsum("shqk,sqhd->skhd", dscores, query_heads, preferred_element_type=jnp.float32)
            * 0.125
        )
        return (dquery, jnp.stack((dkey, dvalue), 2))

    dq_own, dkv_own = contribute(key_value, me)

    def turn(step, state):
        pair, dkv_acc, dq_acc = state
        pair = shifted(pair, "ctx", 1)
        dkv_acc = pass_grads(dkv_acc)
        source = (me - step) % cycle
        dq_part, dkv_part = contribute(pair, source)
        return (pair, dkv_acc + dkv_part, dq_acc + dq_part)

    final = lax.fori_loop(1, cycle, turn, (key_value, dkv_own, dq_own))
    dkv = pass_grads(final[1])
    dqkv_b = jnp.concatenate(
        [final[2].reshape(tokens, width), dkv.reshape(tokens, 2 * width)], 1
    ).astype(jnp.bfloat16)
    grad_qkv = jnp.einsum("td,te->de", h_first_b, dqkv_b, preferred_element_type=jnp.float32)
    bias_sums = jnp.sum(dqkv_b, 0, dtype=jnp.float32)
    dh_first = jnp.einsum("te,de->td", dqkv_b, full_qkv, preferred_element_type=jnp.float32)
    dx_ln, grad_g1, grad_b1 = pull_first(dh_first)
    input_grad = (dresid + dx_ln).astype(jnp.bfloat16).reshape(seqs, rows, width)
    grad_vec = jnp.concatenate(
        [
            jnp.stack(
                [
                    grad_g1,
                    grad_b1,
                    bias_sums[:width],
                    bias_sums[2 * width :],
                    grad_bo,
                    grad_g2,
                    grad_b2,
                    grad_bp,
                ]
            ),
            grad_bf.reshape(-1, width),
        ],
        0,
    )
    grad_flat = jnp.concatenate(
        [grad_qkv.reshape(-1), grad_out.reshape(-1), grad_fc.reshape(-1), grad_proj.reshape(-1)]
    ).reshape(shards, -1, 128)
    owned_flat, owned_vec = reduce_grads(grad_flat, grad_vec)
    owned_flat = owned_flat.reshape(weights.shape[0], 128)
    new_w = adamw(weights, owned_flat, first_w, second_w, rate_matrix, weight_decay)
    new_vec = adamw(vectors, owned_vec, first_vec, second_vec, rate_vector, 0.0)
    return (outputs, input_grad, new_w[0], new_w[1], new_w[2], new_vec[0], new_vec[1], new_vec[2])


MEMBERS = 8
GROUPS = 4
DEVICES = MEMBERS * GROUPS
MESH = pl.DeviceIdType.MESH
BLOCK = 64
SLOTS = 4
VMEM_BYTES = 60 * 1024 * 1024
OUT_FIRST = 24
FC_FIRST = 32
PROJ_FIRST = 64


def head_start(member):
    return HEADS * member // MEMBERS


class Place:
    def __init__(self):
        self.fsdp, self.ctx = lax.axis_index("fsdp"), lax.axis_index("ctx")
        self.x, self.core = self.fsdp // 2, self.fsdp % 2
        self.far, self.near, self.y = self.ctx // 4, self.ctx // 2 % 2, self.ctx % 2
        self.me = self.member()
        self.group = 2 * self.y + self.far
        self.linear = self.fsdp * MEMBERS + self.ctx

    def member(self, x=None, near=None, core=None):
        x = self.x if x is None else x
        near = self.near if near is None else near
        core = self.core if core is None else core
        return 4 * core + 2 * near + x

    def target(self, x=None, core=None, far=None, near=None, y=None):
        x = self.x if x is None else x
        near = self.near if near is None else near
        core = self.core if core is None else core
        far = self.far if far is None else far
        y = self.y if y is None else y
        return (2 * x + core, 4 * far + 2 * near + y)

    def is_me(self, target):
        return jnp.logical_and(target[0] == self.fsdp, target[1] == self.ctx)


def greet_all(place):
    barrier = pltpu.get_barrier_semaphore()

    def one(step, carry):
        other = (place.linear + step) % DEVICES
        pl.semaphore_signal(
            barrier, inc=1, device_id=(other // MEMBERS, other % MEMBERS), device_id_type=MESH
        )
        return carry

    lax.fori_loop(1, DEVICES, one, 0)
    pl.semaphore_wait(barrier, DEVICES - 1)


def greet(targets):
    barrier = pltpu.get_barrier_semaphore()
    for target in targets:
        pl.semaphore_signal(barrier, inc=1, device_id=target, device_id_type=MESH)
    pl.semaphore_wait(barrier, len(targets))


def remote(source, landing, sems, index, target):
    return pltpu.make_async_remote_copy(
        src_ref=source,
        dst_ref=landing,
        send_sem=sems.at[0, index],
        recv_sem=sems.at[1, index],
        device_id=target,
        device_id_type=MESH,
    )


def arrived(landing, sem):
    pltpu.make_async_copy(landing, landing, sem).wait()


class Move:
    def __init__(self, place, source, landing, send_sem, recv_sem, target, valid=None):
        here = place.is_me(target)
        away = jnp.logical_not(here)
        if valid is not None:
            here, away = jnp.logical_and(here, valid), jnp.logical_and(away, valid)
        self.away = away
        self.copy = pltpu.make_async_remote_copy(
            src_ref=source,
            dst_ref=landing,
            send_sem=send_sem,
            recv_sem=recv_sem,
            device_id=target,
            device_id_type=MESH,
        )

        @pl.when(here)
        def _():
            pltpu.make_async_copy(source, landing, recv_sem).start()

        @pl.when(away)
        def _():
            self.copy.start()

    def sent(self):
        @pl.when(self.away)
        def _():
            self.copy.wait_send()


class Gather:
    def __init__(self, place, out, sems, near_first=False):
        p = place
        step, turn = (0, 1) if near_first else (1 - p.core, p.core)
        x1, near1 = p.x + step * (1 - 2 * p.x), p.near + turn * (1 - 2 * p.near)
        x2, near2 = p.x + turn * (1 - 2 * p.x), p.near + step * (1 - 2 * p.near)
        self.out, self.sems, self.me = out, sems, p.me
        self.first = p.target(x=x1, near=near1)
        self.second = p.target(x=x2, near=near2)
        self.other = p.target(core=1 - p.core)
        self.of_first = p.member(x=x1, near=near1)
        self.of_second = p.member(x=x2, near=near2)
        self.of_both = p.member(x=1 - p.x, near=1 - p.near)
        self.copies = {}

    def _go(self, name, index, block, target):
        item = remote(self.out.at[block], self.out.at[block], self.sems, index, target)
        item.start()
        self.copies[name] = item

    def begin(self):
        self._go("a", 0, self.me, self.first)
        self._go("b", 1, self.me, self.second)
        self._go("c", 2, self.me, self.other)

    def second_hop(self):
        self.copies["a"].wait_recv()
        self._go("d", 3, self.of_first, self.second)
        self._go("e", 4, self.of_first, self.other)

    def third_hop(self):
        self.copies["b"].wait_recv()
        self._go("f", 5, self.of_second, self.other)

    def last_hop(self):
        self.copies["d"].wait_recv()
        self._go("g", 6, self.of_both, self.other)

    def finish(self):
        for name in "cefg":
            self.copies[name].wait_recv()
        for item in self.copies.values():
            item.wait_send()


class Spread:
    def __init__(self, place, at, sems, first):
        p = place
        self.at, self.sems, self.first = at, sems, first
        self.mine, self.theirs = at(p.far, p.y), at(1 - p.far, p.y)
        self.to_far, self.to_y = p.target(far=1 - p.far), p.target(y=1 - p.y)

    def begin(self):
        self.a = remote(self.mine, self.mine, self.sems, self.first, self.to_far)
        self.b = remote(self.mine, self.mine, self.sems, self.first + 1, self.to_y)
        self.a.start()
        self.b.start()

    def middle(self):
        self.a.wait_recv()
        self.c = remote(self.theirs, self.theirs, self.sems, self.first + 2, self.to_y)
        self.c.start()

    def finish(self):
        self.b.wait_recv()
        self.c.wait_recv()
        for item in (self.a, self.b, self.c):
            item.wait_send()


def shard_of(third):
    shard = third // 3
    return (shard // MEMBERS, shard % MEMBERS), third % 3


def lookup(table, index):
    result = 0
    for place, entry in enumerate(table):
        if entry:
            result = result + jnp.where(index == place, entry, 0)
    return result


FC_OF_GROUP = (
    (0, 1, 16, 17, 18, 22, 23, 24),
    (2, 3, 19, 20, 21, 25, 26, 27),
    (4, 5, 6, 10, 11, 12, 28, 29),
    (7, 8, 9, 13, 14, 15, 30, 31),
)
FC_SLOT = [0] * 32
FC_Y = [0] * 32
for _group, _units in enumerate(FC_OF_GROUP):
    for _slot, _unit in enumerate(_units):
        FC_SLOT[_unit] = _slot
        FC_Y[_unit] = _group % 2


def fc_unit(far, y, slot):
    return lookup([units[slot] for units in FC_OF_GROUP], 2 * far + y)


def fc_home(place, unit):
    return lookup(FC_SLOT, unit), lookup(FC_Y, unit)


PROJ_OF_CTX = (
    (8, 9, 10, 3),
    (11, 12, 13, 6),
    (14, 15, 16, 2),
    (17, 18, 19, 5),
    (20, 21, 22, 0),
    (1, 23, 24, 25),
    (4, 26, 27, 28),
    (7, 29, 30, 31),
)


def hidden_of(member):
    core, near, x = member // 4, member // 2 % 2, member % 2
    return [
        PROJ_OF_CTX[4 * far + 2 * near + y][2 * core + x] for y in range(2) for far in range(2)
    ]


HIDDEN = [hidden_of(_member) for _member in range(8)]
HOLDER = {unit: (m, i) for m, units in enumerate(HIDDEN) for i, unit in enumerate(units)}
PROJ_FSDP, PROJ_CTX = [0] * 32, [0] * 32
PROJ_UNIT = [0] * 32
for _ctx, _units in enumerate(PROJ_OF_CTX):
    for _place, _unit in enumerate(_units):
        _fsdp = 2 * (_place % 2) + _place // 2
        PROJ_FSDP[_unit], PROJ_CTX[_unit] = _fsdp, _ctx
        PROJ_UNIT[8 * _fsdp + _ctx] = _unit
FC_POSITION = [0] * 32
for _group, _units in enumerate(FC_OF_GROUP):
    for _slot, _unit in enumerate(_units):
        FC_POSITION[_unit] = 8 * _group + _slot


def piece(tile_of, col, lane, size):
    start = col % 128
    value = tile_of(col // 128)
    if start + size > 128:
        lanes = lax.broadcasted_iota(jnp.int32, value.shape, 1)
        value = jnp.where(lanes < start, tile_of(col // 128 + 1), value)
    shift = (lane - start) % 128
    return pltpu.roll(value, shift, 1) if shift else value


def join(parts):
    result = parts[0][1]
    for lane, value in parts[1:]:
        lanes = lax.broadcasted_iota(jnp.int32, value.shape, 1)
        result = jnp.where(lanes < lane, result, value)
    return result


def out_root(member):
    return jnp.where(member // 3 == 1, 1, 0)


def half_tile(flat, first, count, stride, half):
    at = half // 2
    tile = flat[pl.ds(first + at, count, stride=stride), :]
    if half % 2 == 0:
        return tile
    after = flat[pl.ds(first + at + 1, count, stride=stride), :]
    lane = lax.broadcasted_iota(jnp.int32, tile.shape, 1)
    return pltpu.roll(jnp.where(lane < HD, after, tile), HD, 1)


def lay_qkv(flat, rows, pieces, member, pair):
    count = rows.shape[1] // 2
    halves = 3 * HEADS
    for part in range(3):
        for odd in range(2):
            half = halves * odd + HEADS * part + head_start(member) + 2 * pair
            rows[part, pl.ds(odd, count, stride=2), :] = half_tile(flat, 0, count, halves, half)
    for part in range(3):
        pieces[pair, member, :, 128 * part : 128 * part + 128] = rows[part].astype(jnp.bfloat16)


def lay_fc(flat, first, pieces, part):
    count, hidden = pieces.shape[-2:]
    stride = FF // 128
    block = hidden // GROUPS

    def tile_of(tile):
        return flat[pl.ds(first + tile, count, stride=stride), :]

    for member in range(MEMBERS):
        for tile in range(-(-hidden // 128)):
            size = min(128, hidden - 128 * tile)
            parts, at = [], 128 * tile
            while at < 128 * tile + size:
                which, inside = divmod(at, block)
                length = min(block - inside, 128 * tile + size - at)
                col = block * HIDDEN[member][which] + inside
                parts.append((at - 128 * tile, piece(tile_of, col, at - 128 * tile, length)))
                at += length
            pieces[part, member, :, 128 * tile : 128 * tile + size] = join(parts)[
                :, :size
            ].astype(jnp.bfloat16)


def lay_rows(flat, first, rows, blocks, part):
    count = rows.shape[1] // 2
    width = blocks.shape[-1]
    halves = width // HD
    for odd in range(2):
        for tile in range(-(-width // 128)):
            half = halves * odd + 2 * tile
            size = min(128, width - 128 * tile)
            if size == 128 or half % 2 == 0:
                value = half_tile(flat, first, count, halves, half)
            else:
                value = pltpu.roll(
                    flat[pl.ds(first + half // 2, count, stride=halves), :], HD, 1
                )
            rows[tile, pl.ds(odd, count, stride=2), :] = value
    for tile in range(-(-width // 128)):
        size = min(128, width - 128 * tile)
        blocks[part, :, 128 * tile : 128 * tile + size] = rows[tile, :, :size].astype(
            jnp.bfloat16
        )


def wide(value):
    return value.astype(jnp.float32)


def low(value):
    return value.astype(jnp.bfloat16)


def turn(value, target):
    rows, cols = value.shape
    for first in range(0, rows, 128):
        for lane in range(0, cols, 128):
            part = value[first : first + 128, lane : lane + 128]
            target[lane : lane + 128, first : first + 128] = low(wide(part).T)


def half_of(blocks, core):
    return blocks.at[pl.ds(4 * core, 4)]


class Reduce:
    def __init__(
        self, place, away, kept, from_core, two, got, last, done, sems, near_first=False
    ):
        self.p, self.away, self.kept, self.from_core = place, away, kept, from_core
        self.two, self.got, self.last, self.done, self.sems = two, got, last, done, sems
        self.route = Gather(place, None, None, near_first)
        self.copies = []

    def _go(self, source, landing, index, target):
        item = remote(source, landing, self.sems, index, target)
        item.start()
        self.copies.append(item)
        return item

    def begin(self):
        for j in (3, 2, 1, 0):
            self._go(self.away.at[j], self.from_core.at[j], j, self.route.other)

    def _summed(self, member):
        block = member - 4 * self.p.core
        return wide(self.kept[block]) + wide(self.from_core[block])

    def second(self):
        for item in self.copies[:4]:
            item.wait_recv()
        self.two[0] = low(self._summed(self.route.of_both))
        self.across = self._go(self.two.at[0], self.got.at[0], 4, self.route.second)
        self.two[1] = low(self._summed(self.route.of_second))
        self.beyond = self._go(self.two.at[1], self.got.at[1], 5, self.route.second)

    def third(self):
        self.across.wait_recv()
        self.last[...] = low(self._summed(self.route.of_first) + wide(self.got[0]))
        self.final = self._go(self.last, self.done, 6, self.route.first)

    def result(self):
        self.beyond.wait_recv()
        value = self._summed(self.p.me) + wide(self.got[1])
        self.final.wait_recv()
        return value + wide(self.done[...])

    def sent(self):
        for item in self.copies:
            item.wait_send()


def reduce_buffers(rows, width):
    kind = jnp.bfloat16
    return [
        pltpu.VMEM((4, rows, width), kind),
        pltpu.VMEM((2, rows, width), kind),
        pltpu.VMEM((2, rows, width), kind),
        pltpu.VMEM((rows, width), kind),
        pltpu.VMEM((rows, width), kind),
        pltpu.SemaphoreType.DMA((2, 7)),
    ]


def norm_rows(value, gain, shift):
    center = value - jnp.mean(value, -1, keepdims=True)
    spread = jnp.mean(center * center, -1, keepdims=True)
    return center * lax.rsqrt(spread + epsilon_norm) * gain + shift


def head_rows(member):
    return 8 * member


def member_lanes(row, member, count):
    result = jnp.zeros((row.shape[0], count), row.dtype)
    for other in range(MEMBERS):
        first = head_start(other) * HD
        result = result + jnp.where(member == other, row[:, first : first + count], 0.0)
    return result


def attend_block(query, keys, values, row_pos, col_pos):
    lanes = lane_of(query.shape)
    result = jnp.zeros(query.shape, jnp.float32)
    for head in range(2):
        mine = lanes == head
        own = jnp.where(mine, query, jnp.zeros_like(query))
        probs = probabilities(own, keys, row_pos, col_pos)
        mixed = jnp.dot(probs.astype(jnp.bfloat16), values, preferred_element_type=jnp.float32)
        result = jnp.where(mine, mixed, result)
    return result.astype(jnp.bfloat16)


def forward_kernel(
    x_in, back_in, order_in, vec_in, weights,
    back_all, vecs, row_pos, col_pos, w_qkv_out, h_first_out, qkv_out, attn, w_fc_out, w_proj_out,
    w_heads, x_own, resid_own, h_second,
    x_all, w_qkv, h_first, qkv, w_fc, w_proj,
    flat, rows, qkv_pieces, fc_pieces, blocks, order, vec_all, qkv_land,
    fc, proj, out, fc_part, proj_part, out_part, tail, next_tail, window, unit_rows, h_own,
    branch, from_core, two, got, last, done, reduce_sem,
    order_pad, vec_pad, x_rows, back_rows, move_sem, qkv_sem, fc_send, fc_recv, rows_sem, x_sem, back_sem, spread_sem,
    own_sem, fc_sem, proj_sem, tree_sem, h_sem, store_sem,
):
    p = Place()
    third_rows = weights.shape[0] // 3
    width, count = x_in.shape
    length = MEMBERS * count
    pairs = SLOTS // 2
    barrier = pltpu.get_barrier_semaphore()

    def signal(step, carry):
        other = (p.linear + step) % DEVICES
        pl.semaphore_signal(
            barrier, inc=1, device_id=(other // MEMBERS, other % MEMBERS), device_id_type=MESH
        )
        return carry

    lax.fori_loop(1, DEVICES, signal, 0)
    flat[...] = weights[...].astype(jnp.float32)
    order_pad[...] = jnp.zeros_like(order_pad)
    order_pad[0:1, : order_in.shape[1]] = order_in[...]
    vec_pad[...] = jnp.zeros_like(vec_pad)
    vec_pad[: vec_in.shape[0], : vec_in.shape[1]] = vec_in[...]
    pl.semaphore_wait(barrier, DEVICES - 1)
    home = p.target(
        x=p.ctx % 2, near=p.ctx // 2 % 2, core=p.ctx // 4, y=p.fsdp // 2, far=p.fsdp % 2
    )
    owner = p.fsdp == 0
    qkv_moves = []
    for pair in range(pairs):
        for member in (7, 6, 3, 2, 5, 4, 1, 0):

            @pl.when(owner)
            def _(member=member, pair=pair):
                lay_qkv(flat, rows, qkv_pieces, member, pair)

            target = p.target(x=member % 2, near=member // 2 % 2, core=member // 4)
            qkv_moves.append(
                Move(
                    p, qkv_pieces.at[pair, member], qkv_land.at[pair, p.far, p.near, p.y],
                    qkv_sem.at[0, pair, member], qkv_sem.at[1, pair, p.near], target, owner,
                )
            )
    turn(x_in[...], x_rows)
    x_move = Move(p, x_rows, x_all.at[p.ctx], move_sem.at[0, 0], move_sem.at[1, 0], home)
    order_move = Move(p, order_pad, order, move_sem.at[0, 1], move_sem.at[1, 1], home)
    turn(back_in[...], back_rows)

    def vec_send(step, carry):
        other = (p.linear + step) % DEVICES
        pltpu.make_async_remote_copy(
            src_ref=vec_pad,
            dst_ref=vec_all.at[p.linear],
            send_sem=move_sem.at[0, 2],
            recv_sem=move_sem.at[1, 2],
            device_id=(other // MEMBERS, other % MEMBERS),
            device_id_type=MESH,
        ).start()
        return carry

    lax.fori_loop(1, DEVICES, vec_send, 0)
    pltpu.make_async_copy(vec_pad, vec_all.at[p.linear], move_sem.at[1, 2]).start()
    for part in range(3):
        third = 3 * p.linear + part
        is_fc = jnp.logical_and(third >= FC_FIRST, third < PROJ_FIRST)
        is_rows = jnp.logical_and(third >= OUT_FIRST, jnp.logical_not(is_fc))

        @pl.when(is_fc)
        def _(part=part):
            lay_fc(flat, part * third_rows, fc_pieces, part)

        @pl.when(is_rows)
        def _(part=part):
            lay_rows(flat, part * third_rows, rows, blocks, part)

    arrived(x_all.at[p.me], move_sem.at[1, 0])
    gather_x = Gather(p, x_all, x_sem, True)
    gather_x.begin()
    spreads = []

    def spread(pair):
        for near in range(2):
            arrived(qkv_land.at[pair, p.far, near, p.y], qkv_sem.at[1, pair, near])
            item = Spread(
                p, lambda far, y, near=near: qkv_land.at[pair, far, near, y],
                spread_sem, 6 * pair + 3 * near,
            )
            item.begin()
            spreads.append(item)

    spread(0)
    gather_x.second_hop()
    spread(1)
    gather_x.third_hop()
    fc_moves, rows_moves = [], []
    for part in range(3):
        third = 3 * p.linear + part
        valid = jnp.logical_and(third >= OUT_FIRST, third < FC_FIRST)
        member = jnp.where(valid, third - OUT_FIRST, 0)
        target = p.target(
            x=member % 2, near=member // 2 % 2, core=member // 4, y=out_root(member), far=0
        )
        rows_moves.append(
            Move(
                p, blocks.at[part], out_part,
                rows_sem.at[0, part], rows_sem.at[1, 1], target, valid,
            )
        )
    for part in range(3):
        third = 3 * p.linear + part
        valid = jnp.logical_and(third >= FC_FIRST, third < PROJ_FIRST)
        slot, y = fc_home(p, jnp.where(valid, third - FC_FIRST, 0))
        for member in (7, 6, 3, 2, 5, 4, 1, 0):
            target = p.target(x=member % 2, near=member // 2 % 2, core=member // 4, y=y)
            fc_moves.append(
                Move(
                    p, fc_pieces.at[part, member], fc_part.at[slot],
                    fc_send.at[part, member], fc_recv.at[slot], target, valid,
                )
            )
    for part in range(3):
        third = 3 * p.linear + part
        valid = third >= PROJ_FIRST
        unit = jnp.where(valid, third - PROJ_FIRST, 0)
        target = (lookup(PROJ_FSDP, unit), lookup(PROJ_CTX, unit))
        rows_moves.append(
            Move(
                p, blocks.at[part], proj_part,
                rows_sem.at[0, part], rows_sem.at[1, 0], target, valid,
            )
        )
    gather_x.last_hop()
    back_move = Move(p, back_rows, back_all.at[p.ctx], move_sem.at[0, 3], move_sem.at[1, 3], home)
    arrived(vec_all, move_sem.at[1, 2])
    cols = vec_pad.shape[-1]
    used = width // MEMBERS
    total = jnp.zeros(vecs.shape, jnp.float32)
    for ctx in range(MEMBERS):
        block = jnp.concatenate([vec_all[MEMBERS * f + ctx] for f in range(GROUPS)], 0)
        lane = lax.broadcasted_iota(jnp.int32, (cols, width), 0)
        at = lax.broadcasted_iota(jnp.int32, (cols, width), 1) - used * ctx
        spot = jnp.where(jnp.logical_and(lane == at, lane < used), 1.0, 0.0)
        total = total + jnp.dot(
            block, spot.astype(jnp.bfloat16), preferred_element_type=jnp.float32
        )
    vecs[...] = total
    arrived(order, move_sem.at[1, 1])
    slots = order[0:1, :].astype(jnp.float32)
    lane = lax.broadcasted_iota(jnp.int32, (length, 128), 1)
    row = lax.broadcasted_iota(jnp.int32, (length, 128), 0)
    spot = jnp.where(lane == row // BLOCK, slots, 0.0)
    inner = lax.broadcasted_iota(jnp.int32, (length, 1), 0) % BLOCK
    row_pos[...] = jnp.sum(spot, 1, keepdims=True) * BLOCK + inner.astype(jnp.float32)
    lane = lax.broadcasted_iota(jnp.int32, (128, length), 1)
    row = lax.broadcasted_iota(jnp.int32, (128, length), 0)
    spot = jnp.where(row == lane // BLOCK, 1.0, 0.0)
    inner = lax.broadcasted_iota(jnp.int32, (1, length), 1) % BLOCK
    found = jnp.dot(
        order[...].astype(jnp.bfloat16), spot.astype(jnp.bfloat16),
        preferred_element_type=jnp.float32,
    )
    col_pos[...] = found[0:1, :] * BLOCK + inner.astype(jnp.float32)
    for item in spreads[:2]:
        item.middle()
    arrived(back_all.at[p.me], move_sem.at[1, 3])
    gather_back = Gather(p, back_all, back_sem, True)
    gather_back.begin()
    gather_x.finish()

    def norm_block(step, carry):
        value = norm_rows(x_all[step].astype(jnp.float32), vecs[0:1, :], vecs[1:2, :])
        h_first[pl.ds(pl.multiple_of(step * count, count), count), :] = value.astype(jnp.bfloat16)
        return carry

    lax.fori_loop(0, MEMBERS, norm_block, 0)
    x_own[...] = x_all[p.me]
    stores = []

    def store(source, target):
        copy = pltpu.make_async_copy(source, target, store_sem.at[len(stores)])
        copy.start()
        stores.append(copy)

    store(h_first, h_first_out)
    to_far, to_y = p.target(far=1 - p.far), p.target(y=1 - p.y)
    same_y = p.y == out_root(p.me)
    root = jnp.logical_and(same_y, p.far == 0)
    beside = jnp.logical_and(same_y, p.far == 1)
    out_far = remote(out_part, out, tree_sem, 0, to_far)
    out_y = remote(out_part, out, tree_sem, 1, to_y)
    out_later = remote(out, out, tree_sem, 2, to_y)
    out_own = pltpu.make_async_copy(out_part, out, own_sem.at[8])

    @pl.when(root)
    def _():
        arrived(out_part, rows_sem.at[1, 1])
        out_far.start()
        out_y.start()
        out_own.start()

    fc_far, fc_y, fc_later, own_copies = [], [], [], []
    for slot in range(8):
        arrived(fc_part.at[slot], fc_recv.at[slot])
        landing = fc.at[fc_unit(p.far, p.y, slot)]
        fc_far.append(remote(fc_part.at[slot], landing, fc_sem, slot, to_far))
        fc_far[slot].start()
        fc_y.append(remote(fc_part.at[slot], landing, fc_sem, 8 + slot, to_y))
        fc_y[slot].start()
        own_copies.append(pltpu.make_async_copy(fc_part.at[slot], landing, own_sem.at[slot]))
        own_copies[slot].start()
    gather_back.second_hop()
    gather_back.third_hop()
    arrived(proj_part, rows_sem.at[1, 0])
    my_proj, far_proj = proj.at[p.y, p.far], proj.at[p.y, 1 - p.far]
    proj_far = remote(proj_part, my_proj, proj_sem, 0, to_far)
    proj_y = remote(proj_part, my_proj, proj_sem, 1, to_y)
    proj_far.start()
    proj_y.start()
    proj_own = pltpu.make_async_copy(proj_part, my_proj, own_sem.at[9])
    proj_own.start()
    four = qkv_land.shape[4]
    per_part = SLOTS * HD
    bias_q = member_lanes(vecs[2:3, :], p.me, per_part)
    bias_v = member_lanes(vecs[16:17, :], p.me, per_part)

    def project(pair):
        columns = slice(384 * pair, 384 * pair + 384)
        for item in spreads[2 * pair : 2 * pair + 2]:
            item.finish()
        for far in range(2):
            for near in range(2):
                for y in range(2):
                    first = four * (4 * far + 2 * near + y)
                    w_qkv[first : first + four, columns] = qkv_land[pair, far, near, y]
        part = slice(128 * pair, 128 * pair + 128)
        bias = jnp.concatenate(
            [bias_q[:, part], jnp.zeros((1, 128), jnp.float32), bias_v[:, part]], 1
        )

        def qkv_block(step, carry):
            at = pl.ds(pl.multiple_of(step * 2 * count, 2 * count), 2 * count)
            value = jnp.dot(
                h_first[at, :], w_qkv[:, columns], preferred_element_type=jnp.float32
            )
            qkv[at, columns] = (value + bias).astype(jnp.bfloat16)
            return carry

        lax.fori_loop(0, MEMBERS // 2, qkv_block, 0)

    project(0)
    for item in spreads[2:]:
        item.middle()
    gather_back.last_hop()
    span = 2 * count

    def one_pair(pair):
        def one_block(step, carry):
            at = pl.ds(pl.multiple_of(step * span, span), span)
            attn[pair, at, :] = attend_block(
                qkv[at, 384 * pair : 384 * pair + 128],
                qkv[:, 384 * pair + 128 : 384 * pair + 256],
                qkv[:, 384 * pair + 256 : 384 * pair + 384],
                row_pos[at, :],
                col_pos[...],
            )
            return carry

        lax.fori_loop(0, length // span, one_block, 0)

    one_pair(0)
    project(1)
    store(w_qkv, w_qkv_out)
    store(qkv, qkv_out)

    @pl.when(beside)
    def _():
        out_far.wait_recv()
        out_later.start()

    for slot in range(8):
        fc_far[slot].wait_recv()
        landing = fc.at[fc_unit(1 - p.far, p.y, slot)]
        copy = remote(landing, landing, fc_sem, 16 + slot, to_y)
        copy.start()
        fc_later.append(copy)
    one_pair(1)

    @pl.when(root)
    def _():
        out_own.wait()

    @pl.when(jnp.logical_and(jnp.logical_not(same_y), p.far == 0))
    def _():
        out_y.wait_recv()

    @pl.when(jnp.logical_and(jnp.logical_not(same_y), p.far == 1))
    def _():
        out_later.wait_recv()

    reach = tail.shape[0]
    tail[...] = out[four - reach :, :]
    following, before = (p.me + 1) % MEMBERS, (p.me + MEMBERS - 1) % MEMBERS
    to_next = p.target(
        x=following % 2, near=following // 2 % 2, core=following // 4
    )
    send_tail = remote(tail, next_tail, tree_sem, 3, to_next)
    send_tail.start()
    begin = head_rows(p.me)
    window[...] = jnp.zeros_like(window)
    window[reach : reach + four, :] = wide(out[...])
    span_rows = SLOTS * HD
    unit_rows[...] = low(window[pl.ds(pl.multiple_of(reach - begin, 8), span_rows), :])

    def one_branch(step, carry):
        at = pl.ds(pl.multiple_of(step * span, span), span)
        heads = jnp.concatenate([attn[pair, at, :] for pair in range(pairs)], 1)
        value = low(jnp.dot(heads, unit_rows[...], preferred_element_type=jnp.float32))
        branch[2 * step] = value[:count]
        branch[2 * step + 1] = value[count:]
        return carry

    lax.fori_loop(0, length // span, one_branch, 0)
    reduce = Reduce(
        p, half_of(branch, 1 - p.core), half_of(branch, p.core), from_core, two, got, last, done,
        reduce_sem,
    )
    reduce.begin()
    proj_far.wait_recv()
    proj_later = remote(far_proj, far_proj, proj_sem, 2, to_y)
    proj_later.start()
    reduce.second()
    reduce.third()
    for item in fc_y + fc_later:
        item.wait_recv()
    for item in own_copies:
        item.wait()
    value = wide(x_own[...]) + reduce.result() + vecs[17:18, :]
    resid_own[...] = value
    h_own[...] = low(norm_rows(value, vecs[18:19, :], vecs[32:33, :]))
    gather_h = Gather(p, h_second, h_sem)
    for name, index, target in (
        ("a", 0, gather_h.first), ("b", 1, gather_h.second), ("c", 2, gather_h.other),
    ):
        copy = remote(h_own, h_second.at[p.me], h_sem, index, target)
        copy.start()
        gather_h.copies[name] = copy
    store(h_own, h_second.at[p.me])
    unit = fc.shape[1]
    for block in range(DEVICES):
        w_fc[unit * block : unit * block + unit, :] = fc[block]
    store(w_fc, w_fc_out)
    gather_h.second_hop()
    gather_h.third_hop()
    proj_y.wait_recv()
    proj_later.wait_recv()
    proj_own.wait()
    for group in range(GROUPS):
        w_proj[four * group : four * group + four, :] = proj[group // 2, group % 2]
    store(w_proj, w_proj_out)
    gather_h.last_hop()
    send_tail.wait_recv()
    window[:reach, :] = wide(next_tail[...])
    w_heads[...] = low(window[pl.ds(pl.multiple_of(reach - begin, 8), span_rows), :])
    for item in (gather_h, gather_back):
        item.finish()
    for item in fc_far + fc_y + fc_later + [proj_far, proj_y, proj_later, send_tail]:
        item.wait_send()
    reduce.sent()

    @pl.when(root)
    def _():
        out_far.wait_send()
        out_y.wait_send()

    @pl.when(beside)
    def _():
        out_later.wait_send()

    for copy in stores:
        copy.wait()
    for item in [x_move, order_move, back_move] + qkv_moves + fc_moves + rows_moves:
        item.sent()
    arrived(vec_all.at[pl.ds(1, DEVICES - 1)], move_sem.at[0, 2])


def forward(x, back, order, vectors, weights):
    width, rows = x.shape
    kind, high = jnp.bfloat16, jnp.float32
    unit, hidden = width // DEVICES, FF // MEMBERS
    four, cols = 4 * unit, 3 * SLOTS * HD
    length, pairs = MEMBERS * rows, SLOTS // 2
    vec_cols = -(-vectors.shape[1] // 128) * 128
    any_space = pl.BlockSpec(memory_space=pl.ANY)
    vmem = pl.BlockSpec(memory_space=pltpu.VMEM)
    dma = pltpu.SemaphoreType.DMA

    def like(*shape, dtype=kind):
        return jax.ShapeDtypeStruct(shape, dtype)

    return pl.pallas_call(
        forward_kernel,
        out_shape=[
            like(MEMBERS, rows, width),
            like(GROUPS * 16, width, dtype=high),
            like(length, 1, dtype=high),
            like(1, length, dtype=high),
            like(width, cols),
            like(length, width),
            like(length, cols),
            like(pairs, length, 2 * HD),
            like(width, hidden),
            like(hidden, width),
            like(SLOTS * HD, width),
            like(rows, width),
            like(rows, width, dtype=high),
            like(MEMBERS, rows, width),
        ],
        in_specs=[vmem] * 5,
        out_specs=[any_space] + [vmem] * 3 + [any_space] * 3 + [vmem] + [any_space] * 2
        + [vmem] * 3 + [any_space],
        scratch_shapes=[
            pltpu.VMEM((MEMBERS, rows, width), kind),
            pltpu.VMEM((width, cols), kind),
            pltpu.VMEM((length, width), kind),
            pltpu.VMEM((length, cols), kind),
            pltpu.VMEM((width, hidden), kind),
            pltpu.VMEM((hidden, width), kind),
            pltpu.VMEM(weights.shape, high),
            pltpu.VMEM((-(-width // 128), four, 128), high),
            pltpu.VMEM((pairs, MEMBERS, four, cols // pairs), kind),
            pltpu.VMEM((3, MEMBERS, unit, hidden), kind),
            pltpu.VMEM((3, four, width), kind),
            pltpu.VMEM((128, 128), order.dtype),
            pltpu.VMEM((DEVICES, 16, vec_cols), kind),
            pltpu.VMEM((pairs, 2, 2, 2, four, cols // pairs), kind),
            pltpu.VMEM((DEVICES, unit, hidden), kind),
            pltpu.VMEM((2, 2, four, width), kind),
            pltpu.VMEM((four, width), kind),
            pltpu.VMEM((8, unit, hidden), kind),
            pltpu.VMEM((four, width), kind),
            pltpu.VMEM((four, width), kind),
            pltpu.VMEM((64, width), kind),
            pltpu.VMEM((64, width), kind),
            pltpu.VMEM((64 + SLOTS * HD, width), high),
            pltpu.VMEM((SLOTS * HD, width), kind),
            pltpu.VMEM((rows, width), kind),
            pltpu.VMEM((MEMBERS, rows, width), kind),
        ]
        + reduce_buffers(rows, width)
        + [
            pltpu.VMEM((128, 128), order.dtype),
            pltpu.VMEM((16, vec_cols), kind),
            pltpu.VMEM((rows, width), kind),
            pltpu.VMEM((rows, width), kind),
            dma((2, 4)),
            dma((2, pairs, 8)),
            dma((3, 8)),
            dma((8,)),
            dma((2, 3)),
            dma((2, 7)),
            dma((2, 7)),
            dma((2, 12)),
            dma((9 + 1,)),
            dma((2, 24)),
            dma((2, 3)),
            dma((2, 4)),
            dma((2, 7)),
            dma((6,)),
        ],
        compiler_params=pltpu.CompilerParams(
            collective_id=1, has_side_effects=True, vmem_limit_bytes=VMEM_BYTES
        ),
        name="forward",
    )(x, back, order, vectors, weights)


GELU_SCALE = 0.7978845608028654
GELU_CUBE = 0.044715


def store_rows(target, first, value, lanes=slice(None), at=None):
    places = at
    size = target.shape[1]
    row = 0
    while row < value.shape[0]:
        block, at = divmod(first + row, size)
        count = min(size - at, value.shape[0] - row)
        block = block if places is None else places[block]
        target[block, at : at + count, lanes] = low(value[row : row + count])
        row += count


def middle_kernel(
    h_in, back_all, vecs, resid_own, w_fc_in, w_proj_in,
    grad_fc, grad_proj, proj_go, made, dresid, branch_all, sums, fc_sums,
    h_second, back, w_fc, w_proj, act, dpre, dh_part, made_part, g_fc, g_proj,
    proj_y, from_core, two, got, last, done, reduce_sem,
    load_sem, store_sem, fold_sem,
    dbranch, branch_sem,
):
    p = Place()
    length, width = h_second.shape
    count = length // MEMBERS
    hidden = act.shape[1]
    loads = []
    for index, (source, target) in enumerate(
        (
            (h_in, h_second), (w_fc_in, w_fc), (back_all, back), (w_proj_in, w_proj),
        )
    ):
        copy = pltpu.make_async_copy(source, target, load_sem.at[index])
        copy.start()
        loads.append(copy)
    reduce = Reduce(p, half_of(dh_part, 1 - p.core), half_of(dh_part, p.core), from_core, two, got, last, done, reduce_sem)
    route = reduce.route
    to_y = p.target(y=1 - p.y)
    greet((route.first, route.second, route.other, to_y))
    bias_fc = jnp.zeros((1, hidden), jnp.float32)
    block = hidden // GROUPS
    for member in range(MEMBERS):
        parts = []
        for unit in HIDDEN[member]:
            row, first = divmod(block * unit, width)
            row = (34, 48, 49, 50)[row]
            parts.append(vecs[row : row + 1, first : first + block])
        bias_fc = bias_fc + jnp.where(p.me == member, jnp.concatenate(parts, 1), 0.0)
    fc_sums[...] = jnp.zeros_like(fc_sums)
    for copy in loads:
        copy.wait()
    span = 2 * count

    def one_block(step, carry):
        at = pl.ds(pl.multiple_of(step * span, span), span)
        normed = h_second[at, :]
        pre = jnp.dot(normed, w_fc[...], preferred_element_type=jnp.float32) + bias_fc
        square = pre * pre
        slope = jnp.tanh(GELU_SCALE * (pre + GELU_CUBE * pre * square))
        act[at, :] = low(0.5 * pre * (1.0 + slope))
        tilt = 0.5 * (1.0 + slope) + 0.5 * pre * (1.0 - slope * slope) * GELU_SCALE * (
            1.0 + 3.0 * GELU_CUBE * square
        )
        dpre_block = low(dot_nt(back[at, :], w_proj[...]) * tilt)
        dpre[at, :] = dpre_block
        fc_sums[...] += jnp.sum(wide(dpre_block), 0, keepdims=True)
        value = low(dot_nt(dpre_block, w_fc[...]))
        dh_part[2 * step] = value[:count]
        dh_part[2 * step + 1] = value[count:]
        return carry

    lax.fori_loop(0, MEMBERS // 2, one_block, 0)
    reduce.begin()

    def one_made(step, carry):
        at = pl.ds(pl.multiple_of(step * span, span), span)
        value = low(jnp.dot(act[at, :], w_proj[...], preferred_element_type=jnp.float32))
        made_part[2 * step] = value[:count]
        made_part[2 * step + 1] = value[count:]
        return carry

    lax.fori_loop(0, MEMBERS // 2, one_made, 0)
    reduce.second()
    stores = [pltpu.make_async_copy(made_part, made, store_sem.at[3])]
    stores[0].start()
    chunk = 256

    def one_proj(step, carry):
        lanes = pl.ds(pl.multiple_of(step * chunk, chunk), chunk)
        store_rows(g_proj, 0, dot_tn(act[...], back[:, lanes]), lanes)
        return carry

    lax.fori_loop(0, width // chunk, one_proj, 0)
    tail = slice(width // chunk * chunk, width)
    if width % chunk:
        store_rows(g_proj, 0, dot_tn(act[...], back[:, tail]), tail)
    over_y = remote(
        g_proj.at[2 * (1 - p.y) + 1 - p.far], proj_y, fold_sem, 0, to_y
    )
    over_y.start()
    reduce.third()
    stores.append(pltpu.make_async_copy(g_proj, grad_proj, store_sem.at[0]))
    stores[-1].start()
    for first in range(0, width, chunk):
        size = min(chunk, width - first)
        store_rows(
            g_fc, first, dot_tn(h_second[:, first : first + size], dpre[...]), at=FC_POSITION
        )
    stores.append(pltpu.make_async_copy(g_fc, grad_fc, store_sem.at[1]))
    stores[-1].start()

    dh = reduce.result()
    center = resid_own[...] - jnp.mean(resid_own[...], -1, keepdims=True)
    scale = lax.rsqrt(jnp.mean(center * center, -1, keepdims=True) + epsilon_norm)
    hat = center * scale
    back_own = wide(back[pl.ds(pl.multiple_of(p.me * count, count), count), :])
    scaled = dh * vecs[18:19, :]
    inner = jnp.mean(scaled * hat, -1, keepdims=True)
    value = back_own + (scaled - jnp.mean(scaled, -1, keepdims=True) - hat * inner) * scale
    dresid[...] = value
    branch = low(value)
    dbranch[...] = branch
    gather = Gather(p, branch_all, branch_sem)
    for name, index, target in (
        ("a", 0, gather.first), ("b", 1, gather.second), ("c", 2, gather.other),
    ):
        copy = remote(dbranch, branch_all.at[p.me], branch_sem, index, target)
        copy.start()
        gather.copies[name] = copy
    stores.append(pltpu.make_async_copy(dbranch, branch_all.at[p.me], store_sem.at[2]))
    stores[-1].start()
    sums[0:1, :] = jnp.sum(dh * hat, 0, keepdims=True)
    sums[1:2, :] = jnp.sum(dh, 0, keepdims=True)
    sums[2:3, :] = jnp.sum(wide(branch), 0, keepdims=True)
    sums[3:4, :] = jnp.sum(back_own, 0, keepdims=True)
    sums[4:8, :] = jnp.zeros((4, width), jnp.float32)
    gather.second_hop()
    gather.third_hop()
    over_y.wait_recv()
    proj_go[...] = low(wide(g_proj[2 * p.y + 1 - p.far]) + wide(proj_y[...]))
    over_y.wait_send()
    gather.last_hop()
    gather.finish()
    reduce.sent()
    for copy in stores:
        copy.wait()


def middle(h_second, back_all, vecs, resid_own, w_fc, w_proj):
    kind, high = jnp.bfloat16, jnp.float32
    length, width = h_second.shape
    rows = length // MEMBERS
    hidden = w_proj.shape[0]
    four = width // MEMBERS
    any_space = pl.BlockSpec(memory_space=pl.ANY)
    vmem = pl.BlockSpec(memory_space=pltpu.VMEM)
    dma = pltpu.SemaphoreType.DMA

    def like(*shape, dtype=kind):
        return jax.ShapeDtypeStruct(shape, dtype)

    def buffer(*shape, dtype=kind):
        return pltpu.VMEM(shape, dtype)

    return pl.pallas_call(
        middle_kernel,
        out_shape=[
            like(DEVICES, four // 4, hidden),
            like(GROUPS, four, width),
            like(four, width),
            like(MEMBERS, rows, width),
            like(rows, width, dtype=high),
            like(MEMBERS, rows, width),
            like(8, width, dtype=high),
            like(1, hidden, dtype=high),
        ],
        in_specs=[any_space] * 2 + [vmem] * 2 + [any_space] * 2,
        out_specs=[any_space] * 2 + [vmem, any_space, vmem, any_space] + [vmem] * 2,
        scratch_shapes=[
            buffer(*h_second.shape),
            buffer(*back_all.shape),
            buffer(*w_fc.shape),
            buffer(*w_proj.shape),
            buffer(length, hidden),
            buffer(length, hidden),
            buffer(MEMBERS, rows, width),
            buffer(MEMBERS, rows, width),
            buffer(DEVICES, four // 4, hidden),
            buffer(GROUPS, four, width),
            buffer(four, width),
        ]
        + reduce_buffers(rows, width)
        + [dma((4,)), dma((4,)), dma((2, 1)), buffer(rows, width), dma((2, 7))],
        compiler_params=pltpu.CompilerParams(
            collective_id=3, has_side_effects=True, vmem_limit_bytes=VMEM_BYTES
        ),
        name="middle",
    )(h_second, back_all, vecs, resid_own, w_fc, w_proj)


class Fold:
    def __init__(self, place, away, kept, landing, leaving, last, sems, first):
        p = place
        self.p, self.away, self.kept, self.landing = p, away, kept, landing
        self.leaving, self.last = leaving, last
        self.to_far, self.to_y = p.target(far=1 - p.far), p.target(y=1 - p.y)
        self.sems, self.first = sems, first

    def begin(self):
        other = 1 - self.p.far
        self.a = remote(
            self.away(other), self.landing(other), self.sems, self.first, self.to_y
        )
        self.a.start()

    def rest(self):
        far = self.p.far
        self.b = remote(
            self.away(far), self.landing(far), self.sems, self.first + 1, self.to_y
        )
        self.b.start()

    def middle(self):
        other = 1 - self.p.far
        self.a.wait_recv()
        self.leaving[...] = low(wide(self.kept(other)[...]) + wide(self.landing(other)[...]))
        self.c = remote(self.leaving, self.last, self.sems, self.first + 2, self.to_far)
        self.c.start()

    def end(self):
        far = self.p.far
        self.b.wait_recv()
        partial = wide(self.kept(far)[...]) + wide(self.landing(far)[...])
        self.c.wait_recv()
        return low(partial + wide(self.last[...]))

    def sent(self):
        for item in (self.a, self.b, self.c):
            item.wait_send()


def backward_kernel(
    branch_in, made_in, grad_fc, grad_proj, proj_go, attn, qkv, row_pos, col_pos, w_heads, w_qkv_in,
    h_in, x_own, resid_own, dresid, vecs, sums, fc_sums,
    out_home, grad_home, qkv_back, fc_back, rows_back, vec_back,
    branch_all, dattn, dqkv, key_sum, value_sum, w_qkv, h_first, dh_part, made, result,
    fc_own, proj_own, g_qkv, g_heads, g_out, input_grad, vec_rows, vec_go, vec_got,
    fc_y, proj_y, qkv_y, out_y, fc_go, qkv_go, out_go,
    fc_far, proj_far, qkv_far, out_far, fc_sum, proj_sum, qkv_sum, out_sum,
    core_a, two_a, got_a, last_a, done_a, sem_a, core_b, two_b, got_b, last_b, done_b, sem_b,
    load_sem, fold_sem, tree_sem, vec_sem, home_sem,
    qkv_send, qkv_recv, fc_send, fc_recv, rows_send, rows_recv,
):
    p = Place()
    _, count, width = branch_in.shape
    length = MEMBERS * count
    four = grad_proj.shape[1]
    pairs = SLOTS // 2
    loads = []

    def load(source, target):
        copy = pltpu.make_async_copy(source, target, load_sem.at[len(loads)])
        copy.start()
        loads.append(copy)

    load(branch_in, branch_all)
    load(half_of(made_in, p.core), made)
    load(grad_proj.at[2 * p.y + p.far], proj_own)
    for far in range(2):
        for near in range(2):
            load(grad_fc.at[far, p.y, near], fc_own.at[far, near])
    load(w_qkv_in, w_qkv)
    load(h_in, h_first)
    greet_all(p)
    proj_over_y = remote(
        grad_proj.at[2 * (1 - p.y) + p.far], proj_y, fold_sem, 0, p.target(y=1 - p.y)
    )
    proj_over_far = remote(proj_go, proj_far, fold_sem, 1, p.target(far=1 - p.far))
    fc_folds = [
        Fold(
            p, lambda far, near=near: grad_fc.at[far, 1 - p.y, near],
            lambda far, near=near: fc_own.at[far, near],
            lambda far, near=near: fc_y.at[far, near],
            fc_go.at[near], fc_far.at[near], fold_sem, 3 + 3 * near,
        )
        for near in range(2)
    ]
    qkv_folds = [
        Fold(
            p, lambda far, pair=pair: g_qkv.at[pair, pl.ds(4 * far + 2 * (1 - p.y), 2)],
            lambda far, pair=pair: g_qkv.at[pair, pl.ds(4 * far + 2 * p.y, 2)],
            lambda far, pair=pair: qkv_y.at[pair, far],
            qkv_go.at[pair], qkv_far.at[pair], fold_sem, 9 + 3 * pair,
        )
        for pair in range(pairs)
    ]
    reduce_made = Reduce(
        p, half_of(made_in, 1 - p.core), made, core_a, two_a, got_a, last_a, done_a, sem_a
    )
    reduce_made.begin()
    proj_over_far.start()
    for item in fc_folds:
        item.begin()
    for copy in loads:
        copy.wait()
    proj_over_y.start()
    span = 2 * count

    def one_dattn(step, carry):
        at = pl.ds(pl.multiple_of(step * span, span), span)
        grad = jnp.concatenate([branch_all[2 * step], branch_all[2 * step + 1]], 0)
        value = low(dot_nt(grad, w_heads[...]))
        for pair in range(pairs):
            dattn[pair, at, :] = value[:, 128 * pair : 128 * pair + 128]
        return carry

    lax.fori_loop(0, length // span, one_dattn, 0)
    def one_pair(pair):
        key_sum[...] = jnp.zeros_like(key_sum)
        value_sum[...] = jnp.zeros_like(value_sum)

        def columns(part):
            return slice(384 * pair + 128 * part, 384 * pair + 128 * part + 128)

        def one_block(step, carry):
            at = pl.ds(pl.multiple_of(step * span, span), span)
            query, grad = qkv[at, columns(0)], dattn[pair, at, :]
            keys, values = qkv[:, columns(1)], qkv[:, columns(2)]
            lanes = lane_of(query.shape)
            total = jnp.zeros(query.shape, jnp.float32)
            add_keys = add_values = 0.0
            for head in range(2):
                mine = lanes == head
                own = jnp.where(mine, query, jnp.zeros_like(query))
                own_grad = jnp.where(mine, grad, jnp.zeros_like(grad))
                probs = probabilities(own, keys, row_pos[at, :], col_pos[...])
                dprobs = dot_nt(own_grad, values)
                delta = jnp.sum(probs * dprobs, -1, keepdims=True)
                dscores = low(probs * (dprobs - delta))
                mixed = jnp.dot(dscores, keys, preferred_element_type=jnp.float32)
                total = jnp.where(mine, mixed, total)
                add_keys = add_keys + dot_tn(dscores, own)
                add_values = add_values + dot_tn(low(probs), own_grad)
            dqkv[at, columns(0)] = low(total * 0.125)
            key_sum[...] += add_keys
            value_sum[...] += add_values
            return carry

        lax.fori_loop(0, length // span, one_block, 0)
        dqkv[:, columns(1)] = low(key_sum[...] * 0.125)
        dqkv[:, columns(2)] = low(value_sum[...])

    chunk = 256

    def one_grad(pair):
        columns = slice(384 * pair, 384 * pair + 384)
        for first in range(0, width, chunk):
            size = min(chunk, width - first)
            value = dot_tn(h_first[:, first : first + size], dqkv[:, columns])
            store_rows(g_qkv.at[pair], first, value, at=(0, 2, 1, 3, 4, 6, 5, 7))
        qkv_folds[pair].begin()

    reduce_made.second()
    one_pair(0)
    reduce_made.third()
    one_grad(0)
    for item in fc_folds:
        item.middle()
    for item in fc_folds:
        item.rest()
    one_pair(1)
    for part in range(3):
        last = 384 * (pairs - 1) + 128 * part
        value = dqkv[:, last : last + 128]
        keep = jnp.logical_or(lane_of(value.shape) == 0, p.me == MEMBERS - 1)
        dqkv[:, last : last + 128] = jnp.where(keep, value, jnp.zeros_like(value))
    one_grad(1)
    qkv_folds[0].middle()
    for item in qkv_folds:
        item.rest()

    def one_part(step, carry):
        at = pl.ds(pl.multiple_of(step * span, span), span)
        value = low(dot_nt(dqkv[at, :], w_qkv[...]))
        dh_part[2 * step] = value[:count]
        dh_part[2 * step + 1] = value[count:]
        return carry

    lax.fori_loop(0, length // span, one_part, 0)
    reduce_dh = Reduce(
        p, half_of(dh_part, 1 - p.core), half_of(dh_part, p.core), core_b, two_b, got_b, last_b,
        done_b, sem_b, True,
    )
    reduce_dh.begin()
    home = p.target(
        x=p.ctx % 2, near=p.ctx // 2 % 2, core=p.ctx // 4, y=p.fsdp // 2, far=p.fsdp % 2
    )
    turn(low(resid_own[...] + reduce_made.result() + vecs[33:34, :]), result)
    moves = [Move(p, result, out_home, home_sem.at[0, 0], home_sem.at[1, 0], home)]
    reduce_dh.second()
    proj_over_y.wait_recv()
    proj_over_far.wait_recv()
    proj_sum[...] = low(wide(proj_own[...]) + wide(proj_y[...]) + wide(proj_far[...]))
    target, part = shard_of(PROJ_FIRST + lookup(PROJ_UNIT, p.linear))
    moves.append(
        Move(p, proj_sum, rows_back.at[part], rows_send.at[0], rows_recv.at[part], target)
    )
    for pair in range(pairs):
        total = 0.0
        for block in range(MEMBERS):
            at = slice(block * count, block * count + count)
            total = total + dot_tn(attn[pair, at, :], branch_all[block])
        g_heads[128 * pair : 128 * pair + 128, :] = total
    g_out[...] = low(g_heads[pl.ds(pl.multiple_of(head_rows(p.me), 8), four), :])
    root_y = out_root(p.me)
    same_y = p.y == root_y
    root = jnp.logical_and(same_y, p.far == 0)
    beside = jnp.logical_and(same_y, p.far == 1)
    over_y = remote(g_out, out_y, tree_sem, 0, p.target(y=1 - p.y))
    over_far = remote(out_go, out_far, tree_sem, 1, p.target(far=1 - p.far))

    @pl.when(jnp.logical_not(same_y))
    def _():
        over_y.start()

    reduce_dh.third()
    for near in range(2):
        fc_sum[near] = fc_folds[near].end()
        for slot in range(4):
            target, part = shard_of(FC_FIRST + fc_unit(p.far, p.y, 4 * near + slot))
            moves.append(
                Move(
                    p, fc_sum.at[near, slot], fc_back.at[part, p.me],
                    fc_send.at[near, slot], fc_recv.at[part, p.me], target,
                )
            )

    @pl.when(same_y)
    def _():
        over_y.wait_recv()

    @pl.when(beside)
    def _():
        out_go[...] = low(wide(g_out[...]) + wide(out_y[...]))
        over_far.start()

    dh = reduce_dh.result()
    x = wide(x_own[...])
    center = x - jnp.mean(x, -1, keepdims=True)
    scale = lax.rsqrt(jnp.mean(center * center, -1, keepdims=True) + epsilon_norm)
    hat = center * scale
    scaled = dh * vecs[0:1, :]
    inner = jnp.mean(scaled * hat, -1, keepdims=True)
    value = (scaled - jnp.mean(scaled, -1, keepdims=True) - hat * inner) * scale
    turn(low(dresid[...] + value), input_grad)
    moves.append(Move(p, input_grad, grad_home, home_sem.at[0, 1], home_sem.at[1, 1], home))
    bias_sums = jnp.sum(wide(dqkv[...]), 0, keepdims=True)

    def placed(value, starts, me):
        total = jnp.zeros((1, width), jnp.float32)
        for index, start in enumerate(starts):
            parts = [value]
            if start:
                parts.insert(0, jnp.zeros((1, start), jnp.float32))
            after = width - start - value.shape[1]
            if after:
                parts.append(jnp.zeros((1, after), jnp.float32))
            row = jnp.concatenate(parts, 1) if len(parts) > 1 else value
            total = total + jnp.where(me == index, row, 0.0)
        return total

    heads = [head_start(member) * HD for member in range(MEMBERS)]
    vec_rows[0:1, :] = jnp.sum(dh * hat, 0, keepdims=True)
    vec_rows[1:2, :] = jnp.sum(dh, 0, keepdims=True)
    for row, part in ((2, 0), (3, 2)):
        value = jnp.concatenate(
            [
                bias_sums[:, 384 * pair + 128 * part : 384 * pair + 128 * part + 128]
                for pair in range(pairs)
            ],
            1,
        )
        vec_rows[row : row + 1, :] = placed(value, heads, p.me)
    vec_rows[4:5, :] = sums[2:3, :]
    vec_rows[5:7, :] = sums[0:2, :]
    vec_rows[7:8, :] = sums[3:4, :]
    used = width // MEMBERS
    vec_go[...] = jnp.zeros_like(vec_go)
    for f in range(GROUPS):
        for c in range(MEMBERS):
            vec_go[MEMBERS * f + c, 0:3, 0:used] = vec_rows[
                3 * f : 3 * f + 3, used * c : used * c + used
            ]
    for unit, (holder, which) in HOLDER.items():
        f, row = divmod(8 + unit // MEMBERS, 3)
        value = fc_sums[:, used * which : used * which + used]
        vec_go[MEMBERS * f + unit % MEMBERS, row : row + 1, 0:used] = jnp.where(
            p.me == holder, value, 0.0
        )

    def vec_send(step, carry):
        other = (p.linear + step) % DEVICES
        pltpu.make_async_remote_copy(
            src_ref=vec_go.at[other],
            dst_ref=vec_got.at[p.linear],
            send_sem=vec_sem.at[0],
            recv_sem=vec_sem.at[1],
            device_id=(other // MEMBERS, other % MEMBERS),
            device_id_type=MESH,
        ).start()
        return carry

    lax.fori_loop(1, DEVICES, vec_send, 0)
    pltpu.make_async_copy(vec_go.at[p.linear], vec_got.at[p.linear], vec_sem.at[1]).start()
    qkv_folds[1].middle()
    @pl.when(root)
    def _():
        over_far.wait_recv()
        out_sum[...] = low(wide(g_out[...]) + wide(out_y[...]) + wide(out_far[...]))

    target, part = shard_of(OUT_FIRST + p.me)
    moves.append(
        Move(p, out_sum, rows_back.at[part], rows_send.at[1], rows_recv.at[part], target, root)
    )
    for pair in range(pairs):
        qkv_sum[pair] = qkv_folds[pair].end()
        for near in range(2):
            target = (0 * p.fsdp, 4 * p.far + 2 * near + p.y)
            moves.append(
                Move(
                    p, qkv_sum.at[pair, near], qkv_back.at[p.me, pair],
                    qkv_send.at[pair, near], qkv_recv.at[p.me, pair], target,
                )
            )
    arrived(vec_got, vec_sem.at[1])
    vec_back[...] = jnp.sum(vec_got[...], 0)

    @pl.when(p.fsdp == 0)
    def _():
        for member in range(MEMBERS):
            for pair in range(pairs):
                arrived(qkv_back.at[member, pair], qkv_recv.at[member, pair])

    for part in range(3):
        third = 3 * p.linear + part
        is_fc = jnp.logical_and(third >= FC_FIRST, third < PROJ_FIRST)
        is_rows = jnp.logical_and(third >= OUT_FIRST, jnp.logical_not(is_fc))

        @pl.when(is_fc)
        def _(part=part):
            for member in range(MEMBERS):
                arrived(fc_back.at[part, member], fc_recv.at[part, member])

        @pl.when(is_rows)
        def _(part=part):
            arrived(rows_back.at[part], rows_recv.at[part])

    arrived(out_home, home_sem.at[1, 0])
    arrived(grad_home, home_sem.at[1, 1])
    arrived(vec_got.at[pl.ds(1, DEVICES - 1)], vec_sem.at[0])
    for item in [reduce_made, reduce_dh] + fc_folds + qkv_folds + moves:
        item.sent()
    proj_over_y.wait_send()
    proj_over_far.wait_send()

    @pl.when(jnp.logical_not(same_y))
    def _():
        over_y.wait_send()

    @pl.when(beside)
    def _():
        over_far.wait_send()


def backward(
    branch_all, made, grad_fc, grad_proj, proj_go, attn, qkv, row_pos, col_pos, w_heads, w_qkv,
    h_first, x_own, resid_own, dresid, vecs, sums, fc_sums,
):
    kind, high = jnp.bfloat16, jnp.float32
    _, rows, width = branch_all.shape
    length = MEMBERS * rows
    four, cols = width // MEMBERS, qkv.shape[1]
    unit, hidden = four // 4, fc_sums.shape[1]
    per_part = SLOTS * HD
    any_space = pl.BlockSpec(memory_space=pl.ANY)
    vmem = pl.BlockSpec(memory_space=pltpu.VMEM)
    dma = pltpu.SemaphoreType.DMA

    def like(*shape, dtype=kind):
        return jax.ShapeDtypeStruct(shape, dtype)

    def buffer(*shape, dtype=kind):
        return pltpu.VMEM(shape, dtype)

    used = -(-width // MEMBERS // 128) * 128
    return pl.pallas_call(
        backward_kernel,
        out_shape=[
            like(width, rows),
            like(width, rows),
            like(MEMBERS, 2, four, cols // 2),
            like(3, MEMBERS, unit, hidden),
            like(3, four, width),
            like(8, used, dtype=high),
        ],
        in_specs=[any_space] * 4 + [vmem] * 6 + [any_space] * 2 + [vmem] * 6,
        out_specs=[any_space] * 5 + [vmem],
        scratch_shapes=[
            buffer(MEMBERS, rows, width),
            buffer(SLOTS // 2, length, 2 * HD),
            buffer(length, cols),
            buffer(length, 2 * HD, dtype=high),
            buffer(length, 2 * HD, dtype=high),
            buffer(*w_qkv.shape),
            buffer(*h_first.shape),
            buffer(MEMBERS, rows, width),
            buffer(MEMBERS // 2, rows, width),
            buffer(width, rows),
            buffer(2, 2, 4, unit, hidden),
            buffer(four, width),
            buffer(2, MEMBERS, four, cols // 2),
            buffer(per_part, width, dtype=high),
            buffer(four, width),
            buffer(width, rows),
            buffer(16, width, dtype=high),
            buffer(DEVICES, 8, used, dtype=high),
            buffer(DEVICES, 8, used, dtype=high),
        ]
        + [
            buffer(2, 2, 4, unit, hidden), buffer(four, width),
            buffer(2, 2, 2, four, cols // 2), buffer(four, width),
            buffer(2, 4, unit, hidden), buffer(2, 2, four, cols // 2), buffer(four, width),
        ]
        + [
            buffer(2, 4, unit, hidden), buffer(four, width), buffer(2, 2, four, cols // 2),
            buffer(four, width),
        ]
        * 2
        + reduce_buffers(rows, width)
        + reduce_buffers(rows, width)
        + [
            dma((12,)),
            dma((2, 15)),
            dma((2, 2)),
            dma((2,)),
            dma((2, 2)),
            dma((2, 2)),
            dma((8, 2)),
            dma((2, 4)),
            dma((3, 8)),
            dma((2,)),
            dma((3,)),
        ],
        compiler_params=pltpu.CompilerParams(
            collective_id=2, has_side_effects=True, vmem_limit_bytes=VMEM_BYTES
        ),
        name="backward",
    )(
        branch_all, made, grad_fc, grad_proj, proj_go, attn, qkv, row_pos, col_pos, w_heads, w_qkv,
        h_first, x_own, resid_own, dresid, vecs, sums, fc_sums,
    )


def lane_of(shape):
    return lax.broadcasted_iota(jnp.int32, shape, 1) // HD


def dot_nt(a, b):
    return lax.dot_general(a, b, (((1,), (1,)), ((), ())), preferred_element_type=jnp.float32)


def dot_tn(a, b):
    return lax.dot_general(a, b, (((0,), (0,)), ((), ())), preferred_element_type=jnp.float32)


def probabilities(query, keys, row_pos, col_pos):
    scores = dot_nt(query, keys) * 0.125
    scores = jnp.where(col_pos <= row_pos, scores, -1e30)
    weights = jnp.exp(scores - jnp.max(scores, -1, keepdims=True))
    return weights / jnp.sum(weights, -1, keepdims=True)


def head_place(head):
    member = max(m for m in range(MEMBERS) if head_start(m) <= head)
    return member, head - head_start(member)


def unlay_qkv(flat, tiles, back):
    count = back.shape[2] // 2
    each = 3 * SLOTS // 2
    for member in range(MEMBERS):
        for pair in range(SLOTS // 2):
            for part in range(3):
                tiles[member * each + 3 * pair + part] = wide(
                    back[member, pair, :, 128 * part : 128 * part + 128]
                )
    halves = 3 * HEADS

    def half(index, lane):
        odd, at = divmod(index, halves)
        part, head = divmod(at, HEADS)
        member, slot = head_place(head)
        tile = member * each + 3 * (slot // 2) + part
        return piece(
            lambda _: tiles[tile, pl.ds(odd, count, stride=2), :], HD * (slot % 2), lane, HD
        )

    for row in range(halves):
        flat[pl.ds(row, count, stride=halves), :] = join(
            [(0, half(2 * row, 0)), (HD, half(2 * row + 1, HD))]
        )


def unlay_fc(flat, first, tiles, back, part):
    count, hidden = back.shape[-2:]
    each = -(-hidden // 128)
    for member in range(MEMBERS):
        for tile in range(each):
            size = min(128, hidden - 128 * tile)
            tiles[member * each + tile, :count, :size] = wide(
                back[part, member, :, 128 * tile : 128 * tile + size]
            )
    stride, block = FF // 128, hidden // GROUPS
    for row in range(stride):
        parts, col = [], 128 * row
        while col < 128 * row + 128:
            unit, inside = divmod(col, block)
            size = min(block - inside, 128 * row + 128 - col)
            member, which = HOLDER[unit]
            lane = col - 128 * row
            value = piece(
                lambda t, m=member: tiles[m * each + t, :count, :],
                block * which + inside, lane, size,
            )
            parts.append((lane, value))
            col += size
        flat[pl.ds(first + row, count, stride=stride), :] = join(parts)


def unlay_rows(flat, first, tiles, back, part):
    count, width = back.shape[1] // 2, back.shape[2]
    for tile in range(-(-width // 128)):
        size = min(128, width - 128 * tile)
        tiles[tile, :, :size] = wide(back[part, :, 128 * tile : 128 * tile + size])
    halves = width // HD

    def half(index, lane):
        odd, at = divmod(index, halves)
        return piece(
            lambda t: tiles[t, pl.ds(odd, count, stride=2), :], HD * at, lane, HD
        )

    for row in range(halves):
        flat[pl.ds(first + row, count, stride=halves), :] = join(
            [(0, half(2 * row, 0)), (HD, half(2 * row + 1, HD))]
        )


def update_kernel(
    qkv_in, fc_in, rows_in, vec_back, vectors, first_vec, second_vec,
    weights, first, second,
    moment_vec, squares_vec, new_vec, moment, squares, new,
    flat, tiles, qkv_back, fc_back, rows_back, sem,
):
    step = pl.program_id(0)
    linear = lax.axis_index("fsdp") * MEMBERS + lax.axis_index("ctx")

    @pl.when(step == 0)
    def _():
        rows, cols = vectors.shape
        result = adamw(
            vectors[...], vec_back[:rows, :cols], first_vec[...], second_vec[...],
            rate_vector, 0.0,
        )
        moment_vec[...], squares_vec[...], new_vec[...] = result

        @pl.when(linear < MEMBERS)
        def _():
            copy = pltpu.make_async_copy(qkv_in, qkv_back, sem.at[0])
            copy.start()
            copy.wait()
            unlay_qkv(flat, tiles, qkv_back)

        @pl.when(linear >= MEMBERS)
        def _():
            copies = [
                pltpu.make_async_copy(fc_in, fc_back, sem.at[0]),
                pltpu.make_async_copy(rows_in, rows_back, sem.at[1]),
            ]
            for copy in copies:
                copy.start()
            for copy in copies:
                copy.wait()
            third_rows = fc_back.shape[2] * FF // 128
            for part in range(3):
                third = 3 * linear + part
                is_fc = jnp.logical_and(third >= FC_FIRST, third < PROJ_FIRST)

                @pl.when(is_fc)
                def _(part=part):
                    unlay_fc(flat, part * third_rows, tiles, fc_back, part)

                @pl.when(jnp.logical_not(is_fc))
                def _(part=part):
                    unlay_rows(flat, part * third_rows, tiles, rows_back, part)

    size = weights.shape[0]
    grad = flat[pl.ds(pl.multiple_of(step * size, 8), size), :]
    result = adamw(weights[...], grad, first[...], second[...], rate_matrix, weight_decay)
    moment[...], squares[...], new[...] = result


def update(
    qkv_back, fc_back, rows_back, vec_back, vectors, first_vec, second_vec,
    weights, first, second,
):
    high = jnp.float32
    local = weights.shape[0]
    steps = 10
    size = -(-local // (16 * steps)) * 16
    block = pl.BlockSpec((size, 128), lambda i: (i, 0))
    any_space = pl.BlockSpec(memory_space=pl.ANY)
    vmem = pl.BlockSpec(memory_space=pltpu.VMEM)
    kind = jax.ShapeDtypeStruct((local, 128), high)
    small = jax.ShapeDtypeStruct(vectors.shape, high)
    tile_count = MEMBERS * max(3 * SLOTS // 2, -(-fc_back.shape[3] // 128))
    return pl.pallas_call(
        update_kernel,
        grid=(steps,),
        in_specs=[any_space] * 3 + [vmem] * 4 + [block] * 3,
        out_specs=[vmem] * 3 + [block] * 3,
        out_shape=[small] * 3 + [kind] * 3,
        scratch_shapes=[
            pltpu.VMEM((size * steps, 128), high),
            pltpu.VMEM((tile_count, qkv_back.shape[2], 128), high),
            pltpu.VMEM(qkv_back.shape, qkv_back.dtype),
            pltpu.VMEM(fc_back.shape, fc_back.dtype),
            pltpu.VMEM(rows_back.shape, rows_back.dtype),
            pltpu.SemaphoreType.DMA((2,)),
        ],
        compiler_params=pltpu.CompilerParams(vmem_limit_bytes=VMEM_BYTES),
        name="update",
    )(
        qkv_back, fc_back, rows_back, vec_back, vectors, first_vec, second_vec, weights, first,
        second,
    )


def per_device_groups(
    inputs, cotangent, slot_order, weights, vectors, first_w, second_w, first_vec, second_vec
):
    _, rows, width = inputs.shape
    length = rows * MEMBERS
    (
        back_all, vecs, row_pos, col_pos, own_qkv, h_first, qkv, attn, own_fc, own_proj, w_heads,
        x_own, resid_own, h_second,
    ) = forward(
        inputs[0].T, cotangent[0].T, slot_order, vectors, weights
    )
    grad_fc, grad_proj, proj_go, made, dresid, branch_all, sums, fc_sums = middle(
        h_second.reshape(length, width), back_all.reshape(length, width), vecs, resid_own,
        own_fc, own_proj,
    )
    out_home, grad_home, qkv_back, fc_back, rows_back, vec_back = backward(
        branch_all, made, grad_fc.reshape((2, 2, 2, 4) + grad_fc.shape[1:]), grad_proj, proj_go,
        attn, qkv, row_pos, col_pos, w_heads, own_qkv, h_first, x_own, resid_own, dresid, vecs,
        sums, fc_sums,
    )
    new = update(
        qkv_back, fc_back, rows_back, vec_back, vectors, first_vec, second_vec, weights,
        first_w, second_w,
    )
    moment_vec, squares_vec, new_vec, moment_w, squares_w, new_w = new
    return (
        out_home.T[None], grad_home.T[None], moment_w, squares_w, new_w, moment_vec, squares_vec, new_vec
    )


def solution(mesh):
    in_specs = (
        P("fsdp", "ctx", None),
        P("fsdp", "ctx", None),
        P("fsdp", None),
        P(("fsdp", "ctx"), None),
        P("fsdp", "ctx"),
        P(("fsdp", "ctx"), None),
        P(("fsdp", "ctx"), None),
        P("fsdp", "ctx"),
        P("fsdp", "ctx"),
    )
    out_specs = (
        P("fsdp", "ctx", None),
        P("fsdp", "ctx", None),
        P(("fsdp", "ctx"), None),
        P(("fsdp", "ctx"), None),
        P(("fsdp", "ctx"), None),
        P("fsdp", "ctx"),
        P("fsdp", "ctx"),
        P("fsdp", "ctx"),
    )
    per_device = per_device_groups if mesh.shape["ctx"] == MEMBERS else per_device_ring
    return jax.shard_map(
        per_device, mesh=mesh, in_specs=in_specs, out_specs=out_specs, check_vma=False
    )
```

```python
import jax
import jax.numpy as jnp
from jax import lax
from jax.experimental import pallas as pl
from jax.experimental.pallas import tpu as pltpu
from jax.sharding import PartitionSpec as P

HEADS = 25
HD = 64
FF = 6400
STEP = 10


epsilon_norm = 1e-05
beta_first = 0.9
beta_second = 0.999
epsilon_adam = 1e-08
weight_decay = 0.1
rate_matrix = 0.1
rate_vector = 0.8


def shifted(value, axis, steps):
    count = lax.axis_size(axis)
    pairs = [(source, (source + steps) % count) for source in range(count)]
    return lax.ppermute(value, axis, pairs)


def layer_norm(value, gain, shift):
    center = value - jnp.mean(value, -1, keepdims=True)
    spread = jnp.mean(center * center, -1, keepdims=True)
    return center * lax.rsqrt(spread + epsilon_norm) * gain + shift


def gelu_tanh(value):
    return jax.nn.gelu(value, approximate=True)


def key_positions(slot_order, first_slot, slots, block):
    groups = lax.dynamic_slice_in_dim(slot_order, first_slot, slots, 1)
    offsets = jnp.arange(block, dtype=jnp.int32)
    return (groups[:, :, None] * block + offsets).reshape(slot_order.shape[0], slots * block)


def unpack_flat(flat, width, hidden):
    flat = flat.reshape(-1)
    first_end = 3 * width * width
    second_end = 4 * width * width
    third_end = 4 * width * width + width * hidden
    return (
        flat[:first_end].reshape(width, 3 * width),
        flat[first_end:second_end].reshape(width, width),
        flat[second_end:third_end].reshape(width, hidden),
        flat[third_end:].reshape(hidden, width),
    )


def gather_params(weights, vectors):
    local = weights.reshape(1, weights.shape[0], weights.shape[1])
    part = (
        lax.all_gather(local, "fsdp", axis=0, tiled=True),
        lax.all_gather(vectors, "fsdp", axis=0, tiled=True),
    )
    return (
        lax.all_gather(part[0], "ctx", axis=1, tiled=True),
        lax.all_gather(part[1], "ctx", axis=1, tiled=True),
    )


def reduce_grads(grad_flat, grad_vec):
    part = (
        lax.psum_scatter(
            grad_flat.astype(jnp.bfloat16), "fsdp", scatter_dimension=0, tiled=True
        ).astype(jnp.float32),
        lax.psum_scatter(
            grad_vec.astype(jnp.bfloat16), "fsdp", scatter_dimension=0, tiled=True
        ).astype(jnp.float32),
    )
    return (
        lax.psum_scatter(
            part[0].astype(jnp.bfloat16), "ctx", scatter_dimension=1, tiled=True
        ).astype(jnp.float32),
        lax.psum_scatter(
            part[1].astype(jnp.bfloat16), "ctx", scatter_dimension=1, tiled=True
        ).astype(jnp.float32),
    )


def pass_grads(grad_pairs):
    return shifted(grad_pairs.astype(jnp.bfloat16), "ctx", 1).astype(grad_pairs.dtype)


def adamw(weight, grad, first, second, rate, decay):
    first = beta_first * first + (1.0 - beta_first) * grad
    second = beta_second * second + (1.0 - beta_second) * grad * grad
    first_hat = first / (1.0 - beta_first**STEP)
    second_hat = second / (1.0 - beta_second**STEP)
    weight = weight.astype(jnp.float32)
    updated = weight - rate * (first_hat / (jnp.sqrt(second_hat) + epsilon_adam) + decay * weight)
    return (first, second, updated)


def per_device_ring(
    inputs, cotangent, slot_order, weights, vectors, first_w, second_w, first_vec, second_vec
):
    seqs, rows, width = inputs.shape
    tokens = seqs * rows
    block = rows // 2
    cycle = lax.axis_size("ctx")
    shards = lax.axis_size("fsdp")
    me = lax.axis_index("ctx")
    full_flat, full_vec = gather_params(weights, vectors)
    full_qkv, full_out, full_fc, full_proj = unpack_flat(full_flat, width, FF)
    vec = full_vec.astype(jnp.float32)
    bias_fc = vec[8:].reshape(-1)
    x_in = inputs.reshape(tokens, width).astype(jnp.float32)
    h_first, pull_first = jax.vjp(layer_norm, x_in, vec[0], vec[1])
    h_first_b = h_first.astype(jnp.bfloat16)
    zero_row = jnp.zeros((width,), jnp.float32)
    qkv = jnp.dot(h_first_b, full_qkv, preferred_element_type=jnp.float32)
    qkv_b = (qkv + jnp.concatenate([vec[2], zero_row, vec[3]])).astype(jnp.bfloat16)
    query_heads = qkv_b[:, :width].reshape(seqs, rows, HEADS, HD)
    key_value = qkv_b[:, width:].reshape(seqs, rows, 2, width)
    query_pos = key_positions(slot_order, 2 * me, 2, block)

    def online(state, item):
        top, total, accum = state
        keys_i, values_i, pos_i = item
        scores = (
            jnp.einsum("sqhd,skhd->shqk", query_heads, keys_i, preferred_element_type=jnp.float32)
            * 0.125
        )
        allowed = pos_i[:, None, None, :] <= query_pos[:, None, :, None]
        scores = jnp.where(allowed, scores, -1e30)
        peak = jnp.maximum(top, jnp.max(scores, -1))
        weights_p = jnp.where(allowed, jnp.exp(scores - peak[..., None]), 0.0)
        factor = jnp.exp(top - peak)
        total = total * factor + jnp.sum(weights_p, -1)
        mixed = jnp.einsum(
            "shqk,skhd->sqhd",
            weights_p.astype(jnp.bfloat16),
            values_i,
            preferred_element_type=jnp.float32,
        )
        accum = accum * jnp.transpose(factor, (0, 2, 1))[..., None] + mixed
        return ((peak, total, accum), None)

    start_state = (
        jnp.full((seqs, HEADS, rows), -1e30, jnp.float32),
        jnp.zeros((seqs, HEADS, rows), jnp.float32),
        jnp.zeros((seqs, rows, HEADS, HD), jnp.float32),
    )
    state = start_state
    piece = lax.all_gather(key_value, "ctx", axis=1, tiled=True)
    count = piece.shape[1]
    turns = count // rows
    pos_all = key_positions(slot_order, jnp.int32(0) // block, count // block, block)
    stack = piece.reshape(seqs, turns, rows, 2, HEADS, HD).transpose(1, 0, 2, 3, 4, 5)
    pos_stack = pos_all.reshape(seqs, turns, rows).transpose(1, 0, 2)
    state, _ = lax.scan(online, state, (stack[:, :, :, 0], stack[:, :, :, 1], pos_stack))
    top, total, accum = state
    attn = accum / jnp.transpose(total, (0, 2, 1))[..., None]
    logsum = top + jnp.log(total)
    attn_b = attn.reshape(tokens, width).astype(jnp.bfloat16)
    resid = x_in + jnp.dot(attn_b, full_out, preferred_element_type=jnp.float32) + vec[4]
    h_second, pull_second = jax.vjp(layer_norm, resid, vec[5], vec[6])
    h_second_b = h_second.astype(jnp.bfloat16)
    pre = jnp.dot(h_second_b, full_fc, preferred_element_type=jnp.float32) + bias_fc
    act, pull_gelu = jax.vjp(gelu_tanh, pre)
    act_b = act.astype(jnp.bfloat16)
    result = resid + jnp.dot(act_b, full_proj, preferred_element_type=jnp.float32) + vec[7]
    outputs = result.astype(jnp.bfloat16).reshape(seqs, rows, width)
    back_b = cotangent.reshape(tokens, width)
    back = back_b.astype(jnp.float32)
    grad_proj = jnp.einsum("tf,td->fd", act_b, back_b, preferred_element_type=jnp.float32)
    grad_bp = jnp.sum(back, 0)
    dact = jnp.einsum("td,fd->tf", back_b, full_proj, preferred_element_type=jnp.float32)
    dpre_b = pull_gelu(dact)[0].astype(jnp.bfloat16)
    grad_fc = jnp.einsum("td,tf->df", h_second_b, dpre_b, preferred_element_type=jnp.float32)
    grad_bf = jnp.sum(dpre_b, 0, dtype=jnp.float32)
    dh_second = jnp.einsum("tf,df->td", dpre_b, full_fc, preferred_element_type=jnp.float32)
    dres_ln, grad_g2, grad_b2 = pull_second(dh_second)
    dresid = back + dres_ln
    dbranch_b = dresid.astype(jnp.bfloat16)
    grad_bo = jnp.sum(dbranch_b, 0, dtype=jnp.float32)
    grad_out = jnp.einsum("td,te->de", attn_b, dbranch_b, preferred_element_type=jnp.float32)
    dattn_b = jnp.einsum(
        "te,de->td", dbranch_b, full_out, preferred_element_type=jnp.float32
    ).astype(jnp.bfloat16)
    grad_heads = dattn_b.reshape(seqs, rows, HEADS, HD)
    delta = jnp.transpose(jnp.sum(grad_heads.astype(jnp.float32) * attn, -1), (0, 2, 1))

    def contribute(pair, source):
        pos_k = key_positions(slot_order, 2 * source, 2, block)
        key_h = pair[:, :, 0].reshape(seqs, rows, HEADS, HD)
        value_h = pair[:, :, 1].reshape(seqs, rows, HEADS, HD)
        scores = (
            jnp.einsum("sqhd,skhd->shqk", query_heads, key_h, preferred_element_type=jnp.float32)
            * 0.125
        )
        allowed = pos_k[:, None, None, :] <= query_pos[:, None, :, None]
        probs = jnp.where(allowed, jnp.exp(scores - logsum[..., None]), 0.0)
        dvalue = jnp.einsum(
            "shqk,sqhd->skhd",
            probs.astype(jnp.bfloat16),
            grad_heads,
            preferred_element_type=jnp.float32,
        )
        dprobs = jnp.einsum(
            "sqhd,skhd->shqk", grad_heads, value_h, preferred_element_type=jnp.float32
        )
        dscores = (probs * (dprobs - delta[..., None])).astype(jnp.bfloat16)
        dquery = (
            jnp.einsum("shqk,skhd->sqhd", dscores, key_h, preferred_element_type=jnp.float32)
            * 0.125
        )
        dkey = (
            jnp.einsum("shqk,sqhd->skhd", dscores, query_heads, preferred_element_type=jnp.float32)
            * 0.125
        )
        return (dquery, jnp.stack((dkey, dvalue), 2))

    dq_own, dkv_own = contribute(key_value, me)

    def turn(step, state):
        pair, dkv_acc, dq_acc = state
        pair = shifted(pair, "ctx", 1)
        dkv_acc = pass_grads(dkv_acc)
        source = (me - step) % cycle
        dq_part, dkv_part = contribute(pair, source)
        return (pair, dkv_acc + dkv_part, dq_acc + dq_part)

    final = lax.fori_loop(1, cycle, turn, (key_value, dkv_own, dq_own))
    dkv = pass_grads(final[1])
    dqkv_b = jnp.concatenate(
        [final[2].reshape(tokens, width), dkv.reshape(tokens, 2 * width)], 1
    ).astype(jnp.bfloat16)
    grad_qkv = jnp.einsum("td,te->de", h_first_b, dqkv_b, preferred_element_type=jnp.float32)
    bias_sums = jnp.sum(dqkv_b, 0, dtype=jnp.float32)
    dh_first = jnp.einsum("te,de->td", dqkv_b, full_qkv, preferred_element_type=jnp.float32)
    dx_ln, grad_g1, grad_b1 = pull_first(dh_first)
    input_grad = (dresid + dx_ln).astype(jnp.bfloat16).reshape(seqs, rows, width)
    grad_vec = jnp.concatenate(
        [
            jnp.stack(
                [
                    grad_g1,
                    grad_b1,
                    bias_sums[:width],
                    bias_sums[2 * width :],
                    grad_bo,
                    grad_g2,
                    grad_b2,
                    grad_bp,
                ]
            ),
            grad_bf.reshape(-1, width),
        ],
        0,
    )
    grad_flat = jnp.concatenate(
        [grad_qkv.reshape(-1), grad_out.reshape(-1), grad_fc.reshape(-1), grad_proj.reshape(-1)]
    ).reshape(shards, -1, 128)
    owned_flat, owned_vec = reduce_grads(grad_flat, grad_vec)
    owned_flat = owned_flat.reshape(weights.shape[0], 128)
    new_w = adamw(weights, owned_flat, first_w, second_w, rate_matrix, weight_decay)
    new_vec = adamw(vectors, owned_vec, first_vec, second_vec, rate_vector, 0.0)
    return (outputs, input_grad, new_w[0], new_w[1], new_w[2], new_vec[0], new_vec[1], new_vec[2])


MEMBERS = 8
GROUPS = 4
DEVICES = MEMBERS * GROUPS
MESH = pl.DeviceIdType.MESH
BLOCK = 64
SLOTS = 4
VMEM_BYTES = 60 * 1024 * 1024
OUT_FIRST = 24
FC_FIRST = 32
PROJ_FIRST = 64


def head_start(member):
    return HEADS * member // MEMBERS


class Place:
    def __init__(self):
        self.fsdp, self.ctx = lax.axis_index("fsdp"), lax.axis_index("ctx")
        self.x, self.core = self.fsdp // 2, self.fsdp % 2
        self.far, self.near, self.y = self.ctx // 4, self.ctx // 2 % 2, self.ctx % 2
        self.me = self.member()
        self.group = 2 * self.y + self.far
        self.linear = self.fsdp * MEMBERS + self.ctx

    def member(self, x=None, near=None, core=None):
        x = self.x if x is None else x
        near = self.near if near is None else near
        core = self.core if core is None else core
        return 4 * core + 2 * near + x

    def target(self, x=None, core=None, far=None, near=None, y=None):
        x = self.x if x is None else x
        near = self.near if near is None else near
        core = self.core if core is None else core
        far = self.far if far is None else far
        y = self.y if y is None else y
        return (2 * x + core, 4 * far + 2 * near + y)

    def group_home(self):
        x, core, far, near, y = self.x, self.core, self.far, self.near, self.y
        new_x = (y + far + core) % 2
        target = self.target(x=new_x, core=far, far=core, y=(x + core) % 2)
        return target, 4 * far + 2 * near + new_x

    def shard_home(self):
        x, core, far, y = self.x, self.core, self.far, self.y
        return self.target(x=(y + far) % 2, core=far, far=core, y=(x + core + far) % 2)

    def is_me(self, target):
        return jnp.logical_and(target[0] == self.fsdp, target[1] == self.ctx)


def greet_all(place):
    barrier = pltpu.get_barrier_semaphore()

    def one(step, carry):
        other = (place.linear + step) % DEVICES
        pl.semaphore_signal(
            barrier, inc=1, device_id=(other // MEMBERS, other % MEMBERS), device_id_type=MESH
        )
        return carry

    lax.fori_loop(1, DEVICES, one, 0)
    pl.semaphore_wait(barrier, DEVICES - 1)


def greet(targets):
    barrier = pltpu.get_barrier_semaphore()
    for target in targets:
        pl.semaphore_signal(barrier, inc=1, device_id=target, device_id_type=MESH)
    pl.semaphore_wait(barrier, len(targets))


def remote(source, landing, sems, index, target):
    return pltpu.make_async_remote_copy(
        src_ref=source,
        dst_ref=landing,
        send_sem=sems.at[0, index],
        recv_sem=sems.at[1, index],
        device_id=target,
        device_id_type=MESH,
    )


def arrived(landing, sem):
    pltpu.make_async_copy(landing, landing, sem).wait()


class Move:
    def __init__(self, place, source, landing, send_sem, recv_sem, target, valid=None):
        here = place.is_me(target)
        away = jnp.logical_not(here)
        if valid is not None:
            here, away = jnp.logical_and(here, valid), jnp.logical_and(away, valid)
        self.away = away
        self.copy = pltpu.make_async_remote_copy(
            src_ref=source,
            dst_ref=landing,
            send_sem=send_sem,
            recv_sem=recv_sem,
            device_id=target,
            device_id_type=MESH,
        )

        @pl.when(here)
        def _():
            pltpu.make_async_copy(source, landing, recv_sem).start()

        @pl.when(away)
        def _():
            self.copy.start()

    def sent(self):
        @pl.when(self.away)
        def _():
            self.copy.wait_send()


class Gather:
    def __init__(self, place, out, sems, near_first=False):
        p = place
        step, turn = (0, 1) if near_first else (1 - p.core, p.core)
        x1, near1 = p.x + step * (1 - 2 * p.x), p.near + turn * (1 - 2 * p.near)
        x2, near2 = p.x + turn * (1 - 2 * p.x), p.near + step * (1 - 2 * p.near)
        self.out, self.sems, self.me = out, sems, p.me
        self.first = p.target(x=x1, near=near1)
        self.second = p.target(x=x2, near=near2)
        self.other = p.target(core=1 - p.core)
        self.of_first = p.member(x=x1, near=near1)
        self.of_second = p.member(x=x2, near=near2)
        self.of_both = p.member(x=1 - p.x, near=1 - p.near)
        self.copies = {}

    def _go(self, name, index, block, target):
        item = remote(self.out.at[block], self.out.at[block], self.sems, index, target)
        item.start()
        self.copies[name] = item

    def begin(self):
        self._go("a", 0, self.me, self.first)
        self._go("b", 1, self.me, self.second)
        self._go("c", 2, self.me, self.other)

    def begin_from(self, own):
        for name, index, target in (
            ("a", 0, self.first), ("b", 1, self.second), ("c", 2, self.other),
        ):
            item = remote(own, self.out.at[self.me], self.sems, index, target)
            item.start()
            self.copies[name] = item

    def second_hop(self):
        self.copies["a"].wait_recv()
        self._go("d", 3, self.of_first, self.second)
        self._go("e", 4, self.of_first, self.other)

    def third_hop(self):
        self.copies["b"].wait_recv()
        self._go("f", 5, self.of_second, self.other)

    def last_hop(self):
        self.copies["d"].wait_recv()
        self._go("g", 6, self.of_both, self.other)

    def finish(self):
        for name in "cefg":
            self.copies[name].wait_recv()
        for item in self.copies.values():
            item.wait_send()


class Spread:
    def __init__(self, place, at, sems, first, source=None):
        p = place
        self.at, self.sems, self.first = at, sems, first
        self.mine, self.theirs = at(p.far, p.y), at(1 - p.far, p.y)
        self.source = self.mine if source is None else source
        self.to_far, self.to_y = p.target(far=1 - p.far), p.target(y=1 - p.y)

    def begin(self):
        self.a = remote(self.source, self.mine, self.sems, self.first, self.to_far)
        self.b = remote(self.source, self.mine, self.sems, self.first + 1, self.to_y)
        self.a.start()
        self.b.start()

    def middle(self):
        self.a.wait_recv()
        self.c = remote(self.theirs, self.theirs, self.sems, self.first + 2, self.to_y)
        self.c.start()

    def finish(self):
        self.b.wait_recv()
        self.c.wait_recv()
        for item in (self.a, self.b, self.c):
            item.wait_send()


def shard_of(third):
    shard = third // 3
    return (shard // MEMBERS, shard % MEMBERS), third % 3


def lookup(table, index):
    result = 0
    for place, entry in enumerate(table):
        if entry:
            result = result + jnp.where(index == place, entry, 0)
    return result


FC_OF_GROUP = (
    (0, 1, 16, 17, 18, 22, 23, 24),
    (2, 3, 19, 20, 21, 25, 26, 27),
    (4, 5, 6, 10, 11, 12, 28, 29),
    (7, 8, 9, 13, 14, 15, 30, 31),
)
FC_SLOT = [0] * 32
FC_Y = [0] * 32
for _group, _units in enumerate(FC_OF_GROUP):
    for _slot, _unit in enumerate(_units):
        FC_SLOT[_unit] = _slot
        FC_Y[_unit] = _group % 2


def fc_unit(far, y, slot):
    return lookup([units[slot] for units in FC_OF_GROUP], 2 * far + y)


def fc_home(place, unit):
    return lookup(FC_SLOT, unit), lookup(FC_Y, unit)


PROJ_OF_CTX = (
    (8, 9, 10, 3),
    (11, 12, 13, 6),
    (14, 15, 16, 2),
    (17, 18, 19, 5),
    (20, 21, 22, 0),
    (1, 23, 24, 25),
    (4, 26, 27, 28),
    (7, 29, 30, 31),
)


def hidden_of(member):
    core, near, x = member // 4, member // 2 % 2, member % 2
    return [
        PROJ_OF_CTX[4 * far + 2 * near + y][2 * core + x] for y in range(2) for far in range(2)
    ]


HIDDEN = [hidden_of(_member) for _member in range(8)]
HOLDER = {unit: (m, i) for m, units in enumerate(HIDDEN) for i, unit in enumerate(units)}
PROJ_FSDP, PROJ_CTX = [0] * 32, [0] * 32
PROJ_UNIT = [0] * 32
for _ctx, _units in enumerate(PROJ_OF_CTX):
    for _place, _unit in enumerate(_units):
        _fsdp = 2 * (_place % 2) + _place // 2
        PROJ_FSDP[_unit], PROJ_CTX[_unit] = _fsdp, _ctx
        PROJ_UNIT[8 * _fsdp + _ctx] = _unit
FC_POSITION = [0] * 32
for _group, _units in enumerate(FC_OF_GROUP):
    for _slot, _unit in enumerate(_units):
        FC_POSITION[_unit] = 8 * _group + _slot


def piece(tile_of, col, lane, size):
    start = col % 128
    value = tile_of(col // 128)
    if start + size > 128:
        lanes = lax.broadcasted_iota(jnp.int32, value.shape, 1)
        value = jnp.where(lanes < start, tile_of(col // 128 + 1), value)
    shift = (lane - start) % 128
    return pltpu.roll(value, shift, 1) if shift else value


def join(parts):
    result = parts[0][1]
    for lane, value in parts[1:]:
        lanes = lax.broadcasted_iota(jnp.int32, value.shape, 1)
        result = jnp.where(lanes < lane, result, value)
    return result


def out_root(member):
    return jnp.where(member // 3 == 1, 1, 0)


def half_tile(flat, first, count, stride, half):
    at = half // 2
    tile = flat[pl.ds(first + at, count, stride=stride), :]
    if half % 2 == 0:
        return tile
    after = flat[pl.ds(first + at + 1, count, stride=stride), :]
    lane = lax.broadcasted_iota(jnp.int32, tile.shape, 1)
    return pltpu.roll(jnp.where(lane < HD, after, tile), HD, 1)


def lay_qkv(flat, rows, pieces, member, pair):
    count = rows.shape[1] // 2
    halves = 3 * HEADS
    for part in range(3):
        for odd in range(2):
            half = halves * odd + HEADS * part + head_start(member) + 2 * pair
            rows[part, pl.ds(odd, count, stride=2), :] = half_tile(flat, 0, count, halves, half)
    for part in range(3):
        pieces[pair, member, :, 128 * part : 128 * part + 128] = rows[part].astype(jnp.bfloat16)


def lay_fc(flat, first, pieces, part):
    count, hidden = pieces.shape[-2:]
    stride = FF // 128
    block = hidden // GROUPS

    def tile_of(tile):
        return flat[pl.ds(first + tile, count, stride=stride), :]

    for member in range(MEMBERS):
        for tile in range(-(-hidden // 128)):
            size = min(128, hidden - 128 * tile)
            parts, at = [], 128 * tile
            while at < 128 * tile + size:
                which, inside = divmod(at, block)
                length = min(block - inside, 128 * tile + size - at)
                col = block * HIDDEN[member][which] + inside
                parts.append((at - 128 * tile, piece(tile_of, col, at - 128 * tile, length)))
                at += length
            pieces[part, member, :, 128 * tile : 128 * tile + size] = join(parts)[
                :, :size
            ].astype(jnp.bfloat16)


def lay_rows(flat, first, rows, blocks, part):
    count = rows.shape[1] // 2
    width = blocks.shape[-1]
    halves = width // HD
    for odd in range(2):
        for tile in range(-(-width // 128)):
            half = halves * odd + 2 * tile
            size = min(128, width - 128 * tile)
            if size == 128 or half % 2 == 0:
                value = half_tile(flat, first, count, halves, half)
            else:
                value = pltpu.roll(
                    flat[pl.ds(first + half // 2, count, stride=halves), :], HD, 1
                )
            rows[tile, pl.ds(odd, count, stride=2), :] = value
    for tile in range(-(-width // 128)):
        size = min(128, width - 128 * tile)
        blocks[part, :, 128 * tile : 128 * tile + size] = rows[tile, :, :size].astype(
            jnp.bfloat16
        )


def wide(value):
    return value.astype(jnp.float32)


def low(value):
    return value.astype(jnp.bfloat16)


def turn(value, target):
    rows, cols = value.shape
    for first in range(0, rows, 128):
        for lane in range(0, cols, 128):
            part = value[first : first + 128, lane : lane + 128]
            target[lane : lane + 128, first : first + 128] = low(wide(part).T)


def store_halves(target, block, value):
    some = target.shape[2]
    for place in range(2):
        for half in range(2):
            first = (2 * place + half) * some
            target[half, block + place] = value[first : first + some]


def half_of(blocks, core):
    return blocks.at[pl.ds(4 * core, 4)]


class Reduce:
    def __init__(
        self, place, away, kept, from_core, two, got, last, done, sems, near_first=False
    ):
        self.p, self.away, self.kept, self.from_core = place, away, kept, from_core
        self.two, self.got, self.last, self.done, self.sems = two, got, last, done, sems
        self.route = Gather(place, None, None, near_first)
        self.copies = []

    def _go(self, source, landing, index, target):
        item = remote(source, landing, self.sems, index, target)
        item.start()
        self.copies.append(item)
        return item

    def begin(self):
        for j in (3, 2, 1, 0):
            self._go(self.away.at[j], self.from_core.at[j], j, self.route.other)

    def _summed(self, member):
        block = member - 4 * self.p.core
        return wide(self.kept[block]) + wide(self.from_core[block])

    def second(self):
        for item in self.copies[:4]:
            item.wait_recv()
        self.two[0] = low(self._summed(self.route.of_both))
        self.across = self._go(self.two.at[0], self.got.at[0], 4, self.route.second)
        self.two[1] = low(self._summed(self.route.of_second))
        self.beyond = self._go(self.two.at[1], self.got.at[1], 5, self.route.second)

    def third(self):
        self.across.wait_recv()
        self.last[...] = low(self._summed(self.route.of_first) + wide(self.got[0]))
        self.final = self._go(self.last, self.done, 6, self.route.first)

    def result(self):
        self.beyond.wait_recv()
        value = self._summed(self.p.me) + wide(self.got[1])
        self.final.wait_recv()
        return value + wide(self.done[...])

    def sent(self):
        for item in self.copies:
            item.wait_send()


def reduce_buffers(rows, width):
    kind = jnp.bfloat16
    return [
        pltpu.VMEM((4, rows, width), kind),
        pltpu.VMEM((2, rows, width), kind),
        pltpu.VMEM((2, rows, width), kind),
        pltpu.VMEM((rows, width), kind),
        pltpu.VMEM((rows, width), kind),
        pltpu.SemaphoreType.DMA((2, 7)),
    ]


def norm_rows(value, gain, shift):
    center = value - jnp.mean(value, -1, keepdims=True)
    spread = jnp.mean(center * center, -1, keepdims=True)
    return center * lax.rsqrt(spread + epsilon_norm) * gain + shift


def head_rows(member):
    return 8 * member


def member_lanes(row, member, count):
    result = jnp.zeros((row.shape[0], count), row.dtype)
    for other in range(MEMBERS):
        first = head_start(other) * HD
        result = result + jnp.where(member == other, row[:, first : first + count], 0.0)
    return result


def attend_block(query, keys, values, row_pos, col_pos):
    lanes = lane_of(query.shape)
    result = jnp.zeros(query.shape, jnp.float32)
    for head in range(2):
        mine = lanes == head
        own = jnp.where(mine, query, jnp.zeros_like(query))
        probs = probabilities(own, keys, row_pos, col_pos)
        mixed = jnp.dot(probs.astype(jnp.bfloat16), values, preferred_element_type=jnp.float32)
        result = jnp.where(mine, mixed, result)
    return result.astype(jnp.bfloat16)


def forward_kernel(
    x_in, back_in, order_in, vec_in, weights,
    back_all, vecs, row_pos, col_pos, w_qkv_out, h_first_out, qkv_out, attn, w_fc_out, w_proj_out,
    w_heads, x_own, resid_own, h_second,
    x_all, w_qkv, h_first, qkv, w_fc, w_proj,
    flat, rows, qkv_pieces, fc_pieces, blocks, order, vec_all, qkv_land,
    fc, proj, out, fc_part, fc_mine, proj_part, out_part, tail, next_tail, window, unit_rows, h_own,
    branch, core_a, two_a, got_a, last_a, done_a, sem_a,
    core_b, two_b, got_b, last_b, done_b, sem_b,
    order_pad, vec_pad, x_rows, back_rows, move_sem, qkv_sem, fc_send, fc_recv, rows_sem, x_sem, back_sem, spread_sem,
    own_sem, fc_sem, proj_sem, tree_sem, h_sem, store_sem,
):
    p = Place()
    third_rows = weights.shape[0] // 3
    width, count = x_in.shape
    length = MEMBERS * count
    pairs = SLOTS // 2
    barrier = pltpu.get_barrier_semaphore()

    def signal(step, carry):
        other = (p.linear + step) % DEVICES
        pl.semaphore_signal(
            barrier, inc=1, device_id=(other // MEMBERS, other % MEMBERS), device_id_type=MESH
        )
        return carry

    lax.fori_loop(1, DEVICES, signal, 0)
    flat[...] = weights[...].astype(jnp.float32)
    order_pad[...] = jnp.zeros_like(order_pad)
    order_pad[0:1, : order_in.shape[1]] = order_in[...]
    vec_pad[...] = jnp.zeros_like(vec_pad)
    vec_pad[: vec_in.shape[0], : vec_in.shape[1]] = vec_in[...]
    pl.semaphore_wait(barrier, DEVICES - 1)
    home, home_member = p.group_home()
    owner = p.fsdp == 0
    qkv_moves = []
    for pair in range(pairs):
        for member in (7, 6, 3, 2, 5, 4, 1, 0):

            @pl.when(owner)
            def _(member=member, pair=pair):
                lay_qkv(flat, rows, qkv_pieces, member, pair)

            target = p.target(x=member % 2, near=member // 2 % 2, core=member // 4)
            qkv_moves.append(
                Move(
                    p, qkv_pieces.at[pair, member], qkv_land.at[pair, p.far, p.near, p.y],
                    qkv_sem.at[0, pair, member], qkv_sem.at[1, pair, p.near], target, owner,
                )
            )
    turn(x_in[...], x_rows)
    x_move = Move(p, x_rows, x_all.at[home_member], move_sem.at[0, 0], move_sem.at[1, 0], home)
    order_move = Move(p, order_pad, order, move_sem.at[0, 1], move_sem.at[1, 1], home)
    turn(back_in[...], back_rows)

    def vec_send(step, carry):
        other = (p.linear + step) % DEVICES
        pltpu.make_async_remote_copy(
            src_ref=vec_pad,
            dst_ref=vec_all.at[p.linear],
            send_sem=move_sem.at[0, 2],
            recv_sem=move_sem.at[1, 2],
            device_id=(other // MEMBERS, other % MEMBERS),
            device_id_type=MESH,
        ).start()
        return carry

    lax.fori_loop(1, DEVICES, vec_send, 0)
    pltpu.make_async_copy(vec_pad, vec_all.at[p.linear], move_sem.at[1, 2]).start()
    for part in range(3):
        third = 3 * p.linear + part
        is_fc = jnp.logical_and(third >= FC_FIRST, third < PROJ_FIRST)
        is_rows = jnp.logical_and(third >= OUT_FIRST, jnp.logical_not(is_fc))

        @pl.when(is_fc)
        def _(part=part):
            lay_fc(flat, part * third_rows, fc_pieces, part)

        @pl.when(is_rows)
        def _(part=part):
            lay_rows(flat, part * third_rows, rows, blocks, part)

    arrived(x_all.at[p.me], move_sem.at[1, 0])
    gather_x = Gather(p, x_all, x_sem, True)
    gather_x.begin()
    spreads = []

    def spread(pair):
        for near in range(2):
            arrived(qkv_land.at[pair, p.far, near, p.y], qkv_sem.at[1, pair, near])
            item = Spread(
                p, lambda far, y, near=near: qkv_land.at[pair, far, near, y],
                spread_sem, 6 * pair + 3 * near,
            )
            item.begin()
            spreads.append(item)

    spread(0)
    gather_x.second_hop()
    spread(1)
    gather_x.third_hop()
    fc_moves, rows_moves = [], []
    for part in range(3):
        third = 3 * p.linear + part
        valid = jnp.logical_and(third >= OUT_FIRST, third < FC_FIRST)
        member = jnp.where(valid, third - OUT_FIRST, 0)
        target = p.target(
            x=member % 2, near=member // 2 % 2, core=member // 4, y=out_root(member), far=0
        )
        rows_moves.append(
            Move(
                p, blocks.at[part], out_part,
                rows_sem.at[0, part], rows_sem.at[1, 1], target, valid,
            )
        )
    for part in range(3):
        third = 3 * p.linear + part
        valid = jnp.logical_and(third >= FC_FIRST, third < PROJ_FIRST)
        slot, y = fc_home(p, jnp.where(valid, third - FC_FIRST, 0))
        for member in (7, 6, 3, 2, 5, 4, 1, 0):
            target = p.target(x=member % 2, near=member // 2 % 2, core=member // 4, y=y)
            fc_moves.append(
                Move(
                    p, fc_pieces.at[part, member], fc_part.at[slot],
                    fc_send.at[part, member], fc_recv.at[slot], target, valid,
                )
            )
    for part in range(3):
        third = 3 * p.linear + part
        valid = third >= PROJ_FIRST
        unit = jnp.where(valid, third - PROJ_FIRST, 0)
        target = (lookup(PROJ_FSDP, unit), lookup(PROJ_CTX, unit))
        rows_moves.append(
            Move(
                p, blocks.at[part], proj_part,
                rows_sem.at[0, part], rows_sem.at[1, 0], target, valid,
            )
        )
    gather_x.last_hop()
    back_move = Move(p, back_rows, back_all.at[home_member], move_sem.at[0, 3], move_sem.at[1, 3], home)
    arrived(vec_all, move_sem.at[1, 2])
    cols = vec_pad.shape[-1]
    used = width // MEMBERS
    total = jnp.zeros(vecs.shape, jnp.float32)
    for ctx in range(MEMBERS):
        block = jnp.concatenate([vec_all[MEMBERS * f + ctx] for f in range(GROUPS)], 0)
        lane = lax.broadcasted_iota(jnp.int32, (cols, width), 0)
        at = lax.broadcasted_iota(jnp.int32, (cols, width), 1) - used * ctx
        spot = jnp.where(jnp.logical_and(lane == at, lane < used), 1.0, 0.0)
        total = total + jnp.dot(
            block, spot.astype(jnp.bfloat16), preferred_element_type=jnp.float32
        )
    vecs[...] = total
    arrived(order, move_sem.at[1, 1])
    slots = order[0:1, :].astype(jnp.float32)
    lane = lax.broadcasted_iota(jnp.int32, (length, 128), 1)
    row = lax.broadcasted_iota(jnp.int32, (length, 128), 0)
    each = count // BLOCK

    def slot_of(row):
        member = row // count
        turned = (member % 2 + member // 4 + p.far) % 2
        return each * (member - member % 2 + turned) + row // BLOCK % each

    spot = jnp.where(lane == slot_of(row), slots, 0.0)
    inner = lax.broadcasted_iota(jnp.int32, (length, 1), 0) % BLOCK
    row_pos[...] = jnp.sum(spot, 1, keepdims=True) * BLOCK + inner.astype(jnp.float32)
    lane = lax.broadcasted_iota(jnp.int32, (128, length), 1)
    row = lax.broadcasted_iota(jnp.int32, (128, length), 0)
    spot = jnp.where(row == slot_of(lane), 1.0, 0.0)
    inner = lax.broadcasted_iota(jnp.int32, (1, length), 1) % BLOCK
    found = jnp.dot(
        order[...].astype(jnp.bfloat16), spot.astype(jnp.bfloat16),
        preferred_element_type=jnp.float32,
    )
    col_pos[...] = found[0:1, :] * BLOCK + inner.astype(jnp.float32)
    for item in spreads[:2]:
        item.middle()
    to_far, to_y = p.target(far=1 - p.far), p.target(y=1 - p.y)
    same_y = p.y == out_root(p.me)
    root = jnp.logical_and(same_y, p.far == 0)
    beside = jnp.logical_and(same_y, p.far == 1)
    out_far = remote(out_part, out, tree_sem, 0, to_far)
    out_y = remote(out_part, out, tree_sem, 1, to_y)
    out_later = remote(out, out, tree_sem, 2, to_y)
    out_own = pltpu.make_async_copy(out_part, out, own_sem.at[8])

    @pl.when(root)
    def _():
        arrived(out_part, rows_sem.at[1, 1])
        out_far.start()
        out_y.start()
        out_own.start()

    gather_x.finish()

    def norm_block(step, carry):
        value = norm_rows(x_all[step].astype(jnp.float32), vecs[0:1, :], vecs[1:2, :])
        h_first[pl.ds(pl.multiple_of(step * count, count), count), :] = value.astype(jnp.bfloat16)
        return carry

    lax.fori_loop(0, MEMBERS, norm_block, 0)
    x_own[...] = x_all[p.me]
    stores = []

    def store(source, target):
        copy = pltpu.make_async_copy(source, target, store_sem.at[len(stores)])
        copy.start()
        stores.append(copy)

    store(h_first, h_first_out)
    four = qkv_land.shape[4]
    per_part = SLOTS * HD
    bias_q = member_lanes(vecs[2:3, :], p.me, per_part)
    bias_v = member_lanes(vecs[16:17, :], p.me, per_part)

    def project(pair):
        columns = slice(384 * pair, 384 * pair + 384)
        for item in spreads[2 * pair : 2 * pair + 2]:
            item.finish()
        for far in range(2):
            for near in range(2):
                for y in range(2):
                    first = four * (4 * far + 2 * near + y)
                    w_qkv[first : first + four, columns] = qkv_land[pair, far, near, y]
        part = slice(128 * pair, 128 * pair + 128)
        bias = jnp.concatenate(
            [bias_q[:, part], jnp.zeros((1, 128), jnp.float32), bias_v[:, part]], 1
        )

        def qkv_block(step, carry):
            at = pl.ds(pl.multiple_of(step * 2 * count, 2 * count), 2 * count)
            value = jnp.dot(
                h_first[at, :], w_qkv[:, columns], preferred_element_type=jnp.float32
            )
            qkv[at, columns] = (value + bias).astype(jnp.bfloat16)
            return carry

        lax.fori_loop(0, MEMBERS // 2, qkv_block, 0)

    project(0)
    for item in spreads[2:]:
        item.middle()

    @pl.when(beside)
    def _():
        out_far.wait_recv()
        out_later.start()

    arrived(back_all.at[p.me], move_sem.at[1, 3])
    gather_back = Gather(p, back_all, back_sem, True)
    gather_back.begin()
    fc_spreads = []
    unit = fc_part.shape[1]
    for half in range(2):
        for slot in range(4):
            arrived(fc_part.at[4 * half + slot], fc_recv.at[4 * half + slot])
            fc_mine[half, unit * slot : unit * slot + unit, :] = fc_part[4 * half + slot]
        item = Spread(
            p, lambda far, y, half=half: fc.at[far, y, half], fc_sem, 3 * half, fc_mine.at[half]
        )
        item.begin()
        fc_spreads.append(item)
    span = 2 * count

    def one_pair(pair):
        def one_block(step, carry):
            at = pl.ds(pl.multiple_of(step * span, span), span)
            attn[pair, at, :] = attend_block(
                qkv[at, 384 * pair : 384 * pair + 128],
                qkv[:, 384 * pair + 128 : 384 * pair + 256],
                qkv[:, 384 * pair + 256 : 384 * pair + 384],
                row_pos[at, :],
                col_pos[...],
            )
            return carry

        lax.fori_loop(0, length // span, one_block, 0)

    one_pair(0)
    project(1)
    gather_back.second_hop()
    gather_back.third_hop()
    arrived(proj_part, rows_sem.at[1, 0])
    my_proj, far_proj = proj.at[p.y, p.far], proj.at[p.y, 1 - p.far]
    proj_far = remote(proj_part, my_proj, proj_sem, 0, to_far)
    proj_y = remote(proj_part, my_proj, proj_sem, 1, to_y)
    proj_far.start()
    proj_y.start()
    proj_own = pltpu.make_async_copy(proj_part, my_proj, own_sem.at[9])
    proj_own.start()
    store(w_qkv, w_qkv_out)
    store(qkv, qkv_out)

    for item in fc_spreads:
        item.middle()
    one_pair(1)
    gather_back.last_hop()

    @pl.when(root)
    def _():
        out_own.wait()

    @pl.when(jnp.logical_and(jnp.logical_not(same_y), p.far == 0))
    def _():
        out_y.wait_recv()

    @pl.when(jnp.logical_and(jnp.logical_not(same_y), p.far == 1))
    def _():
        out_later.wait_recv()

    reach = tail.shape[0]
    tail[...] = out[four - reach :, :]
    following, before = (p.me + 1) % MEMBERS, (p.me + MEMBERS - 1) % MEMBERS
    to_next = p.target(
        x=following % 2, near=following // 2 % 2, core=following // 4
    )
    send_tail = remote(tail, next_tail, tree_sem, 3, to_next)
    send_tail.start()
    begin = head_rows(p.me)
    window[...] = jnp.zeros_like(window)
    window[reach : reach + four, :] = wide(out[...])
    span_rows = SLOTS * HD
    unit_rows[...] = low(window[pl.ds(pl.multiple_of(reach - begin, 8), span_rows), :])

    def one_branch(step, carry):
        at = pl.ds(pl.multiple_of(step * span, span), span)
        heads = jnp.concatenate([attn[pair, at, :] for pair in range(pairs)], 1)
        value = low(jnp.dot(heads, unit_rows[...], preferred_element_type=jnp.float32))
        store_halves(branch, 2 * step, value)
        return carry

    lax.fori_loop(0, length // span, one_branch, 0)
    reduces = [
        Reduce(
            p, half_of(branch.at[half], 1 - p.core), half_of(branch.at[half], p.core), *buffers
        )
        for half, buffers in enumerate(
            (
                (core_a, two_a, got_a, last_a, done_a, sem_a),
                (core_b, two_b, got_b, last_b, done_b, sem_b),
            )
        )
    ]
    for item in reduces:
        item.begin()
    proj_far.wait_recv()
    proj_later = remote(far_proj, far_proj, proj_sem, 2, to_y)
    proj_later.start()
    for item in reduces:
        item.second()
    for item in reduces:
        item.third()
    for item in fc_spreads:
        item.finish()
    gathers = []
    some = count // 2
    for half, item in enumerate(reduces):
        at = slice(some * half, some * half + some)
        value = wide(x_own[at, :]) + item.result() + vecs[17:18, :]
        resid_own[at, :] = value
        h_own[half] = low(norm_rows(value, vecs[18:19, :], vecs[32:33, :]))
        gather = Gather(p, h_second.at[half], h_sem.at[half])
        gather.begin_from(h_own.at[half])
        gathers.append(gather)
        store(h_own.at[half], h_second.at[half, p.me])
    for group, units in enumerate(FC_OF_GROUP):
        far, y = group // 2, group % 2
        for half in range(2):
            inside = jnp.logical_and(p.far == far, p.y == y)

            @pl.when(inside)
            def _(far=far, y=y, half=half):
                fc[far, y, half] = fc_mine[half]

            for slot in range(4):
                first = unit * units[4 * half + slot]
                w_fc[first : first + unit, :] = fc[far, y, half, unit * slot : unit * slot + unit]
    store(w_fc, w_fc_out)
    for item in gathers:
        item.second_hop()
        item.third_hop()
    proj_y.wait_recv()
    proj_later.wait_recv()
    proj_own.wait()
    for group in range(GROUPS):
        w_proj[four * group : four * group + four, :] = proj[group // 2, group % 2]
    store(w_proj, w_proj_out)
    for item in gathers:
        item.last_hop()
    send_tail.wait_recv()
    window[:reach, :] = wide(next_tail[...])
    w_heads[...] = low(window[pl.ds(pl.multiple_of(reach - begin, 8), span_rows), :])
    for item in gathers + [gather_back]:
        item.finish()
    for item in [proj_far, proj_y, proj_later, send_tail]:
        item.wait_send()
    for item in reduces:
        item.sent()

    @pl.when(root)
    def _():
        out_far.wait_send()
        out_y.wait_send()

    @pl.when(beside)
    def _():
        out_later.wait_send()

    for copy in stores:
        copy.wait()
    for item in [x_move, order_move, back_move] + qkv_moves + fc_moves + rows_moves:
        item.sent()
    arrived(vec_all.at[pl.ds(1, DEVICES - 1)], move_sem.at[0, 2])


def forward(x, back, order, vectors, weights):
    width, rows = x.shape
    kind, high = jnp.bfloat16, jnp.float32
    unit, hidden = width // DEVICES, FF // MEMBERS
    four, cols = 4 * unit, 3 * SLOTS * HD
    length, pairs = MEMBERS * rows, SLOTS // 2
    vec_cols = -(-vectors.shape[1] // 128) * 128
    any_space = pl.BlockSpec(memory_space=pl.ANY)
    vmem = pl.BlockSpec(memory_space=pltpu.VMEM)
    dma = pltpu.SemaphoreType.DMA

    def like(*shape, dtype=kind):
        return jax.ShapeDtypeStruct(shape, dtype)

    return pl.pallas_call(
        forward_kernel,
        out_shape=[
            like(MEMBERS, rows, width),
            like(GROUPS * 16, width, dtype=high),
            like(length, 1, dtype=high),
            like(1, length, dtype=high),
            like(width, cols),
            like(length, width),
            like(length, cols),
            like(pairs, length, 2 * HD),
            like(width, hidden),
            like(hidden, width),
            like(SLOTS * HD, width),
            like(rows, width),
            like(rows, width, dtype=high),
            like(2, MEMBERS, rows // 2, width),
        ],
        in_specs=[vmem] * 5,
        out_specs=[any_space] + [vmem] * 3 + [any_space] * 3 + [vmem] + [any_space] * 2
        + [vmem] * 3 + [any_space],
        scratch_shapes=[
            pltpu.VMEM((MEMBERS, rows, width), kind),
            pltpu.VMEM((width, cols), kind),
            pltpu.VMEM((length, width), kind),
            pltpu.VMEM((length, cols), kind),
            pltpu.VMEM((width, hidden), kind),
            pltpu.VMEM((hidden, width), kind),
            pltpu.VMEM(weights.shape, high),
            pltpu.VMEM((-(-width // 128), four, 128), high),
            pltpu.VMEM((pairs, MEMBERS, four, cols // pairs), kind),
            pltpu.VMEM((3, MEMBERS, unit, hidden), kind),
            pltpu.VMEM((3, four, width), kind),
            pltpu.VMEM((128, 128), order.dtype),
            pltpu.VMEM((DEVICES, 16, vec_cols), kind),
            pltpu.VMEM((pairs, 2, 2, 2, four, cols // pairs), kind),
            pltpu.VMEM((2, 2, 2, four, hidden), kind),
            pltpu.VMEM((2, 2, four, width), kind),
            pltpu.VMEM((four, width), kind),
            pltpu.VMEM((8, unit, hidden), kind),
            pltpu.VMEM((2, four, hidden), kind),
            pltpu.VMEM((four, width), kind),
            pltpu.VMEM((four, width), kind),
            pltpu.VMEM((64, width), kind),
            pltpu.VMEM((64, width), kind),
            pltpu.VMEM((64 + SLOTS * HD, width), high),
            pltpu.VMEM((SLOTS * HD, width), kind),
            pltpu.VMEM((2, rows // 2, width), kind),
            pltpu.VMEM((2, MEMBERS, rows // 2, width), kind),
        ]
        + reduce_buffers(rows // 2, width)
        + reduce_buffers(rows // 2, width)
        + [
            pltpu.VMEM((128, 128), order.dtype),
            pltpu.VMEM((16, vec_cols), kind),
            pltpu.VMEM((rows, width), kind),
            pltpu.VMEM((rows, width), kind),
            dma((2, 4)),
            dma((2, pairs, 8)),
            dma((3, 8)),
            dma((8,)),
            dma((2, 3)),
            dma((2, 7)),
            dma((2, 7)),
            dma((2, 12)),
            dma((9 + 1,)),
            dma((2, 6)),
            dma((2, 3)),
            dma((2, 4)),
            dma((2, 2, 7)),
            dma((7,)),
        ],
        compiler_params=pltpu.CompilerParams(
            collective_id=1, has_side_effects=True, vmem_limit_bytes=VMEM_BYTES
        ),
        name="forward",
    )(x, back, order, vectors, weights)


GELU_SCALE = 0.7978845608028654
GELU_CUBE = 0.044715


def store_rows(target, first, value, lanes=slice(None), at=None, unit=None):
    places = at
    size = target.shape[1] if unit is None else unit
    row = 0
    while row < value.shape[0]:
        block, at = divmod(first + row, size)
        count = min(size - at, value.shape[0] - row)
        if places is None:
            target[block, at : at + count, lanes] = low(value[row : row + count])
        else:
            four = target.shape[1]
            block, place = divmod(size * places[block], four)
            at = at + place
            target[block, at : at + count, lanes] = low(value[row : row + count])
        row += count


def middle_kernel(
    h_in, back_all, vecs, resid_own, w_fc_in, w_proj_in,
    grad_fc, proj_sum, made, dresid, branch_all, sums, fc_sums,
    h_second, back, w_fc, w_proj, act, dpre, dh_part, made_part, g_fc, g_proj,
    proj_y, proj_go, proj_far, core_a, two_a, got_a, last_a, done_a, sem_a,
    core_b, two_b, got_b, last_b, done_b, sem_b,
    load_sem, store_sem, fold_sem,
    dbranch, branch_sem,
):
    p = Place()
    length, width = h_second.shape
    count = length // MEMBERS
    hidden = act.shape[1]
    loads = []

    def load(source, target):
        copy = pltpu.make_async_copy(source, target, load_sem.at[len(loads)])
        copy.start()
        loads.append(copy)

    some = count // 2
    for member in range(MEMBERS):
        for half in range(2):
            first = count * member + some * half
            load(h_in.at[half, member], h_second.at[pl.ds(first, some)])
    load(w_fc_in, w_fc)
    load(back_all, back)
    load(w_proj_in, w_proj)
    reduces = [
        Reduce(
            p, half_of(dh_part.at[half], 1 - p.core), half_of(dh_part.at[half], p.core), *buffers
        )
        for half, buffers in enumerate(
            (
                (core_a, two_a, got_a, last_a, done_a, sem_a),
                (core_b, two_b, got_b, last_b, done_b, sem_b),
            )
        )
    ]
    route = reduces[0].route
    to_far, to_y = p.target(far=1 - p.far), p.target(y=1 - p.y)
    greet((route.first, route.second, route.other, to_far, to_y))
    bias_fc = jnp.zeros((1, hidden), jnp.float32)
    block = hidden // GROUPS
    for member in range(MEMBERS):
        parts = []
        for unit in HIDDEN[member]:
            row, first = divmod(block * unit, width)
            row = (34, 48, 49, 50)[row]
            parts.append(vecs[row : row + 1, first : first + block])
        bias_fc = bias_fc + jnp.where(p.me == member, jnp.concatenate(parts, 1), 0.0)
    fc_sums[...] = jnp.zeros_like(fc_sums)
    for copy in loads:
        copy.wait()
    span = 2 * count

    def one_block(step, carry):
        at = pl.ds(pl.multiple_of(step * span, span), span)
        normed = h_second[at, :]
        pre = jnp.dot(normed, w_fc[...], preferred_element_type=jnp.float32) + bias_fc
        square = pre * pre
        slope = jnp.tanh(GELU_SCALE * (pre + GELU_CUBE * pre * square))
        act[at, :] = low(0.5 * pre * (1.0 + slope))
        tilt = 0.5 * (1.0 + slope) + 0.5 * pre * (1.0 - slope * slope) * GELU_SCALE * (
            1.0 + 3.0 * GELU_CUBE * square
        )
        dpre_block = low(dot_nt(back[at, :], w_proj[...]) * tilt)
        dpre[at, :] = dpre_block
        fc_sums[...] += jnp.sum(wide(dpre_block), 0, keepdims=True)
        value = low(dot_nt(dpre_block, w_fc[...]))
        store_halves(dh_part, 2 * step, value)
        return carry

    lax.fori_loop(0, MEMBERS // 2, one_block, 0)
    for item in reduces:
        item.begin()

    def one_made(step, carry):
        at = pl.ds(pl.multiple_of(step * span, span), span)
        value = low(jnp.dot(act[at, :], w_proj[...], preferred_element_type=jnp.float32))
        made_part[2 * step] = value[:count]
        made_part[2 * step + 1] = value[count:]
        return carry

    lax.fori_loop(0, MEMBERS // 2, one_made, 0)
    for item in reduces:
        item.second()
    stores = [pltpu.make_async_copy(made_part, made, store_sem.at[2])]
    stores[0].start()
    chunk = 256

    def one_proj(step, carry):
        lanes = pl.ds(pl.multiple_of(step * chunk, chunk), chunk)
        store_rows(g_proj, 0, dot_tn(act[...], back[:, lanes]), lanes)
        return carry

    lax.fori_loop(0, width // chunk, one_proj, 0)
    tail = slice(width // chunk * chunk, width)
    if width % chunk:
        store_rows(g_proj, 0, dot_tn(act[...], back[:, tail]), tail)
    fold = Fold(
        p, lambda far: g_proj.at[2 * (1 - p.y) + far], lambda far: g_proj.at[2 * p.y + far],
        lambda far: proj_y.at[far], proj_go, proj_far, fold_sem, 0,
    )
    fold.begin()
    for item in reduces:
        item.third()
    for first in range(0, width, chunk):
        size = min(chunk, width - first)
        store_rows(
            g_fc, first, dot_tn(h_second[:, first : first + size], dpre[...]), at=FC_POSITION,
            unit=width // DEVICES,
        )
    fold.rest()
    fold.middle()
    stores.append(pltpu.make_async_copy(g_fc, grad_fc, store_sem.at[0]))
    stores[-1].start()

    gathers = []
    sums[...] = jnp.zeros_like(sums)
    for half, item in enumerate(reduces):
        at = slice(some * half, some * half + some)
        dh = item.result()
        center = resid_own[at, :] - jnp.mean(resid_own[at, :], -1, keepdims=True)
        scale = lax.rsqrt(jnp.mean(center * center, -1, keepdims=True) + epsilon_norm)
        hat = center * scale
        first = pl.multiple_of(p.me * count + some * half, some)
        back_own = wide(back[pl.ds(first, some), :])
        scaled = dh * vecs[18:19, :]
        inner = jnp.mean(scaled * hat, -1, keepdims=True)
        value = back_own + (scaled - jnp.mean(scaled, -1, keepdims=True) - hat * inner) * scale
        dresid[at, :] = value
        part = low(value)
        dbranch[half] = part
        gather = Gather(p, branch_all.at[half], branch_sem.at[half])
        gather.begin_from(dbranch.at[half])
        gathers.append(gather)
        copy = pltpu.make_async_copy(
            dbranch.at[half], branch_all.at[half, p.me], store_sem.at[1 + 2 * half]
        )
        copy.start()
        stores.append(copy)
        sums[0:1, :] += jnp.sum(dh * hat, 0, keepdims=True)
        sums[1:2, :] += jnp.sum(dh, 0, keepdims=True)
        sums[2:3, :] += jnp.sum(wide(part), 0, keepdims=True)
        sums[3:4, :] += jnp.sum(back_own, 0, keepdims=True)
    for item in gathers:
        item.second_hop()
        item.third_hop()
    for item in gathers:
        item.last_hop()
    proj_sum[...] = fold.end()
    for item in gathers:
        item.finish()
    fold.sent()
    for item in reduces:
        item.sent()
    for copy in stores:
        copy.wait()


def middle(h_second, back_all, vecs, resid_own, w_fc, w_proj):
    kind, high = jnp.bfloat16, jnp.float32
    length, width = back_all.shape
    rows = length // MEMBERS
    hidden = w_proj.shape[0]
    four = width // MEMBERS
    any_space = pl.BlockSpec(memory_space=pl.ANY)
    vmem = pl.BlockSpec(memory_space=pltpu.VMEM)
    dma = pltpu.SemaphoreType.DMA

    def like(*shape, dtype=kind):
        return jax.ShapeDtypeStruct(shape, dtype)

    def buffer(*shape, dtype=kind):
        return pltpu.VMEM(shape, dtype)

    return pl.pallas_call(
        middle_kernel,
        out_shape=[
            like(MEMBERS, four, hidden),
            like(four, width),
            like(MEMBERS, rows, width),
            like(rows, width, dtype=high),
            like(2, MEMBERS, rows // 2, width),
            like(8, width, dtype=high),
            like(1, hidden, dtype=high),
        ],
        in_specs=[any_space] * 2 + [vmem] * 2 + [any_space] * 2,
        out_specs=[any_space, vmem, any_space, vmem, any_space] + [vmem] * 2,
        scratch_shapes=[
            buffer(length, width),
            buffer(*back_all.shape),
            buffer(*w_fc.shape),
            buffer(*w_proj.shape),
            buffer(length, hidden),
            buffer(length, hidden),
            buffer(2, MEMBERS, rows // 2, width),
            buffer(MEMBERS, rows, width),
            buffer(MEMBERS, four, hidden),
            buffer(GROUPS, four, width),
            buffer(2, four, width),
            buffer(four, width),
            buffer(four, width),
        ]
        + reduce_buffers(rows // 2, width)
        + reduce_buffers(rows // 2, width)
        + [
            dma((2 * MEMBERS + 3,)), dma((4,)), dma((2, 3)), buffer(2, rows // 2, width),
            dma((2, 2, 7)),
        ],
        compiler_params=pltpu.CompilerParams(
            collective_id=3, has_side_effects=True, vmem_limit_bytes=VMEM_BYTES
        ),
        name="middle",
    )(h_second, back_all, vecs, resid_own, w_fc, w_proj)


class Fold:
    def __init__(self, place, away, kept, landing, leaving, last, sems, first):
        p = place
        self.p, self.away, self.kept, self.landing = p, away, kept, landing
        self.leaving, self.last = leaving, last
        self.to_far, self.to_y = p.target(far=1 - p.far), p.target(y=1 - p.y)
        self.sems, self.first = sems, first

    def begin(self):
        other = 1 - self.p.far
        self.a = remote(
            self.away(other), self.landing(other), self.sems, self.first, self.to_y
        )
        self.a.start()

    def rest(self):
        far = self.p.far
        self.b = remote(
            self.away(far), self.landing(far), self.sems, self.first + 1, self.to_y
        )
        self.b.start()

    def middle(self):
        other = 1 - self.p.far
        self.a.wait_recv()
        self.leaving[...] = low(wide(self.kept(other)[...]) + wide(self.landing(other)[...]))
        self.c = remote(self.leaving, self.last, self.sems, self.first + 2, self.to_far)
        self.c.start()

    def end(self):
        far = self.p.far
        self.b.wait_recv()
        partial = wide(self.kept(far)[...]) + wide(self.landing(far)[...])
        self.c.wait_recv()
        return low(partial + wide(self.last[...]))

    def sent(self):
        for item in (self.a, self.b, self.c):
            item.wait_send()


def backward_kernel(
    branch_in, made_in, grad_fc, proj_sum, attn, qkv, row_pos, col_pos, w_heads, w_qkv_in,
    h_in, x_own, resid_own, dresid, vecs, sums, fc_sums,
    out_home, grad_home, qkv_back, fc_back, rows_back, vec_back,
    branch_all, dattn, dqkv, key_sum, value_sum, w_qkv, h_first, dh_part, made, result,
    fc_own, g_qkv, g_heads, g_out, input_grad, vec_rows, vec_go, vec_got,
    fc_y, qkv_y, out_y, fc_go, qkv_go, out_go,
    fc_far, qkv_far, out_far, fc_sum, qkv_sum, out_sum,
    core_a, two_a, got_a, last_a, done_a, sem_a, core_b, two_b, got_b, last_b, done_b, sem_b,
    load_sem, fold_sem, tree_sem, vec_sem, home_sem,
    qkv_send, qkv_recv, fc_send, fc_recv, rows_send, rows_recv,
):
    p = Place()
    _, _, some, width = branch_in.shape
    count = 2 * some
    length = MEMBERS * count
    four = proj_sum.shape[0]
    pairs = SLOTS // 2
    loads = []

    def load(source, target):
        copy = pltpu.make_async_copy(source, target, load_sem.at[len(loads)])
        copy.start()
        loads.append(copy)

    for member in range(MEMBERS):
        for half in range(2):
            load(branch_in.at[half, member], branch_all.at[member, pl.ds(some * half, some)])
    load(half_of(made_in, p.core), made)
    for far in range(2):
        for near in range(2):
            load(grad_fc.at[far, p.y, near], fc_own.at[far, near])
    load(w_qkv_in, w_qkv)
    load(h_in, h_first)
    greet_all(p)
    fc_folds = [
        Fold(
            p, lambda far, near=near: grad_fc.at[far, 1 - p.y, near],
            lambda far, near=near: fc_own.at[far, near],
            lambda far, near=near: fc_y.at[far, near],
            fc_go.at[near], fc_far.at[near], fold_sem, 3 + 3 * near,
        )
        for near in range(2)
    ]
    qkv_folds = [
        Fold(
            p, lambda far, pair=pair: g_qkv.at[pair, pl.ds(4 * far + 2 * (1 - p.y), 2)],
            lambda far, pair=pair: g_qkv.at[pair, pl.ds(4 * far + 2 * p.y, 2)],
            lambda far, pair=pair: qkv_y.at[pair, far],
            qkv_go.at[pair], qkv_far.at[pair], fold_sem, 9 + 3 * pair,
        )
        for pair in range(pairs)
    ]
    reduce_made = Reduce(
        p, half_of(made_in, 1 - p.core), made, core_a, two_a, got_a, last_a, done_a, sem_a
    )
    reduce_made.begin()
    target, part = shard_of(PROJ_FIRST + lookup(PROJ_UNIT, p.linear))
    moves = [
        Move(p, proj_sum, rows_back.at[part], rows_send.at[0], rows_recv.at[part], target)
    ]
    for item in fc_folds:
        item.begin()
    for copy in loads:
        copy.wait()
    span = 2 * count

    def one_dattn(step, carry):
        at = pl.ds(pl.multiple_of(step * span, span), span)
        grad = jnp.concatenate([branch_all[2 * step], branch_all[2 * step + 1]], 0)
        value = low(dot_nt(grad, w_heads[...]))
        for pair in range(pairs):
            dattn[pair, at, :] = value[:, 128 * pair : 128 * pair + 128]
        return carry

    lax.fori_loop(0, length // span, one_dattn, 0)
    def one_pair(pair):
        key_sum[...] = jnp.zeros_like(key_sum)
        value_sum[...] = jnp.zeros_like(value_sum)

        def columns(part):
            return slice(384 * pair + 128 * part, 384 * pair + 128 * part + 128)

        def one_block(step, carry):
            at = pl.ds(pl.multiple_of(step * span, span), span)
            query, grad = qkv[at, columns(0)], dattn[pair, at, :]
            keys, values = qkv[:, columns(1)], qkv[:, columns(2)]
            lanes = lane_of(query.shape)
            total = jnp.zeros(query.shape, jnp.float32)
            add_keys = add_values = 0.0
            for head in range(2):
                mine = lanes == head
                own = jnp.where(mine, query, jnp.zeros_like(query))
                own_grad = jnp.where(mine, grad, jnp.zeros_like(grad))
                probs = probabilities(own, keys, row_pos[at, :], col_pos[...])
                dprobs = dot_nt(own_grad, values)
                delta = jnp.sum(probs * dprobs, -1, keepdims=True)
                dscores = low(probs * (dprobs - delta))
                mixed = jnp.dot(dscores, keys, preferred_element_type=jnp.float32)
                total = jnp.where(mine, mixed, total)
                add_keys = add_keys + dot_tn(dscores, own)
                add_values = add_values + dot_tn(low(probs), own_grad)
            dqkv[at, columns(0)] = low(total * 0.125)
            key_sum[...] += add_keys
            value_sum[...] += add_values
            return carry

        lax.fori_loop(0, length // span, one_block, 0)
        dqkv[:, columns(1)] = low(key_sum[...] * 0.125)
        dqkv[:, columns(2)] = low(value_sum[...])

    chunk = 256

    def one_grad(pair):
        columns = slice(384 * pair, 384 * pair + 384)
        for first in range(0, width, chunk):
            size = min(chunk, width - first)
            value = dot_tn(h_first[:, first : first + size], dqkv[:, columns])
            store_rows(g_qkv.at[pair], first, value, at=(0, 2, 1, 3, 4, 6, 5, 7))
        qkv_folds[pair].begin()

    reduce_made.second()
    one_pair(0)
    reduce_made.third()
    one_grad(0)
    for item in fc_folds:
        item.middle()
    for item in fc_folds:
        item.rest()
    one_pair(1)
    for part in range(3):
        last = 384 * (pairs - 1) + 128 * part
        value = dqkv[:, last : last + 128]
        keep = jnp.logical_or(lane_of(value.shape) == 0, p.me == MEMBERS - 1)
        dqkv[:, last : last + 128] = jnp.where(keep, value, jnp.zeros_like(value))
    one_grad(1)
    qkv_folds[0].middle()
    for item in qkv_folds:
        item.rest()

    def one_part(step, carry):
        at = pl.ds(pl.multiple_of(step * span, span), span)
        value = low(dot_nt(dqkv[at, :], w_qkv[...]))
        dh_part[2 * step] = value[:count]
        dh_part[2 * step + 1] = value[count:]
        return carry

    lax.fori_loop(0, length // span, one_part, 0)
    reduce_dh = Reduce(
        p, half_of(dh_part, 1 - p.core), half_of(dh_part, p.core), core_b, two_b, got_b, last_b,
        done_b, sem_b, True,
    )
    reduce_dh.begin()
    home = p.shard_home()
    turn(low(resid_own[...] + reduce_made.result() + vecs[33:34, :]), result)
    moves.append(Move(p, result, out_home, home_sem.at[0, 0], home_sem.at[1, 0], home))
    reduce_dh.second()
    for pair in range(pairs):
        total = 0.0
        for block in range(MEMBERS):
            at = slice(block * count, block * count + count)
            total = total + dot_tn(attn[pair, at, :], branch_all[block])
        g_heads[128 * pair : 128 * pair + 128, :] = total
    g_out[...] = low(g_heads[pl.ds(pl.multiple_of(head_rows(p.me), 8), four), :])
    root_y = out_root(p.me)
    same_y = p.y == root_y
    root = jnp.logical_and(same_y, p.far == 0)
    beside = jnp.logical_and(same_y, p.far == 1)
    over_y = remote(g_out, out_y, tree_sem, 0, p.target(y=1 - p.y))
    over_far = remote(out_go, out_far, tree_sem, 1, p.target(far=1 - p.far))

    @pl.when(jnp.logical_not(same_y))
    def _():
        over_y.start()

    reduce_dh.third()
    for near in range(2):
        block = fc_folds[near].end()
        unit = fc_sum.shape[2]
        for slot in range(4):
            fc_sum[near, slot] = block[unit * slot : unit * slot + unit]
            target, part = shard_of(FC_FIRST + fc_unit(p.far, p.y, 4 * near + slot))
            moves.append(
                Move(
                    p, fc_sum.at[near, slot], fc_back.at[part, p.me],
                    fc_send.at[near, slot], fc_recv.at[part, p.me], target,
                )
            )

    @pl.when(same_y)
    def _():
        over_y.wait_recv()

    @pl.when(beside)
    def _():
        out_go[...] = low(wide(g_out[...]) + wide(out_y[...]))
        over_far.start()

    dh = reduce_dh.result()
    x = wide(x_own[...])
    center = x - jnp.mean(x, -1, keepdims=True)
    scale = lax.rsqrt(jnp.mean(center * center, -1, keepdims=True) + epsilon_norm)
    hat = center * scale
    scaled = dh * vecs[0:1, :]
    inner = jnp.mean(scaled * hat, -1, keepdims=True)
    value = (scaled - jnp.mean(scaled, -1, keepdims=True) - hat * inner) * scale
    turn(low(dresid[...] + value), input_grad)
    moves.append(Move(p, input_grad, grad_home, home_sem.at[0, 1], home_sem.at[1, 1], home))
    bias_sums = jnp.sum(wide(dqkv[...]), 0, keepdims=True)

    def placed(value, starts, me):
        total = jnp.zeros((1, width), jnp.float32)
        for index, start in enumerate(starts):
            parts = [value]
            if start:
                parts.insert(0, jnp.zeros((1, start), jnp.float32))
            after = width - start - value.shape[1]
            if after:
                parts.append(jnp.zeros((1, after), jnp.float32))
            row = jnp.concatenate(parts, 1) if len(parts) > 1 else value
            total = total + jnp.where(me == index, row, 0.0)
        return total

    heads = [head_start(member) * HD for member in range(MEMBERS)]
    vec_rows[0:1, :] = jnp.sum(dh * hat, 0, keepdims=True)
    vec_rows[1:2, :] = jnp.sum(dh, 0, keepdims=True)
    for row, part in ((2, 0), (3, 2)):
        value = jnp.concatenate(
            [
                bias_sums[:, 384 * pair + 128 * part : 384 * pair + 128 * part + 128]
                for pair in range(pairs)
            ],
            1,
        )
        vec_rows[row : row + 1, :] = placed(value, heads, p.me)
    vec_rows[4:5, :] = sums[2:3, :]
    vec_rows[5:7, :] = sums[0:2, :]
    vec_rows[7:8, :] = sums[3:4, :]
    used = width // MEMBERS
    vec_go[...] = jnp.zeros_like(vec_go)
    for f in range(GROUPS):
        for c in range(MEMBERS):
            vec_go[MEMBERS * f + c, 0:3, 0:used] = vec_rows[
                3 * f : 3 * f + 3, used * c : used * c + used
            ]
    for unit, (holder, which) in HOLDER.items():
        f, row = divmod(8 + unit // MEMBERS, 3)
        value = fc_sums[:, used * which : used * which + used]
        vec_go[MEMBERS * f + unit % MEMBERS, row : row + 1, 0:used] = jnp.where(
            p.me == holder, value, 0.0
        )

    def vec_send(step, carry):
        other = (p.linear + step) % DEVICES
        pltpu.make_async_remote_copy(
            src_ref=vec_go.at[other],
            dst_ref=vec_got.at[p.linear],
            send_sem=vec_sem.at[0],
            recv_sem=vec_sem.at[1],
            device_id=(other // MEMBERS, other % MEMBERS),
            device_id_type=MESH,
        ).start()
        return carry

    lax.fori_loop(1, DEVICES, vec_send, 0)
    pltpu.make_async_copy(vec_go.at[p.linear], vec_got.at[p.linear], vec_sem.at[1]).start()
    qkv_folds[1].middle()
    @pl.when(root)
    def _():
        over_far.wait_recv()
        out_sum[...] = low(wide(g_out[...]) + wide(out_y[...]) + wide(out_far[...]))

    target, part = shard_of(OUT_FIRST + p.me)
    moves.append(
        Move(p, out_sum, rows_back.at[part], rows_send.at[1], rows_recv.at[part], target, root)
    )
    for pair in range(pairs):
        qkv_sum[pair] = qkv_folds[pair].end()
        for near in range(2):
            target = (0 * p.fsdp, 4 * p.far + 2 * near + p.y)
            moves.append(
                Move(
                    p, qkv_sum.at[pair, near], qkv_back.at[p.me, pair],
                    qkv_send.at[pair, near], qkv_recv.at[p.me, pair], target,
                )
            )
    arrived(vec_got, vec_sem.at[1])
    vec_back[...] = jnp.sum(vec_got[...], 0)

    @pl.when(p.fsdp == 0)
    def _():
        for member in range(MEMBERS):
            for pair in range(pairs):
                arrived(qkv_back.at[member, pair], qkv_recv.at[member, pair])

    for part in range(3):
        third = 3 * p.linear + part
        is_fc = jnp.logical_and(third >= FC_FIRST, third < PROJ_FIRST)
        is_rows = jnp.logical_and(third >= OUT_FIRST, jnp.logical_not(is_fc))

        @pl.when(is_fc)
        def _(part=part):
            for member in range(MEMBERS):
                arrived(fc_back.at[part, member], fc_recv.at[part, member])

        @pl.when(is_rows)
        def _(part=part):
            arrived(rows_back.at[part], rows_recv.at[part])

    arrived(out_home, home_sem.at[1, 0])
    arrived(grad_home, home_sem.at[1, 1])
    arrived(vec_got.at[pl.ds(1, DEVICES - 1)], vec_sem.at[0])
    for item in [reduce_made, reduce_dh] + fc_folds + qkv_folds + moves:
        item.sent()

    @pl.when(jnp.logical_not(same_y))
    def _():
        over_y.wait_send()

    @pl.when(beside)
    def _():
        over_far.wait_send()


def backward(
    branch_all, made, grad_fc, proj_sum, attn, qkv, row_pos, col_pos, w_heads, w_qkv,
    h_first, x_own, resid_own, dresid, vecs, sums, fc_sums,
):
    kind, high = jnp.bfloat16, jnp.float32
    rows, width = x_own.shape
    length = MEMBERS * rows
    four, cols = width // MEMBERS, qkv.shape[1]
    unit, hidden = four // 4, fc_sums.shape[1]
    per_part = SLOTS * HD
    any_space = pl.BlockSpec(memory_space=pl.ANY)
    vmem = pl.BlockSpec(memory_space=pltpu.VMEM)
    dma = pltpu.SemaphoreType.DMA

    def like(*shape, dtype=kind):
        return jax.ShapeDtypeStruct(shape, dtype)

    def buffer(*shape, dtype=kind):
        return pltpu.VMEM(shape, dtype)

    used = -(-width // MEMBERS // 128) * 128
    return pl.pallas_call(
        backward_kernel,
        out_shape=[
            like(width, rows),
            like(width, rows),
            like(MEMBERS, 2, four, cols // 2),
            like(3, MEMBERS, unit, hidden),
            like(3, four, width),
            like(8, used, dtype=high),
        ],
        in_specs=[any_space] * 3 + [vmem] * 6 + [any_space] * 2 + [vmem] * 6,
        out_specs=[any_space] * 5 + [vmem],
        scratch_shapes=[
            buffer(MEMBERS, rows, width),
            buffer(SLOTS // 2, length, 2 * HD),
            buffer(length, cols),
            buffer(length, 2 * HD, dtype=high),
            buffer(length, 2 * HD, dtype=high),
            buffer(*w_qkv.shape),
            buffer(*h_first.shape),
            buffer(MEMBERS, rows, width),
            buffer(MEMBERS // 2, rows, width),
            buffer(width, rows),
            buffer(2, 2, four, hidden),
            buffer(2, MEMBERS, four, cols // 2),
            buffer(per_part, width, dtype=high),
            buffer(four, width),
            buffer(width, rows),
            buffer(16, width, dtype=high),
            buffer(DEVICES, 8, used, dtype=high),
            buffer(DEVICES, 8, used, dtype=high),
        ]
        + [
            buffer(2, 2, four, hidden),
            buffer(2, 2, 2, four, cols // 2), buffer(four, width),
            buffer(2, four, hidden), buffer(2, 2, four, cols // 2), buffer(four, width),
        ]
        + [
            buffer(2, four, hidden), buffer(2, 2, four, cols // 2), buffer(four, width),
        ]
        + [
            buffer(2, 4, unit, hidden), buffer(2, 2, four, cols // 2), buffer(four, width),
        ]
        + reduce_buffers(rows, width)
        + reduce_buffers(rows, width)
        + [
            dma((2 * MEMBERS + 8,)),
            dma((2, 15)),
            dma((2, 2)),
            dma((2,)),
            dma((2, 2)),
            dma((2, 2)),
            dma((8, 2)),
            dma((2, 4)),
            dma((3, 8)),
            dma((2,)),
            dma((3,)),
        ],
        compiler_params=pltpu.CompilerParams(
            collective_id=2, has_side_effects=True, vmem_limit_bytes=VMEM_BYTES
        ),
        name="backward",
    )(
        branch_all, made, grad_fc, proj_sum, attn, qkv, row_pos, col_pos, w_heads, w_qkv,
        h_first, x_own, resid_own, dresid, vecs, sums, fc_sums,
    )


def lane_of(shape):
    return lax.broadcasted_iota(jnp.int32, shape, 1) // HD


def dot_nt(a, b):
    return lax.dot_general(a, b, (((1,), (1,)), ((), ())), preferred_element_type=jnp.float32)


def dot_tn(a, b):
    return lax.dot_general(a, b, (((0,), (0,)), ((), ())), preferred_element_type=jnp.float32)


def probabilities(query, keys, row_pos, col_pos):
    scores = dot_nt(query, keys) * 0.125
    scores = jnp.where(col_pos <= row_pos, scores, -1e30)
    weights = jnp.exp(scores - jnp.max(scores, -1, keepdims=True))
    return weights / jnp.sum(weights, -1, keepdims=True)


def head_place(head):
    member = max(m for m in range(MEMBERS) if head_start(m) <= head)
    return member, head - head_start(member)


def unlay_qkv(flat, tiles, back):
    count = back.shape[2] // 2
    each = 3 * SLOTS // 2
    for member in range(MEMBERS):
        for pair in range(SLOTS // 2):
            for part in range(3):
                tiles[member * each + 3 * pair + part] = wide(
                    back[member, pair, :, 128 * part : 128 * part + 128]
                )
    halves = 3 * HEADS

    def half(index, lane):
        odd, at = divmod(index, halves)
        part, head = divmod(at, HEADS)
        member, slot = head_place(head)
        tile = member * each + 3 * (slot // 2) + part
        return piece(
            lambda _: tiles[tile, pl.ds(odd, count, stride=2), :], HD * (slot % 2), lane, HD
        )

    for row in range(halves):
        flat[pl.ds(row, count, stride=halves), :] = join(
            [(0, half(2 * row, 0)), (HD, half(2 * row + 1, HD))]
        )


def unlay_fc(flat, first, tiles, back, part):
    count, hidden = back.shape[-2:]
    each = -(-hidden // 128)
    for member in range(MEMBERS):
        for tile in range(each):
            size = min(128, hidden - 128 * tile)
            tiles[member * each + tile, :count, :size] = wide(
                back[part, member, :, 128 * tile : 128 * tile + size]
            )
    stride, block = FF // 128, hidden // GROUPS
    for row in range(stride):
        parts, col = [], 128 * row
        while col < 128 * row + 128:
            unit, inside = divmod(col, block)
            size = min(block - inside, 128 * row + 128 - col)
            member, which = HOLDER[unit]
            lane = col - 128 * row
            value = piece(
                lambda t, m=member: tiles[m * each + t, :count, :],
                block * which + inside, lane, size,
            )
            parts.append((lane, value))
            col += size
        flat[pl.ds(first + row, count, stride=stride), :] = join(parts)


def unlay_rows(flat, first, tiles, back, part):
    count, width = back.shape[1] // 2, back.shape[2]
    for tile in range(-(-width // 128)):
        size = min(128, width - 128 * tile)
        tiles[tile, :, :size] = wide(back[part, :, 128 * tile : 128 * tile + size])
    halves = width // HD

    def half(index, lane):
        odd, at = divmod(index, halves)
        return piece(
            lambda t: tiles[t, pl.ds(odd, count, stride=2), :], HD * at, lane, HD
        )

    for row in range(halves):
        flat[pl.ds(first + row, count, stride=halves), :] = join(
            [(0, half(2 * row, 0)), (HD, half(2 * row + 1, HD))]
        )


def update_kernel(
    qkv_in, fc_in, rows_in, vec_back, vectors, first_vec, second_vec,
    weights, first, second,
    moment_vec, squares_vec, new_vec, moment, squares, new,
    flat, tiles, qkv_back, fc_back, rows_back, sem,
):
    step = pl.program_id(0)
    linear = lax.axis_index("fsdp") * MEMBERS + lax.axis_index("ctx")

    @pl.when(step == 0)
    def _():
        rows, cols = vectors.shape
        result = adamw(
            vectors[...], vec_back[:rows, :cols], first_vec[...], second_vec[...],
            rate_vector, 0.0,
        )
        moment_vec[...], squares_vec[...], new_vec[...] = result

        @pl.when(linear < MEMBERS)
        def _():
            copy = pltpu.make_async_copy(qkv_in, qkv_back, sem.at[0])
            copy.start()
            copy.wait()
            unlay_qkv(flat, tiles, qkv_back)

        @pl.when(linear >= MEMBERS)
        def _():
            copies = [
                pltpu.make_async_copy(fc_in, fc_back, sem.at[0]),
                pltpu.make_async_copy(rows_in, rows_back, sem.at[1]),
            ]
            for copy in copies:
                copy.start()
            for copy in copies:
                copy.wait()
            third_rows = fc_back.shape[2] * FF // 128
            for part in range(3):
                third = 3 * linear + part
                is_fc = jnp.logical_and(third >= FC_FIRST, third < PROJ_FIRST)

                @pl.when(is_fc)
                def _(part=part):
                    unlay_fc(flat, part * third_rows, tiles, fc_back, part)

                @pl.when(jnp.logical_not(is_fc))
                def _(part=part):
                    unlay_rows(flat, part * third_rows, tiles, rows_back, part)

    size = weights.shape[0]
    grad = flat[pl.ds(pl.multiple_of(step * size, 8), size), :]
    result = adamw(weights[...], grad, first[...], second[...], rate_matrix, weight_decay)
    moment[...], squares[...], new[...] = result


def update(
    qkv_back, fc_back, rows_back, vec_back, vectors, first_vec, second_vec,
    weights, first, second,
):
    high = jnp.float32
    local = weights.shape[0]
    steps = 10
    size = -(-local // (16 * steps)) * 16
    block = pl.BlockSpec((size, 128), lambda i: (i, 0))
    any_space = pl.BlockSpec(memory_space=pl.ANY)
    vmem = pl.BlockSpec(memory_space=pltpu.VMEM)
    kind = jax.ShapeDtypeStruct((local, 128), high)
    small = jax.ShapeDtypeStruct(vectors.shape, high)
    tile_count = MEMBERS * max(3 * SLOTS // 2, -(-fc_back.shape[3] // 128))
    return pl.pallas_call(
        update_kernel,
        grid=(steps,),
        in_specs=[any_space] * 3 + [vmem] * 4 + [block] * 3,
        out_specs=[vmem] * 3 + [block] * 3,
        out_shape=[small] * 3 + [kind] * 3,
        scratch_shapes=[
            pltpu.VMEM((size * steps, 128), high),
            pltpu.VMEM((tile_count, qkv_back.shape[2], 128), high),
            pltpu.VMEM(qkv_back.shape, qkv_back.dtype),
            pltpu.VMEM(fc_back.shape, fc_back.dtype),
            pltpu.VMEM(rows_back.shape, rows_back.dtype),
            pltpu.SemaphoreType.DMA((2,)),
        ],
        compiler_params=pltpu.CompilerParams(vmem_limit_bytes=VMEM_BYTES),
        name="update",
    )(
        qkv_back, fc_back, rows_back, vec_back, vectors, first_vec, second_vec, weights, first,
        second,
    )


def per_device_groups(
    inputs, cotangent, slot_order, weights, vectors, first_w, second_w, first_vec, second_vec
):
    _, rows, width = inputs.shape
    length = rows * MEMBERS
    (
        back_all, vecs, row_pos, col_pos, own_qkv, h_first, qkv, attn, own_fc, own_proj, w_heads,
        x_own, resid_own, h_second,
    ) = forward(
        inputs[0].T, cotangent[0].T, slot_order, vectors, weights
    )
    grad_fc, proj_sum, made, dresid, branch_all, sums, fc_sums = middle(
        h_second, back_all.reshape(length, width), vecs, resid_own,
        own_fc, own_proj,
    )
    out_home, grad_home, qkv_back, fc_back, rows_back, vec_back = backward(
        branch_all, made, grad_fc.reshape((2, 2, 2) + grad_fc.shape[1:]), proj_sum, attn, qkv,
        row_pos, col_pos, w_heads, own_qkv, h_first, x_own, resid_own, dresid, vecs, sums,
        fc_sums,
    )
    new = update(
        qkv_back, fc_back, rows_back, vec_back, vectors, first_vec, second_vec, weights,
        first_w, second_w,
    )
    moment_vec, squares_vec, new_vec, moment_w, squares_w, new_w = new
    return (
        out_home.T[None], grad_home.T[None], moment_w, squares_w, new_w, moment_vec, squares_vec, new_vec
    )


def solution(mesh):
    in_specs = (
        P("fsdp", "ctx", None),
        P("fsdp", "ctx", None),
        P("fsdp", None),
        P(("fsdp", "ctx"), None),
        P("fsdp", "ctx"),
        P(("fsdp", "ctx"), None),
        P(("fsdp", "ctx"), None),
        P("fsdp", "ctx"),
        P("fsdp", "ctx"),
    )
    out_specs = (
        P("fsdp", "ctx", None),
        P("fsdp", "ctx", None),
        P(("fsdp", "ctx"), None),
        P(("fsdp", "ctx"), None),
        P(("fsdp", "ctx"), None),
        P("fsdp", "ctx"),
        P("fsdp", "ctx"),
        P("fsdp", "ctx"),
    )
    per_device = per_device_groups if mesh.shape["ctx"] == MEMBERS else per_device_ring
    return jax.shard_map(
        per_device, mesh=mesh, in_specs=in_specs, out_specs=out_specs, check_vma=False
    )
```

```python
import jax
import jax.numpy as jnp
from jax import lax
from jax.experimental import pallas as pl
from jax.experimental.pallas import tpu as pltpu
from jax.sharding import PartitionSpec as P

HEADS = 25
HD = 64
FF = 6400
STEP = 10


epsilon_norm = 1e-05
beta_first = 0.9
beta_second = 0.999
epsilon_adam = 1e-08
weight_decay = 0.1
rate_matrix = 0.1
rate_vector = 0.8


def shifted(value, axis, steps):
    count = lax.axis_size(axis)
    pairs = [(source, (source + steps) % count) for source in range(count)]
    return lax.ppermute(value, axis, pairs)


def layer_norm(value, gain, shift):
    center = value - jnp.mean(value, -1, keepdims=True)
    spread = jnp.mean(center * center, -1, keepdims=True)
    return center * lax.rsqrt(spread + epsilon_norm) * gain + shift


def gelu_tanh(value):
    return jax.nn.gelu(value, approximate=True)


def key_positions(slot_order, first_slot, slots, block):
    groups = lax.dynamic_slice_in_dim(slot_order, first_slot, slots, 1)
    offsets = jnp.arange(block, dtype=jnp.int32)
    return (groups[:, :, None] * block + offsets).reshape(slot_order.shape[0], slots * block)


def unpack_flat(flat, width, hidden):
    flat = flat.reshape(-1)
    first_end = 3 * width * width
    second_end = 4 * width * width
    third_end = 4 * width * width + width * hidden
    return (
        flat[:first_end].reshape(width, 3 * width),
        flat[first_end:second_end].reshape(width, width),
        flat[second_end:third_end].reshape(width, hidden),
        flat[third_end:].reshape(hidden, width),
    )


def gather_params(weights, vectors):
    local = weights.reshape(1, weights.shape[0], weights.shape[1])
    part = (
        lax.all_gather(local, "fsdp", axis=0, tiled=True),
        lax.all_gather(vectors, "fsdp", axis=0, tiled=True),
    )
    return (
        lax.all_gather(part[0], "ctx", axis=1, tiled=True),
        lax.all_gather(part[1], "ctx", axis=1, tiled=True),
    )


def reduce_grads(grad_flat, grad_vec):
    part = (
        lax.psum_scatter(
            grad_flat.astype(jnp.bfloat16), "fsdp", scatter_dimension=0, tiled=True
        ).astype(jnp.float32),
        lax.psum_scatter(
            grad_vec.astype(jnp.bfloat16), "fsdp", scatter_dimension=0, tiled=True
        ).astype(jnp.float32),
    )
    return (
        lax.psum_scatter(
            part[0].astype(jnp.bfloat16), "ctx", scatter_dimension=1, tiled=True
        ).astype(jnp.float32),
        lax.psum_scatter(
            part[1].astype(jnp.bfloat16), "ctx", scatter_dimension=1, tiled=True
        ).astype(jnp.float32),
    )


def pass_grads(grad_pairs):
    return shifted(grad_pairs.astype(jnp.bfloat16), "ctx", 1).astype(grad_pairs.dtype)


def adamw(weight, grad, first, second, rate, decay):
    first = beta_first * first + (1.0 - beta_first) * grad
    second = beta_second * second + (1.0 - beta_second) * grad * grad
    first_hat = first / (1.0 - beta_first**STEP)
    second_hat = second / (1.0 - beta_second**STEP)
    weight = weight.astype(jnp.float32)
    updated = weight - rate * (first_hat / (jnp.sqrt(second_hat) + epsilon_adam) + decay * weight)
    return (first, second, updated)


def per_device_ring(
    inputs, cotangent, slot_order, weights, vectors, first_w, second_w, first_vec, second_vec
):
    seqs, rows, width = inputs.shape
    tokens = seqs * rows
    block = rows // 2
    cycle = lax.axis_size("ctx")
    shards = lax.axis_size("fsdp")
    me = lax.axis_index("ctx")
    full_flat, full_vec = gather_params(weights, vectors)
    full_qkv, full_out, full_fc, full_proj = unpack_flat(full_flat, width, FF)
    vec = full_vec.astype(jnp.float32)
    bias_fc = vec[8:].reshape(-1)
    x_in = inputs.reshape(tokens, width).astype(jnp.float32)
    h_first, pull_first = jax.vjp(layer_norm, x_in, vec[0], vec[1])
    h_first_b = h_first.astype(jnp.bfloat16)
    zero_row = jnp.zeros((width,), jnp.float32)
    qkv = jnp.dot(h_first_b, full_qkv, preferred_element_type=jnp.float32)
    qkv_b = (qkv + jnp.concatenate([vec[2], zero_row, vec[3]])).astype(jnp.bfloat16)
    query_heads = qkv_b[:, :width].reshape(seqs, rows, HEADS, HD)
    key_value = qkv_b[:, width:].reshape(seqs, rows, 2, width)
    query_pos = key_positions(slot_order, 2 * me, 2, block)

    def online(state, item):
        top, total, accum = state
        keys_i, values_i, pos_i = item
        scores = (
            jnp.einsum("sqhd,skhd->shqk", query_heads, keys_i, preferred_element_type=jnp.float32)
            * 0.125
        )
        allowed = pos_i[:, None, None, :] <= query_pos[:, None, :, None]
        scores = jnp.where(allowed, scores, -1e30)
        peak = jnp.maximum(top, jnp.max(scores, -1))
        weights_p = jnp.where(allowed, jnp.exp(scores - peak[..., None]), 0.0)
        factor = jnp.exp(top - peak)
        total = total * factor + jnp.sum(weights_p, -1)
        mixed = jnp.einsum(
            "shqk,skhd->sqhd",
            weights_p.astype(jnp.bfloat16),
            values_i,
            preferred_element_type=jnp.float32,
        )
        accum = accum * jnp.transpose(factor, (0, 2, 1))[..., None] + mixed
        return ((peak, total, accum), None)

    start_state = (
        jnp.full((seqs, HEADS, rows), -1e30, jnp.float32),
        jnp.zeros((seqs, HEADS, rows), jnp.float32),
        jnp.zeros((seqs, rows, HEADS, HD), jnp.float32),
    )
    state = start_state
    piece = lax.all_gather(key_value, "ctx", axis=1, tiled=True)
    count = piece.shape[1]
    turns = count // rows
    pos_all = key_positions(slot_order, jnp.int32(0) // block, count // block, block)
    stack = piece.reshape(seqs, turns, rows, 2, HEADS, HD).transpose(1, 0, 2, 3, 4, 5)
    pos_stack = pos_all.reshape(seqs, turns, rows).transpose(1, 0, 2)
    state, _ = lax.scan(online, state, (stack[:, :, :, 0], stack[:, :, :, 1], pos_stack))
    top, total, accum = state
    attn = accum / jnp.transpose(total, (0, 2, 1))[..., None]
    logsum = top + jnp.log(total)
    attn_b = attn.reshape(tokens, width).astype(jnp.bfloat16)
    resid = x_in + jnp.dot(attn_b, full_out, preferred_element_type=jnp.float32) + vec[4]
    h_second, pull_second = jax.vjp(layer_norm, resid, vec[5], vec[6])
    h_second_b = h_second.astype(jnp.bfloat16)
    pre = jnp.dot(h_second_b, full_fc, preferred_element_type=jnp.float32) + bias_fc
    act, pull_gelu = jax.vjp(gelu_tanh, pre)
    act_b = act.astype(jnp.bfloat16)
    result = resid + jnp.dot(act_b, full_proj, preferred_element_type=jnp.float32) + vec[7]
    outputs = result.astype(jnp.bfloat16).reshape(seqs, rows, width)
    back_b = cotangent.reshape(tokens, width)
    back = back_b.astype(jnp.float32)
    grad_proj = jnp.einsum("tf,td->fd", act_b, back_b, preferred_element_type=jnp.float32)
    grad_bp = jnp.sum(back, 0)
    dact = jnp.einsum("td,fd->tf", back_b, full_proj, preferred_element_type=jnp.float32)
    dpre_b = pull_gelu(dact)[0].astype(jnp.bfloat16)
    grad_fc = jnp.einsum("td,tf->df", h_second_b, dpre_b, preferred_element_type=jnp.float32)
    grad_bf = jnp.sum(dpre_b, 0, dtype=jnp.float32)
    dh_second = jnp.einsum("tf,df->td", dpre_b, full_fc, preferred_element_type=jnp.float32)
    dres_ln, grad_g2, grad_b2 = pull_second(dh_second)
    dresid = back + dres_ln
    dbranch_b = dresid.astype(jnp.bfloat16)
    grad_bo = jnp.sum(dbranch_b, 0, dtype=jnp.float32)
    grad_out = jnp.einsum("td,te->de", attn_b, dbranch_b, preferred_element_type=jnp.float32)
    dattn_b = jnp.einsum(
        "te,de->td", dbranch_b, full_out, preferred_element_type=jnp.float32
    ).astype(jnp.bfloat16)
    grad_heads = dattn_b.reshape(seqs, rows, HEADS, HD)
    delta = jnp.transpose(jnp.sum(grad_heads.astype(jnp.float32) * attn, -1), (0, 2, 1))

    def contribute(pair, source):
        pos_k = key_positions(slot_order, 2 * source, 2, block)
        key_h = pair[:, :, 0].reshape(seqs, rows, HEADS, HD)
        value_h = pair[:, :, 1].reshape(seqs, rows, HEADS, HD)
        scores = (
            jnp.einsum("sqhd,skhd->shqk", query_heads, key_h, preferred_element_type=jnp.float32)
            * 0.125
        )
        allowed = pos_k[:, None, None, :] <= query_pos[:, None, :, None]
        probs = jnp.where(allowed, jnp.exp(scores - logsum[..., None]), 0.0)
        dvalue = jnp.einsum(
            "shqk,sqhd->skhd",
            probs.astype(jnp.bfloat16),
            grad_heads,
            preferred_element_type=jnp.float32,
        )
        dprobs = jnp.einsum(
            "sqhd,skhd->shqk", grad_heads, value_h, preferred_element_type=jnp.float32
        )
        dscores = (probs * (dprobs - delta[..., None])).astype(jnp.bfloat16)
        dquery = (
            jnp.einsum("shqk,skhd->sqhd", dscores, key_h, preferred_element_type=jnp.float32)
            * 0.125
        )
        dkey = (
            jnp.einsum("shqk,sqhd->skhd", dscores, query_heads, preferred_element_type=jnp.float32)
            * 0.125
        )
        return (dquery, jnp.stack((dkey, dvalue), 2))

    dq_own, dkv_own = contribute(key_value, me)

    def turn(step, state):
        pair, dkv_acc, dq_acc = state
        pair = shifted(pair, "ctx", 1)
        dkv_acc = pass_grads(dkv_acc)
        source = (me - step) % cycle
        dq_part, dkv_part = contribute(pair, source)
        return (pair, dkv_acc + dkv_part, dq_acc + dq_part)

    final = lax.fori_loop(1, cycle, turn, (key_value, dkv_own, dq_own))
    dkv = pass_grads(final[1])
    dqkv_b = jnp.concatenate(
        [final[2].reshape(tokens, width), dkv.reshape(tokens, 2 * width)], 1
    ).astype(jnp.bfloat16)
    grad_qkv = jnp.einsum("td,te->de", h_first_b, dqkv_b, preferred_element_type=jnp.float32)
    bias_sums = jnp.sum(dqkv_b, 0, dtype=jnp.float32)
    dh_first = jnp.einsum("te,de->td", dqkv_b, full_qkv, preferred_element_type=jnp.float32)
    dx_ln, grad_g1, grad_b1 = pull_first(dh_first)
    input_grad = (dresid + dx_ln).astype(jnp.bfloat16).reshape(seqs, rows, width)
    grad_vec = jnp.concatenate(
        [
            jnp.stack(
                [
                    grad_g1,
                    grad_b1,
                    bias_sums[:width],
                    bias_sums[2 * width :],
                    grad_bo,
                    grad_g2,
                    grad_b2,
                    grad_bp,
                ]
            ),
            grad_bf.reshape(-1, width),
        ],
        0,
    )
    grad_flat = jnp.concatenate(
        [grad_qkv.reshape(-1), grad_out.reshape(-1), grad_fc.reshape(-1), grad_proj.reshape(-1)]
    ).reshape(shards, -1, 128)
    owned_flat, owned_vec = reduce_grads(grad_flat, grad_vec)
    owned_flat = owned_flat.reshape(weights.shape[0], 128)
    new_w = adamw(weights, owned_flat, first_w, second_w, rate_matrix, weight_decay)
    new_vec = adamw(vectors, owned_vec, first_vec, second_vec, rate_vector, 0.0)
    return (outputs, input_grad, new_w[0], new_w[1], new_w[2], new_vec[0], new_vec[1], new_vec[2])


MEMBERS = 8
GROUPS = 4
DEVICES = MEMBERS * GROUPS
MESH = pl.DeviceIdType.MESH
BLOCK = 64
SLOTS = 4
VMEM_BYTES = 60 * 1024 * 1024
OUT_FIRST = 24
FC_FIRST = 32
PROJ_FIRST = 64


def head_start(member):
    return HEADS * member // MEMBERS


class Place:
    def __init__(self):
        self.fsdp, self.ctx = lax.axis_index("fsdp"), lax.axis_index("ctx")
        self.x, self.core = self.fsdp // 2, self.fsdp % 2
        self.far, self.near, self.y = self.ctx // 4, self.ctx // 2 % 2, self.ctx % 2
        self.me = self.member()
        self.group = 2 * self.y + self.far
        self.linear = self.fsdp * MEMBERS + self.ctx

    def member(self, x=None, near=None, core=None):
        x = self.x if x is None else x
        near = self.near if near is None else near
        core = self.core if core is None else core
        return 4 * core + 2 * near + x

    def target(self, x=None, core=None, far=None, near=None, y=None):
        x = self.x if x is None else x
        near = self.near if near is None else near
        core = self.core if core is None else core
        far = self.far if far is None else far
        y = self.y if y is None else y
        return (2 * x + core, 4 * far + 2 * near + y)

    def group_home(self):
        x, core, far, near, y = self.x, self.core, self.far, self.near, self.y
        new_x = (y + far + core) % 2
        target = self.target(x=new_x, core=far, far=core, y=(x + core) % 2)
        return target, 4 * far + 2 * near + new_x

    def shard_home(self):
        x, core, far, y = self.x, self.core, self.far, self.y
        return self.target(x=(y + far) % 2, core=far, far=core, y=(x + core + far) % 2)

    def is_me(self, target):
        return jnp.logical_and(target[0] == self.fsdp, target[1] == self.ctx)


def greet_all(place):
    barrier = pltpu.get_barrier_semaphore()

    def one(step, carry):
        other = (place.linear + step) % DEVICES
        pl.semaphore_signal(
            barrier, inc=1, device_id=(other // MEMBERS, other % MEMBERS), device_id_type=MESH
        )
        return carry

    lax.fori_loop(1, DEVICES, one, 0)


def await_all():
    pl.semaphore_wait(pltpu.get_barrier_semaphore(), DEVICES - 1)


def greet(targets):
    barrier = pltpu.get_barrier_semaphore()
    for target in targets:
        pl.semaphore_signal(barrier, inc=1, device_id=target, device_id_type=MESH)


def await_greeted(count):
    pl.semaphore_wait(pltpu.get_barrier_semaphore(), count)


def remote(source, landing, sems, index, target):
    return pltpu.make_async_remote_copy(
        src_ref=source,
        dst_ref=landing,
        send_sem=sems.at[0, index],
        recv_sem=sems.at[1, index],
        device_id=target,
        device_id_type=MESH,
    )


def arrived(landing, sem):
    pltpu.make_async_copy(landing, landing, sem).wait()


class Move:
    def __init__(self, place, source, landing, send_sem, recv_sem, target, valid=None):
        here = place.is_me(target)
        away = jnp.logical_not(here)
        if valid is not None:
            here, away = jnp.logical_and(here, valid), jnp.logical_and(away, valid)
        self.away = away
        self.copy = pltpu.make_async_remote_copy(
            src_ref=source,
            dst_ref=landing,
            send_sem=send_sem,
            recv_sem=recv_sem,
            device_id=target,
            device_id_type=MESH,
        )

        @pl.when(here)
        def _():
            pltpu.make_async_copy(source, landing, recv_sem).start()

        @pl.when(away)
        def _():
            self.copy.start()

    def sent(self):
        @pl.when(self.away)
        def _():
            self.copy.wait_send()


class Gather:
    def __init__(self, place, out, sems, near_first=False):
        p = place
        step, turn = (0, 1) if near_first else (1 - p.core, p.core)
        x1, near1 = p.x + step * (1 - 2 * p.x), p.near + turn * (1 - 2 * p.near)
        x2, near2 = p.x + turn * (1 - 2 * p.x), p.near + step * (1 - 2 * p.near)
        self.out, self.sems, self.me = out, sems, p.me
        self.first = p.target(x=x1, near=near1)
        self.second = p.target(x=x2, near=near2)
        self.other = p.target(core=1 - p.core)
        self.of_first = p.member(x=x1, near=near1)
        self.of_second = p.member(x=x2, near=near2)
        self.of_both = p.member(x=1 - p.x, near=1 - p.near)
        self.copies = {}

    def _go(self, name, index, block, target):
        item = remote(self.out.at[block], self.out.at[block], self.sems, index, target)
        item.start()
        self.copies[name] = item

    def begin(self):
        self._go("a", 0, self.me, self.first)
        self._go("b", 1, self.me, self.second)
        self._go("c", 2, self.me, self.other)

    def begin_from(self, own):
        for name, index, target in (
            ("a", 0, self.first), ("b", 1, self.second), ("c", 2, self.other),
        ):
            item = remote(own, self.out.at[self.me], self.sems, index, target)
            item.start()
            self.copies[name] = item

    def second_hop(self):
        self.copies["a"].wait_recv()
        self._go("d", 3, self.of_first, self.second)
        self._go("e", 4, self.of_first, self.other)

    def third_hop(self):
        self.copies["b"].wait_recv()
        self._go("f", 5, self.of_second, self.other)

    def last_hop(self):
        self.copies["d"].wait_recv()
        self._go("g", 6, self.of_both, self.other)

    def finish(self):
        for name in "cefg":
            self.copies[name].wait_recv()
        for item in self.copies.values():
            item.wait_send()


class Spread:
    def __init__(self, place, at, sems, first, source=None):
        p = place
        self.at, self.sems, self.first = at, sems, first
        self.mine, self.theirs = at(p.far, p.y), at(1 - p.far, p.y)
        self.source = self.mine if source is None else source
        self.to_far, self.to_y = p.target(far=1 - p.far), p.target(y=1 - p.y)

    def begin(self):
        self.a = remote(self.source, self.mine, self.sems, self.first, self.to_far)
        self.b = remote(self.source, self.mine, self.sems, self.first + 1, self.to_y)
        self.a.start()
        self.b.start()

    def middle(self):
        self.a.wait_recv()
        self.c = remote(self.theirs, self.theirs, self.sems, self.first + 2, self.to_y)
        self.c.start()

    def finish(self):
        self.b.wait_recv()
        self.c.wait_recv()
        for item in (self.a, self.b, self.c):
            item.wait_send()


def shard_of(third):
    shard = third // 3
    return (shard // MEMBERS, shard % MEMBERS), third % 3


def lookup(table, index):
    result = 0
    for place, entry in enumerate(table):
        if entry:
            result = result + jnp.where(index == place, entry, 0)
    return result


FC_OF_GROUP = (
    (0, 1, 16, 17, 18, 22, 23, 24),
    (2, 3, 19, 20, 21, 25, 26, 27),
    (4, 5, 6, 10, 11, 12, 28, 29),
    (7, 8, 9, 13, 14, 15, 30, 31),
)
FC_SLOT = [0] * 32
FC_Y = [0] * 32
for _group, _units in enumerate(FC_OF_GROUP):
    for _slot, _unit in enumerate(_units):
        FC_SLOT[_unit] = _slot
        FC_Y[_unit] = _group % 2


def fc_unit(far, y, slot):
    return lookup([units[slot] for units in FC_OF_GROUP], 2 * far + y)


def fc_home(place, unit):
    return lookup(FC_SLOT, unit), lookup(FC_Y, unit)


PROJ_OF_CTX = (
    (8, 9, 10, 3),
    (11, 12, 13, 6),
    (14, 15, 16, 2),
    (17, 18, 19, 5),
    (20, 21, 22, 0),
    (1, 23, 24, 25),
    (4, 26, 27, 28),
    (7, 29, 30, 31),
)


def hidden_of(member):
    core, near, x = member // 4, member // 2 % 2, member % 2
    return [
        PROJ_OF_CTX[4 * far + 2 * near + y][2 * core + x] for y in range(2) for far in range(2)
    ]


HIDDEN = [hidden_of(_member) for _member in range(8)]
HOLDER = {unit: (m, i) for m, units in enumerate(HIDDEN) for i, unit in enumerate(units)}
PROJ_FSDP, PROJ_CTX = [0] * 32, [0] * 32
PROJ_UNIT = [0] * 32
for _ctx, _units in enumerate(PROJ_OF_CTX):
    for _place, _unit in enumerate(_units):
        _fsdp = 2 * (_place % 2) + _place // 2
        PROJ_FSDP[_unit], PROJ_CTX[_unit] = _fsdp, _ctx
        PROJ_UNIT[8 * _fsdp + _ctx] = _unit
FC_POSITION = [0] * 32
for _group, _units in enumerate(FC_OF_GROUP):
    for _slot, _unit in enumerate(_units):
        FC_POSITION[_unit] = 8 * _group + _slot


def piece(tile_of, col, lane, size):
    start = col % 128
    value = tile_of(col // 128)
    if start + size > 128:
        lanes = lax.broadcasted_iota(jnp.int32, value.shape, 1)
        value = jnp.where(lanes < start, tile_of(col // 128 + 1), value)
    shift = (lane - start) % 128
    return pltpu.roll(value, shift, 1) if shift else value


def join(parts):
    result = parts[0][1]
    for lane, value in parts[1:]:
        lanes = lax.broadcasted_iota(jnp.int32, value.shape, 1)
        result = jnp.where(lanes < lane, result, value)
    return result


def out_root(member):
    return jnp.where(member // 3 == 1, 1, 0)


def half_tile(flat, first, count, stride, half):
    at = half // 2
    tile = flat[pl.ds(first + at, count, stride=stride), :]
    if half % 2 == 0:
        return tile
    after = flat[pl.ds(first + at + 1, count, stride=stride), :]
    lane = lax.broadcasted_iota(jnp.int32, tile.shape, 1)
    return pltpu.roll(jnp.where(lane < HD, after, tile), HD, 1)


def lay_qkv(flat, rows, pieces, member, pair):
    count = rows.shape[1] // 2
    halves = 3 * HEADS
    for part in range(3):
        for odd in range(2):
            half = halves * odd + HEADS * part + head_start(member) + 2 * pair
            rows[part, pl.ds(odd, count, stride=2), :] = half_tile(flat, 0, count, halves, half)
    for part in range(3):
        pieces[pair, member, :, 128 * part : 128 * part + 128] = rows[part].astype(jnp.bfloat16)


def lay_fc(flat, first, pieces, part):
    count, hidden = pieces.shape[-2:]
    stride = FF // 128
    block = hidden // GROUPS

    def tile_of(tile):
        return flat[pl.ds(first + tile, count, stride=stride), :]

    for member in range(MEMBERS):
        for tile in range(-(-hidden // 128)):
            size = min(128, hidden - 128 * tile)
            parts, at = [], 128 * tile
            while at < 128 * tile + size:
                which, inside = divmod(at, block)
                length = min(block - inside, 128 * tile + size - at)
                col = block * HIDDEN[member][which] + inside
                parts.append((at - 128 * tile, piece(tile_of, col, at - 128 * tile, length)))
                at += length
            pieces[part, member, :, 128 * tile : 128 * tile + size] = join(parts)[
                :, :size
            ].astype(jnp.bfloat16)


def lay_rows(flat, first, rows, blocks, part):
    count = rows.shape[1] // 2
    width = blocks.shape[-1]
    halves = width // HD
    for odd in range(2):
        for tile in range(-(-width // 128)):
            half = halves * odd + 2 * tile
            size = min(128, width - 128 * tile)
            if size == 128 or half % 2 == 0:
                value = half_tile(flat, first, count, halves, half)
            else:
                value = pltpu.roll(
                    flat[pl.ds(first + half // 2, count, stride=halves), :], HD, 1
                )
            rows[tile, pl.ds(odd, count, stride=2), :] = value
    for tile in range(-(-width // 128)):
        size = min(128, width - 128 * tile)
        blocks[part, :, 128 * tile : 128 * tile + size] = rows[tile, :, :size].astype(
            jnp.bfloat16
        )


def wide(value):
    return value.astype(jnp.float32)


def low(value):
    return value.astype(jnp.bfloat16)


def turn(value, target):
    rows, cols = value.shape
    for first in range(0, rows, 128):
        for lane in range(0, cols, 128):
            part = value[first : first + 128, lane : lane + 128]
            target[lane : lane + 128, first : first + 128] = low(wide(part).T)


def store_halves(target, block, value):
    some = target.shape[2]
    for place in range(2):
        for half in range(2):
            first = (2 * place + half) * some
            target[half, block + place] = value[first : first + some]


def half_of(blocks, core):
    return blocks.at[pl.ds(4 * core, 4)]


class Reduce:
    def __init__(
        self, place, away, kept, from_core, two, got, last, done, sems, near_first=False
    ):
        self.p, self.away, self.kept, self.from_core = place, away, kept, from_core
        self.two, self.got, self.last, self.done, self.sems = two, got, last, done, sems
        self.route = Gather(place, None, None, near_first)
        self.copies = []

    def _go(self, source, landing, index, target):
        item = remote(source, landing, self.sems, index, target)
        item.start()
        self.copies.append(item)
        return item

    def begin(self):
        for j in (3, 2, 1, 0):
            self._go(self.away.at[j], self.from_core.at[j], j, self.route.other)

    def _summed(self, member):
        block = member - 4 * self.p.core
        return wide(self.kept[block]) + wide(self.from_core[block])

    def second(self):
        for item in self.copies[:4]:
            item.wait_recv()
        self.two[0] = low(self._summed(self.route.of_both))
        self.across = self._go(self.two.at[0], self.got.at[0], 4, self.route.second)
        self.two[1] = low(self._summed(self.route.of_second))
        self.beyond = self._go(self.two.at[1], self.got.at[1], 5, self.route.second)

    def third(self):
        self.across.wait_recv()
        self.last[...] = low(self._summed(self.route.of_first) + wide(self.got[0]))
        self.final = self._go(self.last, self.done, 6, self.route.first)

    def result(self):
        self.beyond.wait_recv()
        value = self._summed(self.p.me) + wide(self.got[1])
        self.final.wait_recv()
        return value + wide(self.done[...])

    def sent(self):
        for item in self.copies:
            item.wait_send()


def reduce_buffers(rows, width):
    kind = jnp.bfloat16
    return [
        pltpu.VMEM((4, rows, width), kind),
        pltpu.VMEM((2, rows, width), kind),
        pltpu.VMEM((2, rows, width), kind),
        pltpu.VMEM((rows, width), kind),
        pltpu.VMEM((rows, width), kind),
        pltpu.SemaphoreType.DMA((2, 7)),
    ]


def norm_rows(value, gain, shift):
    center = value - jnp.mean(value, -1, keepdims=True)
    spread = jnp.mean(center * center, -1, keepdims=True)
    return center * lax.rsqrt(spread + epsilon_norm) * gain + shift


def head_rows(member):
    return 8 * member


def member_lanes(row, member, count):
    result = jnp.zeros((row.shape[0], count), row.dtype)
    for other in range(MEMBERS):
        first = head_start(other) * HD
        result = result + jnp.where(member == other, row[:, first : first + count], 0.0)
    return result


def attend_block(query, keys, values, row_pos, col_pos):
    lanes = lane_of(query.shape)
    result = jnp.zeros(query.shape, jnp.float32)
    for head in range(2):
        mine = lanes == head
        own = jnp.where(mine, query, jnp.zeros_like(query))
        probs = probabilities(own, keys, row_pos, col_pos)
        mixed = jnp.dot(probs.astype(jnp.bfloat16), values, preferred_element_type=jnp.float32)
        result = jnp.where(mine, mixed, result)
    return result.astype(jnp.bfloat16)


def forward_kernel(
    x_in, back_in, order_in, vec_in, weights,
    back_all, vecs, row_pos, col_pos, w_qkv_out, h_first_out, qkv_out, attn, w_fc_out, w_proj_out,
    w_heads, x_own, resid_own, h_second,
    x_all, w_qkv, h_first, qkv, w_fc, w_proj,
    flat, rows, qkv_pieces, fc_pieces, blocks, order, vec_all, qkv_land,
    fc, proj, out, fc_part, fc_mine, proj_part, out_part, tail, next_tail, window, unit_rows, h_own,
    branch, core_a, two_a, got_a, last_a, done_a, sem_a,
    core_b, two_b, got_b, last_b, done_b, sem_b,
    order_pad, vec_pad, x_rows, back_rows, move_sem, qkv_sem, fc_send, fc_recv, rows_sem, x_sem, back_sem, spread_sem,
    own_sem, fc_sem, proj_sem, tree_sem, h_sem, store_sem,
):
    p = Place()
    third_rows = weights.shape[0] // 3
    width, count = x_in.shape
    length = MEMBERS * count
    pairs = SLOTS // 2
    barrier = pltpu.get_barrier_semaphore()

    def signal(step, carry):
        other = (p.linear + step) % DEVICES
        pl.semaphore_signal(
            barrier, inc=1, device_id=(other // MEMBERS, other % MEMBERS), device_id_type=MESH
        )
        return carry

    lax.fori_loop(1, DEVICES, signal, 0)
    flat[...] = weights[...].astype(jnp.float32)
    order_pad[...] = jnp.zeros_like(order_pad)
    order_pad[0:1, : order_in.shape[1]] = order_in[...]
    vec_pad[...] = jnp.zeros_like(vec_pad)
    vec_pad[: vec_in.shape[0], : vec_in.shape[1]] = vec_in[...]
    pl.semaphore_wait(barrier, DEVICES - 1)
    home, home_member = p.group_home()
    owner = p.fsdp == 0
    qkv_moves = []
    for pair in range(pairs):
        for member in (7, 6, 3, 2, 5, 4, 1, 0):

            @pl.when(owner)
            def _(member=member, pair=pair):
                lay_qkv(flat, rows, qkv_pieces, member, pair)

            target = p.target(x=member % 2, near=member // 2 % 2, core=member // 4)
            qkv_moves.append(
                Move(
                    p, qkv_pieces.at[pair, member], qkv_land.at[pair, p.far, p.near, p.y],
                    qkv_sem.at[0, pair, member], qkv_sem.at[1, pair, p.near], target, owner,
                )
            )
    turn(x_in[...], x_rows)
    x_move = Move(p, x_rows, x_all.at[home_member], move_sem.at[0, 0], move_sem.at[1, 0], home)
    order_move = Move(p, order_pad, order, move_sem.at[0, 1], move_sem.at[1, 1], home)
    turn(back_in[...], back_rows)

    def vec_send(step, carry):
        other = (p.linear + step) % DEVICES
        pltpu.make_async_remote_copy(
            src_ref=vec_pad,
            dst_ref=vec_all.at[p.linear],
            send_sem=move_sem.at[0, 2],
            recv_sem=move_sem.at[1, 2],
            device_id=(other // MEMBERS, other % MEMBERS),
            device_id_type=MESH,
        ).start()
        return carry

    lax.fori_loop(1, DEVICES, vec_send, 0)
    pltpu.make_async_copy(vec_pad, vec_all.at[p.linear], move_sem.at[1, 2]).start()
    for part in range(3):
        third = 3 * p.linear + part
        is_fc = jnp.logical_and(third >= FC_FIRST, third < PROJ_FIRST)
        is_rows = jnp.logical_and(third >= OUT_FIRST, jnp.logical_not(is_fc))

        @pl.when(is_fc)
        def _(part=part):
            lay_fc(flat, part * third_rows, fc_pieces, part)

        @pl.when(is_rows)
        def _(part=part):
            lay_rows(flat, part * third_rows, rows, blocks, part)

    arrived(x_all.at[p.me], move_sem.at[1, 0])
    gather_x = Gather(p, x_all, x_sem, True)
    gather_x.begin()
    spreads = []

    def spread(pair):
        for near in range(2):
            arrived(qkv_land.at[pair, p.far, near, p.y], qkv_sem.at[1, pair, near])
            item = Spread(
                p, lambda far, y, near=near: qkv_land.at[pair, far, near, y],
                spread_sem, 6 * pair + 3 * near,
            )
            item.begin()
            spreads.append(item)

    spread(0)
    gather_x.second_hop()
    spread(1)
    gather_x.third_hop()
    fc_moves, rows_moves = [], []
    for part in range(3):
        third = 3 * p.linear + part
        valid = jnp.logical_and(third >= OUT_FIRST, third < FC_FIRST)
        member = jnp.where(valid, third - OUT_FIRST, 0)
        target = p.target(
            x=member % 2, near=member // 2 % 2, core=member // 4, y=out_root(member), far=0
        )
        rows_moves.append(
            Move(
                p, blocks.at[part], out_part,
                rows_sem.at[0, part], rows_sem.at[1, 1], target, valid,
            )
        )
    for part in range(3):
        third = 3 * p.linear + part
        valid = jnp.logical_and(third >= FC_FIRST, third < PROJ_FIRST)
        slot, y = fc_home(p, jnp.where(valid, third - FC_FIRST, 0))
        for member in (7, 6, 3, 2, 5, 4, 1, 0):
            target = p.target(x=member % 2, near=member // 2 % 2, core=member // 4, y=y)
            fc_moves.append(
                Move(
                    p, fc_pieces.at[part, member], fc_part.at[slot],
                    fc_send.at[part, member], fc_recv.at[slot], target, valid,
                )
            )
    for part in range(3):
        third = 3 * p.linear + part
        valid = third >= PROJ_FIRST
        unit = jnp.where(valid, third - PROJ_FIRST, 0)
        target = (lookup(PROJ_FSDP, unit), lookup(PROJ_CTX, unit))
        rows_moves.append(
            Move(
                p, blocks.at[part], proj_part,
                rows_sem.at[0, part], rows_sem.at[1, 0], target, valid,
            )
        )
    gather_x.last_hop()
    back_move = Move(p, back_rows, back_all.at[home_member], move_sem.at[0, 3], move_sem.at[1, 3], home)
    arrived(vec_all, move_sem.at[1, 2])
    cols = vec_pad.shape[-1]
    used = width // MEMBERS
    total = jnp.zeros(vecs.shape, jnp.float32)
    for ctx in range(MEMBERS):
        block = jnp.concatenate([vec_all[MEMBERS * f + ctx] for f in range(GROUPS)], 0)
        lane = lax.broadcasted_iota(jnp.int32, (cols, width), 0)
        at = lax.broadcasted_iota(jnp.int32, (cols, width), 1) - used * ctx
        spot = jnp.where(jnp.logical_and(lane == at, lane < used), 1.0, 0.0)
        total = total + jnp.dot(
            block, spot.astype(jnp.bfloat16), preferred_element_type=jnp.float32
        )
    vecs[...] = total
    arrived(order, move_sem.at[1, 1])
    slots = order[0:1, :].astype(jnp.float32)
    lane = lax.broadcasted_iota(jnp.int32, (length, 128), 1)
    row = lax.broadcasted_iota(jnp.int32, (length, 128), 0)
    each = count // BLOCK

    def slot_of(row):
        member = row // count
        turned = (member % 2 + member // 4 + p.far) % 2
        return each * (member - member % 2 + turned) + row // BLOCK % each

    spot = jnp.where(lane == slot_of(row), slots, 0.0)
    inner = lax.broadcasted_iota(jnp.int32, (length, 1), 0) % BLOCK
    row_pos[...] = jnp.sum(spot, 1, keepdims=True) * BLOCK + inner.astype(jnp.float32)
    lane = lax.broadcasted_iota(jnp.int32, (128, length), 1)
    row = lax.broadcasted_iota(jnp.int32, (128, length), 0)
    spot = jnp.where(row == slot_of(lane), 1.0, 0.0)
    inner = lax.broadcasted_iota(jnp.int32, (1, length), 1) % BLOCK
    found = jnp.dot(
        order[...].astype(jnp.bfloat16), spot.astype(jnp.bfloat16),
        preferred_element_type=jnp.float32,
    )
    col_pos[...] = found[0:1, :] * BLOCK + inner.astype(jnp.float32)
    for item in spreads[:2]:
        item.middle()
    to_far, to_y = p.target(far=1 - p.far), p.target(y=1 - p.y)
    same_y = p.y == out_root(p.me)
    root = jnp.logical_and(same_y, p.far == 0)
    beside = jnp.logical_and(same_y, p.far == 1)
    out_far = remote(out_part, out, tree_sem, 0, to_far)
    out_y = remote(out_part, out, tree_sem, 1, to_y)
    out_later = remote(out, out, tree_sem, 2, to_y)
    out_own = pltpu.make_async_copy(out_part, out, own_sem.at[8])

    @pl.when(root)
    def _():
        arrived(out_part, rows_sem.at[1, 1])
        out_far.start()
        out_y.start()
        out_own.start()

    gather_x.finish()

    def norm_block(step, carry):
        value = norm_rows(x_all[step].astype(jnp.float32), vecs[0:1, :], vecs[1:2, :])
        h_first[pl.ds(pl.multiple_of(step * count, count), count), :] = value.astype(jnp.bfloat16)
        return carry

    lax.fori_loop(0, MEMBERS, norm_block, 0)
    x_own[...] = x_all[p.me]
    stores = []

    def store(source, target):
        copy = pltpu.make_async_copy(source, target, store_sem.at[len(stores)])
        copy.start()
        stores.append(copy)

    store(h_first, h_first_out)
    four = qkv_land.shape[4]
    per_part = SLOTS * HD
    bias_q = member_lanes(vecs[2:3, :], p.me, per_part)
    bias_v = member_lanes(vecs[16:17, :], p.me, per_part)

    def project(pair):
        columns = slice(384 * pair, 384 * pair + 384)
        for item in spreads[2 * pair : 2 * pair + 2]:
            item.finish()
        for far in range(2):
            for near in range(2):
                for y in range(2):
                    first = four * (4 * far + 2 * near + y)
                    w_qkv[first : first + four, columns] = qkv_land[pair, far, near, y]
        part = slice(128 * pair, 128 * pair + 128)
        bias = jnp.concatenate(
            [bias_q[:, part], jnp.zeros((1, 128), jnp.float32), bias_v[:, part]], 1
        )

        def qkv_block(step, carry):
            at = pl.ds(pl.multiple_of(step * 2 * count, 2 * count), 2 * count)
            value = jnp.dot(
                h_first[at, :], w_qkv[:, columns], preferred_element_type=jnp.float32
            )
            qkv[at, columns] = (value + bias).astype(jnp.bfloat16)
            return carry

        lax.fori_loop(0, MEMBERS // 2, qkv_block, 0)

    project(0)
    for item in spreads[2:]:
        item.middle()

    @pl.when(beside)
    def _():
        out_far.wait_recv()
        out_later.start()

    arrived(back_all.at[p.me], move_sem.at[1, 3])
    gather_back = Gather(p, back_all, back_sem, True)
    gather_back.begin()
    fc_spreads = []
    unit = fc_part.shape[1]
    for half in range(2):
        for slot in range(4):
            arrived(fc_part.at[4 * half + slot], fc_recv.at[4 * half + slot])
            fc_mine[half, unit * slot : unit * slot + unit, :] = fc_part[4 * half + slot]
        item = Spread(
            p, lambda far, y, half=half: fc.at[far, y, half], fc_sem, 3 * half, fc_mine.at[half]
        )
        item.begin()
        fc_spreads.append(item)
    span = 2 * count

    def one_pair(pair):
        def one_block(step, carry):
            at = pl.ds(pl.multiple_of(step * span, span), span)
            attn[pair, at, :] = attend_block(
                qkv[at, 384 * pair : 384 * pair + 128],
                qkv[:, 384 * pair + 128 : 384 * pair + 256],
                qkv[:, 384 * pair + 256 : 384 * pair + 384],
                row_pos[at, :],
                col_pos[...],
            )
            return carry

        lax.fori_loop(0, length // span, one_block, 0)

    one_pair(0)
    project(1)
    gather_back.second_hop()
    gather_back.third_hop()
    arrived(proj_part, rows_sem.at[1, 0])
    my_proj, far_proj = proj.at[p.y, p.far], proj.at[p.y, 1 - p.far]
    proj_far = remote(proj_part, my_proj, proj_sem, 0, to_far)
    proj_y = remote(proj_part, my_proj, proj_sem, 1, to_y)
    proj_far.start()
    proj_y.start()
    proj_own = pltpu.make_async_copy(proj_part, my_proj, own_sem.at[9])
    proj_own.start()
    store(w_qkv, w_qkv_out)
    store(qkv, qkv_out)

    for item in fc_spreads:
        item.middle()
    one_pair(1)
    gather_back.last_hop()

    @pl.when(root)
    def _():
        out_own.wait()

    @pl.when(jnp.logical_and(jnp.logical_not(same_y), p.far == 0))
    def _():
        out_y.wait_recv()

    @pl.when(jnp.logical_and(jnp.logical_not(same_y), p.far == 1))
    def _():
        out_later.wait_recv()

    reach = tail.shape[0]
    tail[...] = out[four - reach :, :]
    following, before = (p.me + 1) % MEMBERS, (p.me + MEMBERS - 1) % MEMBERS
    to_next = p.target(
        x=following % 2, near=following // 2 % 2, core=following // 4
    )
    send_tail = remote(tail, next_tail, tree_sem, 3, to_next)
    send_tail.start()
    begin = head_rows(p.me)
    window[...] = jnp.zeros_like(window)
    window[reach : reach + four, :] = wide(out[...])
    span_rows = SLOTS * HD
    unit_rows[...] = low(window[pl.ds(pl.multiple_of(reach - begin, 8), span_rows), :])

    def one_branch(step, carry):
        at = pl.ds(pl.multiple_of(step * span, span), span)
        heads = jnp.concatenate([attn[pair, at, :] for pair in range(pairs)], 1)
        value = low(jnp.dot(heads, unit_rows[...], preferred_element_type=jnp.float32))
        store_halves(branch, 2 * step, value)
        return carry

    lax.fori_loop(0, length // span, one_branch, 0)
    reduces = [
        Reduce(
            p, half_of(branch.at[half], 1 - p.core), half_of(branch.at[half], p.core), *buffers
        )
        for half, buffers in enumerate(
            (
                (core_a, two_a, got_a, last_a, done_a, sem_a),
                (core_b, two_b, got_b, last_b, done_b, sem_b),
            )
        )
    ]
    for item in reduces:
        item.begin()
    for item in reduces:
        item.second()
    for item in reduces:
        item.third()
    gathers = []
    some = count // 2
    for half, item in enumerate(reduces):
        at = slice(some * half, some * half + some)
        value = wide(x_own[at, :]) + item.result() + vecs[17:18, :]
        resid_own[at, :] = value
        h_own[half] = low(norm_rows(value, vecs[18:19, :], vecs[32:33, :]))
        gather = Gather(p, h_second.at[half], h_sem.at[half])
        gather.begin_from(h_own.at[half])
        gathers.append(gather)
        store(h_own.at[half], h_second.at[half, p.me])
    proj_far.wait_recv()
    proj_later = remote(far_proj, far_proj, proj_sem, 2, to_y)
    proj_later.start()
    for item in gathers:
        item.second_hop()
        item.third_hop()
    for item in fc_spreads:
        item.finish()
    for group, units in enumerate(FC_OF_GROUP):
        far, y = group // 2, group % 2
        for half in range(2):
            inside = jnp.logical_and(p.far == far, p.y == y)

            @pl.when(inside)
            def _(far=far, y=y, half=half):
                fc[far, y, half] = fc_mine[half]

            for slot in range(4):
                first = unit * units[4 * half + slot]
                w_fc[first : first + unit, :] = fc[far, y, half, unit * slot : unit * slot + unit]
    store(w_fc, w_fc_out)
    proj_y.wait_recv()
    proj_later.wait_recv()
    proj_own.wait()
    for group in range(GROUPS):
        w_proj[four * group : four * group + four, :] = proj[group // 2, group % 2]
    store(w_proj, w_proj_out)
    for item in gathers:
        item.last_hop()
    send_tail.wait_recv()
    window[:reach, :] = wide(next_tail[...])
    w_heads[...] = low(window[pl.ds(pl.multiple_of(reach - begin, 8), span_rows), :])
    for item in gathers + [gather_back]:
        item.finish()
    for item in [proj_far, proj_y, proj_later, send_tail]:
        item.wait_send()
    for item in reduces:
        item.sent()

    @pl.when(root)
    def _():
        out_far.wait_send()
        out_y.wait_send()

    @pl.when(beside)
    def _():
        out_later.wait_send()

    for copy in stores:
        copy.wait()
    for item in [x_move, order_move, back_move] + qkv_moves + fc_moves + rows_moves:
        item.sent()
    arrived(vec_all.at[pl.ds(1, DEVICES - 1)], move_sem.at[0, 2])


def forward(x, back, order, vectors, weights):
    width, rows = x.shape
    kind, high = jnp.bfloat16, jnp.float32
    unit, hidden = width // DEVICES, FF // MEMBERS
    four, cols = 4 * unit, 3 * SLOTS * HD
    length, pairs = MEMBERS * rows, SLOTS // 2
    vec_cols = -(-vectors.shape[1] // 128) * 128
    any_space = pl.BlockSpec(memory_space=pl.ANY)
    vmem = pl.BlockSpec(memory_space=pltpu.VMEM)
    dma = pltpu.SemaphoreType.DMA

    def like(*shape, dtype=kind):
        return jax.ShapeDtypeStruct(shape, dtype)

    return pl.pallas_call(
        forward_kernel,
        out_shape=[
            like(MEMBERS, rows, width),
            like(GROUPS * 16, width, dtype=high),
            like(length, 1, dtype=high),
            like(1, length, dtype=high),
            like(width, cols),
            like(length, width),
            like(length, cols),
            like(pairs, length, 2 * HD),
            like(width, hidden),
            like(hidden, width),
            like(SLOTS * HD, width),
            like(rows, width),
            like(rows, width, dtype=high),
            like(2, MEMBERS, rows // 2, width),
        ],
        in_specs=[vmem] * 5,
        out_specs=[any_space] + [vmem] * 3 + [any_space] * 3 + [vmem] + [any_space] * 2
        + [vmem] * 3 + [any_space],
        scratch_shapes=[
            pltpu.VMEM((MEMBERS, rows, width), kind),
            pltpu.VMEM((width, cols), kind),
            pltpu.VMEM((length, width), kind),
            pltpu.VMEM((length, cols), kind),
            pltpu.VMEM((width, hidden), kind),
            pltpu.VMEM((hidden, width), kind),
            pltpu.VMEM(weights.shape, high),
            pltpu.VMEM((-(-width // 128), four, 128), high),
            pltpu.VMEM((pairs, MEMBERS, four, cols // pairs), kind),
            pltpu.VMEM((3, MEMBERS, unit, hidden), kind),
            pltpu.VMEM((3, four, width), kind),
            pltpu.VMEM((128, 128), order.dtype),
            pltpu.VMEM((DEVICES, 16, vec_cols), kind),
            pltpu.VMEM((pairs, 2, 2, 2, four, cols // pairs), kind),
            pltpu.VMEM((2, 2, 2, four, hidden), kind),
            pltpu.VMEM((2, 2, four, width), kind),
            pltpu.VMEM((four, width), kind),
            pltpu.VMEM((8, unit, hidden), kind),
            pltpu.VMEM((2, four, hidden), kind),
            pltpu.VMEM((four, width), kind),
            pltpu.VMEM((four, width), kind),
            pltpu.VMEM((64, width), kind),
            pltpu.VMEM((64, width), kind),
            pltpu.VMEM((64 + SLOTS * HD, width), high),
            pltpu.VMEM((SLOTS * HD, width), kind),
            pltpu.VMEM((2, rows // 2, width), kind),
            pltpu.VMEM((2, MEMBERS, rows // 2, width), kind),
        ]
        + reduce_buffers(rows // 2, width)
        + reduce_buffers(rows // 2, width)
        + [
            pltpu.VMEM((128, 128), order.dtype),
            pltpu.VMEM((16, vec_cols), kind),
            pltpu.VMEM((rows, width), kind),
            pltpu.VMEM((rows, width), kind),
            dma((2, 4)),
            dma((2, pairs, 8)),
            dma((3, 8)),
            dma((8,)),
            dma((2, 3)),
            dma((2, 7)),
            dma((2, 7)),
            dma((2, 12)),
            dma((9 + 1,)),
            dma((2, 6)),
            dma((2, 3)),
            dma((2, 4)),
            dma((2, 2, 7)),
            dma((7,)),
        ],
        compiler_params=pltpu.CompilerParams(
            collective_id=1, has_side_effects=True, vmem_limit_bytes=VMEM_BYTES
        ),
        name="forward",
    )(x, back, order, vectors, weights)


GELU_SCALE = 0.7978845608028654
GELU_CUBE = 0.044715


def store_rows(target, first, value, lanes=slice(None), at=None, unit=None):
    places = at
    size = target.shape[1] if unit is None else unit
    row = 0
    while row < value.shape[0]:
        block, at = divmod(first + row, size)
        count = min(size - at, value.shape[0] - row)
        if places is None:
            target[block, at : at + count, lanes] = low(value[row : row + count])
        else:
            four = target.shape[1]
            block, place = divmod(size * places[block], four)
            at = at + place
            target[block, at : at + count, lanes] = low(value[row : row + count])
        row += count


def middle_kernel(
    h_in, back_all, vecs, resid_own, w_fc_in, w_proj_in,
    grad_fc, proj_sum, made, dresid, branch_all, sums, fc_sums,
    h_second, back, w_fc, w_proj, act, dpre, dh_part, made_part, g_fc, g_proj,
    proj_y, proj_go, proj_far, core_a, two_a, got_a, last_a, done_a, sem_a,
    core_b, two_b, got_b, last_b, done_b, sem_b,
    load_sem, store_sem, fold_sem,
    dbranch, branch_sem,
):
    p = Place()
    length, width = h_second.shape
    count = length // MEMBERS
    hidden = act.shape[1]
    loads = []

    def load(source, target):
        copy = pltpu.make_async_copy(source, target, load_sem.at[len(loads)])
        copy.start()
        loads.append(copy)

    some = count // 2
    for member in range(MEMBERS):
        for half in range(2):
            first = count * member + some * half
            load(h_in.at[half, member], h_second.at[pl.ds(first, some)])
    load(w_fc_in, w_fc)
    load(back_all, back)
    load(w_proj_in, w_proj)
    reduces = [
        Reduce(
            p, half_of(dh_part.at[half], 1 - p.core), half_of(dh_part.at[half], p.core), *buffers
        )
        for half, buffers in enumerate(
            (
                (core_a, two_a, got_a, last_a, done_a, sem_a),
                (core_b, two_b, got_b, last_b, done_b, sem_b),
            )
        )
    ]
    route = reduces[0].route
    to_far, to_y = p.target(far=1 - p.far), p.target(y=1 - p.y)
    greet((route.first, route.second, route.other, to_far, to_y))
    bias_fc = jnp.zeros((1, hidden), jnp.float32)
    block = hidden // GROUPS
    for member in range(MEMBERS):
        parts = []
        for unit in HIDDEN[member]:
            row, first = divmod(block * unit, width)
            row = (34, 48, 49, 50)[row]
            parts.append(vecs[row : row + 1, first : first + block])
        bias_fc = bias_fc + jnp.where(p.me == member, jnp.concatenate(parts, 1), 0.0)
    fc_sums[...] = jnp.zeros_like(fc_sums)
    for copy in loads:
        copy.wait()
    span = 2 * count

    def one_block(step, carry):
        at = pl.ds(pl.multiple_of(step * span, span), span)
        normed = h_second[at, :]
        pre = jnp.dot(normed, w_fc[...], preferred_element_type=jnp.float32) + bias_fc
        square = pre * pre
        slope = jnp.tanh(GELU_SCALE * (pre + GELU_CUBE * pre * square))
        act[at, :] = low(0.5 * pre * (1.0 + slope))
        tilt = 0.5 * (1.0 + slope) + 0.5 * pre * (1.0 - slope * slope) * GELU_SCALE * (
            1.0 + 3.0 * GELU_CUBE * square
        )
        dpre_block = low(dot_nt(back[at, :], w_proj[...]) * tilt)
        dpre[at, :] = dpre_block
        fc_sums[...] += jnp.sum(wide(dpre_block), 0, keepdims=True)
        value = low(dot_nt(dpre_block, w_fc[...]))
        store_halves(dh_part, 2 * step, value)
        return carry

    lax.fori_loop(0, MEMBERS // 2, one_block, 0)
    await_greeted(5)
    for item in reduces:
        item.begin()

    def one_made(step, carry):
        at = pl.ds(pl.multiple_of(step * span, span), span)
        value = low(jnp.dot(act[at, :], w_proj[...], preferred_element_type=jnp.float32))
        made_part[2 * step] = value[:count]
        made_part[2 * step + 1] = value[count:]
        return carry

    lax.fori_loop(0, MEMBERS // 2, one_made, 0)
    for item in reduces:
        item.second()
    stores = [pltpu.make_async_copy(made_part, made, store_sem.at[2])]
    stores[0].start()
    chunk = 256

    def one_proj(step, carry):
        lanes = pl.ds(pl.multiple_of(step * chunk, chunk), chunk)
        store_rows(g_proj, 0, dot_tn(act[...], back[:, lanes]), lanes)
        return carry

    lax.fori_loop(0, width // chunk, one_proj, 0)
    tail = slice(width // chunk * chunk, width)
    if width % chunk:
        store_rows(g_proj, 0, dot_tn(act[...], back[:, tail]), tail)
    fold = Fold(
        p, lambda far: g_proj.at[2 * (1 - p.y) + far], lambda far: g_proj.at[2 * p.y + far],
        lambda far: proj_y.at[far], proj_go, proj_far, fold_sem, 0,
    )
    fold.begin()
    for item in reduces:
        item.third()
    for first in range(0, width, chunk):
        size = min(chunk, width - first)
        store_rows(
            g_fc, first, dot_tn(h_second[:, first : first + size], dpre[...]), at=FC_POSITION,
            unit=width // DEVICES,
        )
    fold.rest()
    fold.middle()
    stores.append(pltpu.make_async_copy(g_fc, grad_fc, store_sem.at[0]))
    stores[-1].start()

    gathers = []
    sums[...] = jnp.zeros_like(sums)
    for half, item in enumerate(reduces):
        at = slice(some * half, some * half + some)
        dh = item.result()
        center = resid_own[at, :] - jnp.mean(resid_own[at, :], -1, keepdims=True)
        scale = lax.rsqrt(jnp.mean(center * center, -1, keepdims=True) + epsilon_norm)
        hat = center * scale
        first = pl.multiple_of(p.me * count + some * half, some)
        back_own = wide(back[pl.ds(first, some), :])
        scaled = dh * vecs[18:19, :]
        inner = jnp.mean(scaled * hat, -1, keepdims=True)
        value = back_own + (scaled - jnp.mean(scaled, -1, keepdims=True) - hat * inner) * scale
        dresid[at, :] = value
        part = low(value)
        dbranch[half] = part
        gather = Gather(p, branch_all.at[half], branch_sem.at[half])
        gather.begin_from(dbranch.at[half])
        gathers.append(gather)
        copy = pltpu.make_async_copy(
            dbranch.at[half], branch_all.at[half, p.me], store_sem.at[1 + 2 * half]
        )
        copy.start()
        stores.append(copy)
        sums[0:1, :] += jnp.sum(dh * hat, 0, keepdims=True)
        sums[1:2, :] += jnp.sum(dh, 0, keepdims=True)
        sums[2:3, :] += jnp.sum(wide(part), 0, keepdims=True)
        sums[3:4, :] += jnp.sum(back_own, 0, keepdims=True)
    for item in gathers:
        item.second_hop()
        item.third_hop()
    for item in gathers:
        item.last_hop()
    proj_sum[...] = fold.end()
    for item in gathers:
        item.finish()
    fold.sent()
    for item in reduces:
        item.sent()
    for copy in stores:
        copy.wait()


def middle(h_second, back_all, vecs, resid_own, w_fc, w_proj):
    kind, high = jnp.bfloat16, jnp.float32
    length, width = back_all.shape
    rows = length // MEMBERS
    hidden = w_proj.shape[0]
    four = width // MEMBERS
    any_space = pl.BlockSpec(memory_space=pl.ANY)
    vmem = pl.BlockSpec(memory_space=pltpu.VMEM)
    dma = pltpu.SemaphoreType.DMA

    def like(*shape, dtype=kind):
        return jax.ShapeDtypeStruct(shape, dtype)

    def buffer(*shape, dtype=kind):
        return pltpu.VMEM(shape, dtype)

    return pl.pallas_call(
        middle_kernel,
        out_shape=[
            like(MEMBERS, four, hidden),
            like(four, width),
            like(MEMBERS, rows, width),
            like(rows, width, dtype=high),
            like(2, MEMBERS, rows // 2, width),
            like(8, width, dtype=high),
            like(1, hidden, dtype=high),
        ],
        in_specs=[any_space] * 2 + [vmem] * 2 + [any_space] * 2,
        out_specs=[any_space, vmem, any_space, vmem, any_space] + [vmem] * 2,
        scratch_shapes=[
            buffer(length, width),
            buffer(*back_all.shape),
            buffer(*w_fc.shape),
            buffer(*w_proj.shape),
            buffer(length, hidden),
            buffer(length, hidden),
            buffer(2, MEMBERS, rows // 2, width),
            buffer(MEMBERS, rows, width),
            buffer(MEMBERS, four, hidden),
            buffer(GROUPS, four, width),
            buffer(2, four, width),
            buffer(four, width),
            buffer(four, width),
        ]
        + reduce_buffers(rows // 2, width)
        + reduce_buffers(rows // 2, width)
        + [
            dma((2 * MEMBERS + 3,)), dma((4,)), dma((2, 3)), buffer(2, rows // 2, width),
            dma((2, 2, 7)),
        ],
        compiler_params=pltpu.CompilerParams(
            collective_id=3, has_side_effects=True, vmem_limit_bytes=VMEM_BYTES
        ),
        name="middle",
    )(h_second, back_all, vecs, resid_own, w_fc, w_proj)


class Fold:
    def __init__(self, place, away, kept, landing, leaving, last, sems, first):
        p = place
        self.p, self.away, self.kept, self.landing = p, away, kept, landing
        self.leaving, self.last = leaving, last
        self.to_far, self.to_y = p.target(far=1 - p.far), p.target(y=1 - p.y)
        self.sems, self.first = sems, first

    def begin(self):
        other = 1 - self.p.far
        self.a = remote(
            self.away(other), self.landing(other), self.sems, self.first, self.to_y
        )
        self.a.start()

    def rest(self):
        far = self.p.far
        self.b = remote(
            self.away(far), self.landing(far), self.sems, self.first + 1, self.to_y
        )
        self.b.start()

    def middle(self):
        other = 1 - self.p.far
        self.a.wait_recv()
        self.leaving[...] = low(wide(self.kept(other)[...]) + wide(self.landing(other)[...]))
        self.c = remote(self.leaving, self.last, self.sems, self.first + 2, self.to_far)
        self.c.start()

    def end(self):
        far = self.p.far
        self.b.wait_recv()
        partial = wide(self.kept(far)[...]) + wide(self.landing(far)[...])
        self.c.wait_recv()
        return low(partial + wide(self.last[...]))

    def sent(self):
        for item in (self.a, self.b, self.c):
            item.wait_send()


def backward_kernel(
    branch_in, made_in, grad_fc, proj_sum, attn, qkv, row_pos, col_pos, w_heads, w_qkv_in,
    h_in, x_own, resid_own, dresid, vecs, sums, fc_sums,
    out_home, grad_home, qkv_back, fc_back, rows_back, vec_back,
    branch_all, dattn, dqkv, key_sum, value_sum, w_qkv, h_first, dh_part, made, result,
    fc_own, g_qkv, g_heads, g_out, input_grad, vec_rows, vec_go, vec_got,
    fc_y, qkv_y, out_y, fc_go, qkv_go, out_go,
    fc_far, qkv_far, out_far, fc_sum, qkv_sum, out_sum,
    core_a, two_a, got_a, last_a, done_a, sem_a, core_b, two_b, got_b, last_b, done_b, sem_b,
    core_c, two_c, got_c, last_c, done_c, sem_c,
    load_sem, fold_sem, tree_sem, vec_sem, home_sem,
    qkv_send, qkv_recv, fc_send, fc_recv, rows_send, rows_recv,
):
    p = Place()
    _, _, some, width = branch_in.shape
    count = 2 * some
    length = MEMBERS * count
    four = proj_sum.shape[0]
    pairs = SLOTS // 2
    loads = []

    def load(source, target):
        copy = pltpu.make_async_copy(source, target, load_sem.at[len(loads)])
        copy.start()
        loads.append(copy)

    for member in range(MEMBERS):
        for half in range(2):
            load(branch_in.at[half, member], branch_all.at[member, pl.ds(some * half, some)])
    load(half_of(made_in, p.core), made)
    for far in range(2):
        for near in range(2):
            load(grad_fc.at[far, p.y, near], fc_own.at[far, near])
    load(w_qkv_in, w_qkv)
    load(h_in, h_first)
    greet_all(p)
    for copy in loads[: 2 * MEMBERS]:
        copy.wait()
    span = 2 * count

    def one_dattn(step, carry):
        at = pl.ds(pl.multiple_of(step * span, span), span)
        grad = jnp.concatenate([branch_all[2 * step], branch_all[2 * step + 1]], 0)
        value = low(dot_nt(grad, w_heads[...]))
        for pair in range(pairs):
            dattn[pair, at, :] = value[:, 128 * pair : 128 * pair + 128]
        return carry

    lax.fori_loop(0, length // span, one_dattn, 0)
    for pair in range(pairs):
        total = 0.0
        for block in range(MEMBERS):
            at = slice(block * count, block * count + count)
            total = total + dot_tn(attn[pair, at, :], branch_all[block])
        g_heads[128 * pair : 128 * pair + 128, :] = total
    g_out[...] = low(g_heads[pl.ds(pl.multiple_of(head_rows(p.me), 8), four), :])
    await_all()
    fc_folds = [
        Fold(
            p, lambda far, near=near: grad_fc.at[far, 1 - p.y, near],
            lambda far, near=near: fc_own.at[far, near],
            lambda far, near=near: fc_y.at[far, near],
            fc_go.at[near], fc_far.at[near], fold_sem, 3 + 3 * near,
        )
        for near in range(2)
    ]
    qkv_folds = [
        Fold(
            p, lambda far, pair=pair: g_qkv.at[pair, pl.ds(4 * far + 2 * (1 - p.y), 2)],
            lambda far, pair=pair: g_qkv.at[pair, pl.ds(4 * far + 2 * p.y, 2)],
            lambda far, pair=pair: qkv_y.at[pair, far],
            qkv_go.at[pair], qkv_far.at[pair], fold_sem, 9 + 3 * pair,
        )
        for pair in range(pairs)
    ]
    reduce_made = Reduce(
        p, half_of(made_in, 1 - p.core), made, core_a, two_a, got_a, last_a, done_a, sem_a
    )
    reduce_made.begin()
    target, part = shard_of(PROJ_FIRST + lookup(PROJ_UNIT, p.linear))
    moves = [
        Move(p, proj_sum, rows_back.at[part], rows_send.at[0], rows_recv.at[part], target)
    ]
    for item in fc_folds:
        item.begin()
    for copy in loads[2 * MEMBERS :]:
        copy.wait()
    def one_pair(pair):
        key_sum[...] = jnp.zeros_like(key_sum)
        value_sum[...] = jnp.zeros_like(value_sum)

        def columns(part):
            return slice(384 * pair + 128 * part, 384 * pair + 128 * part + 128)

        def one_block(step, carry):
            at = pl.ds(pl.multiple_of(step * span, span), span)
            query, grad = qkv[at, columns(0)], dattn[pair, at, :]
            keys, values = qkv[:, columns(1)], qkv[:, columns(2)]
            lanes = lane_of(query.shape)
            total = jnp.zeros(query.shape, jnp.float32)
            add_keys = add_values = 0.0
            for head in range(2):
                mine = lanes == head
                own = jnp.where(mine, query, jnp.zeros_like(query))
                own_grad = jnp.where(mine, grad, jnp.zeros_like(grad))
                probs = probabilities(own, keys, row_pos[at, :], col_pos[...])
                dprobs = dot_nt(own_grad, values)
                delta = jnp.sum(probs * dprobs, -1, keepdims=True)
                dscores = low(probs * (dprobs - delta))
                mixed = jnp.dot(dscores, keys, preferred_element_type=jnp.float32)
                total = jnp.where(mine, mixed, total)
                add_keys = add_keys + dot_tn(dscores, own)
                add_values = add_values + dot_tn(low(probs), own_grad)
            dqkv[at, columns(0)] = low(total * 0.125)
            key_sum[...] += add_keys
            value_sum[...] += add_values
            return carry

        lax.fori_loop(0, length // span, one_block, 0)
        dqkv[:, columns(1)] = low(key_sum[...] * 0.125)
        dqkv[:, columns(2)] = low(value_sum[...])

    chunk = 256

    def one_grad(pair):
        columns = slice(384 * pair, 384 * pair + 384)
        for first in range(0, width, chunk):
            size = min(chunk, width - first)
            value = dot_tn(h_first[:, first : first + size], dqkv[:, columns])
            store_rows(g_qkv.at[pair], first, value, at=(0, 2, 1, 3, 4, 6, 5, 7))
        qkv_folds[pair].begin()

    reduce_made.second()
    one_pair(0)
    reduce_made.third()
    one_grad(0)
    for item in fc_folds:
        item.middle()
    for item in fc_folds:
        item.rest()
    one_pair(1)
    for part in range(3):
        last = 384 * (pairs - 1) + 128 * part
        value = dqkv[:, last : last + 128]
        keep = jnp.logical_or(lane_of(value.shape) == 0, p.me == MEMBERS - 1)
        dqkv[:, last : last + 128] = jnp.where(keep, value, jnp.zeros_like(value))
    one_grad(1)
    qkv_folds[0].middle()
    for item in qkv_folds:
        item.rest()

    def one_part(step, carry):
        at = pl.ds(pl.multiple_of(step * span, span), span)
        value = low(dot_nt(dqkv[at, :], w_qkv[...]))
        store_halves(dh_part, 2 * step, value)
        return carry

    lax.fori_loop(0, length // span, one_part, 0)
    reduces = [
        Reduce(
            p, half_of(dh_part.at[half], 1 - p.core), half_of(dh_part.at[half], p.core),
            *buffers, True,
        )
        for half, buffers in enumerate(
            (
                (core_b, two_b, got_b, last_b, done_b, sem_b),
                (core_c, two_c, got_c, last_c, done_c, sem_c),
            )
        )
    ]
    for item in reduces:
        item.begin()
    home = p.shard_home()
    turn(low(resid_own[...] + reduce_made.result() + vecs[33:34, :]), result)
    moves.append(Move(p, result, out_home, home_sem.at[0, 0], home_sem.at[1, 0], home))
    for item in reduces:
        item.second()
    root_y = out_root(p.me)
    same_y = p.y == root_y
    root = jnp.logical_and(same_y, p.far == 0)
    beside = jnp.logical_and(same_y, p.far == 1)
    over_y = remote(g_out, out_y, tree_sem, 0, p.target(y=1 - p.y))
    over_far = remote(out_go, out_far, tree_sem, 1, p.target(far=1 - p.far))

    @pl.when(jnp.logical_not(same_y))
    def _():
        over_y.start()

    qkv_folds[1].middle()
    for item in reduces:
        item.third()
    for near in range(2):
        block = fc_folds[near].end()
        unit = fc_sum.shape[2]
        for slot in range(4):
            fc_sum[near, slot] = block[unit * slot : unit * slot + unit]
            target, part = shard_of(FC_FIRST + fc_unit(p.far, p.y, 4 * near + slot))
            moves.append(
                Move(
                    p, fc_sum.at[near, slot], fc_back.at[part, p.me],
                    fc_send.at[near, slot], fc_recv.at[part, p.me], target,
                )
            )

    @pl.when(same_y)
    def _():
        over_y.wait_recv()

    @pl.when(beside)
    def _():
        out_go[...] = low(wide(g_out[...]) + wide(out_y[...]))
        over_far.start()

    for pair in range(pairs):
        qkv_sum[pair] = qkv_folds[pair].end()
        for near in range(2):
            target = (0 * p.fsdp, 4 * p.far + 2 * near + p.y)
            moves.append(
                Move(
                    p, qkv_sum.at[pair, near], qkv_back.at[p.me, pair],
                    qkv_send.at[pair, near], qkv_recv.at[p.me, pair], target,
                )
            )
    dh = jnp.concatenate([item.result() for item in reduces], 0)
    x = wide(x_own[...])
    center = x - jnp.mean(x, -1, keepdims=True)
    scale = lax.rsqrt(jnp.mean(center * center, -1, keepdims=True) + epsilon_norm)
    hat = center * scale
    scaled = dh * vecs[0:1, :]
    inner = jnp.mean(scaled * hat, -1, keepdims=True)
    value = (scaled - jnp.mean(scaled, -1, keepdims=True) - hat * inner) * scale
    turn(low(dresid[...] + value), input_grad)
    moves.append(Move(p, input_grad, grad_home, home_sem.at[0, 1], home_sem.at[1, 1], home))
    bias_sums = jnp.sum(wide(dqkv[...]), 0, keepdims=True)

    def placed(value, starts, me):
        total = jnp.zeros((1, width), jnp.float32)
        for index, start in enumerate(starts):
            parts = [value]
            if start:
                parts.insert(0, jnp.zeros((1, start), jnp.float32))
            after = width - start - value.shape[1]
            if after:
                parts.append(jnp.zeros((1, after), jnp.float32))
            row = jnp.concatenate(parts, 1) if len(parts) > 1 else value
            total = total + jnp.where(me == index, row, 0.0)
        return total

    heads = [head_start(member) * HD for member in range(MEMBERS)]
    vec_rows[0:1, :] = jnp.sum(dh * hat, 0, keepdims=True)
    vec_rows[1:2, :] = jnp.sum(dh, 0, keepdims=True)
    for row, part in ((2, 0), (3, 2)):
        value = jnp.concatenate(
            [
                bias_sums[:, 384 * pair + 128 * part : 384 * pair + 128 * part + 128]
                for pair in range(pairs)
            ],
            1,
        )
        vec_rows[row : row + 1, :] = placed(value, heads, p.me)
    vec_rows[4:5, :] = sums[2:3, :]
    vec_rows[5:7, :] = sums[0:2, :]
    vec_rows[7:8, :] = sums[3:4, :]
    used = width // MEMBERS
    vec_go[...] = jnp.zeros_like(vec_go)
    for f in range(GROUPS):
        for c in range(MEMBERS):
            vec_go[MEMBERS * f + c, 0:3, 0:used] = vec_rows[
                3 * f : 3 * f + 3, used * c : used * c + used
            ]
    for unit, (holder, which) in HOLDER.items():
        f, row = divmod(8 + unit // MEMBERS, 3)
        value = fc_sums[:, used * which : used * which + used]
        vec_go[MEMBERS * f + unit % MEMBERS, row : row + 1, 0:used] = jnp.where(
            p.me == holder, value, 0.0
        )

    def vec_send(step, carry):
        other = (p.linear + step) % DEVICES
        pltpu.make_async_remote_copy(
            src_ref=vec_go.at[other],
            dst_ref=vec_got.at[p.linear],
            send_sem=vec_sem.at[0],
            recv_sem=vec_sem.at[1],
            device_id=(other // MEMBERS, other % MEMBERS),
            device_id_type=MESH,
        ).start()
        return carry

    lax.fori_loop(1, DEVICES, vec_send, 0)
    pltpu.make_async_copy(vec_go.at[p.linear], vec_got.at[p.linear], vec_sem.at[1]).start()
    @pl.when(root)
    def _():
        over_far.wait_recv()
        out_sum[...] = low(wide(g_out[...]) + wide(out_y[...]) + wide(out_far[...]))

    target, part = shard_of(OUT_FIRST + p.me)
    moves.append(
        Move(p, out_sum, rows_back.at[part], rows_send.at[1], rows_recv.at[part], target, root)
    )
    arrived(vec_got, vec_sem.at[1])
    vec_back[...] = jnp.sum(vec_got[...], 0)

    @pl.when(p.fsdp == 0)
    def _():
        for member in range(MEMBERS):
            for pair in range(pairs):
                arrived(qkv_back.at[member, pair], qkv_recv.at[member, pair])

    for part in range(3):
        third = 3 * p.linear + part
        is_fc = jnp.logical_and(third >= FC_FIRST, third < PROJ_FIRST)
        is_rows = jnp.logical_and(third >= OUT_FIRST, jnp.logical_not(is_fc))

        @pl.when(is_fc)
        def _(part=part):
            for member in range(MEMBERS):
                arrived(fc_back.at[part, member], fc_recv.at[part, member])

        @pl.when(is_rows)
        def _(part=part):
            arrived(rows_back.at[part], rows_recv.at[part])

    arrived(out_home, home_sem.at[1, 0])
    arrived(grad_home, home_sem.at[1, 1])
    arrived(vec_got.at[pl.ds(1, DEVICES - 1)], vec_sem.at[0])
    for item in [reduce_made] + reduces + fc_folds + qkv_folds + moves:
        item.sent()

    @pl.when(jnp.logical_not(same_y))
    def _():
        over_y.wait_send()

    @pl.when(beside)
    def _():
        over_far.wait_send()


def backward(
    branch_all, made, grad_fc, proj_sum, attn, qkv, row_pos, col_pos, w_heads, w_qkv,
    h_first, x_own, resid_own, dresid, vecs, sums, fc_sums,
):
    kind, high = jnp.bfloat16, jnp.float32
    rows, width = x_own.shape
    length = MEMBERS * rows
    four, cols = width // MEMBERS, qkv.shape[1]
    unit, hidden = four // 4, fc_sums.shape[1]
    per_part = SLOTS * HD
    any_space = pl.BlockSpec(memory_space=pl.ANY)
    vmem = pl.BlockSpec(memory_space=pltpu.VMEM)
    dma = pltpu.SemaphoreType.DMA

    def like(*shape, dtype=kind):
        return jax.ShapeDtypeStruct(shape, dtype)

    def buffer(*shape, dtype=kind):
        return pltpu.VMEM(shape, dtype)

    used = -(-width // MEMBERS // 128) * 128
    return pl.pallas_call(
        backward_kernel,
        out_shape=[
            like(width, rows),
            like(width, rows),
            like(MEMBERS, 2, four, cols // 2),
            like(3, MEMBERS, unit, hidden),
            like(3, four, width),
            like(8, used, dtype=high),
        ],
        in_specs=[any_space] * 3 + [vmem] * 6 + [any_space] * 2 + [vmem] * 6,
        out_specs=[any_space] * 5 + [vmem],
        scratch_shapes=[
            buffer(MEMBERS, rows, width),
            buffer(SLOTS // 2, length, 2 * HD),
            buffer(length, cols),
            buffer(length, 2 * HD, dtype=high),
            buffer(length, 2 * HD, dtype=high),
            buffer(*w_qkv.shape),
            buffer(*h_first.shape),
            buffer(2, MEMBERS, rows // 2, width),
            buffer(MEMBERS // 2, rows, width),
            buffer(width, rows),
            buffer(2, 2, four, hidden),
            buffer(2, MEMBERS, four, cols // 2),
            buffer(per_part, width, dtype=high),
            buffer(four, width),
            buffer(width, rows),
            buffer(16, width, dtype=high),
            buffer(DEVICES, 8, used, dtype=high),
            buffer(DEVICES, 8, used, dtype=high),
        ]
        + [
            buffer(2, 2, four, hidden),
            buffer(2, 2, 2, four, cols // 2), buffer(four, width),
            buffer(2, four, hidden), buffer(2, 2, four, cols // 2), buffer(four, width),
        ]
        + [
            buffer(2, four, hidden), buffer(2, 2, four, cols // 2), buffer(four, width),
        ]
        + [
            buffer(2, 4, unit, hidden), buffer(2, 2, four, cols // 2), buffer(four, width),
        ]
        + reduce_buffers(rows, width)
        + reduce_buffers(rows // 2, width)
        + reduce_buffers(rows // 2, width)
        + [
            dma((2 * MEMBERS + 8,)),
            dma((2, 15)),
            dma((2, 2)),
            dma((2,)),
            dma((2, 2)),
            dma((2, 2)),
            dma((8, 2)),
            dma((2, 4)),
            dma((3, 8)),
            dma((2,)),
            dma((3,)),
        ],
        compiler_params=pltpu.CompilerParams(
            collective_id=2, has_side_effects=True, vmem_limit_bytes=VMEM_BYTES
        ),
        name="backward",
    )(
        branch_all, made, grad_fc, proj_sum, attn, qkv, row_pos, col_pos, w_heads, w_qkv,
        h_first, x_own, resid_own, dresid, vecs, sums, fc_sums,
    )


def lane_of(shape):
    return lax.broadcasted_iota(jnp.int32, shape, 1) // HD


def dot_nt(a, b):
    return lax.dot_general(a, b, (((1,), (1,)), ((), ())), preferred_element_type=jnp.float32)


def dot_tn(a, b):
    return lax.dot_general(a, b, (((0,), (0,)), ((), ())), preferred_element_type=jnp.float32)


def probabilities(query, keys, row_pos, col_pos):
    scores = dot_nt(query, keys) * 0.125
    scores = jnp.where(col_pos <= row_pos, scores, -1e30)
    weights = jnp.exp(scores - jnp.max(scores, -1, keepdims=True))
    return weights / jnp.sum(weights, -1, keepdims=True)


def head_place(head):
    member = max(m for m in range(MEMBERS) if head_start(m) <= head)
    return member, head - head_start(member)


def unlay_qkv(flat, tiles, back):
    count = back.shape[2] // 2
    each = 3 * SLOTS // 2
    for member in range(MEMBERS):
        for pair in range(SLOTS // 2):
            for part in range(3):
                tiles[member * each + 3 * pair + part] = wide(
                    back[member, pair, :, 128 * part : 128 * part + 128]
                )
    halves = 3 * HEADS

    def half(index, lane):
        odd, at = divmod(index, halves)
        part, head = divmod(at, HEADS)
        member, slot = head_place(head)
        tile = member * each + 3 * (slot // 2) + part
        return piece(
            lambda _: tiles[tile, pl.ds(odd, count, stride=2), :], HD * (slot % 2), lane, HD
        )

    for row in range(halves):
        flat[pl.ds(row, count, stride=halves), :] = join(
            [(0, half(2 * row, 0)), (HD, half(2 * row + 1, HD))]
        )


def unlay_fc(flat, first, tiles, back, part):
    count, hidden = back.shape[-2:]
    each = -(-hidden // 128)
    for member in range(MEMBERS):
        for tile in range(each):
            size = min(128, hidden - 128 * tile)
            tiles[member * each + tile, :count, :size] = wide(
                back[part, member, :, 128 * tile : 128 * tile + size]
            )
    stride, block = FF // 128, hidden // GROUPS
    for row in range(stride):
        parts, col = [], 128 * row
        while col < 128 * row + 128:
            unit, inside = divmod(col, block)
            size = min(block - inside, 128 * row + 128 - col)
            member, which = HOLDER[unit]
            lane = col - 128 * row
            value = piece(
                lambda t, m=member: tiles[m * each + t, :count, :],
                block * which + inside, lane, size,
            )
            parts.append((lane, value))
            col += size
        flat[pl.ds(first + row, count, stride=stride), :] = join(parts)


def unlay_rows(flat, first, tiles, back, part):
    count, width = back.shape[1] // 2, back.shape[2]
    for tile in range(-(-width // 128)):
        size = min(128, width - 128 * tile)
        tiles[tile, :, :size] = wide(back[part, :, 128 * tile : 128 * tile + size])
    halves = width // HD

    def half(index, lane):
        odd, at = divmod(index, halves)
        return piece(
            lambda t: tiles[t, pl.ds(odd, count, stride=2), :], HD * at, lane, HD
        )

    for row in range(halves):
        flat[pl.ds(first + row, count, stride=halves), :] = join(
            [(0, half(2 * row, 0)), (HD, half(2 * row + 1, HD))]
        )


def update_kernel(
    qkv_in, fc_in, rows_in, vec_back, vectors, first_vec, second_vec,
    weights, first, second,
    moment_vec, squares_vec, new_vec, moment, squares, new,
    flat, tiles, qkv_back, fc_back, rows_back, sem,
):
    step = pl.program_id(0)
    linear = lax.axis_index("fsdp") * MEMBERS + lax.axis_index("ctx")

    @pl.when(step == 0)
    def _():
        rows, cols = vectors.shape
        result = adamw(
            vectors[...], vec_back[:rows, :cols], first_vec[...], second_vec[...],
            rate_vector, 0.0,
        )
        moment_vec[...], squares_vec[...], new_vec[...] = result

        @pl.when(linear < MEMBERS)
        def _():
            copy = pltpu.make_async_copy(qkv_in, qkv_back, sem.at[0])
            copy.start()
            copy.wait()
            unlay_qkv(flat, tiles, qkv_back)

        @pl.when(linear >= MEMBERS)
        def _():
            copies = [
                pltpu.make_async_copy(fc_in, fc_back, sem.at[0]),
                pltpu.make_async_copy(rows_in, rows_back, sem.at[1]),
            ]
            for copy in copies:
                copy.start()
            for copy in copies:
                copy.wait()
            third_rows = fc_back.shape[2] * FF // 128
            for part in range(3):
                third = 3 * linear + part
                is_fc = jnp.logical_and(third >= FC_FIRST, third < PROJ_FIRST)

                @pl.when(is_fc)
                def _(part=part):
                    unlay_fc(flat, part * third_rows, tiles, fc_back, part)

                @pl.when(jnp.logical_not(is_fc))
                def _(part=part):
                    unlay_rows(flat, part * third_rows, tiles, rows_back, part)

    size = weights.shape[0]
    grad = flat[pl.ds(pl.multiple_of(step * size, 8), size), :]
    result = adamw(weights[...], grad, first[...], second[...], rate_matrix, weight_decay)
    moment[...], squares[...], new[...] = result


def update(
    qkv_back, fc_back, rows_back, vec_back, vectors, first_vec, second_vec,
    weights, first, second,
):
    high = jnp.float32
    local = weights.shape[0]
    steps = 5
    size = -(-local // (16 * steps)) * 16
    block = pl.BlockSpec((size, 128), lambda i: (i, 0))
    any_space = pl.BlockSpec(memory_space=pl.ANY)
    vmem = pl.BlockSpec(memory_space=pltpu.VMEM)
    kind = jax.ShapeDtypeStruct((local, 128), high)
    small = jax.ShapeDtypeStruct(vectors.shape, high)
    tile_count = MEMBERS * max(3 * SLOTS // 2, -(-fc_back.shape[3] // 128))
    return pl.pallas_call(
        update_kernel,
        grid=(steps,),
        in_specs=[any_space] * 3 + [vmem] * 4 + [block] * 3,
        out_specs=[vmem] * 3 + [block] * 3,
        out_shape=[small] * 3 + [kind] * 3,
        scratch_shapes=[
            pltpu.VMEM((size * steps, 128), high),
            pltpu.VMEM((tile_count, qkv_back.shape[2], 128), high),
            pltpu.VMEM(qkv_back.shape, qkv_back.dtype),
            pltpu.VMEM(fc_back.shape, fc_back.dtype),
            pltpu.VMEM(rows_back.shape, rows_back.dtype),
            pltpu.SemaphoreType.DMA((2,)),
        ],
        compiler_params=pltpu.CompilerParams(vmem_limit_bytes=VMEM_BYTES),
        name="update",
    )(
        qkv_back, fc_back, rows_back, vec_back, vectors, first_vec, second_vec, weights, first,
        second,
    )


def per_device_groups(
    inputs, cotangent, slot_order, weights, vectors, first_w, second_w, first_vec, second_vec
):
    _, rows, width = inputs.shape
    length = rows * MEMBERS
    (
        back_all, vecs, row_pos, col_pos, own_qkv, h_first, qkv, attn, own_fc, own_proj, w_heads,
        x_own, resid_own, h_second,
    ) = forward(
        inputs[0].T, cotangent[0].T, slot_order, vectors, weights
    )
    grad_fc, proj_sum, made, dresid, branch_all, sums, fc_sums = middle(
        h_second, back_all.reshape(length, width), vecs, resid_own,
        own_fc, own_proj,
    )
    out_home, grad_home, qkv_back, fc_back, rows_back, vec_back = backward(
        branch_all, made, grad_fc.reshape((2, 2, 2) + grad_fc.shape[1:]), proj_sum, attn, qkv,
        row_pos, col_pos, w_heads, own_qkv, h_first, x_own, resid_own, dresid, vecs, sums,
        fc_sums,
    )
    new = update(
        qkv_back, fc_back, rows_back, vec_back, vectors, first_vec, second_vec, weights,
        first_w, second_w,
    )
    moment_vec, squares_vec, new_vec, moment_w, squares_w, new_w = new
    return (
        out_home.T[None], grad_home.T[None], moment_w, squares_w, new_w, moment_vec, squares_vec, new_vec
    )


def solution(mesh):
    in_specs = (
        P("fsdp", "ctx", None),
        P("fsdp", "ctx", None),
        P("fsdp", None),
        P(("fsdp", "ctx"), None),
        P("fsdp", "ctx"),
        P(("fsdp", "ctx"), None),
        P(("fsdp", "ctx"), None),
        P("fsdp", "ctx"),
        P("fsdp", "ctx"),
    )
    out_specs = (
        P("fsdp", "ctx", None),
        P("fsdp", "ctx", None),
        P(("fsdp", "ctx"), None),
        P(("fsdp", "ctx"), None),
        P(("fsdp", "ctx"), None),
        P("fsdp", "ctx"),
        P("fsdp", "ctx"),
        P("fsdp", "ctx"),
    )
    per_device = per_device_groups if mesh.shape["ctx"] == MEMBERS else per_device_ring
    return jax.shard_map(
        per_device, mesh=mesh, in_specs=in_specs, out_specs=out_specs, check_vma=False
    )
```
